32 devices in a mesh: dp: 4 (over x, core), fsdp: 8 (over z, y).
Axes of the slice: x: 2, y: 2, z: 4, core: 2. Of those that a mesh axis runs over, the one named last changes fastest.
Arguments:
- patches: bfloat16 [8, 16, 197, 768], P('fsdp', 'dp'), may hold values from -64 to 64
- counts: int32 [8], P('fsdp'), may hold values from 8 to 16, as said below
- captions: bfloat16 [32, 512], P(('dp', 'fsdp')), may hold values from -6 to 6
- matches: int32 [8], P('fsdp'), may hold values from 0 to 31
- courier: bfloat16 [768, 768], P('fsdp'), may hold values from -0.21875 to 0.21875
- courier_gain: bfloat16 [768], P('fsdp'), may hold values from 0.5 to 1.5
- courier_heads: bfloat16 [768, 2304], P('fsdp'), may hold values from -0.21875 to 0.21875
- courier_merge: bfloat16 [768, 768], P('fsdp'), may hold values from -0.4375 to 0.4375
- attend_gain: bfloat16 [768], P('fsdp'), may hold values from 0.5 to 1.5
- attend_heads: bfloat16 [768, 2304], P('fsdp'), may hold values from -0.21875 to 0.21875
- attend_merge: bfloat16 [768, 768], P('fsdp'), may hold values from -0.875 to 0.875
- expand_gain: bfloat16 [768], P('fsdp'), may hold values from 0.5 to 1.5
- expand_weight: bfloat16 [768, 3072], P('fsdp'), may hold values from -0.21875 to 0.21875
- shrink_weight: bfloat16 [3072, 768], P('fsdp'), may hold values from -0.109375 to 0.109375
- projection: bfloat16 [768, 512], P('fsdp'), may hold values from -0.21875 to 0.21875
Outputs:
- loss: float32 [8], P('fsdp')
- patch_gradient: bfloat16 [8, 16, 197, 768], P('fsdp', 'dp')
- courier_gradient: float32 [768, 768], P('fsdp')
- courier_gain_gradient: float32 [768], P('fsdp')
- courier_heads_gradient: float32 [768, 2304], P('fsdp')
- courier_merge_gradient: float32 [768, 768], P('fsdp')
- attend_gain_gradient: float32 [768], P('fsdp')
- attend_heads_gradient: float32 [768, 2304], P('fsdp')
- attend_merge_gradient: float32 [768, 768], P('fsdp')
- expand_gain_gradient: float32 [768], P('fsdp')
- expand_weight_gradient: float32 [768, 3072], P('fsdp')
- shrink_weight_gradient: float32 [3072, 768], P('fsdp')
- projection_gradient: float32 [768, 512], P('fsdp')
The draws below stay inside these ranges and needn't reach their ends.
Inputs may be any that keep to these rules, and one draw needn't show every extreme that they name: `counts`: each video has 8 or 16 frames, and both occur in every draw.
All inputs are finite; a program needn't handle non-finite values.
Results may differ from the reference program's by a relative error of at most 0.018.
Values may be sent and summed in bfloat16 or wider, within the bound.
A program may use at most 192 MiB of HBM per device.

```python
import jax
import jax.numpy as jnp
from jax import lax

D = 768
HEADS = 12
HEAD = 64
MLP = 3072
EMBED = 512
PATCHES = 197
FRAMES = 16
FR_DEV = 4
VIDEOS = 8
TEXTS = 32


def draw_patches(key, part):
    noise_key, row_key, column_key = jax.random.split(key, 3)
    shape = (VIDEOS, FRAMES, PATCHES, D)
    base = jax.random.normal(noise_key, shape, jnp.float32)
    rows = jnp.exp(jax.random.uniform(row_key, (VIDEOS, FRAMES, PATCHES, 1), jnp.float32, -1.15, 1.15))
    columns = jnp.exp(jax.random.uniform(column_key, (D,), jnp.float32, -0.7, 0.7))
    return (base * rows * columns).astype(jnp.bfloat16)


def draw_counts(key, part):
    pick_key, order_key = jax.random.split(key)
    picks = jax.random.randint(pick_key, (VIDEOS,), 0, 2)
    order = jax.random.permutation(order_key, VIDEOS)
    picks = jnp.where(order == 0, 1, jnp.where(order == 1, 0, picks))
    return (FRAMES // 2 * (1 + picks)).astype(jnp.int32)


def draw_captions(key, part):
    noise_key, anchor_key = jax.random.split(jax.random.fold_in(key, 7))
    groups = FRAMES // FR_DEV
    per_group = TEXTS // groups
    anchors = jnp.clip(jax.random.normal(anchor_key, (per_group, EMBED), jnp.float32), -4.0, 4.0)
    noise = jnp.clip(jax.random.normal(noise_key, (TEXTS, EMBED), jnp.float32), -6.0, 6.0)
    index = jnp.arange(TEXTS, dtype=jnp.int32)
    group_of = index // per_group
    local = index % per_group
    distinct = jnp.maximum(per_group // jnp.left_shift(jnp.ones_like(group_of), group_of), 1)
    pick = local % distinct
    mixed = anchors[pick] + 0.2 * noise
    return mixed.astype(jnp.bfloat16)


def place_ends(values, stream_key, low, top_value):
    longest = values.shape.index(max(values.shape))
    spots = []
    for shift in (0, 1):
        where = [jax.random.randint(jax.random.fold_in(stream_key, axis), (), 0, length) for axis, length in enumerate(values.shape)]
        where[longest] = (where[longest] + shift) % values.shape[longest]
        spots.append(tuple(where))
    return values.at[spots[0]].set(low).at[spots[1]].set(top_value)


def levels(stream_key, extent, shards, low, largest):
    factor_of = 1.0
    for dim, blocks in shards:
        draws = jax.random.uniform(jax.random.fold_in(jax.random.fold_in(stream_key, 6), dim), (blocks,), jnp.float32, low / len(shards), largest / len(shards))
        factor_of = factor_of * jnp.repeat(jnp.exp(draws), extent[dim] // blocks).reshape((-1,) + (1,) * (len(extent) - 1 - dim))
    return factor_of


def normal_values(stream_key, extent, deviation, reach, shards=(), kind=jnp.bfloat16):
    values = deviation * jax.random.normal(stream_key, extent, jnp.float32)
    if shards:
        values = values * levels(stream_key, extent, shards, -0.22, 0.18)
    return jnp.clip(values, -reach, reach).astype(kind)


def setup_inputs(seed: int = 0) -> dict:
    seeds = jax.random.split(jax.random.key(seed), 16)
    return {
        "patches": draw_patches(jax.random.fold_in(seeds[15], 71), 0),
        "counts": draw_counts(jax.random.fold_in(seeds[15], 71), 0),
        "captions": draw_captions(jax.random.fold_in(seeds[15], 71), 0),
        "matches": place_ends(jax.random.randint(seeds[3], (VIDEOS,), 0, TEXTS), jax.random.fold_in(seeds[3], 1), 0, TEXTS - 1).astype(jnp.int32),
        "courier": normal_values(seeds[4], (D, D), D ** -0.5, 0.21875, ((0, 8),)),
        "courier_gain": jnp.clip(1.0 + 0.1 * jax.random.normal(seeds[5], (D,), jnp.float32), 0.5, 1.5).astype(jnp.bfloat16),
        "courier_heads": normal_values(seeds[6], (D, 3 * D), D ** -0.5, 0.21875, ((0, 8),)),
        "courier_merge": normal_values(seeds[7], (D, D), (D // 4) ** -0.5, 0.4375, ((0, 8),)),
        "attend_gain": jnp.clip(1.0 + 0.1 * jax.random.normal(seeds[8], (D,), jnp.float32), 0.5, 1.5).astype(jnp.bfloat16),
        "attend_heads": normal_values(seeds[9], (D, 3 * D), D ** -0.5, 0.21875, ((0, 8),)),
        "attend_merge": normal_values(seeds[10], (D, D), (D // 16) ** -0.5, 0.875, ((0, 8),)),
        "expand_gain": jnp.clip(1.0 + 0.1 * jax.random.normal(seeds[11], (D,), jnp.float32), 0.5, 1.5).astype(jnp.bfloat16),
        "expand_weight": normal_values(seeds[12], (D, MLP), D ** -0.5, 0.21875, ((0, 8),)),
        "shrink_weight": normal_values(seeds[13], (MLP, D), MLP ** -0.5, 0.109375, ((0, 8),)),
        "projection": normal_values(seeds[14], (D, EMBED), D ** -0.5, 0.21875, ((0, 8),)),
    }


EPSILON = 1e-05
LOGIT_SCALE = 64.0
highest = lax.Precision.HIGHEST

@jax.custom_vjp
def low(v):
    return lax.optimization_barrier(v.astype(jnp.bfloat16)).astype(jnp.float32)

@jax.custom_vjp
def low_back(v):
    return v

def low_keep(v):
    return (low(v), None)

def low_pass(kept, grad):
    return (grad,)

def back_keep(v):
    return (v, None)

def back_low(kept, grad):
    return (low(grad),)
low.defvjp(low_keep, low_pass)
low_back.defvjp(back_keep, back_low)

def layer_norm(value, gain):
    center = value - lax.optimization_barrier(jnp.mean(value, -1, keepdims=True))
    spread = lax.optimization_barrier(jnp.mean(center * center, -1, keepdims=True))
    return center * lax.rsqrt(spread + EPSILON) * gain

def product(left, right, form):
    return jnp.einsum(form, left, right, precision=highest)

def attention(mixed, key_mask, query_count):
    batch, length, triple = mixed.shape
    width = HEADS * HEAD
    queries = low(mixed[:, :query_count, :width]).reshape(batch, query_count, HEADS, HEAD)
    keys = low(mixed[:, :, width:2 * width]).reshape(batch, length, HEADS, HEAD)
    values = low(mixed[:, :, 2 * width:]).reshape(batch, length, HEADS, HEAD)
    scores = low_back(product(queries, keys, 'bqhd,bkhd->bhqk') * HEAD ** (-0.5))
    scores = jnp.where(key_mask[:, None, None, :], scores, -1000000000.0)
    shares = jax.nn.softmax(scores, -1)
    joined = low_back(product(low(shares), values, 'bhqk,bkhd->bqhd'))
    return low(joined.reshape(batch, query_count, width))

def video_pool(frames, count, params):
    courier, courier_gain, courier_heads, courier_merge, attend_gain, attend_heads, attend_merge, expand_gain, expand_weight, shrink_weight = params
    present = jnp.arange(FRAMES) < count
    message = low_back(product(frames[:, 0, :], courier, 'fd,de->fe'))
    message_mixed = low_back(product(low(layer_norm(message, courier_gain)), courier_heads, 'fd,de->fe'))
    told = attention(message_mixed[None], present[None], FRAMES)[0]
    message_out = message + low_back(product(told, courier_merge, 'fd,de->fe'))
    tokens = jnp.concatenate([frames, message_out[:, None, :]], 1)
    mixed = low_back(product(low(layer_norm(tokens, attend_gain)), attend_heads, 'ftd,de->fte'))
    everyone = jnp.ones((FRAMES, PATCHES + 1), jnp.bool_)
    seen = attention(mixed, everyone, PATCHES)
    hidden = frames + low_back(product(seen, attend_merge, 'fpd,de->fpe'))
    grown = low_back(product(low(layer_norm(hidden, expand_gain)), expand_weight, 'fpd,dm->fpm'))
    gated = low(grown * jax.nn.sigmoid(1.702 * grown))
    result = hidden + low_back(product(gated, shrink_weight, 'fpm,md->fpd'))
    frame_sums = lax.optimization_barrier(jnp.sum(result, 1))
    kept = jnp.where(present[:, None], frame_sums, 0.0)
    return lax.optimization_barrier(jnp.sum(kept, 0)) / (count * PATCHES).astype(jnp.float32)

def reference(patches, counts, captions, matches, courier, courier_gain, courier_heads, courier_merge, attend_gain, attend_heads, attend_merge, expand_gain, expand_weight, shrink_weight, projection):
    params = tuple((weight.astype(jnp.float32) for weight in (courier, courier_gain, courier_heads, courier_merge, attend_gain, attend_heads, attend_merge, expand_gain, expand_weight, shrink_weight)))
    frames_all = patches.astype(jnp.float32)
    project = projection.astype(jnp.float32)
    text = captions.astype(jnp.float32)
    text_unit = low(text * lax.rsqrt(lax.optimization_barrier(jnp.sum(text * text, -1, keepdims=True)) + 1e-06))

    def objective(frames_all, params, project):
        pool_one = jax.checkpoint(video_pool)

        def step(carry, item):
            frames, count = item
            return (carry, pool_one(frames, count, params))
        _, pooled = lax.scan(step, jnp.zeros((), jnp.float32), (frames_all, counts))
        embed = low_back(product(low(pooled), project, 'vd,de->ve'))
        unit = low(embed * lax.rsqrt(lax.optimization_barrier(jnp.sum(embed * embed, -1, keepdims=True)) + 1e-06))
        logits = low_back(product(unit, text_unit, 've,te->vt') * LOGIT_SCALE)
        normalizer = jax.nn.logsumexp(logits, -1)
        picked = jnp.take_along_axis(logits, matches[:, None].astype(jnp.int32), 1)[:, 0]
        return normalizer - picked
    loss, pull = jax.vjp(objective, frames_all, params, project)
    frame_grad, param_grads, project_grad = pull(jnp.ones_like(loss))
    return (loss, frame_grad.astype(jnp.bfloat16), param_grads[0], param_grads[1], param_grads[2], param_grads[3], param_grads[4], param_grads[5], param_grads[6], param_grads[7], param_grads[8], param_grads[9], project_grad)
```

```python
import functools

import jax
import jax.numpy as jnp
from jax import lax
from jax.experimental import pallas as pl
from jax.experimental.pallas import tpu as pltpu
from jax.sharding import PartitionSpec as P

MESH = pl.DeviceIdType.MESH
Z, Y = 4, 2
HEADS = 12
HEAD = 64
EPSILON = 1e-05
LOGIT_SCALE = 64.0
PAD = 208
ROWS = 832
D = 768
F32 = jnp.float32
B16 = jnp.bfloat16

MICRO = 2

COURIER, GAINS, CHEADS, AHEADS, CMERGE, AMERGE, EXPAND, PROJ = 0, 768, 896, 3200, 5504, 6272, 7040, 10112
NCOLS = 10624
JOBS = ((0, 896), (896, 768), (1664, 768), (2432, 768), (3200, 768), (3968, 768), (4736, 768), (5504, 768), (6272, 768),
        (7040, 768), (7808, 768), (8576, 768), (9344, 768), (10112, 512))


class Pos:
    def __init__(self):
        self.dp = lax.axis_index("dp")
        self.k = lax.axis_index("fsdp")
        self.x, self.c = self.dp // 2, lax.rem(self.dp, 2)
        self.z, self.y = self.k // Y, lax.rem(self.k, Y)
        self.core = (self.x * 2 + 1 - self.c, self.k)
        self.xp = ((1 - self.x) * 2 + self.c, self.k)
        self.cross = ((1 - self.x) * 2 + 1 - self.c, self.k)
        self.yp = (self.dp, self.z * Y + 1 - self.y)
        self.team = (self.core, self.xp, self.cross)

    def ahead(self, d):
        return lax.rem(self.z + d, Z)

    def behind(self, d):
        return lax.rem(self.z - d + Z, Z)

    def column(self):
        return [(self.dp, self.ahead(d) * Y + self.y) for d in (1, 2, 3)]

    def peers(self):
        return [self.core, self.xp, self.yp] + self.column()

    def plane(self):
        return [(self.dp, lax.rem(self.k + d, Z * Y)) for d in range(1, Z * Y)]


def barrier(peers):
    semaphore = pltpu.get_barrier_semaphore()
    for peer in peers:
        pl.semaphore_signal(semaphore, inc=1, device_id=peer, device_id_type=MESH)
    pl.semaphore_wait(semaphore, len(peers))


def remote(source, target, send, receive, device):
    return pltpu.make_async_remote_copy(
        src_ref=source, dst_ref=target, send_sem=send, recv_sem=receive, device_id=device, device_id_type=MESH)


class Gather:
    def __init__(self, p, block, jobs, send, receive):
        self.p, self.block, self.jobs, self.send, self.receive = p, block, jobs, send, receive

    def copy(self, job, index, k, first, count, device):
        ref = self.block(k, first, count, job)
        return remote(ref, ref, self.send.at[job, index], self.receive.at[job, index], device)

    def far(self, d):
        p = self.p
        return p.behind(d + 1) * Y + p.y if d < 3 else p.behind(d - 3) * Y + 1 - p.y

    def stage(self, stage, job):
        if job < 0 or job >= self.jobs:
            return
        p, copy = self.p, self.copy
        own, single = 3 * p.c + p.x, 3 * p.c + 2 * p.x
        other = 3 * p.c + 2 * (1 - p.x)
        if stage == 0:
            for d, device in enumerate(p.column()):
                copy(job, d, p.k, own, 2, device).start()
            copy(job, 3, p.k, own, 2, p.yp).start()
        elif stage == 1:
            for d in range(3):
                k = self.far(d)
                copy(job, d, k, own, 2, p.core).wait_recv()
                copy(job, 4 + d, k, own, 2, p.yp).start()
                copy(job, 7 + d, k, single, 1, p.xp).start()
                copy(job, 14 + d, k, own, 2, p.core).start()
        elif stage == 2:
            for d in range(3, 7):
                k = self.far(d)
                copy(job, d, k, own, 2, p.core).wait_recv()
                copy(job, 7 + d, k, single, 1, p.xp).start()
                copy(job, 14 + d, k, own, 2, p.core).start()
        elif stage == 3:
            for d in range(7):
                k = self.far(d)
                copy(job, 7 + d, k, other, 1, p.core).wait_recv()
                copy(job, 21 + d, k, other, 1, p.core).start()
        elif stage == 4:
            for d in range(7):
                copy(job, 14 + d, self.far(d), 3 * (1 - p.c) + p.x, 2, p.core).wait_recv()
            for d in range(7):
                copy(job, 21 + d, self.far(d), 3 * (1 - p.c) + 2 * (1 - p.x), 1, p.core).wait_recv()
        elif stage == 5:
            for index in range(28):
                copy(job, index, p.k, 0, 2 if index < 7 or 14 <= index < 21 else 1, p.core).wait_send()

    def tick(self, t, lag):
        for stage in (5, 4, 3, 2, 1, 0):
            self.stage(stage, t - lag[stage])


class Spread:
    def __init__(self, p, source, target, send, receive, same=False):
        self.p, self.target = p, target
        count = Z * Y
        self.copies = []
        for d in range(1, count):
            to = lax.rem(p.k + d, count)
            part = source if same else source.at[to]
            self.copies.append(remote(part, target.at[p.k], send.at[d - 1], receive.at[d - 1], (p.dp, to)))
        self.arrivals = []
        for d in range(1, count):
            origin = lax.rem(p.k - d + count, count)
            self.arrivals.append(
                remote(target.at[origin], target.at[origin], send.at[d - 1], receive.at[d - 1], (p.dp, origin)))
        target[p.k] = source[...] if same else source[p.k]
        for copy in self.copies:
            copy.start()

    def wait(self):
        for copy in self.arrivals:
            copy.wait_recv()

    def done(self):
        for copy in self.copies:
            copy.wait_send()


class Team:
    def __init__(self, p, source, target, send, receive):
        self.copies, self.arrivals = [], []
        target[p.dp] = source[...]
        for index, other in enumerate(p.team):
            self.copies.append(remote(source, target.at[p.dp], send.at[index], receive.at[index], other))
            self.arrivals.append(remote(source, target.at[other[0]], send.at[index], receive.at[index], other))
        for copy in self.copies:
            copy.start()

    def wait(self):
        for copy in self.arrivals:
            copy.wait_recv()

    def done(self):
        for copy in self.copies:
            copy.wait_send()


class Reduce:
    def __init__(self, p, stage, buffers, out, jobs, send, receive):
        self.p, self.stage, self.out, self.jobs, self.send, self.receive = p, stage, out, jobs, send, receive
        self.rc, self.rx, self.ry, self.rz, self.own, self.rf, self.fin, self.rcf = buffers

    def copies(self, job, step):
        p = self.p
        first, count = self.jobs[job]
        cols = pl.ds(first, count)
        half, other = pl.ds(pl.multiple_of(48 * p.c, 16), 48), pl.ds(pl.multiple_of(48 * (1 - p.c), 16), 48)
        carried = pl.ds(pl.multiple_of((3 * p.c + p.x) * 16, 16), 32)
        away = pl.ds(pl.multiple_of((3 * p.c + 2 * (1 - p.x)) * 16, 16), 16)
        s, r = self.send, self.receive
        if step == 0:
            return [remote(self.stage.at[:, other, cols], self.rc.at[:, :, cols], s.at[job, 0], r.at[job, 0], p.core)]
        if step == 1:
            return [remote(self.stage.at[:, away, cols], self.rx.at[:, :, cols], s.at[job, 1], r.at[job, 1], p.xp)]
        if step == 2:
            return [remote(self.stage.at[z * Y + 1 - p.y, carried, cols], self.ry.at[z, :, cols], s.at[job, 2 + z],
                           r.at[job, 2 + z], p.yp) for z in range(Z)]
        if step == 3:
            return [remote(self.stage.at[device[1], carried, cols], self.rz.at[d, :, cols], s.at[job, 6 + d],
                           r.at[job, 6 + d], device) for d, device in enumerate(p.column())]
        if step == 4:
            return [remote(self.own.at[:, cols], self.rf.at[:, cols], s.at[job, 9], r.at[job, 9], p.xp)]
        return [remote(self.fin.at[half, cols], self.rcf.at[:, cols], s.at[job, 10], r.at[job, 10], p.core)]

    def step(self, step, job):
        if job < 0 or job >= len(self.jobs):
            return
        p = self.p
        first, count = self.jobs[job]
        cols = pl.ds(first, count)
        if step > 0 and step < 7:
            for copy in self.copies(job, step - 1):
                copy.wait_recv()
        if step == 1:
            half = pl.ds(pl.multiple_of(48 * p.c, 16), 48)
            for k in range(Z * Y):
                self.stage[k, half, cols] = (self.stage[k, half, cols].astype(F32) + self.rc[k, :, cols].astype(F32)).astype(B16)
        elif step == 2:
            single = pl.ds(pl.multiple_of((3 * p.c + 2 * p.x) * 16, 16), 16)
            for k in range(Z * Y):
                self.stage[k, single, cols] = (self.stage[k, single, cols].astype(F32) + self.rx[k, :, cols].astype(F32)).astype(B16)
        elif step == 3:
            carried = pl.ds(pl.multiple_of((3 * p.c + p.x) * 16, 16), 32)
            for z in range(Z):
                k = z * Y + p.y
                self.stage[k, carried, cols] = (self.stage[k, carried, cols].astype(F32) + self.ry[z, :, cols].astype(F32)).astype(B16)
        elif step == 4:
            carried = pl.ds(pl.multiple_of((3 * p.c + p.x) * 16, 16), 32)
            total = self.stage[p.k, carried, cols].astype(F32)
            for d in range(3):
                total = total + self.rz[d, :, cols].astype(F32)
            self.own[:, cols] = total.astype(B16)
        elif step == 5:
            mine, theirs = self.own[:, cols].astype(F32), self.rf[:, cols].astype(F32)
            left = jnp.where(p.x == 0, mine[0:16], theirs[0:16])
            right = jnp.where(p.x == 0, theirs[16:32], mine[16:32])
            middle = jnp.where(p.x == 0, mine[16:32], mine[0:16]) + jnp.where(p.x == 0, theirs[0:16], theirs[16:32])
            half = pl.ds(pl.multiple_of(48 * p.c, 16), 48)
            self.fin[half, cols] = jnp.concatenate([left, middle, right], 0).astype(B16)
        elif step == 6:
            other = pl.ds(pl.multiple_of(48 * (1 - p.c), 16), 48)
            half = pl.ds(pl.multiple_of(48 * p.c, 16), 48)
            self.out[half, cols] = self.fin[half, cols].astype(F32)
            self.out[other, cols] = self.rcf[:, cols].astype(F32)
        if step < 6:
            for copy in self.copies(job, step):
                copy.start()
        if step == 7:
            for earlier in range(6):
                for copy in self.copies(job, earlier):
                    copy.wait_send()

    def tick(self, t, lag):
        for step in (7, 6, 5, 4, 3, 2, 1, 0):
            self.step(step, t - lag[step])


def dot(a, b, ca=1, cb=0):
    return lax.dot_general(a, b, (((ca,), (cb,)), ((), ())), preferred_element_type=F32)


def normalize(value):
    center = value - jnp.mean(value, -1, keepdims=True)
    rate = lax.rsqrt(jnp.mean(center * center, -1, keepdims=True) + EPSILON)
    return center * rate, rate


def head_mask():
    return lax.broadcasted_iota(jnp.int32, (192, D), 0) // 16 == lax.broadcasted_iota(jnp.int32, (192, D), 1) // HEAD


def spread_heads(value):
    return jnp.where(head_mask(), jnp.concatenate([value.astype(F32)] * HEADS, 0), 0.0).astype(B16)


def join_heads(value):
    value = jnp.where(head_mask(), value, 0.0)
    total = value[0:16]
    for head in range(1, HEADS):
        total = total + value[16 * head : 16 * head + 16]
    return total


def row_of(value, index):
    rows = lax.broadcasted_iota(jnp.int32, value.shape, 0)
    return jnp.sum(jnp.where(rows == index, value, 0.0), 0, keepdims=True)


def forward_kernel(
    xs, lead, caption, counts, courier, gains, cheads, aheads, cmerge, amerge, expand, projection,
    full_o, normt_o, mixed_o, shares_o, seen_o, seent_o, hidden_o, n2t_o, d_o, gsum_o, hsum_o, gains_o,
    leaders_o, message_o, mnorm_o, mmix_o, mshare_o, told_o, mout_o, texts_o,
    full, leadbuf, norm, normt, mixed, shares, seen, seent, hidden, n2, n2t, dd,
    texts, ssem, rsem, lsem, lead_s, lead_r, text_s, text_r, osem,
):
    p = Pos()
    weights = ((courier, COURIER), (gains, GAINS), (cheads, CHEADS), (aheads, AHEADS), (cmerge, CMERGE), (amerge, AMERGE),
               (expand, EXPAND), (projection, PROJ))
    mine = pl.ds(pl.multiple_of(p.k * 96, 16), 96)
    loads = []
    for index, (ref, start) in enumerate(weights):
        copy = pltpu.make_async_copy(ref, full.at[mine, pl.ds(start, ref.shape[1])], lsem.at[index])
        copy.start()
        loads.append(copy)
    leadbuf[p.dp] = lead[...]
    barrier(p.plane() + list(p.team))
    text_hop = Spread(p, caption, texts, text_s, text_r, same=True)
    others = [p.core, p.xp, ((1 - p.x) * 2 + 1 - p.c, p.k)]
    sends = []
    for index, other in enumerate(others):
        copy = pltpu.make_async_remote_copy(
            src_ref=lead, dst_ref=leadbuf.at[p.dp], send_sem=lead_s.at[0, index], recv_sem=lead_r.at[0, index],
            device_id=other, device_id_type=MESH)
        copy.start()
        sends.append(copy)
    for copy in loads:
        copy.wait()
    def block(k, start, count, job):
        first_col, columns = JOBS[job]
        return full.at[pl.ds(pl.multiple_of(k * 96 + start * 16, 16), count * 16), pl.ds(first_col, columns)]

    gather = Gather(p, block, len(JOBS), ssem, rsem)
    lag = (0, 2, 4, 6, 8, 9)
    outs = []

    def out(source, target):
        copy = pltpu.make_async_copy(source, target, osem.at[len(outs)])
        copy.start()
        outs.append(copy)

    def ticks(first, last):
        for t in range(first, last + 1):
            gather.tick(t, lag)

    ticks(0, 4)
    text_hop.wait()
    text_team = Team(p, texts, texts_o, lead_s.at[1], lead_r.at[1])
    ticks(5, 8)
    for index, other in enumerate(others):
        pltpu.make_async_remote_copy(
            src_ref=lead, dst_ref=leadbuf.at[other[0]], send_sem=lead_s.at[0, index], recv_sem=lead_r.at[0, index],
            device_id=other, device_id_type=MESH).wait_recv()
    leaders = jnp.concatenate([leadbuf[index][0:4] for index in range(4)], 0)
    leaders_o[...] = leaders.astype(B16)
    rows = jnp.transpose(full[:, GAINS : GAINS + 128].astype(F32))[0:8]
    gains_o[...] = rows
    courier_gain, attend_gain, expand_gain = rows[0:1], rows[1:2], rows[2:3]
    message = dot(leaders.astype(B16), full[:, COURIER : COURIER + D])
    message_o[...] = message
    xh, _ = normalize(message)
    mnorm = (xh * courier_gain).astype(B16)
    mnorm_o[...] = mnorm

    def norm_frame(f, carry):
        here = pl.ds(pl.multiple_of(f * PAD, 16), PAD)
        xh, _ = normalize(xs[f].astype(F32))
        norm[here, :] = (xh * attend_gain).astype(B16)
        return carry

    lax.fori_loop(0, 4, norm_frame, 0)
    ticks(9, 11)
    mmix = dot(mnorm, full[:, CHEADS : CHEADS + 3 * D])
    mq, mk, mv = mmix[:, :D].astype(B16), mmix[:, D : 2 * D].astype(B16), mmix[:, 2 * D :].astype(B16)
    mmix_o[...] = mmix.astype(B16)
    scores = dot(spread_heads(mq), mk, 1, 1) * HEAD ** (-0.5)
    frames = lax.broadcasted_iota(jnp.int32, (192, 16), 1)
    scores = jnp.where(frames < counts[0], scores, -1000000000.0)
    raised = jnp.exp(scores - jnp.max(scores, -1, keepdims=True))
    mshare = raised / jnp.sum(raised, -1, keepdims=True)
    mshare_o[...] = mshare
    told = join_heads(dot(mshare.astype(B16), mv)).astype(B16)
    told_o[...] = told

    def heads_tile(base, factor):
        def body(n, carry):
            cols = pl.ds(pl.multiple_of(base + n * 256, 256), 256)
            wcols = pl.ds(pl.multiple_of(AHEADS + base + n * 256, 128), 256)
            mixed[:, cols] = (dot(norm[...], full[:, wcols]) * factor).astype(B16)
            return carry
        lax.fori_loop(0, 3, body, 0)

    ticks(12, 12)
    heads_tile(0, HEAD ** (-0.5))
    ticks(13, 13)
    heads_tile(D, 1.0)
    ticks(14, 14)
    heads_tile(2 * D, 1.0)
    ticks(15, 15)
    mout_all = message + dot(told, full[:, CMERGE : CMERGE + D])
    mout = jnp.concatenate([row_of(mout_all, p.dp * 4 + f) for f in range(4)] + [jnp.zeros((4, D), F32)], 0)
    mout_o[...] = mout
    xh, _ = normalize(mout)
    extra = (xh * attend_gain).astype(B16)
    extra_kv = dot(extra, full[:, AHEADS + D : AHEADS + 3 * D])
    extra = extra.astype(F32)
    spot = lax.broadcasted_iota(jnp.int32, (16, 1), 0) == 5
    for f in range(4):
        tail = pl.ds(f * PAD + 192, 16)
        norm[tail, :] = jnp.where(spot, extra[f : f + 1], norm[tail, :].astype(F32)).astype(B16)
        old = mixed[tail, D : 3 * D].astype(F32)
        mixed[tail, D : 3 * D] = jnp.where(spot, extra_kv[f : f + 1], old).astype(B16)
    out(mixed, mixed_o)

    first = lax.broadcasted_iota(jnp.int32, (PAD, 128), 1) < HEAD
    kept = lax.broadcasted_iota(jnp.int32, (PAD, PAD), 0) < 198

    def attend(f, pair):
        here = pl.ds(pl.multiple_of(f * PAD, 16), PAD)
        at = pl.multiple_of(pair * 128, 128)
        q = mixed[here, pl.ds(at, 128)]
        k = mixed[here, pl.ds(pl.multiple_of(D + at, 128), 128)]
        v = mixed[here, pl.ds(pl.multiple_of(2 * D + at, 128), 128)]
        total = None
        for h in range(2):
            mask = first if h == 0 else jnp.logical_not(first)
            kh, vh = jnp.where(mask, k, jnp.zeros_like(k)), jnp.where(mask, v, jnp.zeros_like(v))
            scores = jnp.where(kept, dot(kh, q, 1, 1), -1e30)
            raised = jnp.exp(scores - jnp.max(scores, 0, keepdims=True))
            share = (raised * (1.0 / jnp.sum(raised, 0, keepdims=True))).astype(B16)
            shares[f * HEADS + pair * 2 + h] = share
            part = dot(share, vh, 0, 0)
            total = part if total is None else total + part
        seen[here, pl.ds(at, 128)] = total.astype(B16)

    def attend_frame(f):
        def body(pair, carry):
            attend(f, pair)
            return carry
        lax.fori_loop(0, 6, body, 0)

    def merge_frames():
        def body(n, carry):
            cols = pl.ds(pl.multiple_of(n * 256, 256), 256)
            wcols = pl.ds(pl.multiple_of(AMERGE + n * 256, 128), 256)
            hidden[:, cols] = dot(seen[...], full[:, wcols])
            return carry
        lax.fori_loop(0, 3, body, 0)

    def hidden_frame(f, carry):
        here = pl.ds(pl.multiple_of(f * PAD, 16), PAD)
        value = hidden[here, :] + xs[f].astype(F32)
        hidden[here, :] = value
        xh, _ = normalize(value)
        n2[here, :] = (xh * expand_gain).astype(B16)
        return carry

    def row_mask(shape, axis):
        index = lax.broadcasted_iota(jnp.int32, shape, axis)
        good = index < 0
        for f in range(4):
            lost = jnp.where(p.dp * 4 + f < counts[0], 0, ROWS)
            good = jnp.logical_or(good, jnp.logical_and(index >= f * PAD + lost, index < f * PAD + 197 + lost * 0))
        return good

    mask_row = jnp.where(row_mask((16, ROWS), 1), 1.0, 0.0).astype(B16)

    def expand_tile(base):
        def body(n, carry):
            cols = pl.ds(pl.multiple_of(base + n * 256, 256), 256)
            wcols = pl.ds(pl.multiple_of(EXPAND + base + n * 256, 128), 256)
            grown = dot(n2[...], full[:, wcols])
            s = 0.5 + 0.5 * jnp.tanh(0.851 * grown)
            gated = grown * s
            dd[:, cols] = (s + 1.702 * gated * (1.0 - s)).astype(B16)
            gsum_o[:, cols] = dot(mask_row, gated.astype(B16))[0:8]
            return carry
        lax.fori_loop(0, 3, body, 0)

    attend_frame(0)
    ticks(16, 16)
    attend_frame(1)
    ticks(17, 17)
    attend_frame(2)
    attend_frame(3)
    out(seen, seen_o)
    out(shares, shares_o)
    ticks(18, 18)
    merge_frames()
    lax.fori_loop(0, 4, hidden_frame, 0)
    out(hidden, hidden_o)
    expand_tile(0)
    ticks(19, 19)
    expand_tile(D)
    high = hidden[...].astype(B16)
    low = (hidden[...] - high.astype(F32)).astype(B16)
    hsum_o[...] = (dot(mask_row, high) + dot(mask_row, low))[0:8]
    ticks(20, 20)
    expand_tile(2 * D)
    ticks(21, 21)
    out(full, full_o)
    expand_tile(3 * D)
    out(dd, d_o)
    mask_col = jnp.where(row_mask((ROWS, D), 0), 1.0, 0.0)
    n2t[...] = jnp.transpose((n2[...].astype(F32) * mask_col).astype(B16))
    out(n2t, n2t_o)
    normt[...] = jnp.transpose(norm[...])
    out(normt, normt_o)
    seent[...] = jnp.transpose(seen[...])
    out(seent, seent_o)
    ticks(22, 22)
    for copy in sends:
        copy.wait_send()
    text_team.wait()
    text_team.done()
    text_hop.done()
    for copy in outs:
        copy.wait()


def pack_row(row):
    return jnp.concatenate([row[:, 128 * r : 128 * r + 128] for r in range(6)] + [jnp.zeros((2, 128), F32)], 0)


def unpack_row(value):
    return jnp.concatenate([value[r : r + 1] for r in range(6)], 1)


def twice(value):
    high = value.astype(B16)
    return jnp.concatenate([high, (value - high.astype(F32)).astype(B16)], 0)


def loss_kernel(
    gsum, hsum, shrink, full, texts, counts, matches,
    gg_o, rg_o, loss_o, shrink_grad_o, pooled_o, eg_o,
    projection, bundle, team, gs, gr, ps, pr, rs_, rr, us, ur, team_s, team_r, hop_s, hop_r, lsem,
):
    p = Pos()
    load = pltpu.make_async_copy(full.at[:, pl.ds(PROJ, 512)], projection, lsem)
    load.start()
    barrier(list(p.team) + p.plane())
    bundle[:, 0:384] = jnp.concatenate([gsum[0:1, 384 * k : 384 * k + 384] for k in range(8)], 0)
    bundle[:, 384:512] = pack_row(hsum[0:1, :])
    hop = Team(p, bundle, team, team_s, team_r)
    text = jnp.concatenate(
        [jnp.concatenate([texts[i, :, r, :] for r in range(4)], 1) for i in range(4)], 0)
    text_unit = (text * lax.rsqrt(jnp.sum(text * text, -1, keepdims=True) + 1e-06)).astype(B16)
    hop.wait()
    total = team[0] + team[1] + team[2] + team[3]
    hop.done()
    for k in range(8):
        gs[k] = jnp.broadcast_to(total[k : k + 1, 0:384], (8, 384))
    hop = Spread(p, gs, gr, hop_s.at[0], hop_r.at[0])
    hop.wait()
    gated = jnp.concatenate([gr[v][0:1] for v in range(8)], 0)
    both = dot(twice(gated), shrink[...])
    part = both[0:8] + both[8:16]
    for v in range(8):
        ps[v] = pack_row(part[v : v + 1])
    hop.done()
    hop = Spread(p, ps, pr, hop_s.at[1], hop_r.at[1])
    hop.wait()
    packed = total[:, 384:512]
    for k in range(8):
        packed = packed + pr[k]
    hop.done()
    load.wait()
    denominator = (counts[0] * 197).astype(F32)
    pooled = jnp.broadcast_to(unpack_row(packed / denominator), (8, D))
    pooled_low = pooled.astype(B16)
    embed = dot(pooled_low, projection[...])
    rate = lax.rsqrt(jnp.sum(embed * embed, -1, keepdims=True) + 1e-06)
    unit = embed * rate
    logits = dot(unit.astype(B16), text_unit, 1, 1) * LOGIT_SCALE
    peak = jnp.max(logits, -1, keepdims=True)
    normalizer = peak + jnp.log(jnp.sum(jnp.exp(logits - peak), -1, keepdims=True))
    matched = lax.broadcasted_iota(jnp.int32, logits.shape, 1) == matches[0]
    loss_o[...] = jnp.broadcast_to(normalizer - jnp.sum(jnp.where(matched, logits, 0.0), -1, keepdims=True), (8, 128))
    slope = (jnp.exp(logits - normalizer) - jnp.where(matched, 1.0, 0.0)).astype(B16)
    unit_grad = dot(slope, text_unit) * LOGIT_SCALE
    embed_grad = (rate * (unit_grad - unit * jnp.sum(unit * unit_grad, -1, keepdims=True))).astype(B16)
    rg = dot(embed_grad, projection[...], 1, 1) / denominator
    rg_o[...] = rg
    top = lax.broadcasted_iota(jnp.int32, (16, 1), 0) == 0
    pooled_o[...] = jnp.where(top, jnp.concatenate([pooled, pooled], 0), 0.0).astype(B16)
    eg_o[...] = jnp.where(top, jnp.concatenate([embed_grad.astype(F32)] * 2, 0), 0.0).astype(B16)
    rs_[...] = pack_row(rg.astype(B16).astype(F32)[0:1])
    hop = Spread(p, rs_, rr, hop_s.at[2], hop_r.at[2], same=True)
    hop.wait()
    rows = jnp.concatenate([unpack_row(rr[v]) for v in range(8)], 0).astype(B16)
    grad = dot(rows, shrink[...], 1, 1)
    for v in range(8):
        us[v] = jnp.broadcast_to(grad[v : v + 1], (8, 384))
    hop.done()
    hop = Spread(p, us, ur, hop_s.at[3], hop_r.at[3])
    shrink_grad_o[...] = dot(twice(gated), jnp.concatenate([rows.astype(F32)] * 2, 0).astype(B16), 0, 0)
    hop.wait()
    for k in range(8):
        gg_o[:, 384 * k : 384 * k + 384] = ur[k]
    hop.done()


def backward_kernel(
    xs, normt_h, mixed_h, shares, seen_h, seent_h, hidden_h, n2t_h, d_h, full, gg, rg, gains, mout, counts,
    stage, patch_o, first_o, mog_o,
    wexp, wmerge, wheads, normt, mixed, seen, seent, hidden, n2t, dd, sbuf, hg, low, dout, lsem, psem,
):
    p = Pos()
    jobs = ((n2t_h, n2t), (d_h, dd), (full.at[:, pl.ds(EXPAND, 3072)], wexp), (hidden_h, hidden),
            (seent_h, seent), (full.at[:, pl.ds(AMERGE, D)], wmerge), (mixed_h, mixed), (seen_h, seen), (normt_h, normt),
            (full.at[:, pl.ds(AHEADS, 3 * D)], wheads))
    loads = []
    for index, (source, target) in enumerate(jobs):
        copy = pltpu.make_async_copy(source, target, lsem.at[index])
        copy.start()
        loads.append(copy)
    attend_gain, expand_gain = gains[1:2, :], gains[2:3, :]
    loads[0].wait()
    loads[1].wait()

    def expand_tile(n, carry):
        cols = pl.ds(pl.multiple_of(n * 256, 256), 256)
        tile = dd[:, cols]
        scale = gg[0:1, cols]
        stage[:, :, cols] = (dot(n2t[...], tile) * scale).astype(B16).reshape(8, 96, 256)
        dd[:, cols] = (tile.astype(F32) * scale).astype(B16)
        return carry

    lax.fori_loop(0, 12, expand_tile, 0)
    loads[2].wait()

    def norm_tile(n, carry):
        cols = pl.ds(pl.multiple_of(n * 256, 256), 256)
        hg[:, cols] = dot(dd[...], wexp[cols, :], 1, 1)
        return carry

    lax.fori_loop(0, 3, norm_tile, 0)
    loads[3].wait()

    def hidden_frame(f, total):
        here = pl.ds(pl.multiple_of(f * PAD, 16), PAD)
        limit = jnp.where(p.dp * 4 + f < counts[0], 197, 0)
        good = lax.broadcasted_iota(jnp.int32, (PAD, D), 0) < limit
        xh, rate = normalize(hidden[here, :])
        dy = jnp.where(good, hg[here, :], 0.0)
        e = dy * expand_gain
        grad = rate * (e - jnp.mean(e, -1, keepdims=True) - xh * jnp.mean(e * xh, -1, keepdims=True))
        grad = grad + jnp.where(good, rg[0:1, :], 0.0)
        hg[here, :] = grad
        low[here, :] = grad.astype(B16)
        return total + jnp.sum(dy * xh, 0, keepdims=True)

    expand_gain_grad = lax.fori_loop(0, 4, hidden_frame, jnp.zeros((1, D), F32))
    loads[4].wait()
    loads[5].wait()

    def merge_tile(n, carry):
        cols = pl.ds(pl.multiple_of(n * 256, 256), 256)
        stage[:, :, pl.ds(pl.multiple_of(3072 + n * 256, 128), 256)] = dot(seent[...], low[:, cols]).astype(B16).reshape(8, 96, 256)
        dout[:, cols] = dot(low[...], wmerge[cols, :], 1, 1).astype(B16)
        return carry

    lax.fori_loop(0, 3, merge_tile, 0)
    loads[6].wait()
    loads[7].wait()
    first = lax.broadcasted_iota(jnp.int32, (PAD, 128), 1) < HEAD

    def fetch(index, slot):
        return pltpu.make_async_copy(shares.at[pl.ds(index * 2, 2)], sbuf.at[slot], psem.at[slot])

    fetch(0, 0).start()

    def attend(index, carry):
        f, pair = index // 6, lax.rem(index, 6)
        slot = lax.rem(index, 2)

        @pl.when(index < 23)
        def _():
            fetch(index + 1, 1 - slot).start()

        fetch(index, slot).wait()
        here = pl.ds(pl.multiple_of(f * PAD, 16), PAD)
        at = pl.multiple_of(pair * 128, 128)
        qs, ks, vs = (pl.ds(pl.multiple_of(b + at, 128), 128) for b in (0, D, 2 * D))
        q, k, v = mixed[here, qs], mixed[here, ks], mixed[here, vs]
        do, o = dout[here, qs], seen[here, qs]
        right = jnp.concatenate([do, (-(do.astype(F32) * o.astype(F32))).astype(B16)], 1)
        dq = dk = dv = None
        zero = jnp.zeros_like(q)
        for h in range(2):
            mask = first if h == 0 else jnp.logical_not(first)
            share = sbuf[slot, h]
            left = jnp.concatenate([jnp.where(mask, v, zero), jnp.where(mask, jnp.ones_like(v), zero)], 1)
            ds = (share.astype(F32) * dot(left, right, 1, 1)).astype(B16)
            pq = dot(ds, jnp.where(mask, k, zero), 0, 0)
            pk = dot(ds, jnp.where(mask, q, zero))
            pv = dot(share, jnp.where(mask, do, zero))
            dq, dk, dv = (pq, pk, pv) if h == 0 else (dq + pq, dk + pk, dv + pv)
        mixed[here, qs] = (dq * HEAD ** (-0.5)).astype(B16)
        mixed[here, ks] = dk.astype(B16)
        mixed[here, vs] = dv.astype(B16)
        return carry

    lax.fori_loop(0, 24, attend, 0)
    loads[8].wait()

    def heads_tile(n, carry):
        cols = pl.ds(pl.multiple_of(n * 256, 256), 256)
        stage[:, :, pl.ds(pl.multiple_of(3840 + n * 256, 128), 256)] = dot(normt[...], mixed[:, cols]).astype(B16).reshape(8, 96, 256)
        return carry

    lax.fori_loop(0, 9, heads_tile, 0)
    loads[9].wait()

    def tokens_tile(n, carry):
        cols = pl.ds(pl.multiple_of(n * 256, 256), 256)
        hidden[:, cols] = dot(mixed[...], wheads[cols, :], 1, 1)
        return carry

    lax.fori_loop(0, 3, tokens_tile, 0)
    attend_gain_grad = jnp.zeros((1, D), F32)
    firsts, messages = [], []
    spot = lax.broadcasted_iota(jnp.int32, (PAD, 1), 0) == 197
    for f in range(4):
        here = pl.ds(f * PAD, PAD)
        xh, rate = normalize(jnp.where(spot, mout[f : f + 1, :], xs[f].astype(F32)))
        dy = hidden[here, :]
        e = dy * attend_gain
        grad = rate * (e - jnp.mean(e, -1, keepdims=True) - xh * jnp.mean(e * xh, -1, keepdims=True))
        attend_gain_grad = attend_gain_grad + jnp.sum(dy * xh, 0, keepdims=True)
        patch = hg[here, :] + grad
        patch_o[f] = patch.astype(B16)
        firsts.append(patch[0:1])
        messages.append(grad[197:198])
    first_o[...] = jnp.concatenate(firsts + [jnp.zeros((4, D), F32)], 0)
    mog_o[...] = jnp.concatenate(messages + [jnp.zeros((4, D), F32)], 0)
    tall = jnp.concatenate([attend_gain_grad, expand_gain_grad, jnp.zeros((126, D), F32)], 0)
    stage[:, :, 6144:6272] = jnp.transpose(tall).astype(B16).reshape(8, 96, 128)


RJOBS = ((0, 768), (768, 768), (1536, 768), (2304, 768), (3072, 768), (3840, 768), (4608, 768), (5376, 896))
BUNDLE = 8448
SIXTH = BUNDLE // 6


def reduce_kernel(
    stage_h, mog, first, full, leaders, message, mnorm, mmix, mshare, told, pooled, eg, gains,
    out, courier_o, cheads_o, cmerge_o, proj_o, cgain_o, lead_o,
    stage, rc, rx, ry, rz, own, rf, fin, rcf, bundle, team, weights, s_r, r_r, s_b, r_b, team_s, team_r, lsem,
):
    p = Pos()
    loads = []
    for index, (first_col, count, target) in enumerate(((CMERGE, D, 3072), (CHEADS, 3 * D, D), (COURIER, D, 0))):
        loads.append(pltpu.make_async_copy(full.at[:, pl.ds(first_col, count)], weights.at[:, pl.ds(target, count)], lsem.at[index]))
        loads[-1].start()
    big = pltpu.make_async_copy(stage_h, stage, lsem.at[3])
    big.start()
    barrier(p.peers() + [p.cross])
    hop = Team(p, mog, team, team_s, team_r)
    big.wait()
    reduce = Reduce(p, stage, (rc, rx, ry, rz, own, rf, fin, rcf), out, RJOBS, s_r, r_r)
    lag = (0, 1, 2, 3, 4, 5, 6, 7)
    reduce.tick(0, lag)
    reduce.tick(1, lag)
    hop.wait()
    out_grad = jnp.concatenate([team[i][0:4] for i in range(4)], 0)
    for load in loads:
        load.wait()
    courier_gain = gains[0:1, :]
    mq, mk, mv = mmix[:, 0:D], mmix[:, D : 2 * D], mmix[:, 2 * D : 3 * D]
    out_low = out_grad.astype(B16)
    told_grad = dot(out_low, weights[:, 3072:3840], 1, 1).astype(B16)
    upstream = spread_heads(told_grad)
    share = mshare[...]
    share_grad = dot(upstream, mv, 1, 1)
    dv = dot(share.astype(B16), upstream, 0, 0)
    inner = jnp.sum(share * share_grad, -1, keepdims=True)
    ds = (share * (share_grad - inner)).astype(B16)
    dq = join_heads(dot(ds, mk)) * HEAD ** (-0.5)
    dk = dot(ds, spread_heads(mq), 0, 0) * HEAD ** (-0.5)
    mixed_grad = jnp.concatenate([dq, dk, dv], 1).astype(B16)
    norm_grad = dot(mixed_grad, weights[:, D : 4 * D], 1, 1)
    xh, rate = normalize(message[...])
    e = norm_grad * courier_gain
    grad = rate * (e - jnp.mean(e, -1, keepdims=True) - xh * jnp.mean(e * xh, -1, keepdims=True))
    message_grad = (out_grad + grad).astype(B16)
    leader_grad = dot(message_grad, weights[:, 0:D], 1, 1)
    lead_o[...] = jnp.concatenate([row_of(leader_grad, p.dp * 4 + f) for f in range(4)] + [jnp.zeros((4, D), F32)], 0) + first[...]
    parts = (message_grad, mixed_grad, out_low, leaders[...], mnorm[...], told[...], pooled[...], eg[...],
             (norm_grad * xh).astype(B16))
    col = 0
    for part in parts:
        bundle[p.k, :, col : col + part.shape[1]] = part
        col += part.shape[1]

    def block(k, start, count, job):
        return bundle.at[k, :, pl.ds(pl.multiple_of(start * SIXTH, 128), count * SIXTH)]

    gather = Gather(p, block, 1, s_b, r_b)
    for t in range(2, 8):
        gather.stage(t - 2, 0)
        reduce.tick(t, lag)
    whole = bundle[...].reshape(128, BUNDLE)
    pick = jnp.where(
        jnp.logical_and(lax.broadcasted_iota(jnp.int32, (D, 128), 0) == p.k * 96 + lax.broadcasted_iota(jnp.int32, (D, 128), 1),
                        lax.broadcasted_iota(jnp.int32, (D, 128), 1) < 96), 1.0, 0.0).astype(B16)

    def product(left, width, right, columns):
        chosen = dot(whole[:, left : left + width], pick).astype(B16)
        return dot(chosen, whole[:, right : right + columns], 0, 0)[0:96]

    courier_o[...] = product(3840, D, 0, D)
    cheads_o[...] = product(4608, D, D, 3 * D)
    cmerge_o[...] = product(5376, D, 3072, D)
    proj_o[...] = product(6144, D, 6912, 512)
    gain_grad = jnp.sum(whole[:, 7424:8192].astype(F32), 0, keepdims=True)
    gain_grad = twice(jnp.broadcast_to(gain_grad, (8, D)))
    both = dot(pick, gain_grad, 0, 1)
    cgain_o[...] = both[0:96, 0:8] + both[0:96, 8:16]
    for t in range(8, len(RJOBS) + 7):
        reduce.tick(t, lag)
    hop.done()


def any_spec():
    return pl.BlockSpec(memory_space=pl.ANY)


def vmem_spec():
    return pl.BlockSpec(memory_space=pltpu.VMEM)


def smem_spec():
    return pl.BlockSpec(memory_space=pltpu.SMEM)


def sds(shape, dtype):
    return jax.ShapeDtypeStruct(shape, dtype)


def dma(*shape):
    return pltpu.SemaphoreType.DMA(shape)


def vm(shape, dtype):
    return pltpu.VMEM(shape, dtype)


def fast(
    patches, counts, captions, matches, courier, courier_gain, courier_heads, courier_merge, attend_gain, attend_heads,
    attend_merge, expand_gain, expand_weight, shrink_weight, projection,
):
    caption = jnp.pad(captions.astype(F32).reshape(4, 128), ((0, 4), (0, 0)))
    xs = jnp.pad(patches[0], ((0, 0), (0, PAD - 197), (0, 0)))
    lead = jnp.pad(patches[0, :, 0, :].astype(F32), ((0, 4), (0, 0)))
    gain_block = jnp.stack([courier_gain, attend_gain, expand_gain], 1)
    gain_block = jnp.pad(gain_block, ((0, 0), (0, 125)))
    anys, vmem, smem = any_spec(), vmem_spec(), smem_spec()
    (full, normt, mixed, shares, seen, seent, hidden, n2t, dd, gsum, hsum, gains,
     leaders, message, mnorm, mmix, mshare, told, mout, texts) = pl.pallas_call(
        forward_kernel,
        out_shape=(
            sds((D, NCOLS), B16), sds((D, ROWS), B16), sds((ROWS, 3 * D), B16), sds((48, PAD, PAD), B16), sds((ROWS, D), B16),
            sds((D, ROWS), B16), sds((ROWS, D), F32), sds((D, ROWS), B16), sds((ROWS, 4 * D), B16), sds((8, 4 * D), F32),
            sds((8, D), F32), sds((8, D), F32), sds((16, D), B16), sds((16, D), F32), sds((16, D), B16), sds((16, 3 * D), B16),
            sds((192, 16), F32), sds((16, D), B16), sds((8, D), F32), sds((4, 8, 8, 128), F32)),
        in_specs=[vmem, vmem, vmem, smem] + [anys] * 8,
        out_specs=tuple([anys] * 9 + [vmem] * 11),
        scratch_shapes=[
            vm((D, NCOLS), B16), vm((4, 8, D), F32), vm((ROWS, D), B16), vm((D, ROWS), B16), vm((ROWS, 3 * D), B16),
            vm((48, PAD, PAD), B16), vm((ROWS, D), B16), vm((D, ROWS), B16), vm((ROWS, D), F32), vm((ROWS, D), B16),
            vm((D, ROWS), B16), vm((ROWS, 4 * D), B16),
            vm((8, 8, 128), F32), dma(len(JOBS), 28), dma(len(JOBS), 28), dma(8), dma(2, 3), dma(2, 3), dma(7), dma(7), dma(9)],
        compiler_params=pltpu.CompilerParams(collective_id=0, has_side_effects=True, vmem_limit_bytes=60 << 20),
        name="forward",
    )(xs, lead, caption, counts, courier, gain_block, courier_heads, attend_heads, courier_merge, attend_merge, expand_weight, projection)
    gg, rg, loss, shrink_grad, pooled, eg = pl.pallas_call(
        loss_kernel,
        out_shape=(sds((8, 4 * D), F32), sds((8, D), F32), sds((8, 128), F32), sds((384, D), F32), sds((16, D), B16),
                   sds((16, 512), B16)),
        in_specs=[vmem, vmem, vmem, anys, vmem, smem, smem],
        out_specs=tuple([vmem] * 6),
        scratch_shapes=[
            vm((D, 512), B16), vm((8, 512), F32), vm((4, 8, 512), F32), vm((8, 8, 384), F32), vm((8, 8, 384), F32),
            vm((8, 8, 128), F32), vm((8, 8, 128), F32), vm((8, 128), F32), vm((8, 8, 128), F32), vm((8, 8, 384), F32),
            vm((8, 8, 384), F32), dma(3), dma(3), dma(4, 7), dma(4, 7), pltpu.SemaphoreType.DMA],
        compiler_params=pltpu.CompilerParams(collective_id=1, has_side_effects=True, vmem_limit_bytes=60 << 20),
        name="loss",
    )(gsum, hsum, shrink_weight, full, texts, counts, matches)
    stage, patch, first, mog = pl.pallas_call(
        backward_kernel,
        out_shape=(sds((8, 96, 6272), B16), sds((4, PAD, D), B16), sds((8, D), F32), sds((8, D), F32)),
        in_specs=[vmem, anys, anys, anys, anys, anys, anys, anys, anys, anys, vmem, vmem, vmem, vmem, smem],
        out_specs=tuple([vmem] * 4),
        scratch_shapes=[
            vm((D, 4 * D), B16), vm((D, D), B16), vm((D, 3 * D), B16), vm((D, ROWS), B16), vm((ROWS, 3 * D), B16),
            vm((ROWS, D), B16), vm((D, ROWS), B16), vm((ROWS, D), F32), vm((D, ROWS), B16), vm((ROWS, 4 * D), B16),
            vm((2, 2, PAD, PAD), B16), vm((ROWS, D), F32), vm((ROWS, D), B16), vm((ROWS, D), B16), dma(10), dma(2)],
        compiler_params=pltpu.CompilerParams(vmem_limit_bytes=60 << 20),
        name="backward",
    )(xs, normt, mixed, shares, seen, seent, hidden, n2t, dd, full, gg, rg, gains, mout, counts)
    out, courier_grad, cheads_grad, cmerge_grad, proj_grad, cgain, leads = pl.pallas_call(
        reduce_kernel,
        out_shape=(sds((96, 6272), F32), sds((96, D), F32), sds((96, 3 * D), F32), sds((96, D), F32), sds((96, 512), F32),
                   sds((96, 8), F32), sds((8, D), F32)),
        in_specs=[anys, vmem, vmem, anys] + [vmem] * 9,
        out_specs=tuple([vmem] * 7),
        scratch_shapes=[
            vm((8, 96, 6272), B16), vm((8, 48, 6272), B16), vm((8, 16, 6272), B16), vm((4, 32, 6272), B16),
            vm((3, 32, 6272), B16), vm((32, 6272), B16), vm((32, 6272), B16), vm((96, 6272), B16), vm((48, 6272), B16),
            vm((8, 16, BUNDLE), B16), vm((4, 8, D), F32), vm((D, 5 * D), B16),
            dma(len(RJOBS), 11), dma(len(RJOBS), 11), dma(1, 28), dma(1, 28), dma(3), dma(3), dma(4)],
        compiler_params=pltpu.CompilerParams(collective_id=2, has_side_effects=True, vmem_limit_bytes=60 << 20),
        name="reduce",
    )(stage, mog, first, full, leaders, message, mnorm, mmix, mshare, told, pooled, eg, gains)
    patch_grad = jnp.concatenate([leads[0:4, None, :].astype(B16), patch[:, 1:197]], 1)[None]
    return (
        loss[0:1, 0], patch_grad, courier_grad, cgain[:, 0], cheads_grad, cmerge_grad, out[:, 6144], out[:, 3840:6144],
        out[:, 3072:3840], out[:, 6145], out[:, 0:3072], shrink_grad, proj_grad,
    )


def joined_2(value, axis, join):
    pieces = jax.tree.map(lambda part: lax.all_gather(part, axis), value)
    head = jax.tree.map(lambda part: part[0], pieces)
    tail = jax.tree.map(lambda part: part[1:], pieces)
    running, _ = lax.scan(lambda running, share: (join(running, share), None), head, tail)
    return running


def layer_norm(value, gain):
    center = value - jnp.mean(value, -1, keepdims=True)
    spread = jnp.mean(center * center, -1, keepdims=True)
    return center * lax.rsqrt(spread + EPSILON) * gain


def norm_back(value, gain, upstream):
    _, pull = jax.vjp(layer_norm, value, gain)
    return pull(upstream)


def quick_gelu(value):
    return value * jax.nn.sigmoid(1.702 * value)


def unit_rows(value):
    return value * lax.rsqrt(jnp.sum(value * value, -1, keepdims=True) + 1e-06)


def split_heads(mixed, query_count):
    batch, length, triple = mixed.shape
    width = triple // 3
    rounded = mixed.astype(jnp.bfloat16)
    queries = rounded[:, :query_count, :width].reshape(batch, query_count, HEADS, HEAD)
    keys = rounded[:, :, width : 2 * width].reshape(batch, length, HEADS, HEAD)
    values = rounded[:, :, 2 * width :].reshape(batch, length, HEADS, HEAD)
    return (queries, keys, values)


def scores_of(queries, keys, key_mask):
    scores = jnp.einsum(
        "bqhd,bkhd->bhqk", queries, keys, preferred_element_type=jnp.float32
    ) * HEAD ** (-0.5)
    if key_mask is not None:
        scores = jnp.where(key_mask[:, None, None, :], scores, -1000000000.0)
    return scores


def attend_forward(queries, keys, values, key_mask):
    scores = scores_of(queries, keys, key_mask)
    peak = jnp.max(scores, -1, keepdims=True)
    raised = jnp.exp(scores - peak)
    total = jnp.sum(raised, -1, keepdims=True)
    shares = (raised / total).astype(jnp.bfloat16)
    joined = jnp.einsum("bhqk,bkhd->bqhd", shares, values, preferred_element_type=jnp.float32)
    batch, count = (joined.shape[0], joined.shape[1])
    return (
        joined.reshape(batch, count, HEADS * HEAD).astype(jnp.bfloat16),
        peak + jnp.log(total),
        shares,
    )


def attend_backward(queries, keys, values, key_mask, normalizer, shares, upstream):
    batch, count, width = upstream.shape
    upstream_low = upstream.astype(jnp.bfloat16).reshape(batch, count, HEADS, HEAD)
    chances = jnp.exp(scores_of(queries, keys, key_mask) - normalizer)
    share_grad = jnp.einsum(
        "bqhd,bkhd->bhqk", upstream_low, values, preferred_element_type=jnp.float32
    )
    value_grad = jnp.einsum(
        "bhqk,bqhd->bkhd", shares, upstream_low, preferred_element_type=jnp.float32
    )
    inner = jnp.sum(chances * share_grad, -1, keepdims=True)
    score_grad = (chances * (share_grad - inner)).astype(jnp.bfloat16)
    query_grad = jnp.einsum(
        "bhqk,bkhd->bqhd", score_grad, keys, preferred_element_type=jnp.float32
    ) * HEAD ** (-0.5)
    key_grad = jnp.einsum(
        "bhqk,bqhd->bkhd", score_grad, queries, preferred_element_type=jnp.float32
    ) * HEAD ** (-0.5)
    length = keys.shape[1]
    return (
        query_grad.reshape(batch, count, width),
        key_grad.reshape(batch, length, width),
        value_grad.reshape(batch, length, width),
    )


def frame_forward(block, message_rows, weights):
    attend_gain, attend_heads, attend_merge, expand_gain, expand_weight, shrink_weight = weights
    frames = block.astype(jnp.float32)
    tokens = jnp.concatenate([frames, message_rows[:, None, :]], 1)
    normed = layer_norm(tokens, attend_gain).astype(jnp.bfloat16)
    mixed = jnp.einsum("btd,de->bte", normed, attend_heads, preferred_element_type=jnp.float32)
    queries, keys, values = split_heads(mixed, block.shape[1])
    seen, normalizer, shares = attend_forward(queries, keys, values, None)
    hidden = frames + jnp.einsum(
        "bpd,de->bpe", seen, attend_merge, preferred_element_type=jnp.float32
    )
    normed_two = layer_norm(hidden, expand_gain).astype(jnp.bfloat16)
    grown = jnp.einsum("bpd,dm->bpm", normed_two, expand_weight, preferred_element_type=jnp.float32)
    gated = quick_gelu(grown).astype(jnp.bfloat16)
    result = hidden + jnp.einsum(
        "bpm,md->bpd", gated, shrink_weight, preferred_element_type=jnp.float32
    )
    kept = (
        tokens,
        normed,
        queries,
        keys,
        values,
        shares,
        normalizer,
        seen,
        hidden,
        normed_two,
        grown,
        gated,
    )
    return (jnp.sum(result, 1), kept)


def frame_backward(kept, upstream, weights):
    attend_gain, attend_heads, attend_merge, expand_gain, expand_weight, shrink_weight = weights
    (
        tokens,
        normed,
        queries,
        keys,
        values,
        shares,
        normalizer,
        seen,
        hidden,
        normed_two,
        grown,
        gated,
    ) = kept
    patch_count = hidden.shape[1]
    upstream_low = upstream.astype(jnp.bfloat16)
    shrink_grad = jnp.einsum("bpm,bd->md", gated, upstream_low, preferred_element_type=jnp.float32)
    gated_grad = jnp.einsum(
        "bd,md->bm", upstream_low, shrink_weight, preferred_element_type=jnp.float32
    )
    _, gelu_pull = jax.vjp(quick_gelu, grown)
    grown_grad = gelu_pull(jnp.broadcast_to(gated_grad[:, None, :], grown.shape))[0].astype(
        jnp.bfloat16
    )
    expand_grad = jnp.einsum(
        "bpd,bpm->dm", normed_two, grown_grad, preferred_element_type=jnp.float32
    )
    normed_two_grad = jnp.einsum(
        "bpm,dm->bpd", grown_grad, expand_weight, preferred_element_type=jnp.float32
    )
    hidden_grad, expand_gain_grad = norm_back(hidden, expand_gain, normed_two_grad)
    hidden_grad = hidden_grad + upstream[:, None, :]
    hidden_low = hidden_grad.astype(jnp.bfloat16)
    merge_grad = jnp.einsum("bpd,bpe->de", seen, hidden_low, preferred_element_type=jnp.float32)
    seen_grad = jnp.einsum(
        "bpe,de->bpd", hidden_low, attend_merge, preferred_element_type=jnp.float32
    )
    query_grad, key_grad, value_grad = attend_backward(
        queries, keys, values, None, normalizer, shares, seen_grad
    )
    length = tokens.shape[1]
    query_grad = jnp.pad(query_grad, ((0, 0), (0, length - patch_count), (0, 0)))
    mixed_grad = jnp.concatenate([query_grad, key_grad, value_grad], 2).astype(jnp.bfloat16)
    heads_grad = jnp.einsum("btd,bte->de", normed, mixed_grad, preferred_element_type=jnp.float32)
    normed_grad = jnp.einsum(
        "bte,de->btd", mixed_grad, attend_heads, preferred_element_type=jnp.float32
    )
    token_grad, attend_gain_grad = norm_back(tokens, attend_gain, normed_grad)
    patch_grad = hidden_grad + token_grad[:, :patch_count]
    block_grads = (
        attend_gain_grad,
        heads_grad,
        merge_grad,
        expand_gain_grad,
        expand_grad,
        shrink_grad,
    )
    return (patch_grad, token_grad[:, patch_count], block_grads)


def shards(
    patches,
    counts,
    captions,
    matches,
    courier,
    courier_gain,
    courier_heads,
    courier_merge,
    attend_gain,
    attend_heads,
    attend_merge,
    expand_gain,
    expand_weight,
    shrink_weight,
    projection,
):
    videos, local_frames, patch_count, width = patches.shape
    frame_total = local_frames * lax.axis_size("dp")
    offset = lax.axis_index("dp") * local_frames
    rows = videos * local_frames
    per_block = rows // MICRO
    courier_full, courier_gain_full, heads_full, merge_full, projection_full = (
        lax.all_gather(courier, "fsdp", axis=0, tiled=True),
        lax.all_gather(courier_gain, "fsdp", axis=0, tiled=True),
        lax.all_gather(courier_heads, "fsdp", axis=0, tiled=True),
        lax.all_gather(courier_merge, "fsdp", axis=0, tiled=True),
        lax.all_gather(projection, "fsdp", axis=0, tiled=True),
    )

    def fetch():
        return (
            lax.all_gather(attend_gain, "fsdp", axis=0, tiled=True),
            lax.all_gather(attend_heads, "fsdp", axis=0, tiled=True),
            lax.all_gather(attend_merge, "fsdp", axis=0, tiled=True),
            lax.all_gather(expand_gain, "fsdp", axis=0, tiled=True),
            lax.all_gather(expand_weight, "fsdp", axis=0, tiled=True),
            lax.all_gather(shrink_weight, "fsdp", axis=0, tiled=True),
        )

    leaders = lax.all_gather(patches[:, :, 0, :], "dp", axis=1, tiled=True)
    present = lax.broadcasted_iota(jnp.int32, (videos, frame_total), 1) < counts[:, None]
    message = jnp.einsum("vfd,de->vfe", leaders, courier_full, preferred_element_type=jnp.float32)
    message_norm = layer_norm(message, courier_gain_full).astype(jnp.bfloat16)
    message_mixed = jnp.einsum(
        "vfd,de->vfe", message_norm, heads_full, preferred_element_type=jnp.float32
    )
    told_queries, told_keys, told_values = split_heads(message_mixed, frame_total)
    told, told_normalizer, told_shares = attend_forward(
        told_queries, told_keys, told_values, present
    )
    message_out = message + jnp.einsum(
        "vfd,de->vfe", told, merge_full, preferred_element_type=jnp.float32
    )
    mine = lax.dynamic_slice_in_dim(message_out, offset, local_frames, 1).reshape(rows, width)
    flat = patches.reshape(rows, patch_count, width)
    frame_weights = fetch()
    kept_blocks = []
    sums = []
    for index in range(MICRO):
        if index > 0:
            frame_weights = fetch()
        start = index * per_block
        frame_sums, kept = frame_forward(
            flat[start : start + per_block], mine[start : start + per_block], frame_weights
        )
        kept_blocks.append(kept)
        sums.append(frame_sums)
    frame_sums = jnp.concatenate(sums, 0).reshape(videos, local_frames, width)
    own_present = lax.dynamic_slice_in_dim(present, offset, local_frames, 1)
    partial_value = jnp.sum(jnp.where(own_present[:, :, None], frame_sums, 0.0), 1)
    pooled_sum = lax.psum(partial_value, "dp")
    denominator = (counts * patch_count).astype(jnp.float32)[:, None]
    pooled = pooled_sum / denominator
    pooled_low = pooled.astype(jnp.bfloat16)
    embed = jnp.dot(pooled_low, projection_full, preferred_element_type=jnp.float32)
    video_unit = unit_rows(embed).astype(jnp.bfloat16)
    segment = lax.axis_index("dp") * (captions.shape[0] * lax.axis_size("fsdp"))

    def scores_for(piece):
        text_unit = unit_rows(piece.astype(jnp.float32)).astype(jnp.bfloat16)
        logits = (
            jnp.einsum("ve,te->vt", video_unit, text_unit, preferred_element_type=jnp.float32)
            * LOGIT_SCALE
        )
        positions = segment + lax.broadcasted_iota(jnp.int32, logits.shape, 1)
        return (text_unit, logits, positions == matches[:, None])

    peak = jnp.full((videos,), -1e30, jnp.float32)
    _, logits, matched = scores_for(lax.all_gather(captions, "fsdp", axis=0, tiled=True))
    fresh = jnp.maximum(peak, jnp.max(logits, 1))
    total = jnp.sum(jnp.exp(logits - fresh[:, None]), 1)
    picked = jnp.sum(jnp.where(matched, logits, 0.0), 1)
    peak, total, picked = (fresh, total, picked)

    def combine(first, second):
        top = jnp.maximum(first[0], second[0])
        joined = first[1] * jnp.exp(first[0] - top) + second[1] * jnp.exp(second[0] - top)
        return (top, joined, first[2] + second[2])

    peak, total, picked = joined_2((peak, total, picked), "dp", combine)
    normalizer = peak + jnp.log(total)
    loss = normalizer - picked
    text_unit, logits, matched = scores_for(lax.all_gather(captions, "fsdp", axis=0, tiled=True))
    slope = (jnp.exp(logits - normalizer[:, None]) - matched.astype(jnp.float32)).astype(
        jnp.bfloat16
    )
    unit_grad = jnp.dot(slope, text_unit, preferred_element_type=jnp.float32) * LOGIT_SCALE
    unit_grad = lax.psum(unit_grad, "dp")
    _, unit_pull = jax.vjp(unit_rows, embed)
    embed_grad = unit_pull(unit_grad)[0].astype(jnp.bfloat16)
    projection_grad = jnp.einsum(
        "vd,ve->de", pooled_low, embed_grad, preferred_element_type=jnp.float32
    )
    pooled_grad = jnp.einsum(
        "ve,de->vd", embed_grad, projection_full, preferred_element_type=jnp.float32
    )
    upstream_all = jnp.where(own_present[:, :, None], (pooled_grad / denominator)[:, None, :], 0.0)
    upstream_all = upstream_all.reshape(rows, width)
    collected = None
    patch_list = []
    message_list = []
    for index in range(MICRO):
        frame_weights = fetch()
        start = index * per_block
        patch_grad, message_token_grad, block_grads = frame_backward(
            kept_blocks[index], upstream_all[start : start + per_block], frame_weights
        )
        patch_list.append(patch_grad)
        message_list.append(message_token_grad)
        block_grads = (
            lax.psum_scatter(
                block_grads[0].astype(jnp.float32), "fsdp", scatter_dimension=0, tiled=True
            ),
            lax.psum_scatter(block_grads[1], "fsdp", scatter_dimension=0, tiled=True),
            lax.psum_scatter(block_grads[2], "fsdp", scatter_dimension=0, tiled=True),
            lax.psum_scatter(
                block_grads[3].astype(jnp.float32), "fsdp", scatter_dimension=0, tiled=True
            ),
            lax.psum_scatter(block_grads[4], "fsdp", scatter_dimension=0, tiled=True),
            lax.psum_scatter(block_grads[5], "fsdp", scatter_dimension=0, tiled=True),
        )
        collected = (
            block_grads if collected is None else jax.tree.map(jnp.add, collected, block_grads)
        )
    collected = (
        lax.psum(collected[0].astype(jnp.bfloat16), "dp").astype(jnp.float32),
        lax.psum(collected[1].astype(jnp.bfloat16), "dp").astype(jnp.float32),
        lax.psum(collected[2].astype(jnp.bfloat16), "dp").astype(jnp.float32),
        lax.psum(collected[3].astype(jnp.bfloat16), "dp").astype(jnp.float32),
        lax.psum(collected[4].astype(jnp.bfloat16), "dp").astype(jnp.float32),
        lax.psum(collected[5].astype(jnp.bfloat16), "dp").astype(jnp.float32),
    )
    message_token_grad = jnp.concatenate(message_list, 0).reshape(videos, local_frames, width)
    out_grad = lax.all_gather(message_token_grad, "dp", axis=1, tiled=True)
    out_low = out_grad.astype(jnp.bfloat16)
    merge_message_grad = jnp.einsum(
        "vfd,vfe->de", told, out_low, preferred_element_type=jnp.float32
    )
    told_grad = jnp.einsum("vfe,de->vfd", out_low, merge_full, preferred_element_type=jnp.float32)
    told_query_grad, told_key_grad, told_value_grad = attend_backward(
        told_queries, told_keys, told_values, present, told_normalizer, told_shares, told_grad
    )
    courier_mixed_grad = jnp.concatenate(
        [told_query_grad, told_key_grad, told_value_grad], 2
    ).astype(jnp.bfloat16)
    heads_message_grad = jnp.einsum(
        "vfd,vfe->de", message_norm, courier_mixed_grad, preferred_element_type=jnp.float32
    )
    message_norm_grad = jnp.einsum(
        "vfe,de->vfd", courier_mixed_grad, heads_full, preferred_element_type=jnp.float32
    )
    message_grad, courier_gain_grad = norm_back(message, courier_gain_full, message_norm_grad)
    message_grad = (message_grad + out_grad).astype(jnp.bfloat16)
    courier_grad = jnp.einsum(
        "vfd,vfe->de", leaders, message_grad, preferred_element_type=jnp.float32
    )
    leader_grad = jnp.einsum(
        "vfe,de->vfd", message_grad, courier_full, preferred_element_type=jnp.float32
    )
    own_leader = lax.dynamic_slice_in_dim(leader_grad, offset, local_frames, 1).reshape(rows, width)
    patch_all = jnp.concatenate(patch_list, 0)
    patch_all = patch_all.at[:, 0, :].add(own_leader)
    patch_out = patch_all.reshape(videos, local_frames, patch_count, width).astype(jnp.bfloat16)
    video_grads = (
        lax.psum_scatter(courier_grad, "fsdp", scatter_dimension=0, tiled=True),
        lax.psum_scatter(
            courier_gain_grad.astype(jnp.float32), "fsdp", scatter_dimension=0, tiled=True
        ),
        lax.psum_scatter(heads_message_grad, "fsdp", scatter_dimension=0, tiled=True),
        lax.psum_scatter(merge_message_grad, "fsdp", scatter_dimension=0, tiled=True),
        lax.psum_scatter(projection_grad, "fsdp", scatter_dimension=0, tiled=True),
    )
    return (
        loss,
        patch_out,
        video_grads[0],
        video_grads[1],
        video_grads[2],
        video_grads[3],
        collected[0],
        collected[1],
        collected[2],
        collected[3],
        collected[4],
        collected[5],
        video_grads[4],
    )


def solution(mesh):
    fitting = mesh.shape['dp'] == 4 and mesh.shape['fsdp'] == Z * Y
    return jax.shard_map(
        fast if fitting else shards,
        mesh=mesh,
        in_specs=(
            P("fsdp", "dp", None, None),
            P("fsdp"),
            P(("dp", "fsdp"), None),
            P("fsdp"),
            P("fsdp", None),
            P("fsdp"),
            P("fsdp", None),
            P("fsdp", None),
            P("fsdp"),
            P("fsdp", None),
            P("fsdp", None),
            P("fsdp"),
            P("fsdp", None),
            P("fsdp", None),
            P("fsdp", None),
        ),
        out_specs=(
            P("fsdp"),
            P("fsdp", "dp", None, None),
            P("fsdp", None),
            P("fsdp"),
            P("fsdp", None),
            P("fsdp", None),
            P("fsdp"),
            P("fsdp", None),
            P("fsdp", None),
            P("fsdp"),
            P("fsdp", None),
            P("fsdp", None),
            P("fsdp", None),
        ),
        check_vma=False,
    )
```

```python
import functools

import jax
import jax.numpy as jnp
from jax import lax
from jax.experimental import pallas as pl
from jax.experimental.pallas import tpu as pltpu
from jax.sharding import PartitionSpec as P

MESH = pl.DeviceIdType.MESH
Z, Y = 4, 2
HEADS = 12
HEAD = 64
EPSILON = 1e-05
LOGIT_SCALE = 64.0
PAD = 208
ROWS = 832
D = 768
F32 = jnp.float32
B16 = jnp.bfloat16

MICRO = 2

COURIER, GAINS, CHEADS, AHEADS, CMERGE, AMERGE, EXPAND, PROJ = 0, 768, 896, 3200, 5504, 6272, 7040, 10112
NCOLS = 10624
JOBS = ((0, 896), (896, 768), (1664, 768), (2432, 768), (3200, 768), (3968, 768), (4736, 768), (5504, 768), (6272, 768),
        (7040, 768), (7808, 768), (8576, 768), (9344, 768), (10112, 512))


class Pos:
    def __init__(self):
        self.dp = lax.axis_index("dp")
        self.k = lax.axis_index("fsdp")
        self.x, self.c = self.dp // 2, lax.rem(self.dp, 2)
        self.z, self.y = self.k // Y, lax.rem(self.k, Y)
        self.core = (self.x * 2 + 1 - self.c, self.k)
        self.xp = ((1 - self.x) * 2 + self.c, self.k)
        self.cross = ((1 - self.x) * 2 + 1 - self.c, self.k)
        self.yp = (self.dp, self.z * Y + 1 - self.y)
        self.team = (self.core, self.xp, self.cross)

    def ahead(self, d):
        return lax.rem(self.z + d, Z)

    def behind(self, d):
        return lax.rem(self.z - d + Z, Z)

    def column(self):
        return [(self.dp, self.ahead(d) * Y + self.y) for d in (1, 2, 3)]

    def peers(self):
        return [self.core, self.xp, self.yp] + self.column()

    def plane(self):
        return [(self.dp, lax.rem(self.k + d, Z * Y)) for d in range(1, Z * Y)]


def barrier(peers):
    semaphore = pltpu.get_barrier_semaphore()
    for peer in peers:
        pl.semaphore_signal(semaphore, inc=1, device_id=peer, device_id_type=MESH)
    pl.semaphore_wait(semaphore, len(peers))


def remote(source, target, send, receive, device):
    return pltpu.make_async_remote_copy(
        src_ref=source, dst_ref=target, send_sem=send, recv_sem=receive, device_id=device, device_id_type=MESH)


class Gather:
    def __init__(self, p, block, jobs, send, receive):
        self.p, self.block, self.jobs, self.send, self.receive = p, block, jobs, send, receive

    def copy(self, job, index, k, first, count, device):
        ref = self.block(k, first, count, job)
        return remote(ref, ref, self.send.at[job, index], self.receive.at[job, index], device)

    def far(self, d):
        p = self.p
        return p.behind(d + 1) * Y + p.y if d < 3 else p.behind(d - 3) * Y + 1 - p.y

    def stage(self, stage, job):
        if job < 0 or job >= self.jobs:
            return
        p, copy = self.p, self.copy
        own, single = 3 * p.c + p.x, 3 * p.c + 2 * p.x
        other = 3 * p.c + 2 * (1 - p.x)
        if stage == 0:
            for d, device in enumerate(p.column()):
                copy(job, d, p.k, own, 2, device).start()
            copy(job, 3, p.k, own, 2, p.yp).start()
        elif stage == 1:
            for d in range(3):
                k = self.far(d)
                copy(job, d, k, own, 2, p.core).wait_recv()
                copy(job, 4 + d, k, own, 2, p.yp).start()
                copy(job, 7 + d, k, single, 1, p.xp).start()
                copy(job, 14 + d, k, own, 2, p.core).start()
        elif stage == 2:
            for d in range(3, 7):
                k = self.far(d)
                copy(job, d, k, own, 2, p.core).wait_recv()
                copy(job, 7 + d, k, single, 1, p.xp).start()
                copy(job, 14 + d, k, own, 2, p.core).start()
        elif stage == 3:
            for d in range(7):
                k = self.far(d)
                copy(job, 7 + d, k, other, 1, p.core).wait_recv()
                copy(job, 21 + d, k, other, 1, p.core).start()
        elif stage == 4:
            for d in range(7):
                copy(job, 14 + d, self.far(d), 3 * (1 - p.c) + p.x, 2, p.core).wait_recv()
            for d in range(7):
                copy(job, 21 + d, self.far(d), 3 * (1 - p.c) + 2 * (1 - p.x), 1, p.core).wait_recv()
        elif stage == 5:
            for index in range(28):
                copy(job, index, p.k, 0, 2 if index < 7 or 14 <= index < 21 else 1, p.core).wait_send()

    def tick(self, t, lag):
        for stage in (5, 4, 3, 2, 1, 0):
            self.stage(stage, t - lag[stage])


class Spread:
    def __init__(self, p, source, target, send, receive, same=False):
        self.p, self.target = p, target
        count = Z * Y
        self.copies = []
        for d in range(1, count):
            to = lax.rem(p.k + d, count)
            part = source if same else source.at[to]
            self.copies.append(remote(part, target.at[p.k], send.at[d - 1], receive.at[d - 1], (p.dp, to)))
        self.arrivals = []
        for d in range(1, count):
            origin = lax.rem(p.k - d + count, count)
            self.arrivals.append(
                remote(target.at[origin], target.at[origin], send.at[d - 1], receive.at[d - 1], (p.dp, origin)))
        target[p.k] = source[...] if same else source[p.k]
        for copy in self.copies:
            copy.start()

    def wait(self):
        for copy in self.arrivals:
            copy.wait_recv()

    def done(self):
        for copy in self.copies:
            copy.wait_send()


class Team:
    def __init__(self, p, source, target, send, receive):
        self.copies, self.arrivals = [], []
        target[p.dp] = source[...]
        for index, other in enumerate(p.team):
            self.copies.append(remote(source, target.at[p.dp], send.at[index], receive.at[index], other))
            self.arrivals.append(remote(source, target.at[other[0]], send.at[index], receive.at[index], other))
        for copy in self.copies:
            copy.start()

    def wait(self):
        for copy in self.arrivals:
            copy.wait_recv()

    def done(self):
        for copy in self.copies:
            copy.wait_send()


class Reduce:
    def __init__(self, p, stage, buffers, fin, jobs, send, receive):
        self.p, self.stage, self.fin, self.jobs, self.send, self.receive = p, stage, fin, jobs, send, receive
        self.rc, self.rx, self.ry, self.rz, self.own, self.rf = buffers
        self.at = [0] * len(jobs)

    def copies(self, job, step):
        p = self.p
        first, count = self.jobs[job]
        cols = pl.ds(first, count)
        half, other = pl.ds(pl.multiple_of(48 * p.c, 16), 48), pl.ds(pl.multiple_of(48 * (1 - p.c), 16), 48)
        carried = pl.ds(pl.multiple_of((3 * p.c + p.x) * 16, 16), 32)
        away = pl.ds(pl.multiple_of((3 * p.c + 2 * (1 - p.x)) * 16, 16), 16)
        s, r = self.send, self.receive
        if step == 0:
            target = self.rc.at[job % 4, :, :, pl.ds(0, count)]
            return [remote(self.stage.at[:, other, cols], target, s.at[job, 0], r.at[job, 0], p.core)]
        if step == 1:
            return [remote(self.stage.at[:, away, cols], self.rx.at[:, :, cols], s.at[job, 1], r.at[job, 1], p.xp)]
        if step == 2:
            return [remote(self.stage.at[z * Y + 1 - p.y, carried, cols], self.ry.at[z, :, cols], s.at[job, 2 + z],
                           r.at[job, 2 + z], p.yp) for z in range(Z)]
        if step == 3:
            return [remote(self.stage.at[device[1], carried, cols], self.rz.at[d, :, cols], s.at[job, 6 + d],
                           r.at[job, 6 + d], device) for d, device in enumerate(p.column())]
        if step == 4:
            return [remote(self.own.at[:, cols], self.rf.at[:, cols], s.at[job, 9], r.at[job, 9], p.xp)]
        return [remote(self.fin.at[half, cols], self.fin.at[half, cols], s.at[job, 10], r.at[job, 10], p.core)]

    def next(self, *jobs, scale=None):
        for job in jobs:
            self.step(self.at[job], job, scale)
            self.at[job] += 1

    def step(self, step, job, scale):
        p = self.p
        first, count = self.jobs[job]
        cols = pl.ds(first, count)
        half, other = pl.ds(pl.multiple_of(48 * p.c, 16), 48), pl.ds(pl.multiple_of(48 * (1 - p.c), 16), 48)
        carried = pl.ds(pl.multiple_of((3 * p.c + p.x) * 16, 16), 32)
        if step == 6:
            remote(self.fin.at[other, cols], self.fin.at[other, cols], self.send.at[job, 10], self.receive.at[job, 10],
                   p.core).wait_recv()
        elif step > 0 and step < 6:
            for copy in self.copies(job, step - 1):
                copy.wait_recv()
        if step == 1:
            def add(k, carry):
                value = self.stage[k, half, cols].astype(F32) + self.rc[job % 4, k, :, pl.ds(0, count)].astype(F32)
                self.stage[k, half, cols] = value.astype(B16)
                return carry
            lax.fori_loop(0, Z * Y, add, 0)
        elif step == 2:
            def add(k, carry):
                value = self.stage[k, carried, cols].astype(F32)
                other_x = self.rx[k, :, cols].astype(F32)
                top = value[0:16] + jnp.where(p.x == 0, other_x, 0.0)
                low = value[16:32] + jnp.where(p.x == 0, 0.0, other_x)
                value = jnp.concatenate([top, low], 0)
                if scale is not None:
                    value = value * scale[0:1, cols]
                self.stage[k, carried, cols] = value.astype(B16)
                return carry
            lax.fori_loop(0, Z * Y, add, 0)
        elif step == 3:
            def add(z, carry):
                k = z * Y + p.y
                value = self.stage[k, carried, cols].astype(F32) + self.ry[z, :, cols].astype(F32)
                self.stage[k, carried, cols] = value.astype(B16)
                return carry
            lax.fori_loop(0, Z, add, 0)
        elif step == 4:
            total = self.stage[p.k, carried, cols].astype(F32)
            for d in range(3):
                total = total + self.rz[d, :, cols].astype(F32)
            self.own[:, cols] = total.astype(B16)
        elif step == 5:
            mine, theirs = self.own[:, cols].astype(F32), self.rf[:, cols].astype(F32)
            left = jnp.where(p.x == 0, mine[0:16], theirs[0:16])
            right = jnp.where(p.x == 0, theirs[16:32], mine[16:32])
            middle = jnp.where(p.x == 0, mine[16:32], mine[0:16]) + jnp.where(p.x == 0, theirs[0:16], theirs[16:32])
            self.fin[half, cols] = jnp.concatenate([left, middle, right], 0).astype(B16)
        if step < 6:
            for copy in self.copies(job, step):
                copy.start()
        if step == 7:
            for earlier in range(6):
                for copy in self.copies(job, earlier):
                    copy.wait_send()


def dot(a, b, ca=1, cb=0):
    return lax.dot_general(a, b, (((ca,), (cb,)), ((), ())), preferred_element_type=F32)


def normalize(value):
    center = value - jnp.mean(value, -1, keepdims=True)
    rate = lax.rsqrt(jnp.mean(center * center, -1, keepdims=True) + EPSILON)
    return center * rate, rate


def head_mask():
    return lax.broadcasted_iota(jnp.int32, (192, D), 0) // 16 == lax.broadcasted_iota(jnp.int32, (192, D), 1) // HEAD


def spread_heads(value):
    return jnp.where(head_mask(), jnp.concatenate([value.astype(F32)] * HEADS, 0), 0.0).astype(B16)


def join_heads(value):
    value = jnp.where(head_mask(), value, 0.0)
    total = value[0:16]
    for head in range(1, HEADS):
        total = total + value[16 * head : 16 * head + 16]
    return total


def row_of(value, index):
    rows = lax.broadcasted_iota(jnp.int32, value.shape, 0)
    return jnp.sum(jnp.where(rows == index, value, 0.0), 0, keepdims=True)


def forward_kernel(
    xs, lead, caption, counts, courier, gains, cheads, aheads, cmerge, amerge, expand, projection,
    full_o, normt_o, mixed_o, shares_o, seen_o, seent_o, hidden_o, n2t_o, d_o, gsum_o, hsum_o, gains_o,
    leaders_o, message_o, mnorm_o, mmix_o, mshare_o, told_o, mout_o, texts_o,
    full, leadbuf, norm, normt, mixed, shares, seen, seent, hidden, n2, n2t, dd,
    texts, ssem, rsem, lsem, lead_s, lead_r, text_s, text_r, osem,
):
    p = Pos()
    weights = ((courier, COURIER), (gains, GAINS), (cheads, CHEADS), (aheads, AHEADS), (cmerge, CMERGE), (amerge, AMERGE),
               (expand, EXPAND), (projection, PROJ))
    mine = pl.ds(pl.multiple_of(p.k * 96, 16), 96)
    loads = []
    for index, (ref, start) in enumerate(weights):
        copy = pltpu.make_async_copy(ref, full.at[mine, pl.ds(start, ref.shape[1])], lsem.at[index])
        copy.start()
        loads.append(copy)
    leadbuf[p.dp] = lead[...]
    barrier(p.plane() + list(p.team))
    text_hop = Spread(p, caption, texts, text_s, text_r, same=True)
    others = [p.core, p.xp, ((1 - p.x) * 2 + 1 - p.c, p.k)]
    sends = []
    for index, other in enumerate(others):
        copy = pltpu.make_async_remote_copy(
            src_ref=lead, dst_ref=leadbuf.at[p.dp], send_sem=lead_s.at[0, index], recv_sem=lead_r.at[0, index],
            device_id=other, device_id_type=MESH)
        copy.start()
        sends.append(copy)
    for copy in loads:
        copy.wait()
    def block(k, start, count, job):
        first_col, columns = JOBS[job]
        return full.at[pl.ds(pl.multiple_of(k * 96 + start * 16, 16), count * 16), pl.ds(first_col, columns)]

    gather = Gather(p, block, len(JOBS), ssem, rsem)
    lag = (0, 2, 4, 6, 8, 9)
    outs = []

    def out(source, target):
        copy = pltpu.make_async_copy(source, target, osem.at[len(outs)])
        copy.start()
        outs.append(copy)

    def ticks(first, last):
        for t in range(first, last + 1):
            gather.tick(t, lag)

    ticks(0, 4)
    text_hop.wait()
    text_team = Team(p, texts, texts_o, lead_s.at[1], lead_r.at[1])
    ticks(5, 8)
    for index, other in enumerate(others):
        pltpu.make_async_remote_copy(
            src_ref=lead, dst_ref=leadbuf.at[other[0]], send_sem=lead_s.at[0, index], recv_sem=lead_r.at[0, index],
            device_id=other, device_id_type=MESH).wait_recv()
    leaders = jnp.concatenate([leadbuf[index][0:4] for index in range(4)], 0)
    leaders_o[...] = leaders.astype(B16)
    rows = jnp.transpose(full[:, GAINS : GAINS + 128].astype(F32))[0:8]
    gains_o[...] = rows
    courier_gain, attend_gain, expand_gain = rows[0:1], rows[1:2], rows[2:3]
    message = dot(leaders.astype(B16), full[:, COURIER : COURIER + D])
    message_o[...] = message
    xh, _ = normalize(message)
    mnorm = (xh * courier_gain).astype(B16)
    mnorm_o[...] = mnorm

    def norm_frame(f, carry):
        here = pl.ds(pl.multiple_of(f * PAD, 16), PAD)
        xh, _ = normalize(xs[f].astype(F32))
        norm[here, :] = (xh * attend_gain).astype(B16)
        return carry

    lax.fori_loop(0, 4, norm_frame, 0)
    ticks(9, 11)
    mmix = dot(mnorm, full[:, CHEADS : CHEADS + 3 * D])
    mq, mk, mv = mmix[:, :D].astype(B16), mmix[:, D : 2 * D].astype(B16), mmix[:, 2 * D :].astype(B16)
    mmix_o[...] = mmix.astype(B16)
    scores = dot(spread_heads(mq), mk, 1, 1) * HEAD ** (-0.5)
    frames = lax.broadcasted_iota(jnp.int32, (192, 16), 1)
    scores = jnp.where(frames < counts[0], scores, -1000000000.0)
    raised = jnp.exp(scores - jnp.max(scores, -1, keepdims=True))
    mshare = raised / jnp.sum(raised, -1, keepdims=True)
    mshare_o[...] = mshare
    told = join_heads(dot(mshare.astype(B16), mv)).astype(B16)
    told_o[...] = told

    def heads_tile(base, factor):
        def body(n, carry):
            cols = pl.ds(pl.multiple_of(base + n * 256, 256), 256)
            wcols = pl.ds(pl.multiple_of(AHEADS + base + n * 256, 128), 256)
            mixed[:, cols] = (dot(norm[...], full[:, wcols]) * factor).astype(B16)
            return carry
        lax.fori_loop(0, 3, body, 0)

    ticks(12, 12)
    heads_tile(0, HEAD ** (-0.5))
    ticks(13, 13)
    heads_tile(D, 1.0)
    ticks(14, 14)
    heads_tile(2 * D, 1.0)
    ticks(15, 15)
    mout_all = message + dot(told, full[:, CMERGE : CMERGE + D])
    mout = jnp.concatenate([row_of(mout_all, p.dp * 4 + f) for f in range(4)] + [jnp.zeros((4, D), F32)], 0)
    mout_o[...] = mout
    xh, _ = normalize(mout)
    extra = (xh * attend_gain).astype(B16)
    extra_kv = dot(extra, full[:, AHEADS + D : AHEADS + 3 * D])
    extra = extra.astype(F32)
    spot = lax.broadcasted_iota(jnp.int32, (16, 1), 0) == 5
    for f in range(4):
        tail = pl.ds(f * PAD + 192, 16)
        norm[tail, :] = jnp.where(spot, extra[f : f + 1], norm[tail, :].astype(F32)).astype(B16)
        old = mixed[tail, D : 3 * D].astype(F32)
        mixed[tail, D : 3 * D] = jnp.where(spot, extra_kv[f : f + 1], old).astype(B16)
    out(mixed, mixed_o)

    first = lax.broadcasted_iota(jnp.int32, (PAD, 128), 1) < HEAD
    kept = lax.broadcasted_iota(jnp.int32, (PAD, PAD), 0) < 198

    def attend(f, pair):
        here = pl.ds(pl.multiple_of(f * PAD, 16), PAD)
        at = pl.multiple_of(pair * 128, 128)
        q = mixed[here, pl.ds(at, 128)]
        k = mixed[here, pl.ds(pl.multiple_of(D + at, 128), 128)]
        v = mixed[here, pl.ds(pl.multiple_of(2 * D + at, 128), 128)]
        total = None
        for h in range(2):
            mask = first if h == 0 else jnp.logical_not(first)
            kh, vh = jnp.where(mask, k, jnp.zeros_like(k)), jnp.where(mask, v, jnp.zeros_like(v))
            scores = jnp.where(kept, dot(kh, q, 1, 1), -1e30)
            raised = jnp.exp(scores - jnp.max(scores, 0, keepdims=True))
            share = (raised * (1.0 / jnp.sum(raised, 0, keepdims=True))).astype(B16)
            shares[f * HEADS + pair * 2 + h] = share
            part = dot(share, vh, 0, 0)
            total = part if total is None else total + part
        seen[here, pl.ds(at, 128)] = total.astype(B16)

    def attend_frame(f):
        def body(pair, carry):
            attend(f, pair)
            return carry
        lax.fori_loop(0, 6, body, 0)

    def merge_frames():
        def body(n, carry):
            cols = pl.ds(pl.multiple_of(n * 256, 256), 256)
            wcols = pl.ds(pl.multiple_of(AMERGE + n * 256, 128), 256)
            hidden[:, cols] = dot(seen[...], full[:, wcols])
            return carry
        lax.fori_loop(0, 3, body, 0)

    def hidden_frame(f, carry):
        here = pl.ds(pl.multiple_of(f * PAD, 16), PAD)
        value = hidden[here, :] + xs[f].astype(F32)
        hidden[here, :] = value
        xh, _ = normalize(value)
        n2[here, :] = (xh * expand_gain).astype(B16)
        return carry

    def row_mask(shape, axis):
        index = lax.broadcasted_iota(jnp.int32, shape, axis)
        good = index < 0
        for f in range(4):
            lost = jnp.where(p.dp * 4 + f < counts[0], 0, ROWS)
            good = jnp.logical_or(good, jnp.logical_and(index >= f * PAD + lost, index < f * PAD + 197 + lost * 0))
        return good

    mask_row = jnp.where(row_mask((16, ROWS), 1), 1.0, 0.0).astype(B16)

    def expand_tile(base):
        def body(n, carry):
            cols = pl.ds(pl.multiple_of(base + n * 256, 256), 256)
            wcols = pl.ds(pl.multiple_of(EXPAND + base + n * 256, 128), 256)
            grown = dot(n2[...], full[:, wcols])
            s = 0.5 + 0.5 * jnp.tanh(0.851 * grown)
            gated = grown * s
            dd[:, cols] = (s + 1.702 * gated * (1.0 - s)).astype(B16)
            gsum_o[:, cols] = dot(mask_row, gated.astype(B16))[0:8]
            return carry
        lax.fori_loop(0, 3, body, 0)

    attend_frame(0)
    ticks(16, 16)
    attend_frame(1)
    ticks(17, 17)
    attend_frame(2)
    attend_frame(3)
    out(seen, seen_o)
    out(shares, shares_o)
    ticks(18, 18)
    merge_frames()
    lax.fori_loop(0, 4, hidden_frame, 0)
    out(hidden, hidden_o)
    expand_tile(0)
    ticks(19, 19)
    expand_tile(D)
    high = hidden[...].astype(B16)
    low = (hidden[...] - high.astype(F32)).astype(B16)
    hsum_o[...] = (dot(mask_row, high) + dot(mask_row, low))[0:8]
    ticks(20, 20)
    expand_tile(2 * D)
    ticks(21, 21)
    out(full, full_o)
    expand_tile(3 * D)
    out(dd, d_o)
    mask_col = jnp.where(row_mask((ROWS, D), 0), 1.0, 0.0)
    n2t[...] = jnp.transpose((n2[...].astype(F32) * mask_col).astype(B16))
    out(n2t, n2t_o)
    normt[...] = jnp.transpose(norm[...])
    out(normt, normt_o)
    seent[...] = jnp.transpose(seen[...])
    out(seent, seent_o)
    ticks(22, 22)
    for copy in sends:
        copy.wait_send()
    text_team.wait()
    text_team.done()
    text_hop.done()
    for copy in outs:
        copy.wait()


def pack_row(row):
    return jnp.concatenate([row[:, 128 * r : 128 * r + 128] for r in range(6)] + [jnp.zeros((2, 128), F32)], 0)


def unpack_row(value):
    return jnp.concatenate([value[r : r + 1] for r in range(6)], 1)


def twice(value):
    high = value.astype(B16)
    return jnp.concatenate([high, (value - high.astype(F32)).astype(B16)], 0)


RJOBS = ((0, 768), (768, 768), (1536, 768), (2304, 768), (3072, 768), (3840, 768), (4608, 768), (5376, 768), (6144, 128))
BUNDLE = 8448
SIXTH = BUNDLE // 6


def rear_kernel(
    xs_h, normt_h, mixed_h, shares, seen_h, seent_h, hidden_h, n2t_h, d_h, full,
    gsum, hsum, shrink, texts, gains, mout, leaders, message, mnorm, mmix, mshare, told, counts, matches,
    patch_h, fin, loss_o, shrink_grad_o, courier_o, cheads_o, cmerge_o, proj_o, cgain_o, lead_o,
    stage, rc, rx, ry, rz, own, rf, bundle, wx, wmerge, wheads, normt, mixed, seen, seent, hidden, n2t, dd, sbuf, hg, low, dout,
    projection, vecs, team, gs, gr, ps, pr, rs_, rr, us, ur, gg, first, mog, mog_team,
    s_r, r_r, s_b, r_b, team_s, team_r, hop_s, hop_r, lsem, psem,
):
    p = Pos()
    pending = ((n2t_h, n2t), (d_h, dd), (full.at[:, pl.ds(PROJ, 512)], projection), (full.at[:, pl.ds(EXPAND, 3072)], wx),
               (hidden_h, hidden), (seent_h, seent), (full.at[:, pl.ds(AMERGE, D)], wmerge), (mixed_h, mixed), (seen_h, seen),
               (normt_h, normt), (full.at[:, pl.ds(AHEADS, 3 * D)], wheads))
    loads = []

    def load(source, target):
        copy = pltpu.make_async_copy(source, target, lsem.at[len(loads)])
        copy.start()
        loads.append(copy)
        return copy

    for source, target in pending:
        load(source, target)
    barrier(p.plane() + list(p.team))
    vecs[:, 0:384] = jnp.concatenate([gsum[0:1, 384 * k : 384 * k + 384] for k in range(8)], 0)
    vecs[:, 384:512] = pack_row(hsum[0:1, :])
    hop = Team(p, vecs, team, team_s.at[0], team_r.at[0])
    reduce = Reduce(p, stage, (rc, rx, ry, rz, own, rf), fin, RJOBS, s_r, r_r)

    def expand_tiles(start):
        def body(n, carry):
            cols = pl.ds(pl.multiple_of(start + n * 256, 256), 256)
            stage[:, :, cols] = dot(n2t[...], dd[:, cols]).astype(B16).reshape(8, 96, 256)
            return carry
        lax.fori_loop(0, 3, body, 0)

    text = jnp.concatenate([jnp.concatenate([texts[i, :, r, :] for r in range(4)], 1) for i in range(4)], 0)
    text_unit = (text * lax.rsqrt(jnp.sum(text * text, -1, keepdims=True) + 1e-06)).astype(B16)
    loads[0].wait()
    loads[1].wait()
    hop.wait()
    total = team[0] + team[1] + team[2] + team[3]
    for k in range(8):
        gs[k] = jnp.broadcast_to(total[k : k + 1, 0:384], (8, 384))
    hop.done()
    hop = Spread(p, gs, gr, hop_s.at[0], hop_r.at[0])
    expand_tiles(0)
    reduce.next(0)
    hop.wait()
    gated = jnp.concatenate([gr[v][0:1] for v in range(8)], 0)
    both = dot(twice(gated), shrink[...])
    part = both[0:8] + both[8:16]
    for v in range(8):
        ps[v] = pack_row(part[v : v + 1])
    hop.done()
    hop = Spread(p, ps, pr, hop_s.at[1], hop_r.at[1])
    expand_tiles(D)
    reduce.next(1, 0)
    hop.wait()
    packed = total[:, 384:512]
    for k in range(8):
        packed = packed + pr[k]
    hop.done()
    loads[2].wait()
    denominator = (counts[0] * 197).astype(F32)
    pooled = jnp.broadcast_to(unpack_row(packed / denominator), (8, D))
    embed = dot(pooled.astype(B16), projection[...])
    rate = lax.rsqrt(jnp.sum(embed * embed, -1, keepdims=True) + 1e-06)
    unit = embed * rate
    logits = dot(unit.astype(B16), text_unit, 1, 1) * LOGIT_SCALE
    peak = jnp.max(logits, -1, keepdims=True)
    normalizer = peak + jnp.log(jnp.sum(jnp.exp(logits - peak), -1, keepdims=True))
    matched = lax.broadcasted_iota(jnp.int32, logits.shape, 1) == matches[0]
    loss_o[...] = jnp.broadcast_to(normalizer - jnp.sum(jnp.where(matched, logits, 0.0), -1, keepdims=True), (8, 128))
    slope = (jnp.exp(logits - normalizer) - jnp.where(matched, 1.0, 0.0)).astype(B16)
    unit_grad = dot(slope, text_unit) * LOGIT_SCALE
    embed_grad = (rate * (unit_grad - unit * jnp.sum(unit * unit_grad, -1, keepdims=True))).astype(B16)
    rg = dot(embed_grad, projection[...], 1, 1) / denominator
    rs_[...] = pack_row(rg.astype(B16).astype(F32)[0:1])
    hop = Spread(p, rs_, rr, hop_s.at[2], hop_r.at[2], same=True)
    expand_tiles(2 * D)
    reduce.next(2, 1)
    hop.wait()
    rows = jnp.concatenate([unpack_row(rr[v]) for v in range(8)], 0).astype(B16)
    grad = dot(rows, shrink[...], 1, 1)
    for v in range(8):
        us[v] = jnp.broadcast_to(grad[v : v + 1], (8, 384))
    hop.done()
    hop = Spread(p, us, ur, hop_s.at[3], hop_r.at[3])
    expand_tiles(3 * D)
    reduce.next(3, 2)
    hop.wait()
    for k in range(8):
        gg[:, 384 * k : 384 * k + 384] = ur[k]
    hop.done()

    def scale_tile(n, carry):
        cols = pl.ds(pl.multiple_of(n * 256, 256), 256)
        dd[:, cols] = (dd[:, cols].astype(F32) * gg[0:1, cols]).astype(B16)
        return carry

    lax.fori_loop(0, 12, scale_tile, 0)
    reduce.next(0, 3, scale=gg)
    loads[3].wait()

    def norm_tile(n):
        hg[:, 256 * n : 256 * n + 256] = dot(dd[...], wx[256 * n : 256 * n + 256, :], 1, 1)

    norm_tile(0)
    reduce.next(1, scale=gg)
    norm_tile(1)
    reduce.next(0, 2, scale=gg)
    norm_tile(2)
    weights = [load(full.at[:, pl.ds(CHEADS, 3 * D)], wx.at[:, pl.ds(0, 3 * D)]), load(full.at[:, pl.ds(COURIER, D)], wx.at[:, pl.ds(3 * D, D)])]
    shrink_grad_o[...] = dot(twice(gated), jnp.concatenate([rows.astype(F32)] * 2, 0).astype(B16), 0, 0)
    reduce.next(1, 3, scale=gg)
    loads[4].wait()
    attend_gain, expand_gain = gains[1:2, :], gains[2:3, :]

    def hidden_frame(f, total):
        here = pl.ds(pl.multiple_of(f * PAD, 16), PAD)
        limit = jnp.where(p.dp * 4 + f < counts[0], 197, 0)
        good = lax.broadcasted_iota(jnp.int32, (PAD, D), 0) < limit
        xh, rate = normalize(hidden[here, :])
        dy = jnp.where(good, hg[here, :], 0.0)
        e = dy * expand_gain
        grad = rate * (e - jnp.mean(e, -1, keepdims=True) - xh * jnp.mean(e * xh, -1, keepdims=True))
        grad = grad + jnp.where(good, rg[0:1, :], 0.0)
        hg[here, :] = grad
        low[here, :] = grad.astype(B16)
        return total + jnp.sum(dy * xh, 0, keepdims=True)

    expand_gain_grad = lax.fori_loop(0, 4, hidden_frame, jnp.zeros((1, D), F32))
    reduce.next(0, 2)
    loads[5].wait()
    loads[6].wait()

    def merge_tile(n, carry):
        cols = pl.ds(pl.multiple_of(n * 256, 256), 256)
        stage[:, :, pl.ds(pl.multiple_of(3072 + n * 256, 128), 256)] = dot(seent[...], low[:, cols]).astype(B16).reshape(8, 96, 256)
        dout[:, cols] = dot(low[...], wmerge[cols, :], 1, 1).astype(B16)
        return carry

    lax.fori_loop(0, 3, merge_tile, 0)
    weights.append(load(full.at[:, pl.ds(CMERGE, D)], wmerge))
    reduce.next(4, 1, 3)
    loads[7].wait()
    loads[8].wait()
    half_lanes = lax.broadcasted_iota(jnp.int32, (PAD, 128), 1) < HEAD

    def fetch(index, slot):
        return pltpu.make_async_copy(shares.at[pl.ds(index * 2, 2)], sbuf.at[slot], psem.at[slot])

    fetch(0, 0).start()

    def attend_frame(f):
        def attend(pair, carry):
            index = f * 6 + pair
            slot = lax.rem(index, 2)

            @pl.when(index < 23)
            def _():
                fetch(index + 1, 1 - slot).start()

            fetch(index, slot).wait()
            here = pl.ds(f * PAD, PAD)
            at = pl.multiple_of(pair * 128, 128)
            qs, ks, vs = (pl.ds(pl.multiple_of(b + at, 128), 128) for b in (0, D, 2 * D))
            q, k, v = mixed[here, qs], mixed[here, ks], mixed[here, vs]
            do, o = dout[here, qs], seen[here, qs]
            right = jnp.concatenate([do, (-(do.astype(F32) * o.astype(F32))).astype(B16)], 1)
            dq = dk = dv = None
            zero = jnp.zeros_like(q)
            for h in range(2):
                mask = half_lanes if h == 0 else jnp.logical_not(half_lanes)
                share = sbuf[slot, h]
                left = jnp.concatenate([jnp.where(mask, v, zero), jnp.where(mask, jnp.ones_like(v), zero)], 1)
                ds = (share.astype(F32) * dot(left, right, 1, 1)).astype(B16)
                pq = dot(ds, jnp.where(mask, k, zero), 0, 0)
                pk = dot(ds, jnp.where(mask, q, zero))
                pv = dot(share, jnp.where(mask, do, zero))
                dq, dk, dv = (pq, pk, pv) if h == 0 else (dq + pq, dk + pk, dv + pv)
            mixed[here, qs] = (dq * HEAD ** (-0.5)).astype(B16)
            mixed[here, ks] = dk.astype(B16)
            mixed[here, vs] = dv.astype(B16)
            return carry
        lax.fori_loop(0, 6, attend, 0)

    attend_frame(0)
    reduce.next(4, 2, 0)
    attend_frame(1)
    reduce.next(3, 1)
    attend_frame(2)
    reduce.next(4, 2, 0, 0)
    attend_frame(3)
    tokens = load(xs_h, dout)
    reduce.next(4, 3, 1)
    loads[9].wait()

    def heads_tiles(start):
        def body(n, carry):
            cols = pl.ds(pl.multiple_of(start + n * 256, 256), 256)
            to = pl.ds(pl.multiple_of(3840 + start + n * 256, 128), 256)
            stage[:, :, to] = dot(normt[...], mixed[:, cols]).astype(B16).reshape(8, 96, 256)
            return carry
        lax.fori_loop(0, 3, body, 0)

    heads_tiles(0)
    reduce.next(5, 4)
    heads_tiles(D)
    reduce.next(5, 6, 2, 3)
    heads_tiles(2 * D)
    reduce.next(6, 7, 4)
    loads[10].wait()

    def tokens_tile(n, carry):
        cols = pl.ds(pl.multiple_of(n * 256, 256), 256)
        hidden[:, cols] = dot(mixed[...], wheads[cols, :], 1, 1)
        return carry

    lax.fori_loop(0, 3, tokens_tile, 0)
    reduce.next(5, 7)
    tokens.wait()
    spot = lax.broadcasted_iota(jnp.int32, (PAD, 1), 0) == 197
    place = lax.broadcasted_iota(jnp.int32, (8, D), 0)
    first[...] = jnp.zeros_like(first)
    mog[...] = jnp.zeros_like(mog)

    def token_frame(f, total):
        here = pl.ds(pl.multiple_of(f * PAD, 16), PAD)
        xh, rate = normalize(jnp.where(spot, row_of(mout[...], f), dout[here, :].astype(F32)))
        dy = hidden[here, :]
        e = dy * attend_gain
        grad = rate * (e - jnp.mean(e, -1, keepdims=True) - xh * jnp.mean(e * xh, -1, keepdims=True))
        patch = hg[here, :] + grad
        low[here, :] = patch.astype(B16)
        first[...] = jnp.where(place == f, patch[0:1], first[...])
        mog[...] = jnp.where(place == f, grad[197:198], mog[...])
        return total + jnp.sum(dy * xh, 0, keepdims=True)

    attend_gain_grad = lax.fori_loop(0, 4, token_frame, jnp.zeros((1, D), F32))
    hop = Team(p, mog, mog_team, team_s.at[1], team_r.at[1])
    patch_out = load(low, patch_h)
    reduce.next(6, 5)
    tall = jnp.concatenate([attend_gain_grad, expand_gain_grad, jnp.zeros((126, D), F32)], 0)
    stage[:, :, 6144:6272] = jnp.transpose(tall).astype(B16).reshape(8, 96, 128)
    reduce.next(8, 4)
    for copy in weights:
        copy.wait()
    hop.wait()
    out_grad = jnp.concatenate([mog_team[i][0:4] for i in range(4)], 0)
    courier_gain = gains[0:1, :]
    mq, mk, mv = mmix[:, 0:D], mmix[:, D : 2 * D], mmix[:, 2 * D : 3 * D]
    out_low = out_grad.astype(B16)
    told_grad = dot(out_low, wmerge[...], 1, 1).astype(B16)
    upstream = spread_heads(told_grad)
    share = mshare[...]
    share_grad = dot(upstream, mv, 1, 1)
    dv = dot(share.astype(B16), upstream, 0, 0)
    inner = jnp.sum(share * share_grad, -1, keepdims=True)
    ds = (share * (share_grad - inner)).astype(B16)
    dq = join_heads(dot(ds, mk)) * HEAD ** (-0.5)
    dk = dot(ds, spread_heads(mq), 0, 0) * HEAD ** (-0.5)
    mixed_grad = jnp.concatenate([dq, dk, dv], 1).astype(B16)
    norm_grad = dot(mixed_grad, wx[:, 0 : 3 * D], 1, 1)
    xh, rate = normalize(message[...])
    e = norm_grad * courier_gain
    grad = rate * (e - jnp.mean(e, -1, keepdims=True) - xh * jnp.mean(e * xh, -1, keepdims=True))
    message_grad = (out_grad + grad).astype(B16)
    top = lax.broadcasted_iota(jnp.int32, (16, 1), 0) == 0
    pooled_rows = jnp.where(top, jnp.concatenate([pooled, pooled], 0), 0.0).astype(B16)
    embed_rows = jnp.where(top, jnp.concatenate([embed_grad.astype(F32)] * 2, 0), 0.0).astype(B16)
    parts = (message_grad, mixed_grad, out_low, leaders[...], mnorm[...], told[...], pooled_rows, embed_rows,
             (norm_grad * xh).astype(B16))
    col = 0
    for part in parts:
        bundle[p.k, :, col : col + part.shape[1]] = part
        col += part.shape[1]

    def block(k, start, count, job):
        return bundle.at[k, :, pl.ds(pl.multiple_of(start * SIXTH, 128), count * SIXTH)]

    gather = Gather(p, block, 1, s_b, r_b)
    gather.stage(0, 0)
    leader_grad = dot(message_grad, wx[:, 3 * D : 4 * D], 1, 1)
    lead_o[...] = jnp.concatenate([row_of(leader_grad, p.dp * 4 + f) for f in range(4)] + [jnp.zeros((4, D), F32)], 0) + first[...]
    reduce.next(7, 6, 8)
    gather.stage(1, 0)
    reduce.next(5)
    gather.stage(2, 0)
    reduce.next(7, 6, 8)
    gather.stage(3, 0)
    reduce.next(5, 8)
    gather.stage(4, 0)
    whole = bundle[...].reshape(128, BUNDLE)
    pick = jnp.where(
        jnp.logical_and(lax.broadcasted_iota(jnp.int32, (D, 128), 0) == p.k * 96 + lax.broadcasted_iota(jnp.int32, (D, 128), 1),
                        lax.broadcasted_iota(jnp.int32, (D, 128), 1) < 96), 1.0, 0.0).astype(B16)

    def product(left, width, right, columns):
        chosen = dot(whole[:, left : left + width], pick).astype(B16)
        return dot(chosen, whole[:, right : right + columns], 0, 0)[0:96]

    courier_o[...] = product(3840, D, 0, D)
    cheads_o[...] = product(4608, D, D, 3 * D)
    reduce.next(7, 6, 8)
    cmerge_o[...] = product(5376, D, 3072, D)
    proj_o[...] = product(6144, D, 6912, 512)
    gain_grad = jnp.sum(whole[:, 7424:8192].astype(F32), 0, keepdims=True)
    gain_grad = twice(jnp.broadcast_to(gain_grad, (8, D)))
    both = dot(pick, gain_grad, 0, 1)
    cgain_o[...] = both[0:96, 0:8] + both[0:96, 8:16]
    for _ in range(8):
        for job in range(len(RJOBS)):
            if reduce.at[job] < 7:
                reduce.next(job)
    for job in range(len(RJOBS)):
        reduce.next(job)
    gather.stage(5, 0)
    hop.done()
    patch_out.wait()


VMEM = 62 * 1024 * 1000


def any_spec():
    return pl.BlockSpec(memory_space=pl.ANY)


def vmem_spec():
    return pl.BlockSpec(memory_space=pltpu.VMEM)


def smem_spec():
    return pl.BlockSpec(memory_space=pltpu.SMEM)


def sds(shape, dtype):
    return jax.ShapeDtypeStruct(shape, dtype)


def dma(*shape):
    return pltpu.SemaphoreType.DMA(shape)


def vm(shape, dtype):
    return pltpu.VMEM(shape, dtype)


def fast(
    patches, counts, captions, matches, courier, courier_gain, courier_heads, courier_merge, attend_gain, attend_heads,
    attend_merge, expand_gain, expand_weight, shrink_weight, projection,
):
    caption = jnp.pad(captions.astype(F32).reshape(4, 128), ((0, 4), (0, 0)))
    xs = jnp.pad(patches[0], ((0, 0), (0, PAD - 197), (0, 0)))
    lead = jnp.pad(patches[0, :, 0, :].astype(F32), ((0, 4), (0, 0)))
    gain_block = jnp.stack([courier_gain, attend_gain, expand_gain], 1)
    gain_block = jnp.pad(gain_block, ((0, 0), (0, 125)))
    anys, vmem, smem = any_spec(), vmem_spec(), smem_spec()
    (full, normt, mixed, shares, seen, seent, hidden, n2t, dd, gsum, hsum, gains,
     leaders, message, mnorm, mmix, mshare, told, mout, texts) = pl.pallas_call(
        forward_kernel,
        out_shape=(
            sds((D, NCOLS), B16), sds((D, ROWS), B16), sds((ROWS, 3 * D), B16), sds((48, PAD, PAD), B16), sds((ROWS, D), B16),
            sds((D, ROWS), B16), sds((ROWS, D), F32), sds((D, ROWS), B16), sds((ROWS, 4 * D), B16), sds((8, 4 * D), F32),
            sds((8, D), F32), sds((8, D), F32), sds((16, D), B16), sds((16, D), F32), sds((16, D), B16), sds((16, 3 * D), B16),
            sds((192, 16), F32), sds((16, D), B16), sds((8, D), F32), sds((4, 8, 8, 128), F32)),
        in_specs=[vmem, vmem, vmem, smem] + [anys] * 8,
        out_specs=tuple([anys] * 9 + [vmem] * 11),
        scratch_shapes=[
            vm((D, NCOLS), B16), vm((4, 8, D), F32), vm((ROWS, D), B16), vm((D, ROWS), B16), vm((ROWS, 3 * D), B16),
            vm((48, PAD, PAD), B16), vm((ROWS, D), B16), vm((D, ROWS), B16), vm((ROWS, D), F32), vm((ROWS, D), B16),
            vm((D, ROWS), B16), vm((ROWS, 4 * D), B16),
            vm((8, 8, 128), F32), dma(len(JOBS), 28), dma(len(JOBS), 28), dma(8), dma(2, 3), dma(2, 3), dma(7), dma(7), dma(9)],
        compiler_params=pltpu.CompilerParams(collective_id=0, has_side_effects=True, vmem_limit_bytes=60 << 20),
        name="forward",
    )(xs, lead, caption, counts, courier, gain_block, courier_heads, attend_heads, courier_merge, attend_merge, expand_weight, projection)
    (patch, fin, loss, shrink_grad, courier_grad, cheads_grad, cmerge_grad, proj_grad, cgain, leads) = pl.pallas_call(
        rear_kernel,
        out_shape=(
            sds((ROWS, D), B16), sds((96, 6272), B16), sds((8, 128), F32), sds((384, D), F32), sds((96, D), F32),
            sds((96, 3 * D), F32), sds((96, D), F32), sds((96, 512), F32), sds((96, 8), F32), sds((8, D), F32)),
        in_specs=[anys] * 10 + [vmem] * 12 + [smem] * 2,
        out_specs=tuple([anys] + [vmem] * 9),
        scratch_shapes=[
            vm((8, 96, 6272), B16), vm((4, 8, 48, D), B16), vm((8, 16, 6272), B16), vm((4, 32, 6272), B16),
            vm((3, 32, 6272), B16), vm((32, 6272), B16), vm((32, 6272), B16), vm((8, 16, BUNDLE), B16),
            vm((D, 4 * D), B16), vm((D, D), B16), vm((D, 3 * D), B16), vm((D, ROWS), B16), vm((ROWS, 3 * D), B16),
            vm((ROWS, D), B16), vm((D, ROWS), B16), vm((ROWS, D), F32), vm((D, ROWS), B16), vm((ROWS, 4 * D), B16),
            vm((2, 2, PAD, PAD), B16), vm((ROWS, D), F32), vm((ROWS, D), B16), vm((ROWS, D), B16),
            vm((D, 512), B16), vm((8, 512), F32), vm((4, 8, 512), F32), vm((8, 8, 384), F32), vm((8, 8, 384), F32),
            vm((8, 8, 128), F32), vm((8, 8, 128), F32), vm((8, 128), F32), vm((8, 8, 128), F32), vm((8, 8, 384), F32),
            vm((8, 8, 384), F32), vm((8, 4 * D), F32), vm((8, D), F32), vm((8, D), F32), vm((4, 8, D), F32),
            dma(len(RJOBS), 11), dma(len(RJOBS), 11), dma(1, 28), dma(1, 28), dma(2, 3), dma(2, 3), dma(4, 7), dma(4, 7),
            dma(16), dma(2)],
        compiler_params=pltpu.CompilerParams(collective_id=1, has_side_effects=True, vmem_limit_bytes=VMEM),
        name="rear",
    )(xs.reshape(ROWS, D), normt, mixed, shares, seen, seent, hidden, n2t, dd, full, gsum, hsum, shrink_weight, texts, gains, mout,
      leaders, message, mnorm, mmix, mshare, told, counts, matches)
    patch_grad = jnp.concatenate([leads[0:4, None, :].astype(B16), patch.reshape(4, PAD, D)[:, 1:197]], 1)[None]
    out = fin.astype(F32)
    return (
        loss[0:1, 0], patch_grad, courier_grad, cgain[:, 0], cheads_grad, cmerge_grad, out[:, 6144], out[:, 3840:6144],
        out[:, 3072:3840], out[:, 6145], out[:, 0:3072], shrink_grad, proj_grad,
    )


def joined_2(value, axis, join):
    pieces = jax.tree.map(lambda part: lax.all_gather(part, axis), value)
    head = jax.tree.map(lambda part: part[0], pieces)
    tail = jax.tree.map(lambda part: part[1:], pieces)
    running, _ = lax.scan(lambda running, share: (join(running, share), None), head, tail)
    return running


def layer_norm(value, gain):
    center = value - jnp.mean(value, -1, keepdims=True)
    spread = jnp.mean(center * center, -1, keepdims=True)
    return center * lax.rsqrt(spread + EPSILON) * gain


def norm_back(value, gain, upstream):
    _, pull = jax.vjp(layer_norm, value, gain)
    return pull(upstream)


def quick_gelu(value):
    return value * jax.nn.sigmoid(1.702 * value)


def unit_rows(value):
    return value * lax.rsqrt(jnp.sum(value * value, -1, keepdims=True) + 1e-06)


def split_heads(mixed, query_count):
    batch, length, triple = mixed.shape
    width = triple // 3
    rounded = mixed.astype(jnp.bfloat16)
    queries = rounded[:, :query_count, :width].reshape(batch, query_count, HEADS, HEAD)
    keys = rounded[:, :, width : 2 * width].reshape(batch, length, HEADS, HEAD)
    values = rounded[:, :, 2 * width :].reshape(batch, length, HEADS, HEAD)
    return (queries, keys, values)


def scores_of(queries, keys, key_mask):
    scores = jnp.einsum(
        "bqhd,bkhd->bhqk", queries, keys, preferred_element_type=jnp.float32
    ) * HEAD ** (-0.5)
    if key_mask is not None:
        scores = jnp.where(key_mask[:, None, None, :], scores, -1000000000.0)
    return scores


def attend_forward(queries, keys, values, key_mask):
    scores = scores_of(queries, keys, key_mask)
    peak = jnp.max(scores, -1, keepdims=True)
    raised = jnp.exp(scores - peak)
    total = jnp.sum(raised, -1, keepdims=True)
    shares = (raised / total).astype(jnp.bfloat16)
    joined = jnp.einsum("bhqk,bkhd->bqhd", shares, values, preferred_element_type=jnp.float32)
    batch, count = (joined.shape[0], joined.shape[1])
    return (
        joined.reshape(batch, count, HEADS * HEAD).astype(jnp.bfloat16),
        peak + jnp.log(total),
        shares,
    )


def attend_backward(queries, keys, values, key_mask, normalizer, shares, upstream):
    batch, count, width = upstream.shape
    upstream_low = upstream.astype(jnp.bfloat16).reshape(batch, count, HEADS, HEAD)
    chances = jnp.exp(scores_of(queries, keys, key_mask) - normalizer)
    share_grad = jnp.einsum(
        "bqhd,bkhd->bhqk", upstream_low, values, preferred_element_type=jnp.float32
    )
    value_grad = jnp.einsum(
        "bhqk,bqhd->bkhd", shares, upstream_low, preferred_element_type=jnp.float32
    )
    inner = jnp.sum(chances * share_grad, -1, keepdims=True)
    score_grad = (chances * (share_grad - inner)).astype(jnp.bfloat16)
    query_grad = jnp.einsum(
        "bhqk,bkhd->bqhd", score_grad, keys, preferred_element_type=jnp.float32
    ) * HEAD ** (-0.5)
    key_grad = jnp.einsum(
        "bhqk,bqhd->bkhd", score_grad, queries, preferred_element_type=jnp.float32
    ) * HEAD ** (-0.5)
    length = keys.shape[1]
    return (
        query_grad.reshape(batch, count, width),
        key_grad.reshape(batch, length, width),
        value_grad.reshape(batch, length, width),
    )


def frame_forward(block, message_rows, weights):
    attend_gain, attend_heads, attend_merge, expand_gain, expand_weight, shrink_weight = weights
    frames = block.astype(jnp.float32)
    tokens = jnp.concatenate([frames, message_rows[:, None, :]], 1)
    normed = layer_norm(tokens, attend_gain).astype(jnp.bfloat16)
    mixed = jnp.einsum("btd,de->bte", normed, attend_heads, preferred_element_type=jnp.float32)
    queries, keys, values = split_heads(mixed, block.shape[1])
    seen, normalizer, shares = attend_forward(queries, keys, values, None)
    hidden = frames + jnp.einsum(
        "bpd,de->bpe", seen, attend_merge, preferred_element_type=jnp.float32
    )
    normed_two = layer_norm(hidden, expand_gain).astype(jnp.bfloat16)
    grown = jnp.einsum("bpd,dm->bpm", normed_two, expand_weight, preferred_element_type=jnp.float32)
    gated = quick_gelu(grown).astype(jnp.bfloat16)
    result = hidden + jnp.einsum(
        "bpm,md->bpd", gated, shrink_weight, preferred_element_type=jnp.float32
    )
    kept = (
        tokens,
        normed,
        queries,
        keys,
        values,
        shares,
        normalizer,
        seen,
        hidden,
        normed_two,
        grown,
        gated,
    )
    return (jnp.sum(result, 1), kept)


def frame_backward(kept, upstream, weights):
    attend_gain, attend_heads, attend_merge, expand_gain, expand_weight, shrink_weight = weights
    (
        tokens,
        normed,
        queries,
        keys,
        values,
        shares,
        normalizer,
        seen,
        hidden,
        normed_two,
        grown,
        gated,
    ) = kept
    patch_count = hidden.shape[1]
    upstream_low = upstream.astype(jnp.bfloat16)
    shrink_grad = jnp.einsum("bpm,bd->md", gated, upstream_low, preferred_element_type=jnp.float32)
    gated_grad = jnp.einsum(
        "bd,md->bm", upstream_low, shrink_weight, preferred_element_type=jnp.float32
    )
    _, gelu_pull = jax.vjp(quick_gelu, grown)
    grown_grad = gelu_pull(jnp.broadcast_to(gated_grad[:, None, :], grown.shape))[0].astype(
        jnp.bfloat16
    )
    expand_grad = jnp.einsum(
        "bpd,bpm->dm", normed_two, grown_grad, preferred_element_type=jnp.float32
    )
    normed_two_grad = jnp.einsum(
        "bpm,dm->bpd", grown_grad, expand_weight, preferred_element_type=jnp.float32
    )
    hidden_grad, expand_gain_grad = norm_back(hidden, expand_gain, normed_two_grad)
    hidden_grad = hidden_grad + upstream[:, None, :]
    hidden_low = hidden_grad.astype(jnp.bfloat16)
    merge_grad = jnp.einsum("bpd,bpe->de", seen, hidden_low, preferred_element_type=jnp.float32)
    seen_grad = jnp.einsum(
        "bpe,de->bpd", hidden_low, attend_merge, preferred_element_type=jnp.float32
    )
    query_grad, key_grad, value_grad = attend_backward(
        queries, keys, values, None, normalizer, shares, seen_grad
    )
    length = tokens.shape[1]
    query_grad = jnp.pad(query_grad, ((0, 0), (0, length - patch_count), (0, 0)))
    mixed_grad = jnp.concatenate([query_grad, key_grad, value_grad], 2).astype(jnp.bfloat16)
    heads_grad = jnp.einsum("btd,bte->de", normed, mixed_grad, preferred_element_type=jnp.float32)
    normed_grad = jnp.einsum(
        "bte,de->btd", mixed_grad, attend_heads, preferred_element_type=jnp.float32
    )
    token_grad, attend_gain_grad = norm_back(tokens, attend_gain, normed_grad)
    patch_grad = hidden_grad + token_grad[:, :patch_count]
    block_grads = (
        attend_gain_grad,
        heads_grad,
        merge_grad,
        expand_gain_grad,
        expand_grad,
        shrink_grad,
    )
    return (patch_grad, token_grad[:, patch_count], block_grads)


def shards(
    patches,
    counts,
    captions,
    matches,
    courier,
    courier_gain,
    courier_heads,
    courier_merge,
    attend_gain,
    attend_heads,
    attend_merge,
    expand_gain,
    expand_weight,
    shrink_weight,
    projection,
):
    videos, local_frames, patch_count, width = patches.shape
    frame_total = local_frames * lax.axis_size("dp")
    offset = lax.axis_index("dp") * local_frames
    rows = videos * local_frames
    per_block = rows // MICRO
    courier_full, courier_gain_full, heads_full, merge_full, projection_full = (
        lax.all_gather(courier, "fsdp", axis=0, tiled=True),
        lax.all_gather(courier_gain, "fsdp", axis=0, tiled=True),
        lax.all_gather(courier_heads, "fsdp", axis=0, tiled=True),
        lax.all_gather(courier_merge, "fsdp", axis=0, tiled=True),
        lax.all_gather(projection, "fsdp", axis=0, tiled=True),
    )

    def fetch():
        return (
            lax.all_gather(attend_gain, "fsdp", axis=0, tiled=True),
            lax.all_gather(attend_heads, "fsdp", axis=0, tiled=True),
            lax.all_gather(attend_merge, "fsdp", axis=0, tiled=True),
            lax.all_gather(expand_gain, "fsdp", axis=0, tiled=True),
            lax.all_gather(expand_weight, "fsdp", axis=0, tiled=True),
            lax.all_gather(shrink_weight, "fsdp", axis=0, tiled=True),
        )

    leaders = lax.all_gather(patches[:, :, 0, :], "dp", axis=1, tiled=True)
    present = lax.broadcasted_iota(jnp.int32, (videos, frame_total), 1) < counts[:, None]
    message = jnp.einsum("vfd,de->vfe", leaders, courier_full, preferred_element_type=jnp.float32)
    message_norm = layer_norm(message, courier_gain_full).astype(jnp.bfloat16)
    message_mixed = jnp.einsum(
        "vfd,de->vfe", message_norm, heads_full, preferred_element_type=jnp.float32
    )
    told_queries, told_keys, told_values = split_heads(message_mixed, frame_total)
    told, told_normalizer, told_shares = attend_forward(
        told_queries, told_keys, told_values, present
    )
    message_out = message + jnp.einsum(
        "vfd,de->vfe", told, merge_full, preferred_element_type=jnp.float32
    )
    mine = lax.dynamic_slice_in_dim(message_out, offset, local_frames, 1).reshape(rows, width)
    flat = patches.reshape(rows, patch_count, width)
    frame_weights = fetch()
    kept_blocks = []
    sums = []
    for index in range(MICRO):
        if index > 0:
            frame_weights = fetch()
        start = index * per_block
        frame_sums, kept = frame_forward(
            flat[start : start + per_block], mine[start : start + per_block], frame_weights
        )
        kept_blocks.append(kept)
        sums.append(frame_sums)
    frame_sums = jnp.concatenate(sums, 0).reshape(videos, local_frames, width)
    own_present = lax.dynamic_slice_in_dim(present, offset, local_frames, 1)
    partial_value = jnp.sum(jnp.where(own_present[:, :, None], frame_sums, 0.0), 1)
    pooled_sum = lax.psum(partial_value, "dp")
    denominator = (counts * patch_count).astype(jnp.float32)[:, None]
    pooled = pooled_sum / denominator
    pooled_low = pooled.astype(jnp.bfloat16)
    embed = jnp.dot(pooled_low, projection_full, preferred_element_type=jnp.float32)
    video_unit = unit_rows(embed).astype(jnp.bfloat16)
    segment = lax.axis_index("dp") * (captions.shape[0] * lax.axis_size("fsdp"))

    def scores_for(piece):
        text_unit = unit_rows(piece.astype(jnp.float32)).astype(jnp.bfloat16)
        logits = (
            jnp.einsum("ve,te->vt", video_unit, text_unit, preferred_element_type=jnp.float32)
            * LOGIT_SCALE
        )
        positions = segment + lax.broadcasted_iota(jnp.int32, logits.shape, 1)
        return (text_unit, logits, positions == matches[:, None])

    peak = jnp.full((videos,), -1e30, jnp.float32)
    _, logits, matched = scores_for(lax.all_gather(captions, "fsdp", axis=0, tiled=True))
    fresh = jnp.maximum(peak, jnp.max(logits, 1))
    total = jnp.sum(jnp.exp(logits - fresh[:, None]), 1)
    picked = jnp.sum(jnp.where(matched, logits, 0.0), 1)
    peak, total, picked = (fresh, total, picked)

    def combine(first, second):
        top = jnp.maximum(first[0], second[0])
        joined = first[1] * jnp.exp(first[0] - top) + second[1] * jnp.exp(second[0] - top)
        return (top, joined, first[2] + second[2])

    peak, total, picked = joined_2((peak, total, picked), "dp", combine)
    normalizer = peak + jnp.log(total)
    loss = normalizer - picked
    text_unit, logits, matched = scores_for(lax.all_gather(captions, "fsdp", axis=0, tiled=True))
    slope = (jnp.exp(logits - normalizer[:, None]) - matched.astype(jnp.float32)).astype(
        jnp.bfloat16
    )
    unit_grad = jnp.dot(slope, text_unit, preferred_element_type=jnp.float32) * LOGIT_SCALE
    unit_grad = lax.psum(unit_grad, "dp")
    _, unit_pull = jax.vjp(unit_rows, embed)
    embed_grad = unit_pull(unit_grad)[0].astype(jnp.bfloat16)
    projection_grad = jnp.einsum(
        "vd,ve->de", pooled_low, embed_grad, preferred_element_type=jnp.float32
    )
    pooled_grad = jnp.einsum(
        "ve,de->vd", embed_grad, projection_full, preferred_element_type=jnp.float32
    )
    upstream_all = jnp.where(own_present[:, :, None], (pooled_grad / denominator)[:, None, :], 0.0)
    upstream_all = upstream_all.reshape(rows, width)
    collected = None
    patch_list = []
    message_list = []
    for index in range(MICRO):
        frame_weights = fetch()
        start = index * per_block
        patch_grad, message_token_grad, block_grads = frame_backward(
            kept_blocks[index], upstream_all[start : start + per_block], frame_weights
        )
        patch_list.append(patch_grad)
        message_list.append(message_token_grad)
        block_grads = (
            lax.psum_scatter(
                block_grads[0].astype(jnp.float32), "fsdp", scatter_dimension=0, tiled=True
            ),
            lax.psum_scatter(block_grads[1], "fsdp", scatter_dimension=0, tiled=True),
            lax.psum_scatter(block_grads[2], "fsdp", scatter_dimension=0, tiled=True),
            lax.psum_scatter(
                block_grads[3].astype(jnp.float32), "fsdp", scatter_dimension=0, tiled=True
            ),
            lax.psum_scatter(block_grads[4], "fsdp", scatter_dimension=0, tiled=True),
            lax.psum_scatter(block_grads[5], "fsdp", scatter_dimension=0, tiled=True),
        )
        collected = (
            block_grads if collected is None else jax.tree.map(jnp.add, collected, block_grads)
        )
    collected = (
        lax.psum(collected[0].astype(jnp.bfloat16), "dp").astype(jnp.float32),
        lax.psum(collected[1].astype(jnp.bfloat16), "dp").astype(jnp.float32),
        lax.psum(collected[2].astype(jnp.bfloat16), "dp").astype(jnp.float32),
        lax.psum(collected[3].astype(jnp.bfloat16), "dp").astype(jnp.float32),
        lax.psum(collected[4].astype(jnp.bfloat16), "dp").astype(jnp.float32),
        lax.psum(collected[5].astype(jnp.bfloat16), "dp").astype(jnp.float32),
    )
    message_token_grad = jnp.concatenate(message_list, 0).reshape(videos, local_frames, width)
    out_grad = lax.all_gather(message_token_grad, "dp", axis=1, tiled=True)
    out_low = out_grad.astype(jnp.bfloat16)
    merge_message_grad = jnp.einsum(
        "vfd,vfe->de", told, out_low, preferred_element_type=jnp.float32
    )
    told_grad = jnp.einsum("vfe,de->vfd", out_low, merge_full, preferred_element_type=jnp.float32)
    told_query_grad, told_key_grad, told_value_grad = attend_backward(
        told_queries, told_keys, told_values, present, told_normalizer, told_shares, told_grad
    )
    courier_mixed_grad = jnp.concatenate(
        [told_query_grad, told_key_grad, told_value_grad], 2
    ).astype(jnp.bfloat16)
    heads_message_grad = jnp.einsum(
        "vfd,vfe->de", message_norm, courier_mixed_grad, preferred_element_type=jnp.float32
    )
    message_norm_grad = jnp.einsum(
        "vfe,de->vfd", courier_mixed_grad, heads_full, preferred_element_type=jnp.float32
    )
    message_grad, courier_gain_grad = norm_back(message, courier_gain_full, message_norm_grad)
    message_grad = (message_grad + out_grad).astype(jnp.bfloat16)
    courier_grad = jnp.einsum(
        "vfd,vfe->de", leaders, message_grad, preferred_element_type=jnp.float32
    )
    leader_grad = jnp.einsum(
        "vfe,de->vfd", message_grad, courier_full, preferred_element_type=jnp.float32
    )
    own_leader = lax.dynamic_slice_in_dim(leader_grad, offset, local_frames, 1).reshape(rows, width)
    patch_all = jnp.concatenate(patch_list, 0)
    patch_all = patch_all.at[:, 0, :].add(own_leader)
    patch_out = patch_all.reshape(videos, local_frames, patch_count, width).astype(jnp.bfloat16)
    video_grads = (
        lax.psum_scatter(courier_grad, "fsdp", scatter_dimension=0, tiled=True),
        lax.psum_scatter(
            courier_gain_grad.astype(jnp.float32), "fsdp", scatter_dimension=0, tiled=True
        ),
        lax.psum_scatter(heads_message_grad, "fsdp", scatter_dimension=0, tiled=True),
        lax.psum_scatter(merge_message_grad, "fsdp", scatter_dimension=0, tiled=True),
        lax.psum_scatter(projection_grad, "fsdp", scatter_dimension=0, tiled=True),
    )
    return (
        loss,
        patch_out,
        video_grads[0],
        video_grads[1],
        video_grads[2],
        video_grads[3],
        collected[0],
        collected[1],
        collected[2],
        collected[3],
        collected[4],
        collected[5],
        video_grads[4],
    )


def solution(mesh):
    fitting = mesh.shape['dp'] == 4 and mesh.shape['fsdp'] == Z * Y
    return jax.shard_map(
        fast if fitting else shards,
        mesh=mesh,
        in_specs=(
            P("fsdp", "dp", None, None),
            P("fsdp"),
            P(("dp", "fsdp"), None),
            P("fsdp"),
            P("fsdp", None),
            P("fsdp"),
            P("fsdp", None),
            P("fsdp", None),
            P("fsdp"),
            P("fsdp", None),
            P("fsdp", None),
            P("fsdp"),
            P("fsdp", None),
            P("fsdp", None),
            P("fsdp", None),
        ),
        out_specs=(
            P("fsdp"),
            P("fsdp", "dp", None, None),
            P("fsdp", None),
            P("fsdp"),
            P("fsdp", None),
            P("fsdp", None),
            P("fsdp"),
            P("fsdp", None),
            P("fsdp", None),
            P("fsdp"),
            P("fsdp", None),
            P("fsdp", None),
            P("fsdp", None),
        ),
        check_vma=False,
    )
```

```python
import functools

import jax
import jax.numpy as jnp
from jax import lax
from jax.experimental import pallas as pl
from jax.experimental.pallas import tpu as pltpu
from jax.sharding import PartitionSpec as P

MESH = pl.DeviceIdType.MESH
Z, Y = 4, 2
HEADS = 12
HEAD = 64
EPSILON = 1e-05
LOGIT_SCALE = 64.0
PAD = 208
ROWS = 832
D = 768
F32 = jnp.float32
B16 = jnp.bfloat16

MICRO = 2

COURIER, GAINS, CHEADS, AHEADS, CMERGE, AMERGE, EXPAND, PROJ = 0, 768, 896, 3200, 5504, 6272, 7040, 10112
NCOLS = 10624
JOBS = ((0, 896), (896, 768), (1664, 768), (2432, 768), (3200, 768), (3968, 768), (4736, 768), (5504, 768), (6272, 768),
        (7040, 768), (7808, 768), (8576, 768), (9344, 768), (10112, 512))


class Pos:
    def __init__(self):
        self.dp = lax.axis_index("dp")
        self.k = lax.axis_index("fsdp")
        self.x, self.c = self.dp // 2, lax.rem(self.dp, 2)
        self.z, self.y = self.k // Y, lax.rem(self.k, Y)
        self.core = (self.x * 2 + 1 - self.c, self.k)
        self.xp = ((1 - self.x) * 2 + self.c, self.k)
        self.cross = ((1 - self.x) * 2 + 1 - self.c, self.k)
        self.yp = (self.dp, self.z * Y + 1 - self.y)
        self.team = (self.core, self.xp, self.cross)

    def ahead(self, d):
        return lax.rem(self.z + d, Z)

    def behind(self, d):
        return lax.rem(self.z - d + Z, Z)

    def column(self):
        return [(self.dp, self.ahead(d) * Y + self.y) for d in (1, 2, 3)]

    def peers(self):
        return [self.core, self.xp, self.yp] + self.column()

    def plane(self):
        return [(self.dp, lax.rem(self.k + d, Z * Y)) for d in range(1, Z * Y)]


def barrier(peers):
    semaphore = pltpu.get_barrier_semaphore()
    for peer in peers:
        pl.semaphore_signal(semaphore, inc=1, device_id=peer, device_id_type=MESH)
    pl.semaphore_wait(semaphore, len(peers))


def remote(source, target, send, receive, device):
    return pltpu.make_async_remote_copy(
        src_ref=source, dst_ref=target, send_sem=send, recv_sem=receive, device_id=device, device_id_type=MESH)


class Gather:
    def __init__(self, p, block, jobs, send, receive):
        self.p, self.block, self.jobs, self.send, self.receive = p, block, jobs, send, receive

    def copy(self, job, index, k, first, count, device):
        ref = self.block(k, first, count, job)
        return remote(ref, ref, self.send.at[job, index], self.receive.at[job, index], device)

    def far(self, d):
        p = self.p
        return p.behind(d + 1) * Y + p.y if d < 3 else p.behind(d - 3) * Y + 1 - p.y

    def stage(self, stage, job):
        if job < 0 or job >= self.jobs:
            return
        p, copy = self.p, self.copy
        own, single = 3 * p.c + p.x, 3 * p.c + 2 * p.x
        other = 3 * p.c + 2 * (1 - p.x)
        if stage == 0:
            for d, device in enumerate(p.column()):
                copy(job, d, p.k, own, 2, device).start()
            copy(job, 3, p.k, own, 2, p.yp).start()
        elif stage == 1:
            for d in range(3):
                k = self.far(d)
                copy(job, d, k, own, 2, p.core).wait_recv()
                copy(job, 4 + d, k, own, 2, p.yp).start()
                copy(job, 7 + d, k, single, 1, p.xp).start()
                copy(job, 14 + d, k, own, 2, p.core).start()
        elif stage == 2:
            for d in range(3, 7):
                k = self.far(d)
                copy(job, d, k, own, 2, p.core).wait_recv()
                copy(job, 7 + d, k, single, 1, p.xp).start()
                copy(job, 14 + d, k, own, 2, p.core).start()
        elif stage == 3:
            for d in range(7):
                k = self.far(d)
                copy(job, 7 + d, k, other, 1, p.core).wait_recv()
                copy(job, 21 + d, k, other, 1, p.core).start()
        elif stage == 4:
            for d in range(7):
                copy(job, 14 + d, self.far(d), 3 * (1 - p.c) + p.x, 2, p.core).wait_recv()
            for d in range(7):
                copy(job, 21 + d, self.far(d), 3 * (1 - p.c) + 2 * (1 - p.x), 1, p.core).wait_recv()
        elif stage == 5:
            for index in range(28):
                copy(job, index, p.k, 0, 2 if index < 7 or 14 <= index < 21 else 1, p.core).wait_send()

    def tick(self, t, lag):
        for stage in (5, 4, 3, 2, 1, 0):
            self.stage(stage, t - lag[stage])


class Spread:
    def __init__(self, p, source, target, send, receive, same=False):
        self.p, self.target = p, target
        count = Z * Y
        self.copies = []
        for d in range(1, count):
            to = lax.rem(p.k + d, count)
            part = source if same else source.at[to]
            self.copies.append(remote(part, target.at[p.k], send.at[d - 1], receive.at[d - 1], (p.dp, to)))
        self.arrivals = []
        for d in range(1, count):
            origin = lax.rem(p.k - d + count, count)
            self.arrivals.append(
                remote(target.at[origin], target.at[origin], send.at[d - 1], receive.at[d - 1], (p.dp, origin)))
        target[p.k] = source[...] if same else source[p.k]
        for copy in self.copies:
            copy.start()

    def wait(self):
        for copy in self.arrivals:
            copy.wait_recv()

    def done(self):
        for copy in self.copies:
            copy.wait_send()


class Team:
    def __init__(self, p, source, target, send, receive):
        self.copies, self.arrivals = [], []
        target[p.dp] = source[...]
        for index, other in enumerate(p.team):
            self.copies.append(remote(source, target.at[p.dp], send.at[index], receive.at[index], other))
            self.arrivals.append(remote(source, target.at[other[0]], send.at[index], receive.at[index], other))
        for copy in self.copies:
            copy.start()

    def wait(self):
        for copy in self.arrivals:
            copy.wait_recv()

    def done(self):
        for copy in self.copies:
            copy.wait_send()


class Reduce:
    def __init__(self, p, stage, buffers, fin, jobs, send, receive):
        self.p, self.stage, self.fin, self.jobs, self.send, self.receive = p, stage, fin, jobs, send, receive
        self.rc, self.rx, self.ry, self.rz, self.own, self.rf = buffers
        self.at = [0] * len(jobs)

    def copies(self, job, step):
        p = self.p
        first, count = self.jobs[job]
        cols = pl.ds(first, count)
        half, other = pl.ds(pl.multiple_of(48 * p.c, 16), 48), pl.ds(pl.multiple_of(48 * (1 - p.c), 16), 48)
        carried = pl.ds(pl.multiple_of((3 * p.c + p.x) * 16, 16), 32)
        away = pl.ds(pl.multiple_of((3 * p.c + 2 * (1 - p.x)) * 16, 16), 16)
        s, r = self.send, self.receive
        if step == 0:
            target = self.rc.at[job % 4, :, :, pl.ds(0, count)]
            return [remote(self.stage.at[:, other, cols], target, s.at[job, 0], r.at[job, 0], p.core)]
        if step == 1:
            return [remote(self.stage.at[:, away, cols], self.rx.at[:, :, cols], s.at[job, 1], r.at[job, 1], p.xp)]
        if step == 2:
            return [remote(self.stage.at[z * Y + 1 - p.y, carried, cols], self.ry.at[z, :, cols], s.at[job, 2 + z],
                           r.at[job, 2 + z], p.yp) for z in range(Z)]
        if step == 3:
            return [remote(self.stage.at[device[1], carried, cols], self.rz.at[d, :, cols], s.at[job, 6 + d],
                           r.at[job, 6 + d], device) for d, device in enumerate(p.column())]
        if step == 4:
            return [remote(self.own.at[:, cols], self.rf.at[:, cols], s.at[job, 9], r.at[job, 9], p.xp)]
        return [remote(self.fin.at[half, cols], self.fin.at[half, cols], s.at[job, 10], r.at[job, 10], p.core)]

    def next(self, *jobs, scale=None):
        for job in jobs:
            self.step(self.at[job], job, scale)
            self.at[job] += 1

    def step(self, step, job, scale):
        p = self.p
        first, count = self.jobs[job]
        cols = pl.ds(first, count)
        half, other = pl.ds(pl.multiple_of(48 * p.c, 16), 48), pl.ds(pl.multiple_of(48 * (1 - p.c), 16), 48)
        carried = pl.ds(pl.multiple_of((3 * p.c + p.x) * 16, 16), 32)
        if step == 6:
            remote(self.fin.at[other, cols], self.fin.at[other, cols], self.send.at[job, 10], self.receive.at[job, 10],
                   p.core).wait_recv()
        elif step > 0 and step < 6:
            for copy in self.copies(job, step - 1):
                copy.wait_recv()
        if step == 1:
            def add(k, carry):
                self.stage[k, half, cols] = self.stage[k, half, cols] + self.rc[job % 4, k, :, pl.ds(0, count)]
                return carry
            lax.fori_loop(0, Z * Y, add, 0)
        elif step == 2:
            def add(k, carry):
                value = self.stage[k, carried, cols].astype(F32)
                other_x = self.rx[k, :, cols].astype(F32)
                top = value[0:16] + jnp.where(p.x == 0, other_x, 0.0)
                low = value[16:32] + jnp.where(p.x == 0, 0.0, other_x)
                value = jnp.concatenate([top, low], 0)
                if scale is not None:
                    value = value * scale[0:1, cols]
                self.stage[k, carried, cols] = value.astype(B16)
                return carry
            lax.fori_loop(0, Z * Y, add, 0)
        elif step == 3:
            def add(z, carry):
                k = z * Y + p.y
                self.stage[k, carried, cols] = self.stage[k, carried, cols] + self.ry[z, :, cols]
                return carry
            lax.fori_loop(0, Z, add, 0)
        elif step == 4:
            total = self.stage[p.k, carried, cols].astype(F32)
            for d in range(3):
                total = total + self.rz[d, :, cols].astype(F32)
            self.own[:, cols] = total.astype(B16)
        elif step == 5:
            mine, theirs = self.own[:, cols].astype(F32), self.rf[:, cols].astype(F32)
            left = jnp.where(p.x == 0, mine[0:16], theirs[0:16])
            right = jnp.where(p.x == 0, theirs[16:32], mine[16:32])
            middle = jnp.where(p.x == 0, mine[16:32], mine[0:16]) + jnp.where(p.x == 0, theirs[0:16], theirs[16:32])
            self.fin[half, cols] = jnp.concatenate([left, middle, right], 0).astype(B16)
        if step < 6:
            for copy in self.copies(job, step):
                copy.start()
        if step == 7:
            for earlier in range(6):
                for copy in self.copies(job, earlier):
                    copy.wait_send()


def dot(a, b, ca=1, cb=0):
    return lax.dot_general(a, b, (((ca,), (cb,)), ((), ())), preferred_element_type=F32)


def normalize(value):
    center = value - jnp.mean(value, -1, keepdims=True)
    rate = lax.rsqrt(jnp.mean(center * center, -1, keepdims=True) + EPSILON)
    return center * rate, rate


def head_mask():
    return lax.broadcasted_iota(jnp.int32, (192, D), 0) // 16 == lax.broadcasted_iota(jnp.int32, (192, D), 1) // HEAD


def spread_heads(value):
    return jnp.where(head_mask(), jnp.concatenate([value.astype(F32)] * HEADS, 0), 0.0).astype(B16)


def join_heads(value):
    value = jnp.where(head_mask(), value, 0.0)
    total = value[0:16]
    for head in range(1, HEADS):
        total = total + value[16 * head : 16 * head + 16]
    return total


def row_of(value, index):
    rows = lax.broadcasted_iota(jnp.int32, value.shape, 0)
    return jnp.sum(jnp.where(rows == index, value, 0.0), 0, keepdims=True)


def forward_kernel(
    patches, captions, gains, counts, courier, cheads, aheads, cmerge, amerge, expand, projection,
    full_o, normt_o, mixed_o, shares_o, seen_o, seent_o, hidden_o, n2t_o, d_o, gsum_o, hsum_o, gains_o,
    leaders_o, message_o, mnorm_o, mmix_o, mshare_o, told_o, mout_o, texts_o, xs_o,
    full, xs, lead, caption, leadbuf, norm, normt, mixed, shares, seen, seent, hidden, n2, n2t, dd,
    texts, ssem, rsem, lsem, lead_s, lead_r, text_s, text_r, osem,
):
    p = Pos()
    weights = ((courier, COURIER), (cheads, CHEADS), (aheads, AHEADS), (cmerge, CMERGE), (amerge, AMERGE),
               (expand, EXPAND), (projection, PROJ))
    mine = pl.ds(pl.multiple_of(p.k * 96, 16), 96)
    loads = []
    for index, (ref, start) in enumerate(weights):
        copy = pltpu.make_async_copy(ref, full.at[mine, pl.ds(start, ref.shape[1])], lsem.at[index])
        copy.start()
        loads.append(copy)
    text = captions[...].astype(F32)
    caption[...] = jnp.concatenate([text[:, 128 * r : 128 * r + 128] for r in range(4)] + [jnp.zeros((4, 128), F32)], 0)
    lead[...] = jnp.concatenate([patches[0, f, 0:16, :].astype(F32)[0:1] for f in range(4)] + [jnp.zeros((4, D), F32)], 0)
    square = jnp.concatenate([gains[...].astype(F32), jnp.zeros((3, 32), F32)], 1)
    square = jnp.concatenate([square, jnp.zeros((125, 128), F32)], 0)
    full[mine, GAINS : GAINS + 128] = jnp.transpose(square)[0:96].astype(B16)
    leadbuf[p.dp] = lead[...]
    barrier(p.plane() + list(p.team))
    text_hop = Spread(p, caption, texts, text_s, text_r, same=True)
    others = [p.core, p.xp, ((1 - p.x) * 2 + 1 - p.c, p.k)]
    sends = []
    for index, other in enumerate(others):
        copy = pltpu.make_async_remote_copy(
            src_ref=lead, dst_ref=leadbuf.at[p.dp], send_sem=lead_s.at[0, index], recv_sem=lead_r.at[0, index],
            device_id=other, device_id_type=MESH)
        copy.start()
        sends.append(copy)
    for copy in loads:
        copy.wait()
    def block(k, start, count, job):
        first_col, columns = JOBS[job]
        return full.at[pl.ds(pl.multiple_of(k * 96 + start * 16, 16), count * 16), pl.ds(first_col, columns)]

    gather = Gather(p, block, len(JOBS), ssem, rsem)
    lag = (0, 2, 4, 6, 8, 9)
    outs = []

    def out(source, target):
        copy = pltpu.make_async_copy(source, target, osem.at[len(outs)])
        copy.start()
        outs.append(copy)

    def ticks(first, last):
        for t in range(first, last + 1):
            gather.tick(t, lag)

    for f in range(4):
        xs[f * PAD + 192 : f * PAD + PAD, :] = jnp.zeros((16, D), B16)
        xs[f * PAD : f * PAD + 197, :] = patches[0, f]
    out(xs, xs_o)
    ticks(0, 4)
    text_hop.wait()
    text_team = Team(p, texts, texts_o, lead_s.at[1], lead_r.at[1])
    ticks(5, 8)
    for index, other in enumerate(others):
        pltpu.make_async_remote_copy(
            src_ref=lead, dst_ref=leadbuf.at[other[0]], send_sem=lead_s.at[0, index], recv_sem=lead_r.at[0, index],
            device_id=other, device_id_type=MESH).wait_recv()
    leaders = jnp.concatenate([leadbuf[index][0:4] for index in range(4)], 0)
    leaders_o[...] = leaders.astype(B16)
    rows = jnp.transpose(full[:, GAINS : GAINS + 128].astype(F32))[0:8]
    gains_o[...] = rows
    courier_gain, attend_gain, expand_gain = rows[0:1], rows[1:2], rows[2:3]
    message = dot(leaders.astype(B16), full[:, COURIER : COURIER + D])
    message_o[...] = message
    xh, _ = normalize(message)
    mnorm = (xh * courier_gain).astype(B16)
    mnorm_o[...] = mnorm

    def norm_frame(f, carry):
        here = pl.ds(pl.multiple_of(f * PAD, 16), PAD)
        xh, _ = normalize(xs[here, :].astype(F32))
        norm[here, :] = (xh * attend_gain).astype(B16)
        return carry

    lax.fori_loop(0, 4, norm_frame, 0)
    ticks(9, 11)
    mmix = dot(mnorm, full[:, CHEADS : CHEADS + 3 * D])
    mq, mk, mv = mmix[:, :D].astype(B16), mmix[:, D : 2 * D].astype(B16), mmix[:, 2 * D :].astype(B16)
    mmix_o[...] = mmix.astype(B16)
    scores = dot(spread_heads(mq), mk, 1, 1) * HEAD ** (-0.5)
    frames = lax.broadcasted_iota(jnp.int32, (192, 16), 1)
    scores = jnp.where(frames < counts[0], scores, -1000000000.0)
    raised = jnp.exp(scores - jnp.max(scores, -1, keepdims=True))
    mshare = raised / jnp.sum(raised, -1, keepdims=True)
    mshare_o[...] = mshare
    told = join_heads(dot(mshare.astype(B16), mv)).astype(B16)
    told_o[...] = told

    def heads_tile(base, factor):
        def body(n, carry):
            cols = pl.ds(pl.multiple_of(base + n * 256, 256), 256)
            wcols = pl.ds(pl.multiple_of(AHEADS + base + n * 256, 128), 256)
            mixed[:, cols] = (dot(norm[...], full[:, wcols]) * factor).astype(B16)
            return carry
        lax.fori_loop(0, 3, body, 0)

    ticks(12, 12)
    heads_tile(0, HEAD ** (-0.5))
    ticks(13, 13)
    heads_tile(D, 1.0)
    ticks(14, 14)
    heads_tile(2 * D, 1.0)
    ticks(15, 15)
    mout_all = message + dot(told, full[:, CMERGE : CMERGE + D])
    mout = jnp.concatenate([row_of(mout_all, p.dp * 4 + f) for f in range(4)] + [jnp.zeros((4, D), F32)], 0)
    mout_o[...] = mout
    xh, _ = normalize(mout)
    extra = (xh * attend_gain).astype(B16)
    extra_kv = dot(extra, full[:, AHEADS + D : AHEADS + 3 * D])
    extra = extra.astype(F32)
    spot = lax.broadcasted_iota(jnp.int32, (16, 1), 0) == 5
    for f in range(4):
        tail = pl.ds(f * PAD + 192, 16)
        norm[tail, :] = jnp.where(spot, extra[f : f + 1], norm[tail, :].astype(F32)).astype(B16)
        old = mixed[tail, D : 3 * D].astype(F32)
        mixed[tail, D : 3 * D] = jnp.where(spot, extra_kv[f : f + 1], old).astype(B16)
    out(mixed, mixed_o)

    first = lax.broadcasted_iota(jnp.int32, (PAD, 128), 1) < HEAD
    kept = lax.broadcasted_iota(jnp.int32, (PAD, PAD), 0) < 198

    def attend(f, pair):
        here = pl.ds(pl.multiple_of(f * PAD, 16), PAD)
        at = pl.multiple_of(pair * 128, 128)
        q = mixed[here, pl.ds(at, 128)]
        k = mixed[here, pl.ds(pl.multiple_of(D + at, 128), 128)]
        v = mixed[here, pl.ds(pl.multiple_of(2 * D + at, 128), 128)]
        total = None
        for h in range(2):
            mask = first if h == 0 else jnp.logical_not(first)
            kh, vh = jnp.where(mask, k, jnp.zeros_like(k)), jnp.where(mask, v, jnp.zeros_like(v))
            scores = jnp.where(kept, dot(kh, q, 1, 1), -1e30)
            raised = jnp.exp(scores - jnp.max(scores, 0, keepdims=True))
            share = (raised * (1.0 / jnp.sum(raised, 0, keepdims=True))).astype(B16)
            shares[f * HEADS + pair * 2 + h] = share
            part = dot(share, vh, 0, 0)
            total = part if total is None else total + part
        seen[here, pl.ds(at, 128)] = total.astype(B16)

    def attend_frame(f):
        def body(pair, carry):
            attend(f, pair)
            return carry
        lax.fori_loop(0, 6, body, 0, unroll=6)

    def merge_frames():
        def body(n, carry):
            cols = pl.ds(pl.multiple_of(n * 256, 256), 256)
            wcols = pl.ds(pl.multiple_of(AMERGE + n * 256, 128), 256)
            hidden[:, cols] = dot(seen[...], full[:, wcols])
            return carry
        lax.fori_loop(0, 3, body, 0)

    def hidden_frame(f, carry):
        here = pl.ds(pl.multiple_of(f * PAD, 16), PAD)
        value = hidden[here, :] + xs[here, :].astype(F32)
        hidden[here, :] = value
        xh, _ = normalize(value)
        n2[here, :] = (xh * expand_gain).astype(B16)
        return carry

    def row_mask(shape, axis):
        index = lax.broadcasted_iota(jnp.int32, shape, axis)
        good = index < 0
        for f in range(4):
            lost = jnp.where(p.dp * 4 + f < counts[0], 0, ROWS)
            good = jnp.logical_or(good, jnp.logical_and(index >= f * PAD + lost, index < f * PAD + 197 + lost * 0))
        return good

    mask_row = jnp.where(row_mask((16, ROWS), 1), 1.0, 0.0).astype(B16)

    def expand_tile(base):
        def body(n, carry):
            cols = pl.ds(pl.multiple_of(base + n * 256, 256), 256)
            wcols = pl.ds(pl.multiple_of(EXPAND + base + n * 256, 128), 256)
            grown = dot(n2[...], full[:, wcols])
            s = 0.5 + 0.5 * jnp.tanh(0.851 * grown)
            gated = grown * s
            dd[:, cols] = (s + 1.702 * gated * (1.0 - s)).astype(B16)
            gsum_o[:, cols] = dot(mask_row, gated.astype(B16))[0:8]
            return carry
        lax.fori_loop(0, 3, body, 0)

    attend_frame(0)
    ticks(16, 16)
    attend_frame(1)
    ticks(17, 17)
    attend_frame(2)
    attend_frame(3)
    out(seen, seen_o)
    out(shares, shares_o)
    ticks(18, 18)
    merge_frames()
    lax.fori_loop(0, 4, hidden_frame, 0)
    out(hidden, hidden_o)
    expand_tile(0)
    ticks(19, 19)
    expand_tile(D)
    high = hidden[...].astype(B16)
    low = (hidden[...] - high.astype(F32)).astype(B16)
    hsum_o[...] = (dot(mask_row, high) + dot(mask_row, low))[0:8]
    ticks(20, 20)
    expand_tile(2 * D)
    ticks(21, 21)
    out(full, full_o)
    expand_tile(3 * D)
    out(dd, d_o)
    mask_col = jnp.where(row_mask((ROWS, D), 0), 1.0, 0.0)
    n2t[...] = jnp.transpose((n2[...].astype(F32) * mask_col).astype(B16))
    out(n2t, n2t_o)
    normt[...] = jnp.transpose(norm[...])
    out(normt, normt_o)
    seent[...] = jnp.transpose(seen[...])
    out(seent, seent_o)
    ticks(22, 22)
    for copy in sends:
        copy.wait_send()
    text_team.wait()
    text_team.done()
    text_hop.done()
    for copy in outs:
        copy.wait()


def pack_row(row):
    return jnp.concatenate([row[:, 128 * r : 128 * r + 128] for r in range(6)] + [jnp.zeros((2, 128), F32)], 0)


def unpack_row(value):
    return jnp.concatenate([value[r : r + 1] for r in range(6)], 1)


def twice(value):
    high = value.astype(B16)
    return jnp.concatenate([high, (value - high.astype(F32)).astype(B16)], 0)


RJOBS = ((0, 768), (768, 768), (1536, 768), (2304, 768), (3072, 768), (3840, 768), (4608, 768), (5376, 768), (6144, 128))
BUNDLE = 3840
SIXTH = BUNDLE // 6


def rear_kernel(
    xs_h, normt_h, mixed_h, shares, seen_h, seent_h, hidden_h, n2t_h, d_h, full,
    gsum, hsum, shrink, texts, gains, mout, leaders, message, mnorm, mmix, mshare, told, counts, matches,
    patch_h, fin, loss_o, shrink_grad_o, courier_o, cheads_o, cmerge_o, proj_o, cgain_o, lead_o,
    stage, rc, rx, ry, rz, own, rf, bundle, wx, wmerge, wheads, mixed, seen, seent, hidden, n2t, dd, sbuf, hg, low, dout,
    projection, vecs, team, gs, gr, ps, pr, rs_, rr, us, ur, gg, first, mog, mog_team, chosen, gain_pack, gain_all,
    s_r, r_r, s_b, r_b, team_s, team_r, hop_s, hop_r, lsem, psem,
):
    p = Pos()
    pending = ((n2t_h, n2t), (d_h, dd), (full.at[:, pl.ds(PROJ, 512)], projection), (full.at[:, pl.ds(EXPAND, 3072)], wx),
               (hidden_h, hidden), (seent_h, seent), (full.at[:, pl.ds(AMERGE, D)], wmerge), (mixed_h, mixed), (seen_h, seen),
               (full.at[:, pl.ds(AHEADS, 3 * D)], wheads))
    loads = []

    def load(source, target):
        copy = pltpu.make_async_copy(source, target, lsem.at[len(loads)])
        copy.start()
        loads.append(copy)
        return copy

    for source, target in pending:
        load(source, target)
    barrier(p.plane() + list(p.team))
    vecs[:, 0:384] = jnp.concatenate([gsum[0:1, 384 * k : 384 * k + 384] for k in range(8)], 0)
    vecs[:, 384:512] = pack_row(hsum[0:1, :])
    hop = Team(p, vecs, team, team_s.at[0], team_r.at[0])
    reduce = Reduce(p, stage, (rc, rx, ry, rz, own, rf), fin, RJOBS, s_r, r_r)

    def expand_tiles(start):
        def body(n, carry):
            cols = pl.ds(pl.multiple_of(start + n * 256, 256), 256)
            stage[:, :, cols] = dot(n2t[...], dd[:, cols]).astype(B16).reshape(8, 96, 256)
            return carry
        lax.fori_loop(0, 3, body, 0)

    text = jnp.concatenate([jnp.concatenate([texts[i, :, r, :] for r in range(4)], 1) for i in range(4)], 0)
    text_unit = (text * lax.rsqrt(jnp.sum(text * text, -1, keepdims=True) + 1e-06)).astype(B16)
    loads[0].wait()
    loads[1].wait()
    hop.wait()
    total = team[0] + team[1] + team[2] + team[3]
    for k in range(8):
        gs[k] = jnp.broadcast_to(total[k : k + 1, 0:384], (8, 384))
    hop.done()
    hop = Spread(p, gs, gr, hop_s.at[0], hop_r.at[0])
    expand_tiles(0)
    reduce.next(0)
    hop.wait()
    gated = jnp.concatenate([gr[v][0:1] for v in range(8)], 0)
    both = dot(twice(gated), shrink[...])
    part = both[0:8] + both[8:16]
    for v in range(8):
        ps[v] = pack_row(part[v : v + 1])
    hop.done()
    hop = Spread(p, ps, pr, hop_s.at[1], hop_r.at[1])
    expand_tiles(D)
    reduce.next(1, 0)
    hop.wait()
    packed = total[:, 384:512]
    for k in range(8):
        packed = packed + pr[k]
    hop.done()
    loads[2].wait()
    denominator = (counts[0] * 197).astype(F32)
    pooled = jnp.broadcast_to(unpack_row(packed / denominator), (8, D))
    embed = dot(pooled.astype(B16), projection[...])
    rate = lax.rsqrt(jnp.sum(embed * embed, -1, keepdims=True) + 1e-06)
    unit = embed * rate
    logits = dot(unit.astype(B16), text_unit, 1, 1) * LOGIT_SCALE
    peak = jnp.max(logits, -1, keepdims=True)
    normalizer = peak + jnp.log(jnp.sum(jnp.exp(logits - peak), -1, keepdims=True))
    matched = lax.broadcasted_iota(jnp.int32, logits.shape, 1) == matches[0]
    loss_o[...] = jnp.broadcast_to(normalizer - jnp.sum(jnp.where(matched, logits, 0.0), -1, keepdims=True), (8, 128))
    slope = (jnp.exp(logits - normalizer) - jnp.where(matched, 1.0, 0.0)).astype(B16)
    unit_grad = dot(slope, text_unit) * LOGIT_SCALE
    embed_grad = (rate * (unit_grad - unit * jnp.sum(unit * unit_grad, -1, keepdims=True))).astype(B16)
    rg = dot(embed_grad, projection[...], 1, 1) / denominator
    rs_[...] = pack_row(rg.astype(B16).astype(F32)[0:1])
    hop = Spread(p, rs_, rr, hop_s.at[2], hop_r.at[2], same=True)

    def block(k, start, count, job):
        return bundle.at[job, k, :, pl.ds(pl.multiple_of(start * SIXTH, 128), count * SIXTH)]

    def fill(job, parts):
        col = 0
        for part in parts:
            bundle[job, p.k, :, col : col + part.shape[1]] = part
            col += part.shape[1]

    gather = Gather(p, block, 2, s_b, r_b)
    top = lax.broadcasted_iota(jnp.int32, (16, 1), 0) == 0
    pooled_rows = jnp.where(top, jnp.concatenate([pooled, pooled], 0), 0.0).astype(B16)
    embed_rows = jnp.where(top, jnp.concatenate([embed_grad.astype(F32)] * 2, 0), 0.0).astype(B16)
    fill(0, (leaders[...], mnorm[...], told[...], pooled_rows, embed_rows, jnp.zeros((16, 256), B16)))
    gather.stage(0, 0)
    expand_tiles(2 * D)
    reduce.next(2, 1)
    hop.wait()
    rows = jnp.concatenate([unpack_row(rr[v]) for v in range(8)], 0).astype(B16)
    grad = dot(rows, shrink[...], 1, 1)
    for v in range(8):
        us[v] = jnp.broadcast_to(grad[v : v + 1], (8, 384))
    hop.done()
    hop = Spread(p, us, ur, hop_s.at[3], hop_r.at[3])
    expand_tiles(3 * D)
    normt_load = load(normt_h, n2t)
    reduce.next(3, 2)
    gather.stage(1, 0)
    hop.wait()
    for k in range(8):
        gg[:, 384 * k : 384 * k + 384] = ur[k]
    hop.done()

    def scale_tile(n, carry):
        cols = pl.ds(pl.multiple_of(n * 256, 256), 256)
        dd[:, cols] = (dd[:, cols].astype(F32) * gg[0:1, cols]).astype(B16)
        return carry

    lax.fori_loop(0, 12, scale_tile, 0)
    reduce.next(0, 3, scale=gg)
    loads[3].wait()

    def norm_tile(n):
        hg[:, 256 * n : 256 * n + 256] = dot(dd[...], wx[256 * n : 256 * n + 256, :], 1, 1)

    norm_tile(0)
    reduce.next(1, scale=gg)
    gather.stage(2, 0)
    norm_tile(1)
    reduce.next(2, 0, scale=gg)
    gather.stage(3, 0)
    norm_tile(2)
    weights = [load(full.at[:, pl.ds(CHEADS, 3 * D)], wx.at[:, pl.ds(0, 3 * D)]), load(full.at[:, pl.ds(COURIER, D)], wx.at[:, pl.ds(3 * D, D)])]
    reduce.next(3, scale=gg)
    shrink_grad_o[...] = dot(twice(gated), jnp.concatenate([rows.astype(F32)] * 2, 0).astype(B16), 0, 0)
    loads[4].wait()
    attend_gain, expand_gain = gains[1:2, :], gains[2:3, :]

    def hidden_frame(f, total):
        here = pl.ds(pl.multiple_of(f * PAD, 16), PAD)
        limit = jnp.where(p.dp * 4 + f < counts[0], 197, 0)
        good = lax.broadcasted_iota(jnp.int32, (PAD, D), 0) < limit
        xh, rate = normalize(hidden[here, :])
        dy = jnp.where(good, hg[here, :], 0.0)
        e = dy * expand_gain
        grad = rate * (e - jnp.mean(e, -1, keepdims=True) - xh * jnp.mean(e * xh, -1, keepdims=True))
        grad = grad + jnp.where(good, rg[0:1, :], 0.0)
        hg[here, :] = grad
        low[here, :] = grad.astype(B16)
        return total + jnp.sum(dy * xh, 0, keepdims=True)

    expand_gain_grad = lax.fori_loop(0, 4, hidden_frame, jnp.zeros((1, D), F32))
    reduce.next(1, 0)
    gather.stage(4, 0)
    loads[5].wait()
    loads[6].wait()

    def merge_tile(n, carry):
        cols = pl.ds(pl.multiple_of(n * 256, 256), 256)
        stage[:, :, pl.ds(pl.multiple_of(3072 + n * 256, 128), 256)] = dot(seent[...], low[:, cols]).astype(B16).reshape(8, 96, 256)
        dout[:, cols] = dot(low[...], wmerge[cols, :], 1, 1).astype(B16)
        return carry

    lax.fori_loop(0, 3, merge_tile, 0)
    weights.append(load(full.at[:, pl.ds(CMERGE, D)], wmerge))
    reduce.next(4, 2)
    early = bundle[0].reshape(128, BUNDLE)
    pick = jnp.where(
        jnp.logical_and(lax.broadcasted_iota(jnp.int32, (D, 128), 0) == p.k * 96 + lax.broadcasted_iota(jnp.int32, (D, 128), 1),
                        lax.broadcasted_iota(jnp.int32, (D, 128), 1) < 96), 1.0, 0.0).astype(B16)
    for index in range(3):
        chosen[index] = dot(early[:, D * index : D * index + D], pick).astype(B16)
    proj_o[...] = dot(dot(early[:, 3 * D : 4 * D], pick).astype(B16), early[:, 4 * D : 4 * D + 512], 0, 0)[0:96]
    loads[7].wait()
    loads[8].wait()
    normt_load.wait()
    half_lanes = lax.broadcasted_iota(jnp.int32, (PAD, 128), 1) < HEAD

    def fetch(group):
        return pltpu.make_async_copy(shares.at[:, pl.ds(4 * group, 4)], sbuf.at[group % 2], psem.at[group % 2])

    fetch(0).start()

    def attend_group(group):
        if group < 2:
            fetch(group + 1).start()
        fetch(group).wait()
        inputs, outputs = [], []
        for f in range(4):
            for j in range(2):
                here = pl.ds(f * PAD, PAD)
                qs, ks, vs = (pl.ds(b + (2 * group + j) * 128, 128) for b in (0, D, 2 * D))
                inputs.append((here, qs, ks, vs, mixed[here, qs], mixed[here, ks], mixed[here, vs], dout[here, qs], seen[here, qs],
                               [sbuf[group % 2, f, 2 * j + h] for h in range(2)]))
        for here, qs, ks, vs, q, k, v, do, o, share_of in inputs:
            right = jnp.concatenate([do, (-(do.astype(F32) * o.astype(F32))).astype(B16)], 1)
            dq = dk = dv = None
            zero = jnp.zeros_like(q)
            for h in range(2):
                mask = half_lanes if h == 0 else jnp.logical_not(half_lanes)
                share = share_of[h]
                left = jnp.concatenate([jnp.where(mask, v, zero), jnp.where(mask, jnp.ones_like(v), zero)], 1)
                ds = (share.astype(F32) * dot(left, right, 1, 1)).astype(B16)
                pq = dot(ds, jnp.where(mask, k, zero), 0, 0)
                pk = dot(ds, jnp.where(mask, q, zero))
                pv = dot(share, jnp.where(mask, do, zero))
                dq, dk, dv = (pq, pk, pv) if h == 0 else (dq + pq, dk + pk, dv + pv)
            outputs.append((here, qs, ks, vs, (dq * HEAD ** (-0.5)).astype(B16), dk.astype(B16), dv.astype(B16)))
        for here, qs, ks, vs, dq, dk, dv in outputs:
            mixed[here, qs] = dq
            mixed[here, ks] = dk
            mixed[here, vs] = dv

    def heads_tiles(group):
        def body(n, carry):
            cols = pl.ds(pl.multiple_of(n * D + group * 256, 128), 256)
            to = pl.ds(pl.multiple_of(3840 + group * D + n * 256, 128), 256)
            stage[:, :, to] = dot(n2t[...], mixed[:, cols]).astype(B16).reshape(8, 96, 256)
            return carry
        lax.fori_loop(0, 3, body, 0)

    attend_group(0)
    reduce.next(4, 1, 3)
    heads_tiles(0)
    reduce.next(5, 2, 0)
    attend_group(1)
    reduce.next(4, 5, 1, 3)
    heads_tiles(1)
    reduce.next(6, 2, 0)
    attend_group(2)
    tokens = load(xs_h, dout)
    loads[9].wait()
    tails = [mixed[pl.ds(f * PAD + 192, 16), :].astype(F32)[5:6] for f in range(4)]
    tails = jnp.concatenate(tails + [jnp.zeros((12, 3 * D), F32)], 0).astype(B16)
    xh, rate = normalize(mout[...])
    e = dot(tails, wheads[...], 1, 1)[0:8] * attend_gain
    mog[...] = rate * (e - jnp.mean(e, -1, keepdims=True) - xh * jnp.mean(e * xh, -1, keepdims=True))
    hop = Team(p, mog, mog_team, team_s.at[1], team_r.at[1])
    reduce.next(6, 4, 5)
    heads_tiles(2)
    reduce.next(7, 1, 3)
    for copy in weights:
        copy.wait()
    hop.wait()
    out_grad = jnp.concatenate([mog_team[i][0:4] for i in range(4)], 0)
    courier_gain = gains[0:1, :]
    mq, mk, mv = mmix[:, 0:D], mmix[:, D : 2 * D], mmix[:, 2 * D : 3 * D]
    out_low = out_grad.astype(B16)
    told_grad = dot(out_low, wmerge[...], 1, 1).astype(B16)
    upstream = spread_heads(told_grad)
    share = mshare[...]
    share_grad = dot(upstream, mv, 1, 1)
    dv = dot(share.astype(B16), upstream, 0, 0)
    inner = jnp.sum(share * share_grad, -1, keepdims=True)
    ds = (share * (share_grad - inner)).astype(B16)
    dq = join_heads(dot(ds, mk)) * HEAD ** (-0.5)
    dk = dot(ds, spread_heads(mq), 0, 0) * HEAD ** (-0.5)
    mixed_grad = jnp.concatenate([dq, dk, dv], 1).astype(B16)
    reduce.next(6, 7, 4, 2)
    norm_grad = dot(mixed_grad, wx[:, 0 : 3 * D], 1, 1)
    xh, rate = normalize(message[...])
    e = norm_grad * courier_gain
    grad = rate * (e - jnp.mean(e, -1, keepdims=True) - xh * jnp.mean(e * xh, -1, keepdims=True))
    message_grad = (out_grad + grad).astype(B16)
    fill(1, (message_grad, mixed_grad, out_low))
    gather.stage(0, 1)
    gain_pack[...] = pack_row(jnp.sum(norm_grad * xh, 0, keepdims=True))
    gain_hop = Spread(p, gain_pack, gain_all, hop_s.at[4], hop_r.at[4], same=True)
    leader_grad = dot(message_grad, wx[:, 3 * D : 4 * D], 1, 1)
    reduce.next(5, 3)

    def tokens_tile(n):
        hidden[:, 256 * n : 256 * n + 256] = dot(mixed[...], wheads[256 * n : 256 * n + 256, :], 1, 1)

    tokens_tile(0)
    reduce.next(6, 7)
    gather.stage(1, 1)
    tokens_tile(1)
    reduce.next(4, 5)
    gather.stage(2, 1)
    tokens_tile(2)
    reduce.next(6, 7)
    gather.stage(3, 1)
    tokens.wait()
    spot = lax.broadcasted_iota(jnp.int32, (PAD, 1), 0) == 197
    place = lax.broadcasted_iota(jnp.int32, (8, D), 0)
    first[...] = jnp.zeros_like(first)

    def token_frame(f, total):
        here = pl.ds(pl.multiple_of(f * PAD, 16), PAD)
        xh, rate = normalize(jnp.where(spot, row_of(mout[...], f), dout[here, :].astype(F32)))
        dy = hidden[here, :]
        e = dy * attend_gain
        grad = rate * (e - jnp.mean(e, -1, keepdims=True) - xh * jnp.mean(e * xh, -1, keepdims=True))
        patch = hg[here, :] + grad
        low[here, :] = patch.astype(B16)
        first[...] = jnp.where(place == f, patch[0:1], first[...])
        return total + jnp.sum(dy * xh, 0, keepdims=True)

    attend_gain_grad = lax.fori_loop(0, 4, token_frame, jnp.zeros((1, D), F32))
    lead_o[...] = jnp.concatenate([row_of(leader_grad, p.dp * 4 + f) for f in range(4)] + [jnp.zeros((4, D), F32)], 0) + first[...]
    patch_out = load(low, patch_h)
    tall = jnp.concatenate([attend_gain_grad, expand_gain_grad, jnp.zeros((126, D), F32)], 0)
    stage[:, :, 6144:6272] = jnp.transpose(tall).astype(B16).reshape(8, 96, 128)
    reduce.next(8, 5, 4)
    gather.stage(4, 1)
    late = bundle[1].reshape(128, BUNDLE)
    courier_o[...] = dot(chosen[0], late[:, 0:D], 0, 0)[0:96]
    reduce.next(8, 6, 7)
    cheads_o[...] = dot(chosen[1], late[:, D : 4 * D], 0, 0)[0:96]
    cmerge_o[...] = dot(chosen[2], late[:, 4 * D : 5 * D], 0, 0)[0:96]
    reduce.next(8, 6, 7)
    gain_hop.wait()
    gain_grad = gain_all[0]
    for k in range(1, 8):
        gain_grad = gain_grad + gain_all[k]
    gain_grad = twice(jnp.broadcast_to(unpack_row(gain_grad), (8, D)))
    both = dot(pick, gain_grad, 0, 1)
    cgain_o[...] = both[0:96, 0:8] + both[0:96, 8:16]
    for _ in range(8):
        for job in range(len(RJOBS)):
            if reduce.at[job] < 7:
                reduce.next(job)
    for job in range(len(RJOBS)):
        reduce.next(job)
    gather.stage(5, 0)
    gather.stage(5, 1)
    gain_hop.done()
    hop.done()
    patch_out.wait()


def finish_kernel(patch, lead, fin, cgain, courier, cheads, cmerge, proj, shrink, loss,
                  patch_o, gains_o, heads_o, merge_o, expand_o, courier_o, cheads_o, cmerge_o, proj_o, shrink_o, loss_o):
    for source, target in ((courier, courier_o), (cheads, cheads_o), (cmerge, cmerge_o), (proj, proj_o), (shrink, shrink_o)):
        target[...] = source[...].astype(F32)
    top = lax.broadcasted_iota(jnp.int32, (PAD, 1), 0) == 0
    for f in range(4):
        value = jnp.where(top, lead[f : f + 1, :], patch[f * PAD : f * PAD + PAD, :].astype(F32)).astype(B16)
        patch_o[0, f] = value[0:197]
    expand_o[...] = fin[:, 0:3072].astype(F32)
    merge_o[...] = fin[:, 3072:3840].astype(F32)
    for group in range(3):
        for n in range(3):
            heads_o[:, n * D + group * 256 : n * D + group * 256 + 256] = fin[
                :, 3840 + group * D + n * 256 : 3840 + group * D + n * 256 + 256].astype(F32)
    wide = jnp.concatenate([fin[:, 6144:6272].astype(F32), jnp.zeros((32, 128), F32)], 0)
    columns = jnp.transpose(wide)[0:8, 0:96]
    own = jnp.concatenate([cgain[...], jnp.zeros((96, 120), F32)], 1)
    own = jnp.transpose(jnp.concatenate([own, jnp.zeros((32, 128), F32)], 0))[0:8, 0:96]
    gains_o[...] = jnp.concatenate([columns[0:2], own[0:1], jnp.zeros((5, 96), F32)], 0)
    loss_o[...] = loss[...]


VMEM = 62 * 1024 * 1000


def any_spec():
    return pl.BlockSpec(memory_space=pl.ANY)


def vmem_spec():
    return pl.BlockSpec(memory_space=pltpu.VMEM)


def smem_spec():
    return pl.BlockSpec(memory_space=pltpu.SMEM)


def sds(shape, dtype):
    return jax.ShapeDtypeStruct(shape, dtype)


def dma(*shape):
    return pltpu.SemaphoreType.DMA(shape)


def vm(shape, dtype):
    return pltpu.VMEM(shape, dtype)


def fast(
    patches, counts, captions, matches, courier, courier_gain, courier_heads, courier_merge, attend_gain, attend_heads,
    attend_merge, expand_gain, expand_weight, shrink_weight, projection,
):
    gain_block = jnp.stack([courier_gain, attend_gain, expand_gain], 0)
    anys, vmem, smem = any_spec(), vmem_spec(), smem_spec()
    (full, normt, mixed, shares, seen, seent, hidden, n2t, dd, gsum, hsum, gains,
     leaders, message, mnorm, mmix, mshare, told, mout, texts, xs) = pl.pallas_call(
        forward_kernel,
        out_shape=(
            sds((D, NCOLS), B16), sds((D, ROWS), B16), sds((ROWS, 3 * D), B16), sds((48, PAD, PAD), B16), sds((ROWS, D), B16),
            sds((D, ROWS), B16), sds((ROWS, D), F32), sds((D, ROWS), B16), sds((ROWS, 4 * D), B16), sds((8, 4 * D), F32),
            sds((8, D), F32), sds((8, D), F32), sds((16, D), B16), sds((16, D), F32), sds((16, D), B16), sds((16, 3 * D), B16),
            sds((192, 16), F32), sds((16, D), B16), sds((8, D), F32), sds((4, 8, 8, 128), F32),
            sds((ROWS, D), B16)),
        in_specs=[vmem, vmem, vmem, smem] + [anys] * 7,
        out_specs=tuple([anys] * 9 + [vmem] * 11 + [anys]),
        scratch_shapes=[
            vm((D, NCOLS), B16), vm((ROWS, D), B16), vm((8, D), F32), vm((8, 128), F32), vm((4, 8, D), F32), vm((ROWS, D), B16), vm((D, ROWS), B16), vm((ROWS, 3 * D), B16),
            vm((48, PAD, PAD), B16), vm((ROWS, D), B16), vm((D, ROWS), B16), vm((ROWS, D), F32), vm((ROWS, D), B16),
            vm((D, ROWS), B16), vm((ROWS, 4 * D), B16),
            vm((8, 8, 128), F32), dma(len(JOBS), 28), dma(len(JOBS), 28), dma(7), dma(2, 3), dma(2, 3), dma(7), dma(7), dma(10)],
        compiler_params=pltpu.CompilerParams(collective_id=0, has_side_effects=True, vmem_limit_bytes=60 << 20),
        name="forward",
    )(patches, captions, gain_block, counts, courier, courier_heads, attend_heads, courier_merge, attend_merge, expand_weight, projection)
    (patch, fin, loss, shrink_grad, courier_grad, cheads_grad, cmerge_grad, proj_grad, cgain, leads) = pl.pallas_call(
        rear_kernel,
        out_shape=(
            sds((ROWS, D), B16), sds((96, 6272), B16), sds((8, 128), F32), sds((384, D), F32), sds((96, D), F32),
            sds((96, 3 * D), F32), sds((96, D), F32), sds((96, 512), F32), sds((96, 8), F32), sds((8, D), F32)),
        in_specs=[anys] * 10 + [vmem] * 12 + [smem] * 2,
        out_specs=tuple([anys] + [vmem] * 9),
        scratch_shapes=[
            vm((8, 96, 6272), B16), vm((4, 8, 48, D), B16), vm((8, 16, 6272), B16), vm((4, 32, 6272), B16),
            vm((3, 32, 6272), B16), vm((32, 6272), B16), vm((32, 6272), B16), vm((2, 8, 16, BUNDLE), B16),
            vm((D, 4 * D), B16), vm((D, D), B16), vm((D, 3 * D), B16), vm((ROWS, 3 * D), B16),
            vm((ROWS, D), B16), vm((D, ROWS), B16), vm((ROWS, D), F32), vm((D, ROWS), B16), vm((ROWS, 4 * D), B16),
            vm((2, 4, 4, PAD, PAD), B16), vm((ROWS, D), F32), vm((ROWS, D), B16), vm((ROWS, D), B16),
            vm((D, 512), B16), vm((8, 512), F32), vm((4, 8, 512), F32), vm((8, 8, 384), F32), vm((8, 8, 384), F32),
            vm((8, 8, 128), F32), vm((8, 8, 128), F32), vm((8, 128), F32), vm((8, 8, 128), F32), vm((8, 8, 384), F32),
            vm((8, 8, 384), F32), vm((8, 4 * D), F32), vm((8, D), F32), vm((8, D), F32), vm((4, 8, D), F32),
            vm((3, 128, 128), B16), vm((8, 128), F32), vm((8, 8, 128), F32),
            dma(len(RJOBS), 11), dma(len(RJOBS), 11), dma(2, 28), dma(2, 28), dma(2, 3), dma(2, 3), dma(5, 7), dma(5, 7),
            dma(16), dma(2)],
        compiler_params=pltpu.CompilerParams(collective_id=1, has_side_effects=True, vmem_limit_bytes=VMEM),
        name="rear",
    )(xs, normt, mixed, shares.reshape(4, HEADS, PAD, PAD), seen, seent, hidden, n2t, dd, full, gsum, hsum, shrink_weight, texts, gains, mout,
      leaders, message, mnorm, mmix, mshare, told, counts, matches)
    patch_grad, gain_grads, heads, merge, expand, courier_out, cheads_out, cmerge_out, proj_out, shrink_out, loss_out = pl.pallas_call(
        finish_kernel,
        out_shape=(
            sds(patches.shape, B16), sds((8, 96), F32), sds((96, 3 * D), F32), sds((96, D), F32), sds((96, 4 * D), F32),
            sds((96, D), F32), sds((96, 3 * D), F32), sds((96, D), F32), sds((96, 512), F32), sds((384, D), F32), sds((8, 128), F32)),
        in_specs=[vmem] * 10,
        out_specs=tuple([vmem] * 11),
        compiler_params=pltpu.CompilerParams(vmem_limit_bytes=VMEM),
        name="finish",
    )(patch, leads, fin, cgain, courier_grad, cheads_grad, cmerge_grad, proj_grad, shrink_grad, loss)
    return (
        loss_out[0:1, 0], patch_grad, courier_out, gain_grads[2], cheads_out, cmerge_out, gain_grads[0], heads,
        merge, gain_grads[1], expand, shrink_out, proj_out,
    )


def joined_2(value, axis, join):
    pieces = jax.tree.map(lambda part: lax.all_gather(part, axis), value)
    head = jax.tree.map(lambda part: part[0], pieces)
    tail = jax.tree.map(lambda part: part[1:], pieces)
    running, _ = lax.scan(lambda running, share: (join(running, share), None), head, tail)
    return running


def layer_norm(value, gain):
    center = value - jnp.mean(value, -1, keepdims=True)
    spread = jnp.mean(center * center, -1, keepdims=True)
    return center * lax.rsqrt(spread + EPSILON) * gain


def norm_back(value, gain, upstream):
    _, pull = jax.vjp(layer_norm, value, gain)
    return pull(upstream)


def quick_gelu(value):
    return value * jax.nn.sigmoid(1.702 * value)


def unit_rows(value):
    return value * lax.rsqrt(jnp.sum(value * value, -1, keepdims=True) + 1e-06)


def split_heads(mixed, query_count):
    batch, length, triple = mixed.shape
    width = triple // 3
    rounded = mixed.astype(jnp.bfloat16)
    queries = rounded[:, :query_count, :width].reshape(batch, query_count, HEADS, HEAD)
    keys = rounded[:, :, width : 2 * width].reshape(batch, length, HEADS, HEAD)
    values = rounded[:, :, 2 * width :].reshape(batch, length, HEADS, HEAD)
    return (queries, keys, values)


def scores_of(queries, keys, key_mask):
    scores = jnp.einsum(
        "bqhd,bkhd->bhqk", queries, keys, preferred_element_type=jnp.float32
    ) * HEAD ** (-0.5)
    if key_mask is not None:
        scores = jnp.where(key_mask[:, None, None, :], scores, -1000000000.0)
    return scores


def attend_forward(queries, keys, values, key_mask):
    scores = scores_of(queries, keys, key_mask)
    peak = jnp.max(scores, -1, keepdims=True)
    raised = jnp.exp(scores - peak)
    total = jnp.sum(raised, -1, keepdims=True)
    shares = (raised / total).astype(jnp.bfloat16)
    joined = jnp.einsum("bhqk,bkhd->bqhd", shares, values, preferred_element_type=jnp.float32)
    batch, count = (joined.shape[0], joined.shape[1])
    return (
        joined.reshape(batch, count, HEADS * HEAD).astype(jnp.bfloat16),
        peak + jnp.log(total),
        shares,
    )


def attend_backward(queries, keys, values, key_mask, normalizer, shares, upstream):
    batch, count, width = upstream.shape
    upstream_low = upstream.astype(jnp.bfloat16).reshape(batch, count, HEADS, HEAD)
    chances = jnp.exp(scores_of(queries, keys, key_mask) - normalizer)
    share_grad = jnp.einsum(
        "bqhd,bkhd->bhqk", upstream_low, values, preferred_element_type=jnp.float32
    )
    value_grad = jnp.einsum(
        "bhqk,bqhd->bkhd", shares, upstream_low, preferred_element_type=jnp.float32
    )
    inner = jnp.sum(chances * share_grad, -1, keepdims=True)
    score_grad = (chances * (share_grad - inner)).astype(jnp.bfloat16)
    query_grad = jnp.einsum(
        "bhqk,bkhd->bqhd", score_grad, keys, preferred_element_type=jnp.float32
    ) * HEAD ** (-0.5)
    key_grad = jnp.einsum(
        "bhqk,bqhd->bkhd", score_grad, queries, preferred_element_type=jnp.float32
    ) * HEAD ** (-0.5)
    length = keys.shape[1]
    return (
        query_grad.reshape(batch, count, width),
        key_grad.reshape(batch, length, width),
        value_grad.reshape(batch, length, width),
    )


def frame_forward(block, message_rows, weights):
    attend_gain, attend_heads, attend_merge, expand_gain, expand_weight, shrink_weight = weights
    frames = block.astype(jnp.float32)
    tokens = jnp.concatenate([frames, message_rows[:, None, :]], 1)
    normed = layer_norm(tokens, attend_gain).astype(jnp.bfloat16)
    mixed = jnp.einsum("btd,de->bte", normed, attend_heads, preferred_element_type=jnp.float32)
    queries, keys, values = split_heads(mixed, block.shape[1])
    seen, normalizer, shares = attend_forward(queries, keys, values, None)
    hidden = frames + jnp.einsum(
        "bpd,de->bpe", seen, attend_merge, preferred_element_type=jnp.float32
    )
    normed_two = layer_norm(hidden, expand_gain).astype(jnp.bfloat16)
    grown = jnp.einsum("bpd,dm->bpm", normed_two, expand_weight, preferred_element_type=jnp.float32)
    gated = quick_gelu(grown).astype(jnp.bfloat16)
    result = hidden + jnp.einsum(
        "bpm,md->bpd", gated, shrink_weight, preferred_element_type=jnp.float32
    )
    kept = (
        tokens,
        normed,
        queries,
        keys,
        values,
        shares,
        normalizer,
        seen,
        hidden,
        normed_two,
        grown,
        gated,
    )
    return (jnp.sum(result, 1), kept)


def frame_backward(kept, upstream, weights):
    attend_gain, attend_heads, attend_merge, expand_gain, expand_weight, shrink_weight = weights
    (
        tokens,
        normed,
        queries,
        keys,
        values,
        shares,
        normalizer,
        seen,
        hidden,
        normed_two,
        grown,
        gated,
    ) = kept
    patch_count = hidden.shape[1]
    upstream_low = upstream.astype(jnp.bfloat16)
    shrink_grad = jnp.einsum("bpm,bd->md", gated, upstream_low, preferred_element_type=jnp.float32)
    gated_grad = jnp.einsum(
        "bd,md->bm", upstream_low, shrink_weight, preferred_element_type=jnp.float32
    )
    _, gelu_pull = jax.vjp(quick_gelu, grown)
    grown_grad = gelu_pull(jnp.broadcast_to(gated_grad[:, None, :], grown.shape))[0].astype(
        jnp.bfloat16
    )
    expand_grad = jnp.einsum(
        "bpd,bpm->dm", normed_two, grown_grad, preferred_element_type=jnp.float32
    )
    normed_two_grad = jnp.einsum(
        "bpm,dm->bpd", grown_grad, expand_weight, preferred_element_type=jnp.float32
    )
    hidden_grad, expand_gain_grad = norm_back(hidden, expand_gain, normed_two_grad)
    hidden_grad = hidden_grad + upstream[:, None, :]
    hidden_low = hidden_grad.astype(jnp.bfloat16)
    merge_grad = jnp.einsum("bpd,bpe->de", seen, hidden_low, preferred_element_type=jnp.float32)
    seen_grad = jnp.einsum(
        "bpe,de->bpd", hidden_low, attend_merge, preferred_element_type=jnp.float32
    )
    query_grad, key_grad, value_grad = attend_backward(
        queries, keys, values, None, normalizer, shares, seen_grad
    )
    length = tokens.shape[1]
    query_grad = jnp.pad(query_grad, ((0, 0), (0, length - patch_count), (0, 0)))
    mixed_grad = jnp.concatenate([query_grad, key_grad, value_grad], 2).astype(jnp.bfloat16)
    heads_grad = jnp.einsum("btd,bte->de", normed, mixed_grad, preferred_element_type=jnp.float32)
    normed_grad = jnp.einsum(
        "bte,de->btd", mixed_grad, attend_heads, preferred_element_type=jnp.float32
    )
    token_grad, attend_gain_grad = norm_back(tokens, attend_gain, normed_grad)
    patch_grad = hidden_grad + token_grad[:, :patch_count]
    block_grads = (
        attend_gain_grad,
        heads_grad,
        merge_grad,
        expand_gain_grad,
        expand_grad,
        shrink_grad,
    )
    return (patch_grad, token_grad[:, patch_count], block_grads)


def shards(
    patches,
    counts,
    captions,
    matches,
    courier,
    courier_gain,
    courier_heads,
    courier_merge,
    attend_gain,
    attend_heads,
    attend_merge,
    expand_gain,
    expand_weight,
    shrink_weight,
    projection,
):
    videos, local_frames, patch_count, width = patches.shape
    frame_total = local_frames * lax.axis_size("dp")
    offset = lax.axis_index("dp") * local_frames
    rows = videos * local_frames
    per_block = rows // MICRO
    courier_full, courier_gain_full, heads_full, merge_full, projection_full = (
        lax.all_gather(courier, "fsdp", axis=0, tiled=True),
        lax.all_gather(courier_gain, "fsdp", axis=0, tiled=True),
        lax.all_gather(courier_heads, "fsdp", axis=0, tiled=True),
        lax.all_gather(courier_merge, "fsdp", axis=0, tiled=True),
        lax.all_gather(projection, "fsdp", axis=0, tiled=True),
    )

    def fetch():
        return (
            lax.all_gather(attend_gain, "fsdp", axis=0, tiled=True),
            lax.all_gather(attend_heads, "fsdp", axis=0, tiled=True),
            lax.all_gather(attend_merge, "fsdp", axis=0, tiled=True),
            lax.all_gather(expand_gain, "fsdp", axis=0, tiled=True),
            lax.all_gather(expand_weight, "fsdp", axis=0, tiled=True),
            lax.all_gather(shrink_weight, "fsdp", axis=0, tiled=True),
        )

    leaders = lax.all_gather(patches[:, :, 0, :], "dp", axis=1, tiled=True)
    present = lax.broadcasted_iota(jnp.int32, (videos, frame_total), 1) < counts[:, None]
    message = jnp.einsum("vfd,de->vfe", leaders, courier_full, preferred_element_type=jnp.float32)
    message_norm = layer_norm(message, courier_gain_full).astype(jnp.bfloat16)
    message_mixed = jnp.einsum(
        "vfd,de->vfe", message_norm, heads_full, preferred_element_type=jnp.float32
    )
    told_queries, told_keys, told_values = split_heads(message_mixed, frame_total)
    told, told_normalizer, told_shares = attend_forward(
        told_queries, told_keys, told_values, present
    )
    message_out = message + jnp.einsum(
        "vfd,de->vfe", told, merge_full, preferred_element_type=jnp.float32
    )
    mine = lax.dynamic_slice_in_dim(message_out, offset, local_frames, 1).reshape(rows, width)
    flat = patches.reshape(rows, patch_count, width)
    frame_weights = fetch()
    kept_blocks = []
    sums = []
    for index in range(MICRO):
        if index > 0:
            frame_weights = fetch()
        start = index * per_block
        frame_sums, kept = frame_forward(
            flat[start : start + per_block], mine[start : start + per_block], frame_weights
        )
        kept_blocks.append(kept)
        sums.append(frame_sums)
    frame_sums = jnp.concatenate(sums, 0).reshape(videos, local_frames, width)
    own_present = lax.dynamic_slice_in_dim(present, offset, local_frames, 1)
    partial_value = jnp.sum(jnp.where(own_present[:, :, None], frame_sums, 0.0), 1)
    pooled_sum = lax.psum(partial_value, "dp")
    denominator = (counts * patch_count).astype(jnp.float32)[:, None]
    pooled = pooled_sum / denominator
    pooled_low = pooled.astype(jnp.bfloat16)
    embed = jnp.dot(pooled_low, projection_full, preferred_element_type=jnp.float32)
    video_unit = unit_rows(embed).astype(jnp.bfloat16)
    segment = lax.axis_index("dp") * (captions.shape[0] * lax.axis_size("fsdp"))

    def scores_for(piece):
        text_unit = unit_rows(piece.astype(jnp.float32)).astype(jnp.bfloat16)
        logits = (
            jnp.einsum("ve,te->vt", video_unit, text_unit, preferred_element_type=jnp.float32)
            * LOGIT_SCALE
        )
        positions = segment + lax.broadcasted_iota(jnp.int32, logits.shape, 1)
        return (text_unit, logits, positions == matches[:, None])

    peak = jnp.full((videos,), -1e30, jnp.float32)
    _, logits, matched = scores_for(lax.all_gather(captions, "fsdp", axis=0, tiled=True))
    fresh = jnp.maximum(peak, jnp.max(logits, 1))
    total = jnp.sum(jnp.exp(logits - fresh[:, None]), 1)
    picked = jnp.sum(jnp.where(matched, logits, 0.0), 1)
    peak, total, picked = (fresh, total, picked)

    def combine(first, second):
        top = jnp.maximum(first[0], second[0])
        joined = first[1] * jnp.exp(first[0] - top) + second[1] * jnp.exp(second[0] - top)
        return (top, joined, first[2] + second[2])

    peak, total, picked = joined_2((peak, total, picked), "dp", combine)
    normalizer = peak + jnp.log(total)
    loss = normalizer - picked
    text_unit, logits, matched = scores_for(lax.all_gather(captions, "fsdp", axis=0, tiled=True))
    slope = (jnp.exp(logits - normalizer[:, None]) - matched.astype(jnp.float32)).astype(
        jnp.bfloat16
    )
    unit_grad = jnp.dot(slope, text_unit, preferred_element_type=jnp.float32) * LOGIT_SCALE
    unit_grad = lax.psum(unit_grad, "dp")
    _, unit_pull = jax.vjp(unit_rows, embed)
    embed_grad = unit_pull(unit_grad)[0].astype(jnp.bfloat16)
    projection_grad = jnp.einsum(
        "vd,ve->de", pooled_low, embed_grad, preferred_element_type=jnp.float32
    )
    pooled_grad = jnp.einsum(
        "ve,de->vd", embed_grad, projection_full, preferred_element_type=jnp.float32
    )
    upstream_all = jnp.where(own_present[:, :, None], (pooled_grad / denominator)[:, None, :], 0.0)
    upstream_all = upstream_all.reshape(rows, width)
    collected = None
    patch_list = []
    message_list = []
    for index in range(MICRO):
        frame_weights = fetch()
        start = index * per_block
        patch_grad, message_token_grad, block_grads = frame_backward(
            kept_blocks[index], upstream_all[start : start + per_block], frame_weights
        )
        patch_list.append(patch_grad)
        message_list.append(message_token_grad)
        block_grads = (
            lax.psum_scatter(
                block_grads[0].astype(jnp.float32), "fsdp", scatter_dimension=0, tiled=True
            ),
            lax.psum_scatter(block_grads[1], "fsdp", scatter_dimension=0, tiled=True),
            lax.psum_scatter(block_grads[2], "fsdp", scatter_dimension=0, tiled=True),
            lax.psum_scatter(
                block_grads[3].astype(jnp.float32), "fsdp", scatter_dimension=0, tiled=True
            ),
            lax.psum_scatter(block_grads[4], "fsdp", scatter_dimension=0, tiled=True),
            lax.psum_scatter(block_grads[5], "fsdp", scatter_dimension=0, tiled=True),
        )
        collected = (
            block_grads if collected is None else jax.tree.map(jnp.add, collected, block_grads)
        )
    collected = (
        lax.psum(collected[0].astype(jnp.bfloat16), "dp").astype(jnp.float32),
        lax.psum(collected[1].astype(jnp.bfloat16), "dp").astype(jnp.float32),
        lax.psum(collected[2].astype(jnp.bfloat16), "dp").astype(jnp.float32),
        lax.psum(collected[3].astype(jnp.bfloat16), "dp").astype(jnp.float32),
        lax.psum(collected[4].astype(jnp.bfloat16), "dp").astype(jnp.float32),
        lax.psum(collected[5].astype(jnp.bfloat16), "dp").astype(jnp.float32),
    )
    message_token_grad = jnp.concatenate(message_list, 0).reshape(videos, local_frames, width)
    out_grad = lax.all_gather(message_token_grad, "dp", axis=1, tiled=True)
    out_low = out_grad.astype(jnp.bfloat16)
    merge_message_grad = jnp.einsum(
        "vfd,vfe->de", told, out_low, preferred_element_type=jnp.float32
    )
    told_grad = jnp.einsum("vfe,de->vfd", out_low, merge_full, preferred_element_type=jnp.float32)
    told_query_grad, told_key_grad, told_value_grad = attend_backward(
        told_queries, told_keys, told_values, present, told_normalizer, told_shares, told_grad
    )
    courier_mixed_grad = jnp.concatenate(
        [told_query_grad, told_key_grad, told_value_grad], 2
    ).astype(jnp.bfloat16)
    heads_message_grad = jnp.einsum(
        "vfd,vfe->de", message_norm, courier_mixed_grad, preferred_element_type=jnp.float32
    )
    message_norm_grad = jnp.einsum(
        "vfe,de->vfd", courier_mixed_grad, heads_full, preferred_element_type=jnp.float32
    )
    message_grad, courier_gain_grad = norm_back(message, courier_gain_full, message_norm_grad)
    message_grad = (message_grad + out_grad).astype(jnp.bfloat16)
    courier_grad = jnp.einsum(
        "vfd,vfe->de", leaders, message_grad, preferred_element_type=jnp.float32
    )
    leader_grad = jnp.einsum(
        "vfe,de->vfd", message_grad, courier_full, preferred_element_type=jnp.float32
    )
    own_leader = lax.dynamic_slice_in_dim(leader_grad, offset, local_frames, 1).reshape(rows, width)
    patch_all = jnp.concatenate(patch_list, 0)
    patch_all = patch_all.at[:, 0, :].add(own_leader)
    patch_out = patch_all.reshape(videos, local_frames, patch_count, width).astype(jnp.bfloat16)
    video_grads = (
        lax.psum_scatter(courier_grad, "fsdp", scatter_dimension=0, tiled=True),
        lax.psum_scatter(
            courier_gain_grad.astype(jnp.float32), "fsdp", scatter_dimension=0, tiled=True
        ),
        lax.psum_scatter(heads_message_grad, "fsdp", scatter_dimension=0, tiled=True),
        lax.psum_scatter(merge_message_grad, "fsdp", scatter_dimension=0, tiled=True),
        lax.psum_scatter(projection_grad, "fsdp", scatter_dimension=0, tiled=True),
    )
    return (
        loss,
        patch_out,
        video_grads[0],
        video_grads[1],
        video_grads[2],
        video_grads[3],
        collected[0],
        collected[1],
        collected[2],
        collected[3],
        collected[4],
        collected[5],
        video_grads[4],
    )


def solution(mesh):
    fitting = mesh.shape['dp'] == 4 and mesh.shape['fsdp'] == Z * Y
    return jax.shard_map(
        fast if fitting else shards,
        mesh=mesh,
        in_specs=(
            P("fsdp", "dp", None, None),
            P("fsdp"),
            P(("dp", "fsdp"), None),
            P("fsdp"),
            P("fsdp", None),
            P("fsdp"),
            P("fsdp", None),
            P("fsdp", None),
            P("fsdp"),
            P("fsdp", None),
            P("fsdp", None),
            P("fsdp"),
            P("fsdp", None),
            P("fsdp", None),
            P("fsdp", None),
        ),
        out_specs=(
            P("fsdp"),
            P("fsdp", "dp", None, None),
            P("fsdp", None),
            P("fsdp"),
            P("fsdp", None),
            P("fsdp", None),
            P("fsdp"),
            P("fsdp", None),
            P("fsdp", None),
            P("fsdp"),
            P("fsdp", None),
            P("fsdp", None),
            P("fsdp", None),
        ),
        check_vma=False,
    )
```

```python
import functools

import jax
import jax.numpy as jnp
from jax import lax
from jax.experimental import pallas as pl
from jax.experimental.pallas import tpu as pltpu
from jax.sharding import PartitionSpec as P

MESH = pl.DeviceIdType.MESH
Z, Y = 4, 2
HEADS = 12
HEAD = 64
EPSILON = 1e-05
LOGIT_SCALE = 64.0
PAD = 208
ROWS = 832
D = 768
F32 = jnp.float32
B16 = jnp.bfloat16

MICRO = 2

COURIER, GAINS, CHEADS, AHEADS, CMERGE, AMERGE, EXPAND, PROJ = 0, 768, 896, 3200, 5504, 6272, 7040, 10112
NCOLS = 10624
JOBS = ((0, 896), (896, 768), (1664, 768), (2432, 768), (3200, 768), (3968, 768), (4736, 768), (5504, 768), (6272, 768),
        (7040, 768), (7808, 768), (8576, 768), (10112, 512), (9344, 512), (9856, 256))


class Pos:
    def __init__(self):
        self.dp = lax.axis_index("dp")
        self.k = lax.axis_index("fsdp")
        self.x, self.c = self.dp // 2, lax.rem(self.dp, 2)
        self.z, self.y = self.k // Y, lax.rem(self.k, Y)
        self.core = (self.x * 2 + 1 - self.c, self.k)
        self.xp = ((1 - self.x) * 2 + self.c, self.k)
        self.cross = ((1 - self.x) * 2 + 1 - self.c, self.k)
        self.yp = (self.dp, self.z * Y + 1 - self.y)
        self.team = (self.core, self.xp, self.cross)

    def ahead(self, d):
        return lax.rem(self.z + d, Z)

    def behind(self, d):
        return lax.rem(self.z - d + Z, Z)

    def column(self):
        return [(self.dp, self.ahead(d) * Y + self.y) for d in (1, 2, 3)]

    def peers(self):
        return [self.core, self.xp, self.yp] + self.column()

    def plane(self):
        return [(self.dp, lax.rem(self.k + d, Z * Y)) for d in range(1, Z * Y)]


def barrier(peers):
    semaphore = pltpu.get_barrier_semaphore()
    for peer in peers:
        pl.semaphore_signal(semaphore, inc=1, device_id=peer, device_id_type=MESH)
    pl.semaphore_wait(semaphore, len(peers))


def remote(source, target, send, receive, device):
    return pltpu.make_async_remote_copy(
        src_ref=source, dst_ref=target, send_sem=send, recv_sem=receive, device_id=device, device_id_type=MESH)


class Gather:
    def __init__(self, p, block, jobs, send, receive):
        self.p, self.block, self.jobs, self.send, self.receive = p, block, jobs, send, receive

    def copy(self, job, index, k, first, count, device):
        ref = self.block(k, first, count, job)
        return remote(ref, ref, self.send.at[job, index], self.receive.at[job, index], device)

    def far(self, d):
        p = self.p
        return p.behind(d + 1) * Y + p.y if d < 3 else p.behind(d - 3) * Y + 1 - p.y

    def stage(self, stage, job):
        if job < 0 or job >= self.jobs:
            return
        p, copy = self.p, self.copy
        own, single = 3 * p.c + p.x, 3 * p.c + 2 * p.x
        other = 3 * p.c + 2 * (1 - p.x)
        if stage == 0:
            for d, device in enumerate(p.column()):
                copy(job, d, p.k, own, 2, device).start()
            copy(job, 3, p.k, own, 2, p.yp).start()
        elif stage == 1:
            for d in range(3):
                k = self.far(d)
                copy(job, d, k, own, 2, p.core).wait_recv()
                copy(job, 4 + d, k, own, 2, p.yp).start()
                copy(job, 7 + d, k, single, 1, p.xp).start()
                copy(job, 14 + d, k, own, 2, p.core).start()
        elif stage == 2:
            for d in range(3, 7):
                k = self.far(d)
                copy(job, d, k, own, 2, p.core).wait_recv()
                copy(job, 7 + d, k, single, 1, p.xp).start()
                copy(job, 14 + d, k, own, 2, p.core).start()
        elif stage == 3:
            for d in range(7):
                k = self.far(d)
                copy(job, 7 + d, k, other, 1, p.core).wait_recv()
                copy(job, 21 + d, k, other, 1, p.core).start()
        elif stage == 4:
            for d in range(7):
                copy(job, 14 + d, self.far(d), 3 * (1 - p.c) + p.x, 2, p.core).wait_recv()
            for d in range(7):
                copy(job, 21 + d, self.far(d), 3 * (1 - p.c) + 2 * (1 - p.x), 1, p.core).wait_recv()
        elif stage == 5:
            for index in range(28):
                copy(job, index, p.k, 0, 2 if index < 7 or 14 <= index < 21 else 1, p.core).wait_send()

    def tick(self, t, lag):
        for stage in (0, 1, 2, 3, 4, 5):
            self.stage(stage, t - lag[stage])


class Spread:
    def __init__(self, p, source, target, send, receive, same=False):
        self.p, self.target = p, target
        count = Z * Y
        self.copies = []
        for d in range(1, count):
            to = lax.rem(p.k + d, count)
            part = source if same else source.at[to]
            self.copies.append(remote(part, target.at[p.k], send.at[d - 1], receive.at[d - 1], (p.dp, to)))
        self.arrivals = []
        for d in range(1, count):
            origin = lax.rem(p.k - d + count, count)
            self.arrivals.append(
                remote(target.at[origin], target.at[origin], send.at[d - 1], receive.at[d - 1], (p.dp, origin)))
        target[p.k] = source[...] if same else source[p.k]
        for copy in self.copies:
            copy.start()

    def wait(self):
        for copy in self.arrivals:
            copy.wait_recv()

    def done(self):
        for copy in self.copies:
            copy.wait_send()


class Team:
    def __init__(self, p, source, target, send, receive):
        self.copies, self.arrivals = [], []
        target[p.dp] = source[...]
        for index, other in enumerate(p.team):
            self.copies.append(remote(source, target.at[p.dp], send.at[index], receive.at[index], other))
            self.arrivals.append(remote(source, target.at[other[0]], send.at[index], receive.at[index], other))
        for copy in self.copies:
            copy.start()

    def wait(self):
        for copy in self.arrivals:
            copy.wait_recv()

    def done(self):
        for copy in self.copies:
            copy.wait_send()


class Reduce:
    def __init__(self, p, stage, buffers, fin, jobs, send, receive):
        self.p, self.stage, self.fin, self.jobs, self.send, self.receive = p, stage, fin, jobs, send, receive
        self.rc, self.rx, self.ry, self.rz, self.own, self.rf = buffers
        self.at = [0] * len(jobs)

    def copies(self, job, step):
        p = self.p
        first, count = self.jobs[job]
        cols = pl.ds(first, count)
        half, other = pl.ds(pl.multiple_of(48 * p.c, 16), 48), pl.ds(pl.multiple_of(48 * (1 - p.c), 16), 48)
        carried = pl.ds(pl.multiple_of((3 * p.c + p.x) * 16, 16), 32)
        away = pl.ds(pl.multiple_of((3 * p.c + 2 * (1 - p.x)) * 16, 16), 16)
        s, r = self.send, self.receive
        if step == 0:
            target = self.rc.at[job % 4, :, :, pl.ds(0, count)]
            return [remote(self.stage.at[:, other, cols], target, s.at[job, 0], r.at[job, 0], p.core)]
        if step == 1:
            return [remote(self.stage.at[:, away, cols], self.rx.at[:, :, cols], s.at[job, 1], r.at[job, 1], p.xp)]
        if step == 2:
            return [remote(self.stage.at[z * Y + 1 - p.y, carried, cols], self.ry.at[z, :, cols], s.at[job, 2 + z],
                           r.at[job, 2 + z], p.yp) for z in range(Z)]
        if step == 3:
            return [remote(self.stage.at[device[1], carried, cols], self.rz.at[d, :, cols], s.at[job, 6 + d],
                           r.at[job, 6 + d], device) for d, device in enumerate(p.column())]
        if step == 4:
            return [remote(self.own.at[:, cols], self.rf.at[:, cols], s.at[job, 9], r.at[job, 9], p.xp)]
        return [remote(self.fin.at[half, cols], self.fin.at[half, cols], s.at[job, 10], r.at[job, 10], p.core)]

    def next(self, *jobs, scale=None):
        for job in jobs:
            self.step(self.at[job], job, scale)
            self.at[job] += 1

    def step(self, step, job, scale):
        p = self.p
        first, count = self.jobs[job]
        cols = pl.ds(first, count)
        half, other = pl.ds(pl.multiple_of(48 * p.c, 16), 48), pl.ds(pl.multiple_of(48 * (1 - p.c), 16), 48)
        carried = pl.ds(pl.multiple_of((3 * p.c + p.x) * 16, 16), 32)
        if step == 6:
            remote(self.fin.at[other, cols], self.fin.at[other, cols], self.send.at[job, 10], self.receive.at[job, 10],
                   p.core).wait_recv()
        elif step > 0 and step < 6:
            for copy in self.copies(job, step - 1):
                copy.wait_recv()
        if step == 1:
            def add(k, carry):
                self.stage[k, half, cols] = self.stage[k, half, cols] + self.rc[job % 4, k, :, pl.ds(0, count)]
                return carry
            lax.fori_loop(0, Z * Y, add, 0)
        elif step == 2:
            def add(k, carry):
                value = self.stage[k, carried, cols].astype(F32)
                other_x = self.rx[k, :, cols].astype(F32)
                top = value[0:16] + jnp.where(p.x == 0, other_x, 0.0)
                low = value[16:32] + jnp.where(p.x == 0, 0.0, other_x)
                value = jnp.concatenate([top, low], 0)
                if scale is not None:
                    value = value * scale[0:1, cols]
                self.stage[k, carried, cols] = value.astype(B16)
                return carry
            lax.fori_loop(0, Z * Y, add, 0)
        elif step == 3:
            def add(z, carry):
                k = z * Y + p.y
                self.stage[k, carried, cols] = self.stage[k, carried, cols] + self.ry[z, :, cols]
                return carry
            lax.fori_loop(0, Z, add, 0)
        elif step == 4:
            total = self.stage[p.k, carried, cols].astype(F32)
            for d in range(3):
                total = total + self.rz[d, :, cols].astype(F32)
            self.own[:, cols] = total.astype(B16)
        elif step == 5:
            mine, theirs = self.own[:, cols].astype(F32), self.rf[:, cols].astype(F32)
            left = jnp.where(p.x == 0, mine[0:16], theirs[0:16])
            right = jnp.where(p.x == 0, theirs[16:32], mine[16:32])
            middle = jnp.where(p.x == 0, mine[16:32], mine[0:16]) + jnp.where(p.x == 0, theirs[0:16], theirs[16:32])
            self.fin[half, cols] = jnp.concatenate([left, middle, right], 0).astype(B16)
        if step < 6:
            for copy in self.copies(job, step):
                copy.start()
        if step == 7:
            for earlier in range(6):
                for copy in self.copies(job, earlier):
                    copy.wait_send()


def dot(a, b, ca=1, cb=0):
    return lax.dot_general(a, b, (((ca,), (cb,)), ((), ())), preferred_element_type=F32)


def normalize(value):
    center = value - jnp.mean(value, -1, keepdims=True)
    rate = lax.rsqrt(jnp.mean(center * center, -1, keepdims=True) + EPSILON)
    return center * rate, rate


def head_mask():
    return lax.broadcasted_iota(jnp.int32, (192, D), 0) // 16 == lax.broadcasted_iota(jnp.int32, (192, D), 1) // HEAD


def spread_heads(value):
    return jnp.where(head_mask(), jnp.concatenate([value.astype(F32)] * HEADS, 0), 0.0).astype(B16)


def join_heads(value):
    value = jnp.where(head_mask(), value, 0.0)
    total = value[0:16]
    for head in range(1, HEADS):
        total = total + value[16 * head : 16 * head + 16]
    return total


def row_of(value, index):
    rows = lax.broadcasted_iota(jnp.int32, value.shape, 0)
    return jnp.sum(jnp.where(rows == index, value, 0.0), 0, keepdims=True)


def forward_kernel(
    patches, captions, gain_a, gain_b, gain_c, counts, courier, cheads, aheads, cmerge, amerge, expand, projection,
    full_o, normt_o, mixed_o, shares_o, seen_o, seent_o, hidden_o, n2t_o, d_o, gsum_o, hsum_o, gains_o,
    leaders_o, message_o, mnorm_o, mmix_o, mshare_o, told_o, mout_o, texts_o, xs_o,
    full, xs, lead, caption, leadbuf, norm, normt, mixed, shares, seen, seent, hidden, n2, n2t, dd,
    texts, ssem, rsem, lsem, lead_s, lead_r, text_s, text_r, osem,
):
    p = Pos()
    weights = ((courier, COURIER), (cheads, CHEADS), (aheads, AHEADS), (cmerge, CMERGE), (amerge, AMERGE),
               (expand, EXPAND), (projection, PROJ))
    mine = pl.ds(pl.multiple_of(p.k * 96, 16), 96)
    loads = []
    for index, (ref, start) in enumerate(weights):
        copy = pltpu.make_async_copy(ref, full.at[mine, pl.ds(start, ref.shape[1])], lsem.at[index])
        copy.start()
        loads.append(copy)
    text = captions[...].astype(F32)
    caption[...] = jnp.concatenate([text[:, 128 * r : 128 * r + 128] for r in range(4)] + [jnp.zeros((4, 128), F32)], 0)
    lead[...] = jnp.concatenate([patches[0, f, 0:16, :].astype(F32)[0:1] for f in range(4)] + [jnp.zeros((4, D), F32)], 0)
    square = jnp.concatenate([gain_a[...].astype(F32), gain_b[...].astype(F32), gain_c[...].astype(F32)], 0)
    square = jnp.concatenate([square, jnp.zeros((3, 32), F32)], 1)
    square = jnp.concatenate([square, jnp.zeros((125, 128), F32)], 0)
    full[mine, GAINS : GAINS + 128] = jnp.transpose(square)[0:96].astype(B16)
    leadbuf[p.dp] = lead[...]
    barrier(p.plane() + list(p.team))
    text_hop = Spread(p, caption, texts, text_s, text_r, same=True)
    others = [p.core, p.xp, ((1 - p.x) * 2 + 1 - p.c, p.k)]
    sends = []
    for index, other in enumerate(others):
        copy = pltpu.make_async_remote_copy(
            src_ref=lead, dst_ref=leadbuf.at[p.dp], send_sem=lead_s.at[0, index], recv_sem=lead_r.at[0, index],
            device_id=other, device_id_type=MESH)
        copy.start()
        sends.append(copy)
    for copy in loads:
        copy.wait()
    def block(k, start, count, job):
        first_col, columns = JOBS[job]
        return full.at[pl.ds(pl.multiple_of(k * 96 + start * 16, 16), count * 16), pl.ds(first_col, columns)]

    gather = Gather(p, block, len(JOBS), ssem, rsem)
    lag = (0, 1, 2, 3, 4, 5)
    outs = []

    def out(source, target):
        copy = pltpu.make_async_copy(source, target, osem.at[len(outs)])
        copy.start()
        outs.append(copy)

    ticked, written = [0], [0]

    def upto(job):
        while ticked[0] <= job + lag[4]:
            gather.tick(ticked[0], lag)
            ticked[0] += 1
        while written[0] <= min(job, len(JOBS) - 1):
            cols = pl.ds(*JOBS[written[0]])
            out(full.at[:, cols], full_o.at[:, cols])
            written[0] += 1

    for f in range(4):
        xs[f * PAD + 192 : f * PAD + PAD, :] = jnp.zeros((16, D), B16)
        xs[f * PAD : f * PAD + 197, :] = patches[0, f]
    out(xs, xs_o)
    upto(-3)
    text_hop.wait()
    text_team = Team(p, texts, texts_o, lead_s.at[1], lead_r.at[1])
    upto(0)
    for index, other in enumerate(others):
        pltpu.make_async_remote_copy(
            src_ref=lead, dst_ref=leadbuf.at[other[0]], send_sem=lead_s.at[0, index], recv_sem=lead_r.at[0, index],
            device_id=other, device_id_type=MESH).wait_recv()
    leaders = jnp.concatenate([leadbuf[index][0:4] for index in range(4)], 0)
    leaders_o[...] = leaders.astype(B16)
    rows = jnp.transpose(full[:, GAINS : GAINS + 128].astype(F32))[0:8]
    gains_o[...] = rows
    courier_gain, attend_gain, expand_gain = rows[0:1], rows[1:2], rows[2:3]
    message = dot(leaders.astype(B16), full[:, COURIER : COURIER + D])
    message_o[...] = message
    xh, _ = normalize(message)
    mnorm = (xh * courier_gain).astype(B16)
    mnorm_o[...] = mnorm

    def norm_frame(f, carry):
        here = pl.ds(pl.multiple_of(f * PAD, 16), PAD)
        xh, _ = normalize(xs[here, :].astype(F32))
        norm[here, :] = (xh * attend_gain).astype(B16)
        return carry

    lax.fori_loop(0, 4, norm_frame, 0)
    upto(3)
    mmix = dot(mnorm, full[:, CHEADS : CHEADS + 3 * D])
    mq, mk, mv = mmix[:, :D].astype(B16), mmix[:, D : 2 * D].astype(B16), mmix[:, 2 * D :].astype(B16)
    mmix_o[...] = mmix.astype(B16)
    scores = dot(spread_heads(mq), mk, 1, 1) * HEAD ** (-0.5)
    frames = lax.broadcasted_iota(jnp.int32, (192, 16), 1)
    scores = jnp.where(frames < counts[0], scores, -1000000000.0)
    raised = jnp.exp(scores - jnp.max(scores, -1, keepdims=True))
    mshare = raised / jnp.sum(raised, -1, keepdims=True)
    mshare_o[...] = mshare
    told = join_heads(dot(mshare.astype(B16), mv)).astype(B16)
    told_o[...] = told

    def heads_tile(base, factor):
        def body(n, carry):
            cols = pl.ds(pl.multiple_of(base + n * 256, 256), 256)
            wcols = pl.ds(pl.multiple_of(AHEADS + base + n * 256, 128), 256)
            mixed[:, cols] = (dot(norm[...], full[:, wcols]) * factor).astype(B16)
            return carry
        lax.fori_loop(0, 3, body, 0)

    upto(4)
    heads_tile(0, HEAD ** (-0.5))
    upto(5)
    heads_tile(D, 1.0)
    upto(6)
    heads_tile(2 * D, 1.0)
    upto(7)
    mout_all = message + dot(told, full[:, CMERGE : CMERGE + D])
    mout = jnp.concatenate([row_of(mout_all, p.dp * 4 + f) for f in range(4)] + [jnp.zeros((4, D), F32)], 0)
    mout_o[...] = mout
    xh, _ = normalize(mout)
    extra = (xh * attend_gain).astype(B16)
    extra_kv = dot(extra, full[:, AHEADS + D : AHEADS + 3 * D])
    extra = extra.astype(F32)
    spot = lax.broadcasted_iota(jnp.int32, (16, 1), 0) == 5
    for f in range(4):
        tail = pl.ds(f * PAD + 192, 16)
        norm[tail, :] = jnp.where(spot, extra[f : f + 1], norm[tail, :].astype(F32)).astype(B16)
        old = mixed[tail, D : 3 * D].astype(F32)
        mixed[tail, D : 3 * D] = jnp.where(spot, extra_kv[f : f + 1], old).astype(B16)
    out(mixed, mixed_o)

    first = lax.broadcasted_iota(jnp.int32, (PAD, 128), 1) < HEAD
    kept = lax.broadcasted_iota(jnp.int32, (PAD, PAD), 0) < 198

    def attend(f, pair):
        here = pl.ds(pl.multiple_of(f * PAD, 16), PAD)
        at = pl.multiple_of(pair * 128, 128)
        q = mixed[here, pl.ds(at, 128)]
        k = mixed[here, pl.ds(pl.multiple_of(D + at, 128), 128)]
        v = mixed[here, pl.ds(pl.multiple_of(2 * D + at, 128), 128)]
        total = None
        for h in range(2):
            mask = first if h == 0 else jnp.logical_not(first)
            kh, vh = jnp.where(mask, k, jnp.zeros_like(k)), jnp.where(mask, v, jnp.zeros_like(v))
            scores = jnp.where(kept, dot(kh, q, 1, 1), -1e30)
            raised = jnp.exp(scores - jnp.max(scores, 0, keepdims=True))
            share = (raised * (1.0 / jnp.sum(raised, 0, keepdims=True))).astype(B16)
            shares[f * HEADS + pair * 2 + h] = share
            part = dot(share, vh, 0, 0)
            total = part if total is None else total + part
        seen[here, pl.ds(at, 128)] = total.astype(B16)

    def attend_frame(f):
        def body(pair, carry):
            attend(f, pair)
            return carry
        lax.fori_loop(0, 6, body, 0, unroll=6)

    def merge_frames():
        def body(n, carry):
            cols = pl.ds(pl.multiple_of(n * 256, 256), 256)
            wcols = pl.ds(pl.multiple_of(AMERGE + n * 256, 128), 256)
            hidden[:, cols] = dot(seen[...], full[:, wcols])
            return carry
        lax.fori_loop(0, 3, body, 0)

    def hidden_frame(f, carry):
        here = pl.ds(pl.multiple_of(f * PAD, 16), PAD)
        value = hidden[here, :] + xs[here, :].astype(F32)
        hidden[here, :] = value
        xh, _ = normalize(value)
        n2[here, :] = (xh * expand_gain).astype(B16)
        return carry

    def row_mask(shape, axis):
        index = lax.broadcasted_iota(jnp.int32, shape, axis)
        good = index < 0
        for f in range(4):
            lost = jnp.where(p.dp * 4 + f < counts[0], 0, ROWS)
            good = jnp.logical_or(good, jnp.logical_and(index >= f * PAD + lost, index < f * PAD + 197 + lost * 0))
        return good

    mask_row = jnp.where(row_mask((16, ROWS), 1), 1.0, 0.0).astype(B16)

    def expand_tile(base, count=3):
        def body(n, carry):
            cols = pl.ds(pl.multiple_of(base + n * 256, 256), 256)
            wcols = pl.ds(pl.multiple_of(EXPAND + base + n * 256, 128), 256)
            grown = dot(n2[...], full[:, wcols])
            s = 0.5 + 0.5 * jnp.tanh(0.851 * grown)
            gated = grown * s
            dd[:, cols] = (s + 1.702 * gated * (1.0 - s)).astype(B16)
            gsum_o[:, cols] = dot(mask_row, gated.astype(B16))[0:8]
            return carry
        lax.fori_loop(0, count, body, 0)

    attend_frame(0)
    upto(8)
    attend_frame(1)
    upto(9)
    attend_frame(2)
    attend_frame(3)
    out(seen, seen_o)
    normt[...] = jnp.transpose(norm[...])
    out(normt, normt_o)
    seent[...] = jnp.transpose(seen[...])
    out(seent, seent_o)
    out(shares, shares_o)
    upto(10)
    merge_frames()
    lax.fori_loop(0, 4, hidden_frame, 0)
    out(hidden, hidden_o)
    mask_col = jnp.where(row_mask((ROWS, D), 0), 1.0, 0.0)
    n2t[...] = jnp.transpose((n2[...].astype(F32) * mask_col).astype(B16))
    out(n2t, n2t_o)
    expand_tile(0)
    upto(11)
    expand_tile(D)
    high = hidden[...].astype(B16)
    low = (hidden[...] - high.astype(F32)).astype(B16)
    hsum_o[...] = (dot(mask_row, high) + dot(mask_row, low))[0:8]
    upto(12)
    expand_tile(2 * D)
    out(dd.at[:, pl.ds(0, 3 * D)], d_o.at[:, pl.ds(0, 3 * D)])
    upto(13)
    expand_tile(3 * D, 2)
    upto(14)
    expand_tile(3 * D + 512, 1)
    out(dd.at[:, pl.ds(3 * D, D)], d_o.at[:, pl.ds(3 * D, D)])
    upto(15)
    for copy in sends:
        copy.wait_send()
    text_team.wait()
    text_team.done()
    text_hop.done()
    for copy in outs:
        copy.wait()


def pack_row(row):
    return jnp.concatenate([row[:, 128 * r : 128 * r + 128] for r in range(6)] + [jnp.zeros((2, 128), F32)], 0)


def unpack_row(value):
    return jnp.concatenate([value[r : r + 1] for r in range(6)], 1)


def twice(value):
    high = value.astype(B16)
    return jnp.concatenate([high, (value - high.astype(F32)).astype(B16)], 0)


RJOBS = ((0, 768), (768, 768), (1536, 768), (2304, 768), (3072, 768), (3840, 768), (4608, 768), (5376, 768))
BUNDLE = 3840
SIXTH = BUNDLE // 6


def rear_kernel(
    xs_h, normt_h, mixed_h, shares, seen_h, seent_h, hidden_h, n2t_h, d_h, full,
    gsum, hsum, shrink, texts, gains, mout, leaders, message, mnorm, mmix, mshare, told, counts, matches,
    patch_h, fin, loss_o, shrink_grad_o, courier_o, cheads_o, cmerge_o, proj_o, gains_grad_o, lead_o,
    stage, rc, rx, ry, rz, own, rf, bundle, wx, wmerge, wheads, mixed, seen, seent, hidden, n2t, dd, sbuf, hg, low, dout,
    projection, vecs, team, gs, gr, ps, pr, rs_, rr, us, ur, gg, first, mog, mog_team, chosen, gain_pack, gain_team, gain_send, gain_all,
    s_r, r_r, s_b, r_b, team_s, team_r, hop_s, hop_r, lsem, psem,
):
    p = Pos()
    pending = ((n2t_h, n2t), (d_h, dd), (full.at[:, pl.ds(PROJ, 512)], projection), (full.at[:, pl.ds(EXPAND, 3072)], wx),
               (hidden_h, hidden), (seent_h, seent), (full.at[:, pl.ds(AMERGE, D)], wmerge), (mixed_h, mixed), (seen_h, seen),
               (full.at[:, pl.ds(AHEADS, 3 * D)], wheads))
    loads = []

    def load(source, target):
        copy = pltpu.make_async_copy(source, target, lsem.at[len(loads)])
        copy.start()
        loads.append(copy)
        return copy

    for source, target in pending:
        load(source, target)
    barrier(p.plane() + list(p.team))
    vecs[:, 0:384] = jnp.concatenate([gsum[0:1, 384 * k : 384 * k + 384] for k in range(8)], 0)
    vecs[:, 384:512] = pack_row(hsum[0:1, :])
    hop = Team(p, vecs, team, team_s.at[0], team_r.at[0])
    reduce = Reduce(p, stage, (rc, rx, ry, rz, own, rf), fin, RJOBS, s_r, r_r)

    def expand_tiles(start):
        stage[:, :, start : start + D] = dot(n2t[...], dd[:, start : start + D]).astype(B16).reshape(8, 96, D)

    text = jnp.concatenate([jnp.concatenate([texts[i, :, r, :] for r in range(4)], 1) for i in range(4)], 0)
    text_unit = (text * lax.rsqrt(jnp.sum(text * text, -1, keepdims=True) + 1e-06)).astype(B16)
    loads[0].wait()
    loads[1].wait()
    hop.wait()
    total = team[0] + team[1] + team[2] + team[3]
    for k in range(8):
        gs[k] = jnp.broadcast_to(total[k : k + 1, 0:384], (8, 384))
    hop.done()
    hop = Spread(p, gs, gr, hop_s.at[0], hop_r.at[0])
    expand_tiles(0)
    reduce.next(0)
    hop.wait()
    gated = jnp.concatenate([gr[v][0:1] for v in range(8)], 0)
    both = dot(twice(gated), shrink[...])
    part = both[0:8] + both[8:16]
    for v in range(8):
        ps[v] = pack_row(part[v : v + 1])
    hop.done()
    hop = Spread(p, ps, pr, hop_s.at[1], hop_r.at[1])
    expand_tiles(D)
    reduce.next(1, 0)
    hop.wait()
    packed = total[:, 384:512]
    for k in range(8):
        packed = packed + pr[k]
    hop.done()
    loads[2].wait()
    denominator = (counts[0] * 197).astype(F32)
    pooled = jnp.broadcast_to(unpack_row(packed / denominator), (8, D))
    embed = dot(pooled.astype(B16), projection[...])
    rate = lax.rsqrt(jnp.sum(embed * embed, -1, keepdims=True) + 1e-06)
    unit = embed * rate
    logits = dot(unit.astype(B16), text_unit, 1, 1) * LOGIT_SCALE
    peak = jnp.max(logits, -1, keepdims=True)
    normalizer = peak + jnp.log(jnp.sum(jnp.exp(logits - peak), -1, keepdims=True))
    matched = lax.broadcasted_iota(jnp.int32, logits.shape, 1) == matches[0]
    loss_o[...] = jnp.broadcast_to(normalizer - jnp.sum(jnp.where(matched, logits, 0.0), -1, keepdims=True), (8, 128))
    slope = (jnp.exp(logits - normalizer) - jnp.where(matched, 1.0, 0.0)).astype(B16)
    unit_grad = dot(slope, text_unit) * LOGIT_SCALE
    embed_grad = (rate * (unit_grad - unit * jnp.sum(unit * unit_grad, -1, keepdims=True))).astype(B16)
    rg = dot(embed_grad, projection[...], 1, 1) / denominator
    rs_[...] = pack_row(rg.astype(B16).astype(F32)[0:1])
    hop = Spread(p, rs_, rr, hop_s.at[2], hop_r.at[2], same=True)

    places = ((0, 0, SIXTH), (1, 4 * D, 128), (1, D, 384), (1, 0, 128))

    def block(k, start, count, job):
        slot, offset, sixth = places[job]
        return bundle.at[slot, k, :, pl.ds(pl.multiple_of(offset + start * sixth, 128), count * sixth)]

    def fill(slot, col, parts):
        for part in parts:
            bundle[slot, p.k, :, col : col + part.shape[1]] = part
            col += part.shape[1]

    gather = Gather(p, block, 4, s_b, r_b)
    top = lax.broadcasted_iota(jnp.int32, (16, 1), 0) == 0
    pooled_rows = jnp.where(top, jnp.concatenate([pooled, pooled], 0), 0.0).astype(B16)
    embed_rows = jnp.where(top, jnp.concatenate([embed_grad.astype(F32)] * 2, 0), 0.0).astype(B16)
    fill(0, 0, (leaders[...], mnorm[...], told[...], pooled_rows, embed_rows, jnp.zeros((16, 256), B16)))
    gather.stage(0, 0)
    expand_tiles(2 * D)
    reduce.next(2, 1)
    hop.wait()
    rows = jnp.concatenate([unpack_row(rr[v]) for v in range(8)], 0).astype(B16)
    grad = dot(rows, shrink[...], 1, 1)
    for v in range(8):
        us[v] = jnp.broadcast_to(grad[v : v + 1], (8, 384))
    hop.done()
    hop = Spread(p, us, ur, hop_s.at[3], hop_r.at[3])
    expand_tiles(3 * D)
    normt_load = load(normt_h, n2t)
    reduce.next(3, 2)
    gather.stage(1, 0)
    hop.wait()
    for k in range(8):
        gg[:, 384 * k : 384 * k + 384] = ur[k]
    hop.done()

    def scale_tile(n, carry):
        cols = pl.ds(pl.multiple_of(n * 256, 256), 256)
        dd[:, cols] = (dd[:, cols].astype(F32) * gg[0:1, cols]).astype(B16)
        return carry

    lax.fori_loop(0, 12, scale_tile, 0)
    reduce.next(0, 3, scale=gg)
    loads[3].wait()

    def norm_tile(n):
        hg[:, 256 * n : 256 * n + 256] = dot(dd[...], wx[256 * n : 256 * n + 256, :], 1, 1)

    norm_tile(0)
    reduce.next(1, scale=gg)
    gather.stage(2, 0)
    norm_tile(1)
    reduce.next(2, 0, scale=gg)
    gather.stage(3, 0)
    norm_tile(2)
    weights = [load(full.at[:, pl.ds(CHEADS, 3 * D)], wx.at[:, pl.ds(0, 3 * D)]), load(full.at[:, pl.ds(COURIER, D)], wx.at[:, pl.ds(3 * D, D)])]
    reduce.next(3, scale=gg)
    shrink_grad_o[...] = dot(twice(gated), jnp.concatenate([rows.astype(F32)] * 2, 0).astype(B16), 0, 0)
    loads[4].wait()
    attend_gain, expand_gain = gains[1:2, :], gains[2:3, :]

    def hidden_frame(f, total):
        here = pl.ds(pl.multiple_of(f * PAD, 16), PAD)
        limit = jnp.where(p.dp * 4 + f < counts[0], 197, 0)
        good = lax.broadcasted_iota(jnp.int32, (PAD, D), 0) < limit
        xh, rate = normalize(hidden[here, :])
        dy = jnp.where(good, hg[here, :], 0.0)
        e = dy * expand_gain
        grad = rate * (e - jnp.mean(e, -1, keepdims=True) - xh * jnp.mean(e * xh, -1, keepdims=True))
        grad = grad + jnp.where(good, rg[0:1, :], 0.0)
        hg[here, :] = grad
        low[here, :] = grad.astype(B16)
        return total + jnp.sum(dy * xh, 0, keepdims=True)

    expand_gain_grad = lax.fori_loop(0, 4, hidden_frame, jnp.zeros((1, D), F32))
    reduce.next(1, 0)
    gather.stage(4, 0)
    loads[5].wait()
    loads[6].wait()

    def merge_tile(n, carry):
        cols = pl.ds(pl.multiple_of(n * 256, 256), 256)
        stage[:, :, pl.ds(pl.multiple_of(3072 + n * 256, 128), 256)] = dot(seent[...], low[:, cols]).astype(B16).reshape(8, 96, 256)
        dout[:, cols] = dot(low[...], wmerge[cols, :], 1, 1).astype(B16)
        return carry

    lax.fori_loop(0, 3, merge_tile, 0, unroll=3)
    weights.append(load(full.at[:, pl.ds(CMERGE, D)], wmerge))
    reduce.next(4, 2)
    early = bundle[0].reshape(128, BUNDLE)
    pick = jnp.where(
        jnp.logical_and(lax.broadcasted_iota(jnp.int32, (D, 128), 0) == p.k * 96 + lax.broadcasted_iota(jnp.int32, (D, 128), 1),
                        lax.broadcasted_iota(jnp.int32, (D, 128), 1) < 96), 1.0, 0.0).astype(B16)
    for index in range(3):
        chosen[index] = dot(early[:, D * index : D * index + D], pick).astype(B16)
    proj_o[...] = dot(dot(early[:, 3 * D : 4 * D], pick).astype(B16), early[:, 4 * D : 4 * D + 512], 0, 0)[0:96]
    loads[7].wait()
    loads[8].wait()
    normt_load.wait()
    half_lanes = lax.broadcasted_iota(jnp.int32, (PAD, 128), 1) < HEAD

    def fetch(group):
        return pltpu.make_async_copy(shares.at[:, pl.ds(4 * group, 4)], sbuf.at[group % 2], psem.at[group % 2])

    fetch(0).start()

    def attend_group(group):
        if group < 2:
            fetch(group + 1).start()
        fetch(group).wait()
        inputs, outputs = [], []
        for f in range(4):
            for j in range(2):
                here = pl.ds(f * PAD, PAD)
                qs, ks, vs = (pl.ds(b + (2 * group + j) * 128, 128) for b in (0, D, 2 * D))
                inputs.append((here, qs, ks, vs, mixed[here, qs], mixed[here, ks], mixed[here, vs], dout[here, qs], seen[here, qs],
                               [sbuf[group % 2, f, 2 * j + h] for h in range(2)]))
        for here, qs, ks, vs, q, k, v, do, o, share_of in inputs:
            right = jnp.concatenate([do, (-(do.astype(F32) * o.astype(F32))).astype(B16)], 1)
            dq = dk = dv = None
            zero = jnp.zeros_like(q)
            for h in range(2):
                mask = half_lanes if h == 0 else jnp.logical_not(half_lanes)
                share = share_of[h]
                left = jnp.concatenate([jnp.where(mask, v, zero), jnp.where(mask, jnp.ones_like(v), zero)], 1)
                ds = (share.astype(F32) * dot(left, right, 1, 1)).astype(B16)
                pq = dot(ds, jnp.where(mask, k, zero), 0, 0)
                pk = dot(ds, jnp.where(mask, q, zero))
                pv = dot(share, jnp.where(mask, do, zero))
                dq, dk, dv = (pq, pk, pv) if h == 0 else (dq + pq, dk + pk, dv + pv)
            outputs.append((here, qs, ks, vs, (dq * HEAD ** (-0.5)).astype(B16), dk.astype(B16), dv.astype(B16)))
        for here, qs, ks, vs, dq, dk, dv in outputs:
            mixed[here, qs] = dq
            mixed[here, ks] = dk
            mixed[here, vs] = dv

    def heads_tiles(group):
        def body(n, carry):
            cols = pl.ds(pl.multiple_of(n * D + group * 256, 128), 256)
            to = pl.ds(pl.multiple_of(3840 + group * D + n * 256, 128), 256)
            stage[:, :, to] = dot(n2t[...], mixed[:, cols]).astype(B16).reshape(8, 96, 256)
            return carry
        lax.fori_loop(0, 3, body, 0, unroll=3)

    attend_group(0)
    reduce.next(4, 1, 3)
    heads_tiles(0)
    reduce.next(5, 2, 0)
    attend_group(1)
    reduce.next(4, 5, 1, 3)
    heads_tiles(1)
    reduce.next(6, 2, 0)
    attend_group(2)
    tokens = load(xs_h, dout)
    loads[9].wait()
    tails = [mixed[pl.ds(f * PAD + 192, 16), :].astype(F32)[5:6] for f in range(4)]
    tails = jnp.concatenate(tails + [jnp.zeros((12, 3 * D), F32)], 0).astype(B16)
    xh, rate = normalize(mout[...])
    e = dot(tails, wheads[...], 1, 1)[0:8] * attend_gain
    mog[...] = rate * (e - jnp.mean(e, -1, keepdims=True) - xh * jnp.mean(e * xh, -1, keepdims=True))
    hop = Team(p, mog, mog_team, team_s.at[1], team_r.at[1])
    reduce.next(6, 4, 5)
    heads_tiles(2)
    reduce.next(7, 1, 3)
    for copy in weights:
        copy.wait()
    hop.wait()
    out_grad = jnp.concatenate([mog_team[i][0:4] for i in range(4)], 0)
    out_low = out_grad.astype(B16)
    fill(1, 4 * D, (out_low,))
    gather.stage(0, 1)
    courier_gain = gains[0:1, :]
    mq, mk, mv = mmix[:, 0:D], mmix[:, D : 2 * D], mmix[:, 2 * D : 3 * D]
    told_grad = dot(out_low, wmerge[...], 1, 1).astype(B16)
    upstream = spread_heads(told_grad)
    share = mshare[...]
    share_grad = dot(upstream, mv, 1, 1)
    dv = dot(share.astype(B16), upstream, 0, 0)
    inner = jnp.sum(share * share_grad, -1, keepdims=True)
    ds = (share * (share_grad - inner)).astype(B16)
    dq = join_heads(dot(ds, mk)) * HEAD ** (-0.5)
    dk = dot(ds, spread_heads(mq), 0, 0) * HEAD ** (-0.5)
    mixed_grad = jnp.concatenate([dq, dk, dv], 1).astype(B16)
    fill(1, D, (mixed_grad,))
    gather.stage(0, 2)
    reduce.next(7, 6)
    gather.stage(1, 1)
    norm_grad = dot(mixed_grad, wx[:, 0 : 3 * D], 1, 1)
    xh, rate = normalize(message[...])
    e = norm_grad * courier_gain
    grad = rate * (e - jnp.mean(e, -1, keepdims=True) - xh * jnp.mean(e * xh, -1, keepdims=True))
    message_grad = (out_grad + grad).astype(B16)
    fill(1, 0, (message_grad,))
    gather.stage(0, 3)
    gain_own = jnp.sum(norm_grad * xh, 0, keepdims=True)
    reduce.next(4, 2, 5)

    def tokens_tile(n):
        hidden[:, 256 * n : 256 * n + 256] = dot(mixed[...], wheads[256 * n : 256 * n + 256, :], 1, 1)

    gather.stage(1, 2)
    tokens_tile(0)
    gather.stage(2, 1)
    reduce.next(7, 6, 3)
    gather.stage(1, 3)
    tokens_tile(1)
    gather.stage(2, 2)
    gather.stage(3, 1)
    reduce.next(4, 5)
    tokens_tile(2)
    gather.stage(2, 3)
    gather.stage(3, 2)
    reduce.next(7, 6)
    tokens.wait()
    spot = lax.broadcasted_iota(jnp.int32, (PAD, 1), 0) == 197
    place = lax.broadcasted_iota(jnp.int32, (8, D), 0)
    first[...] = jnp.zeros_like(first)

    def token_frame(f, total):
        here = pl.ds(pl.multiple_of(f * PAD, 16), PAD)
        xh, rate = normalize(jnp.where(spot, row_of(mout[...], f), dout[here, :].astype(F32)))
        dy = hidden[here, :]
        e = dy * attend_gain
        grad = rate * (e - jnp.mean(e, -1, keepdims=True) - xh * jnp.mean(e * xh, -1, keepdims=True))
        patch = hg[here, :] + grad
        low[here, :] = patch.astype(B16)
        first[...] = jnp.where(place == f, patch[0:1], first[...])
        return total + jnp.sum(dy * xh, 0, keepdims=True)

    attend_gain_grad = lax.fori_loop(0, 4, token_frame, jnp.zeros((1, D), F32))
    patch_out = load(low, patch_h)
    gain_pack[0:8, :] = pack_row(attend_gain_grad)
    gain_pack[8:16, :] = pack_row(expand_gain_grad)
    gain_hop = Team(p, gain_pack, gain_team, team_s.at[2], team_r.at[2])
    gather.stage(3, 3)
    gather.stage(4, 1)
    reduce.next(4, 5)
    leader_grad = dot(message_grad, wx[:, 3 * D : 4 * D], 1, 1)
    lead_o[...] = jnp.concatenate([row_of(leader_grad, p.dp * 4 + f) for f in range(4)] + [jnp.zeros((4, D), F32)], 0) + first[...]
    gain_hop.wait()
    gain_send[0:16, :] = gain_team[0] + gain_team[1] + gain_team[2] + gain_team[3]
    gain_send[16:24, :] = pack_row(gain_own)
    gain_spread = Spread(p, gain_send, gain_all, hop_s.at[4], hop_r.at[4], same=True)
    reduce.next(7, 6)
    gather.stage(4, 2)

    def late(start, count):
        return bundle[1, :, :, start : start + count].reshape(128, count)

    cmerge_o[...] = dot(chosen[2], late(4 * D, D), 0, 0)[0:96]
    cheads_o[...] = dot(chosen[1], late(D, 3 * D), 0, 0)[0:96]
    reduce.next(6, 5, 4)
    gather.stage(4, 3)
    courier_o[...] = dot(chosen[0], late(0, D), 0, 0)[0:96]
    reduce.next(7)
    gain_spread.wait()
    total_gain = gain_all[0]
    for k in range(1, 8):
        total_gain = total_gain + gain_all[k]
    total_gain = jnp.concatenate([unpack_row(total_gain[8 * i : 8 * i + 8]) for i in range(3)] + [jnp.zeros((5, D), F32)], 0)
    both = dot(pick, twice(total_gain), 0, 1)
    gains_grad_o[...] = both[0:96, 0:8] + both[0:96, 8:16]
    for _ in range(8):
        for job in range(len(RJOBS)):
            if reduce.at[job] < 7:
                reduce.next(job)
    for job in range(len(RJOBS)):
        reduce.next(job)
    for job in range(4):
        gather.stage(5, job)
    gain_hop.done()
    gain_spread.done()
    hop.done()
    patch_out.wait()


def finish_kernel(patch, lead, fin, cgain, courier, cheads, cmerge, proj, shrink, loss,
                  patch_o, gain_a, gain_b, gain_c, heads_o, merge_o, expand_o, courier_o, cheads_o, cmerge_o, proj_o, shrink_o, loss_o):
    for source, target in ((courier, courier_o), (cheads, cheads_o), (cmerge, cmerge_o), (proj, proj_o), (shrink, shrink_o)):
        target[...] = source[...].astype(F32)
    top = lax.broadcasted_iota(jnp.int32, (PAD, 1), 0) == 0
    for f in range(4):
        value = jnp.where(top, lead[f : f + 1, :], patch[f * PAD : f * PAD + PAD, :].astype(F32)).astype(B16)
        patch_o[0, f] = value[0:197]
    expand_o[...] = fin[:, 0:3072].astype(F32)
    merge_o[...] = fin[:, 3072:3840].astype(F32)
    for group in range(3):
        for n in range(3):
            heads_o[:, n * D + group * 256 : n * D + group * 256 + 256] = fin[
                :, 3840 + group * D + n * 256 : 3840 + group * D + n * 256 + 256].astype(F32)
    own = jnp.concatenate([cgain[...], jnp.zeros((96, 120), F32)], 1)
    own = jnp.transpose(jnp.concatenate([own, jnp.zeros((32, 128), F32)], 0))
    gain_a[...], gain_b[...], gain_c[...] = own[0:1, 0:96], own[1:2, 0:96], own[2:3, 0:96]
    loss_o[...] = loss[0:1, 0:1]


VMEM = 62 * 1024 * 1000


def any_spec():
    return pl.BlockSpec(memory_space=pl.ANY)


def vmem_spec():
    return pl.BlockSpec(memory_space=pltpu.VMEM)


def smem_spec():
    return pl.BlockSpec(memory_space=pltpu.SMEM)


def sds(shape, dtype):
    return jax.ShapeDtypeStruct(shape, dtype)


def dma(*shape):
    return pltpu.SemaphoreType.DMA(shape)


def vm(shape, dtype):
    return pltpu.VMEM(shape, dtype)


def fast(
    patches, counts, captions, matches, courier, courier_gain, courier_heads, courier_merge, attend_gain, attend_heads,
    attend_merge, expand_gain, expand_weight, shrink_weight, projection,
):
    anys, vmem, smem = any_spec(), vmem_spec(), smem_spec()
    (full, normt, mixed, shares, seen, seent, hidden, n2t, dd, gsum, hsum, gains,
     leaders, message, mnorm, mmix, mshare, told, mout, texts, xs) = pl.pallas_call(
        forward_kernel,
        out_shape=(
            sds((D, NCOLS), B16), sds((D, ROWS), B16), sds((ROWS, 3 * D), B16), sds((48, PAD, PAD), B16), sds((ROWS, D), B16),
            sds((D, ROWS), B16), sds((ROWS, D), F32), sds((D, ROWS), B16), sds((ROWS, 4 * D), B16), sds((8, 4 * D), F32),
            sds((8, D), F32), sds((8, D), F32), sds((16, D), B16), sds((16, D), F32), sds((16, D), B16), sds((16, 3 * D), B16),
            sds((192, 16), F32), sds((16, D), B16), sds((8, D), F32), sds((4, 8, 8, 128), F32),
            sds((ROWS, D), B16)),
        in_specs=[vmem] * 5 + [smem] + [anys] * 7,
        out_specs=tuple([anys] * 9 + [vmem] * 11 + [anys]),
        scratch_shapes=[
            vm((D, NCOLS), B16), vm((ROWS, D), B16), vm((8, D), F32), vm((8, 128), F32), vm((4, 8, D), F32), vm((ROWS, D), B16), vm((D, ROWS), B16), vm((ROWS, 3 * D), B16),
            vm((48, PAD, PAD), B16), vm((ROWS, D), B16), vm((D, ROWS), B16), vm((ROWS, D), F32), vm((ROWS, D), B16),
            vm((D, ROWS), B16), vm((ROWS, 4 * D), B16),
            vm((8, 8, 128), F32), dma(len(JOBS), 28), dma(len(JOBS), 28), dma(7), dma(2, 3), dma(2, 3), dma(7), dma(7), dma(32)],
        compiler_params=pltpu.CompilerParams(collective_id=0, has_side_effects=True, vmem_limit_bytes=60 << 20),
        name="forward",
    )(patches, captions, courier_gain[None], attend_gain[None], expand_gain[None], counts, courier, courier_heads, attend_heads, courier_merge, attend_merge, expand_weight, projection)
    (patch, fin, loss, shrink_grad, courier_grad, cheads_grad, cmerge_grad, proj_grad, cgain, leads) = pl.pallas_call(
        rear_kernel,
        out_shape=(
            sds((ROWS, D), B16), sds((96, 6144), B16), sds((8, 128), F32), sds((384, D), F32), sds((96, D), F32),
            sds((96, 3 * D), F32), sds((96, D), F32), sds((96, 512), F32), sds((96, 8), F32), sds((8, D), F32)),
        in_specs=[anys] * 10 + [vmem] * 12 + [smem] * 2,
        out_specs=tuple([anys] + [vmem] * 9),
        scratch_shapes=[
            vm((8, 96, 6144), B16), vm((4, 8, 48, D), B16), vm((8, 16, 6144), B16), vm((4, 32, 6144), B16),
            vm((3, 32, 6144), B16), vm((32, 6144), B16), vm((32, 6144), B16), vm((2, 8, 16, BUNDLE), B16),
            vm((D, 4 * D), B16), vm((D, D), B16), vm((D, 3 * D), B16), vm((ROWS, 3 * D), B16),
            vm((ROWS, D), B16), vm((D, ROWS), B16), vm((ROWS, D), F32), vm((D, ROWS), B16), vm((ROWS, 4 * D), B16),
            vm((2, 4, 4, PAD, PAD), B16), vm((ROWS, D), F32), vm((ROWS, D), B16), vm((ROWS, D), B16),
            vm((D, 512), B16), vm((8, 512), F32), vm((4, 8, 512), F32), vm((8, 8, 384), F32), vm((8, 8, 384), F32),
            vm((8, 8, 128), F32), vm((8, 8, 128), F32), vm((8, 128), F32), vm((8, 8, 128), F32), vm((8, 8, 384), F32),
            vm((8, 8, 384), F32), vm((8, 4 * D), F32), vm((8, D), F32), vm((8, D), F32), vm((4, 8, D), F32),
            vm((3, 128, 128), B16), vm((16, 128), F32), vm((4, 16, 128), F32), vm((24, 128), F32), vm((8, 24, 128), F32),
            dma(len(RJOBS), 11), dma(len(RJOBS), 11), dma(4, 28), dma(4, 28), dma(3, 3), dma(3, 3), dma(5, 7), dma(5, 7),
            dma(16), dma(2)],
        compiler_params=pltpu.CompilerParams(collective_id=1, has_side_effects=True, vmem_limit_bytes=VMEM),
        name="rear",
    )(xs, normt, mixed, shares.reshape(4, HEADS, PAD, PAD), seen, seent, hidden, n2t, dd, full, gsum, hsum, shrink_weight, texts, gains, mout,
      leaders, message, mnorm, mmix, mshare, told, counts, matches)
    patch_grad, gain_a, gain_e, gain_m, heads, merge, expand, courier_out, cheads_out, cmerge_out, proj_out, shrink_out, loss_out = pl.pallas_call(
        finish_kernel,
        out_shape=(
            sds(patches.shape, B16), sds((1, 96), F32), sds((1, 96), F32), sds((1, 96), F32), sds((96, 3 * D), F32), sds((96, D), F32), sds((96, 4 * D), F32),
            sds((96, D), F32), sds((96, 3 * D), F32), sds((96, D), F32), sds((96, 512), F32), sds((384, D), F32), sds((1, 1), F32)),
        in_specs=[vmem] * 10,
        out_specs=tuple([vmem] * 13),
        compiler_params=pltpu.CompilerParams(vmem_limit_bytes=VMEM),
        name="finish",
    )(patch, leads, fin, cgain, courier_grad, cheads_grad, cmerge_grad, proj_grad, shrink_grad, loss)
    return (
        loss_out[0], patch_grad, courier_out, gain_m[0], cheads_out, cmerge_out, gain_a[0], heads,
        merge, gain_e[0], expand, shrink_out, proj_out,
    )


def joined_2(value, axis, join):
    pieces = jax.tree.map(lambda part: lax.all_gather(part, axis), value)
    head = jax.tree.map(lambda part: part[0], pieces)
    tail = jax.tree.map(lambda part: part[1:], pieces)
    running, _ = lax.scan(lambda running, share: (join(running, share), None), head, tail)
    return running


def layer_norm(value, gain):
    center = value - jnp.mean(value, -1, keepdims=True)
    spread = jnp.mean(center * center, -1, keepdims=True)
    return center * lax.rsqrt(spread + EPSILON) * gain


def norm_back(value, gain, upstream):
    _, pull = jax.vjp(layer_norm, value, gain)
    return pull(upstream)


def quick_gelu(value):
    return value * jax.nn.sigmoid(1.702 * value)


def unit_rows(value):
    return value * lax.rsqrt(jnp.sum(value * value, -1, keepdims=True) + 1e-06)


def split_heads(mixed, query_count):
    batch, length, triple = mixed.shape
    width = triple // 3
    rounded = mixed.astype(jnp.bfloat16)
    queries = rounded[:, :query_count, :width].reshape(batch, query_count, HEADS, HEAD)
    keys = rounded[:, :, width : 2 * width].reshape(batch, length, HEADS, HEAD)
    values = rounded[:, :, 2 * width :].reshape(batch, length, HEADS, HEAD)
    return (queries, keys, values)


def scores_of(queries, keys, key_mask):
    scores = jnp.einsum(
        "bqhd,bkhd->bhqk", queries, keys, preferred_element_type=jnp.float32
    ) * HEAD ** (-0.5)
    if key_mask is not None:
        scores = jnp.where(key_mask[:, None, None, :], scores, -1000000000.0)
    return scores


def attend_forward(queries, keys, values, key_mask):
    scores = scores_of(queries, keys, key_mask)
    peak = jnp.max(scores, -1, keepdims=True)
    raised = jnp.exp(scores - peak)
    total = jnp.sum(raised, -1, keepdims=True)
    shares = (raised / total).astype(jnp.bfloat16)
    joined = jnp.einsum("bhqk,bkhd->bqhd", shares, values, preferred_element_type=jnp.float32)
    batch, count = (joined.shape[0], joined.shape[1])
    return (
        joined.reshape(batch, count, HEADS * HEAD).astype(jnp.bfloat16),
        peak + jnp.log(total),
        shares,
    )


def attend_backward(queries, keys, values, key_mask, normalizer, shares, upstream):
    batch, count, width = upstream.shape
    upstream_low = upstream.astype(jnp.bfloat16).reshape(batch, count, HEADS, HEAD)
    chances = jnp.exp(scores_of(queries, keys, key_mask) - normalizer)
    share_grad = jnp.einsum(
        "bqhd,bkhd->bhqk", upstream_low, values, preferred_element_type=jnp.float32
    )
    value_grad = jnp.einsum(
        "bhqk,bqhd->bkhd", shares, upstream_low, preferred_element_type=jnp.float32
    )
    inner = jnp.sum(chances * share_grad, -1, keepdims=True)
    score_grad = (chances * (share_grad - inner)).astype(jnp.bfloat16)
    query_grad = jnp.einsum(
        "bhqk,bkhd->bqhd", score_grad, keys, preferred_element_type=jnp.float32
    ) * HEAD ** (-0.5)
    key_grad = jnp.einsum(
        "bhqk,bqhd->bkhd", score_grad, queries, preferred_element_type=jnp.float32
    ) * HEAD ** (-0.5)
    length = keys.shape[1]
    return (
        query_grad.reshape(batch, count, width),
        key_grad.reshape(batch, length, width),
        value_grad.reshape(batch, length, width),
    )


def frame_forward(block, message_rows, weights):
    attend_gain, attend_heads, attend_merge, expand_gain, expand_weight, shrink_weight = weights
    frames = block.astype(jnp.float32)
    tokens = jnp.concatenate([frames, message_rows[:, None, :]], 1)
    normed = layer_norm(tokens, attend_gain).astype(jnp.bfloat16)
    mixed = jnp.einsum("btd,de->bte", normed, attend_heads, preferred_element_type=jnp.float32)
    queries, keys, values = split_heads(mixed, block.shape[1])
    seen, normalizer, shares = attend_forward(queries, keys, values, None)
    hidden = frames + jnp.einsum(
        "bpd,de->bpe", seen, attend_merge, preferred_element_type=jnp.float32
    )
    normed_two = layer_norm(hidden, expand_gain).astype(jnp.bfloat16)
    grown = jnp.einsum("bpd,dm->bpm", normed_two, expand_weight, preferred_element_type=jnp.float32)
    gated = quick_gelu(grown).astype(jnp.bfloat16)
    result = hidden + jnp.einsum(
        "bpm,md->bpd", gated, shrink_weight, preferred_element_type=jnp.float32
    )
    kept = (
        tokens,
        normed,
        queries,
        keys,
        values,
        shares,
        normalizer,
        seen,
        hidden,
        normed_two,
        grown,
        gated,
    )
    return (jnp.sum(result, 1), kept)


def frame_backward(kept, upstream, weights):
    attend_gain, attend_heads, attend_merge, expand_gain, expand_weight, shrink_weight = weights
    (
        tokens,
        normed,
        queries,
        keys,
        values,
        shares,
        normalizer,
        seen,
        hidden,
        normed_two,
        grown,
        gated,
    ) = kept
    patch_count = hidden.shape[1]
    upstream_low = upstream.astype(jnp.bfloat16)
    shrink_grad = jnp.einsum("bpm,bd->md", gated, upstream_low, preferred_element_type=jnp.float32)
    gated_grad = jnp.einsum(
        "bd,md->bm", upstream_low, shrink_weight, preferred_element_type=jnp.float32
    )
    _, gelu_pull = jax.vjp(quick_gelu, grown)
    grown_grad = gelu_pull(jnp.broadcast_to(gated_grad[:, None, :], grown.shape))[0].astype(
        jnp.bfloat16
    )
    expand_grad = jnp.einsum(
        "bpd,bpm->dm", normed_two, grown_grad, preferred_element_type=jnp.float32
    )
    normed_two_grad = jnp.einsum(
        "bpm,dm->bpd", grown_grad, expand_weight, preferred_element_type=jnp.float32
    )
    hidden_grad, expand_gain_grad = norm_back(hidden, expand_gain, normed_two_grad)
    hidden_grad = hidden_grad + upstream[:, None, :]
    hidden_low = hidden_grad.astype(jnp.bfloat16)
    merge_grad = jnp.einsum("bpd,bpe->de", seen, hidden_low, preferred_element_type=jnp.float32)
    seen_grad = jnp.einsum(
        "bpe,de->bpd", hidden_low, attend_merge, preferred_element_type=jnp.float32
    )
    query_grad, key_grad, value_grad = attend_backward(
        queries, keys, values, None, normalizer, shares, seen_grad
    )
    length = tokens.shape[1]
    query_grad = jnp.pad(query_grad, ((0, 0), (0, length - patch_count), (0, 0)))
    mixed_grad = jnp.concatenate([query_grad, key_grad, value_grad], 2).astype(jnp.bfloat16)
    heads_grad = jnp.einsum("btd,bte->de", normed, mixed_grad, preferred_element_type=jnp.float32)
    normed_grad = jnp.einsum(
        "bte,de->btd", mixed_grad, attend_heads, preferred_element_type=jnp.float32
    )
    token_grad, attend_gain_grad = norm_back(tokens, attend_gain, normed_grad)
    patch_grad = hidden_grad + token_grad[:, :patch_count]
    block_grads = (
        attend_gain_grad,
        heads_grad,
        merge_grad,
        expand_gain_grad,
        expand_grad,
        shrink_grad,
    )
    return (patch_grad, token_grad[:, patch_count], block_grads)


def shards(
    patches,
    counts,
    captions,
    matches,
    courier,
    courier_gain,
    courier_heads,
    courier_merge,
    attend_gain,
    attend_heads,
    attend_merge,
    expand_gain,
    expand_weight,
    shrink_weight,
    projection,
):
    videos, local_frames, patch_count, width = patches.shape
    frame_total = local_frames * lax.axis_size("dp")
    offset = lax.axis_index("dp") * local_frames
    rows = videos * local_frames
    per_block = rows // MICRO
    courier_full, courier_gain_full, heads_full, merge_full, projection_full = (
        lax.all_gather(courier, "fsdp", axis=0, tiled=True),
        lax.all_gather(courier_gain, "fsdp", axis=0, tiled=True),
        lax.all_gather(courier_heads, "fsdp", axis=0, tiled=True),
        lax.all_gather(courier_merge, "fsdp", axis=0, tiled=True),
        lax.all_gather(projection, "fsdp", axis=0, tiled=True),
    )

    def fetch():
        return (
            lax.all_gather(attend_gain, "fsdp", axis=0, tiled=True),
            lax.all_gather(attend_heads, "fsdp", axis=0, tiled=True),
            lax.all_gather(attend_merge, "fsdp", axis=0, tiled=True),
            lax.all_gather(expand_gain, "fsdp", axis=0, tiled=True),
            lax.all_gather(expand_weight, "fsdp", axis=0, tiled=True),
            lax.all_gather(shrink_weight, "fsdp", axis=0, tiled=True),
        )

    leaders = lax.all_gather(patches[:, :, 0, :], "dp", axis=1, tiled=True)
    present = lax.broadcasted_iota(jnp.int32, (videos, frame_total), 1) < counts[:, None]
    message = jnp.einsum("vfd,de->vfe", leaders, courier_full, preferred_element_type=jnp.float32)
    message_norm = layer_norm(message, courier_gain_full).astype(jnp.bfloat16)
    message_mixed = jnp.einsum(
        "vfd,de->vfe", message_norm, heads_full, preferred_element_type=jnp.float32
    )
    told_queries, told_keys, told_values = split_heads(message_mixed, frame_total)
    told, told_normalizer, told_shares = attend_forward(
        told_queries, told_keys, told_values, present
    )
    message_out = message + jnp.einsum(
        "vfd,de->vfe", told, merge_full, preferred_element_type=jnp.float32
    )
    mine = lax.dynamic_slice_in_dim(message_out, offset, local_frames, 1).reshape(rows, width)
    flat = patches.reshape(rows, patch_count, width)
    frame_weights = fetch()
    kept_blocks = []
    sums = []
    for index in range(MICRO):
        if index > 0:
            frame_weights = fetch()
        start = index * per_block
        frame_sums, kept = frame_forward(
            flat[start : start + per_block], mine[start : start + per_block], frame_weights
        )
        kept_blocks.append(kept)
        sums.append(frame_sums)
    frame_sums = jnp.concatenate(sums, 0).reshape(videos, local_frames, width)
    own_present = lax.dynamic_slice_in_dim(present, offset, local_frames, 1)
    partial_value = jnp.sum(jnp.where(own_present[:, :, None], frame_sums, 0.0), 1)
    pooled_sum = lax.psum(partial_value, "dp")
    denominator = (counts * patch_count).astype(jnp.float32)[:, None]
    pooled = pooled_sum / denominator
    pooled_low = pooled.astype(jnp.bfloat16)
    embed = jnp.dot(pooled_low, projection_full, preferred_element_type=jnp.float32)
    video_unit = unit_rows(embed).astype(jnp.bfloat16)
    segment = lax.axis_index("dp") * (captions.shape[0] * lax.axis_size("fsdp"))

    def scores_for(piece):
        text_unit = unit_rows(piece.astype(jnp.float32)).astype(jnp.bfloat16)
        logits = (
            jnp.einsum("ve,te->vt", video_unit, text_unit, preferred_element_type=jnp.float32)
            * LOGIT_SCALE
        )
        positions = segment + lax.broadcasted_iota(jnp.int32, logits.shape, 1)
        return (text_unit, logits, positions == matches[:, None])

    peak = jnp.full((videos,), -1e30, jnp.float32)
    _, logits, matched = scores_for(lax.all_gather(captions, "fsdp", axis=0, tiled=True))
    fresh = jnp.maximum(peak, jnp.max(logits, 1))
    total = jnp.sum(jnp.exp(logits - fresh[:, None]), 1)
    picked = jnp.sum(jnp.where(matched, logits, 0.0), 1)
    peak, total, picked = (fresh, total, picked)

    def combine(first, second):
        top = jnp.maximum(first[0], second[0])
        joined = first[1] * jnp.exp(first[0] - top) + second[1] * jnp.exp(second[0] - top)
        return (top, joined, first[2] + second[2])

    peak, total, picked = joined_2((peak, total, picked), "dp", combine)
    normalizer = peak + jnp.log(total)
    loss = normalizer - picked
    text_unit, logits, matched = scores_for(lax.all_gather(captions, "fsdp", axis=0, tiled=True))
    slope = (jnp.exp(logits - normalizer[:, None]) - matched.astype(jnp.float32)).astype(
        jnp.bfloat16
    )
    unit_grad = jnp.dot(slope, text_unit, preferred_element_type=jnp.float32) * LOGIT_SCALE
    unit_grad = lax.psum(unit_grad, "dp")
    _, unit_pull = jax.vjp(unit_rows, embed)
    embed_grad = unit_pull(unit_grad)[0].astype(jnp.bfloat16)
    projection_grad = jnp.einsum(
        "vd,ve->de", pooled_low, embed_grad, preferred_element_type=jnp.float32
    )
    pooled_grad = jnp.einsum(
        "ve,de->vd", embed_grad, projection_full, preferred_element_type=jnp.float32
    )
    upstream_all = jnp.where(own_present[:, :, None], (pooled_grad / denominator)[:, None, :], 0.0)
    upstream_all = upstream_all.reshape(rows, width)
    collected = None
    patch_list = []
    message_list = []
    for index in range(MICRO):
        frame_weights = fetch()
        start = index * per_block
        patch_grad, message_token_grad, block_grads = frame_backward(
            kept_blocks[index], upstream_all[start : start + per_block], frame_weights
        )
        patch_list.append(patch_grad)
        message_list.append(message_token_grad)
        block_grads = (
            lax.psum_scatter(
                block_grads[0].astype(jnp.float32), "fsdp", scatter_dimension=0, tiled=True
            ),
            lax.psum_scatter(block_grads[1], "fsdp", scatter_dimension=0, tiled=True),
            lax.psum_scatter(block_grads[2], "fsdp", scatter_dimension=0, tiled=True),
            lax.psum_scatter(
                block_grads[3].astype(jnp.float32), "fsdp", scatter_dimension=0, tiled=True
            ),
            lax.psum_scatter(block_grads[4], "fsdp", scatter_dimension=0, tiled=True),
            lax.psum_scatter(block_grads[5], "fsdp", scatter_dimension=0, tiled=True),
        )
        collected = (
            block_grads if collected is None else jax.tree.map(jnp.add, collected, block_grads)
        )
    collected = (
        lax.psum(collected[0].astype(jnp.bfloat16), "dp").astype(jnp.float32),
        lax.psum(collected[1].astype(jnp.bfloat16), "dp").astype(jnp.float32),
        lax.psum(collected[2].astype(jnp.bfloat16), "dp").astype(jnp.float32),
        lax.psum(collected[3].astype(jnp.bfloat16), "dp").astype(jnp.float32),
        lax.psum(collected[4].astype(jnp.bfloat16), "dp").astype(jnp.float32),
        lax.psum(collected[5].astype(jnp.bfloat16), "dp").astype(jnp.float32),
    )
    message_token_grad = jnp.concatenate(message_list, 0).reshape(videos, local_frames, width)
    out_grad = lax.all_gather(message_token_grad, "dp", axis=1, tiled=True)
    out_low = out_grad.astype(jnp.bfloat16)
    merge_message_grad = jnp.einsum(
        "vfd,vfe->de", told, out_low, preferred_element_type=jnp.float32
    )
    told_grad = jnp.einsum("vfe,de->vfd", out_low, merge_full, preferred_element_type=jnp.float32)
    told_query_grad, told_key_grad, told_value_grad = attend_backward(
        told_queries, told_keys, told_values, present, told_normalizer, told_shares, told_grad
    )
    courier_mixed_grad = jnp.concatenate(
        [told_query_grad, told_key_grad, told_value_grad], 2
    ).astype(jnp.bfloat16)
    heads_message_grad = jnp.einsum(
        "vfd,vfe->de", message_norm, courier_mixed_grad, preferred_element_type=jnp.float32
    )
    message_norm_grad = jnp.einsum(
        "vfe,de->vfd", courier_mixed_grad, heads_full, preferred_element_type=jnp.float32
    )
    message_grad, courier_gain_grad = norm_back(message, courier_gain_full, message_norm_grad)
    message_grad = (message_grad + out_grad).astype(jnp.bfloat16)
    courier_grad = jnp.einsum(
        "vfd,vfe->de", leaders, message_grad, preferred_element_type=jnp.float32
    )
    leader_grad = jnp.einsum(
        "vfe,de->vfd", message_grad, courier_full, preferred_element_type=jnp.float32
    )
    own_leader = lax.dynamic_slice_in_dim(leader_grad, offset, local_frames, 1).reshape(rows, width)
    patch_all = jnp.concatenate(patch_list, 0)
    patch_all = patch_all.at[:, 0, :].add(own_leader)
    patch_out = patch_all.reshape(videos, local_frames, patch_count, width).astype(jnp.bfloat16)
    video_grads = (
        lax.psum_scatter(courier_grad, "fsdp", scatter_dimension=0, tiled=True),
        lax.psum_scatter(
            courier_gain_grad.astype(jnp.float32), "fsdp", scatter_dimension=0, tiled=True
        ),
        lax.psum_scatter(heads_message_grad, "fsdp", scatter_dimension=0, tiled=True),
        lax.psum_scatter(merge_message_grad, "fsdp", scatter_dimension=0, tiled=True),
        lax.psum_scatter(projection_grad, "fsdp", scatter_dimension=0, tiled=True),
    )
    return (
        loss,
        patch_out,
        video_grads[0],
        video_grads[1],
        video_grads[2],
        video_grads[3],
        collected[0],
        collected[1],
        collected[2],
        collected[3],
        collected[4],
        collected[5],
        video_grads[4],
    )


def solution(mesh):
    fitting = mesh.shape['dp'] == 4 and mesh.shape['fsdp'] == Z * Y
    return jax.shard_map(
        fast if fitting else shards,
        mesh=mesh,
        in_specs=(
            P("fsdp", "dp", None, None),
            P("fsdp"),
            P(("dp", "fsdp"), None),
            P("fsdp"),
            P("fsdp", None),
            P("fsdp"),
            P("fsdp", None),
            P("fsdp", None),
            P("fsdp"),
            P("fsdp", None),
            P("fsdp", None),
            P("fsdp"),
            P("fsdp", None),
            P("fsdp", None),
            P("fsdp", None),
        ),
        out_specs=(
            P("fsdp"),
            P("fsdp", "dp", None, None),
            P("fsdp", None),
            P("fsdp"),
            P("fsdp", None),
            P("fsdp", None),
            P("fsdp"),
            P("fsdp", None),
            P("fsdp", None),
            P("fsdp"),
            P("fsdp", None),
            P("fsdp", None),
            P("fsdp", None),
        ),
        check_vma=False,
    )
```

```python
import functools

import jax
import jax.numpy as jnp
from jax import lax
from jax.experimental import pallas as pl
from jax.experimental.pallas import tpu as pltpu
from jax.sharding import PartitionSpec as P

MESH = pl.DeviceIdType.MESH
Z, Y = 4, 2
HEADS = 12
HEAD = 64
EPSILON = 1e-05
LOGIT_SCALE = 64.0
PAD = 208
ROWS = 832
D = 768
F32 = jnp.float32
B16 = jnp.bfloat16

MICRO = 2

COURIER, GAINS, CHEADS, AHEADS, CMERGE, AMERGE, EXPAND, PROJ = 0, 768, 896, 3200, 5504, 6272, 7040, 10112
NCOLS = 10624
JOBS = ((0, 896), (896, 768), (1664, 768), (2432, 768), (3200, 768), (3968, 768), (4736, 768), (5504, 768), (6272, 768),
        (7040, 768), (7808, 768), (8576, 768), (10112, 512), (9344, 512), (9856, 256))


class Pos:
    def __init__(self):
        self.dp = lax.axis_index("dp")
        self.k = lax.axis_index("fsdp")
        self.x, self.c = self.dp // 2, lax.rem(self.dp, 2)
        self.z, self.y = self.k // Y, lax.rem(self.k, Y)
        self.core = (self.x * 2 + 1 - self.c, self.k)
        self.xp = ((1 - self.x) * 2 + self.c, self.k)
        self.cross = ((1 - self.x) * 2 + 1 - self.c, self.k)
        self.yp = (self.dp, self.z * Y + 1 - self.y)
        self.team = (self.core, self.xp, self.cross)

    def ahead(self, d):
        return lax.rem(self.z + d, Z)

    def behind(self, d):
        return lax.rem(self.z - d + Z, Z)

    def column(self):
        return [(self.dp, self.ahead(d) * Y + self.y) for d in (1, 2, 3)]

    def peers(self):
        return [self.core, self.xp, self.yp] + self.column()

    def plane(self):
        return [(self.dp, lax.rem(self.k + d, Z * Y)) for d in range(1, Z * Y)]


def barrier(peers):
    semaphore = pltpu.get_barrier_semaphore()
    for peer in peers:
        pl.semaphore_signal(semaphore, inc=1, device_id=peer, device_id_type=MESH)
    pl.semaphore_wait(semaphore, len(peers))


def remote(source, target, send, receive, device):
    return pltpu.make_async_remote_copy(
        src_ref=source, dst_ref=target, send_sem=send, recv_sem=receive, device_id=device, device_id_type=MESH)


class Gather:
    def __init__(self, p, block, jobs, send, receive):
        self.p, self.block, self.jobs, self.send, self.receive = p, block, jobs, send, receive

    def copy(self, job, index, k, first, count, device):
        ref = self.block(k, first, count, job)
        return remote(ref, ref, self.send.at[job, index], self.receive.at[job, index], device)

    def far(self, d):
        p = self.p
        return p.behind(d + 1) * Y + p.y if d < 3 else p.behind(d - 3) * Y + 1 - p.y

    def stage(self, stage, job):
        if job < 0 or job >= self.jobs:
            return
        p, copy = self.p, self.copy
        own, single = 3 * p.c + p.x, 3 * p.c + 2 * p.x
        other = 3 * p.c + 2 * (1 - p.x)
        if stage == 0:
            for d, device in enumerate(p.column()):
                copy(job, d, p.k, own, 2, device).start()
            copy(job, 3, p.k, own, 2, p.yp).start()
        elif stage == 1:
            for d in range(3):
                k = self.far(d)
                copy(job, d, k, own, 2, p.core).wait_recv()
                copy(job, 4 + d, k, own, 2, p.yp).start()
                copy(job, 7 + d, k, single, 1, p.xp).start()
                copy(job, 14 + d, k, own, 2, p.core).start()
        elif stage == 2:
            for d in range(3, 7):
                k = self.far(d)
                copy(job, d, k, own, 2, p.core).wait_recv()
                copy(job, 7 + d, k, single, 1, p.xp).start()
                copy(job, 14 + d, k, own, 2, p.core).start()
        elif stage == 3:
            for d in range(7):
                k = self.far(d)
                copy(job, 7 + d, k, other, 1, p.core).wait_recv()
                copy(job, 21 + d, k, other, 1, p.core).start()
        elif stage == 4:
            for d in range(7):
                copy(job, 14 + d, self.far(d), 3 * (1 - p.c) + p.x, 2, p.core).wait_recv()
            for d in range(7):
                copy(job, 21 + d, self.far(d), 3 * (1 - p.c) + 2 * (1 - p.x), 1, p.core).wait_recv()
        elif stage == 5:
            for index in range(28):
                copy(job, index, p.k, 0, 2 if index < 7 or 14 <= index < 21 else 1, p.core).wait_send()

    def tick(self, t, lag):
        for stage in (0, 1, 2, 3, 4, 5):
            self.stage(stage, t - lag[stage])


class Spread:
    def __init__(self, p, source, target, send, receive, same=False):
        self.p, self.target = p, target
        count = Z * Y
        self.copies = []
        for d in range(1, count):
            to = lax.rem(p.k + d, count)
            part = source if same else source.at[to]
            self.copies.append(remote(part, target.at[p.k], send.at[d - 1], receive.at[d - 1], (p.dp, to)))
        self.arrivals = []
        for d in range(1, count):
            origin = lax.rem(p.k - d + count, count)
            self.arrivals.append(
                remote(target.at[origin], target.at[origin], send.at[d - 1], receive.at[d - 1], (p.dp, origin)))
        target[p.k] = source[...] if same else source[p.k]
        for copy in self.copies:
            copy.start()

    def wait(self):
        for copy in self.arrivals:
            copy.wait_recv()

    def done(self):
        for copy in self.copies:
            copy.wait_send()


class Team:
    def __init__(self, p, source, target, send, receive):
        self.copies, self.arrivals = [], []
        target[p.dp] = source[...]
        for index, other in enumerate(p.team):
            self.copies.append(remote(source, target.at[p.dp], send.at[index], receive.at[index], other))
            self.arrivals.append(remote(source, target.at[other[0]], send.at[index], receive.at[index], other))
        for copy in self.copies:
            copy.start()

    def wait(self):
        for copy in self.arrivals:
            copy.wait_recv()

    def done(self):
        for copy in self.copies:
            copy.wait_send()


class Reduce:
    def __init__(self, p, stage, buffers, fin, jobs, send, receive):
        self.p, self.stage, self.fin, self.jobs, self.send, self.receive = p, stage, fin, jobs, send, receive
        self.rc, self.rx, self.ry, self.rz, self.own, self.rf = buffers
        self.at = [0] * len(jobs)

    def copies(self, job, step):
        p = self.p
        first, count = self.jobs[job]
        cols = pl.ds(first, count)
        half, other = pl.ds(pl.multiple_of(48 * p.c, 16), 48), pl.ds(pl.multiple_of(48 * (1 - p.c), 16), 48)
        carried = pl.ds(pl.multiple_of((3 * p.c + p.x) * 16, 16), 32)
        away = pl.ds(pl.multiple_of((3 * p.c + 2 * (1 - p.x)) * 16, 16), 16)
        s, r = self.send, self.receive
        if step == 0:
            target = self.rc.at[job % 4, :, :, pl.ds(0, count)]
            return [remote(self.stage.at[:, other, cols], target, s.at[job, 0], r.at[job, 0], p.core)]
        if step == 1:
            return [remote(self.stage.at[:, away, cols], self.rx.at[:, :, cols], s.at[job, 1], r.at[job, 1], p.xp)]
        if step == 2:
            return [remote(self.stage.at[z * Y + 1 - p.y, carried, cols], self.ry.at[z, :, cols], s.at[job, 2 + z],
                           r.at[job, 2 + z], p.yp) for z in range(Z)]
        if step == 3:
            return [remote(self.stage.at[device[1], carried, cols], self.rz.at[d, :, cols], s.at[job, 6 + d],
                           r.at[job, 6 + d], device) for d, device in enumerate(p.column())]
        if step == 4:
            return [remote(self.own.at[:, cols], self.rf.at[:, cols], s.at[job, 9], r.at[job, 9], p.xp)]
        return [remote(self.fin.at[half, cols], self.fin.at[half, cols], s.at[job, 10], r.at[job, 10], p.core)]

    def next(self, *jobs, scale=None):
        for job in jobs:
            self.step(self.at[job], job, scale)
            self.at[job] += 1

    def step(self, step, job, scale):
        p = self.p
        first, count = self.jobs[job]
        cols = pl.ds(first, count)
        half, other = pl.ds(pl.multiple_of(48 * p.c, 16), 48), pl.ds(pl.multiple_of(48 * (1 - p.c), 16), 48)
        carried = pl.ds(pl.multiple_of((3 * p.c + p.x) * 16, 16), 32)
        if step == 6:
            remote(self.fin.at[other, cols], self.fin.at[other, cols], self.send.at[job, 10], self.receive.at[job, 10],
                   p.core).wait_recv()
        elif step > 0 and step < 6:
            for copy in self.copies(job, step - 1):
                copy.wait_recv()
        if step == 1:
            def add(k, carry):
                self.stage[k, half, cols] = self.stage[k, half, cols] + self.rc[job % 4, k, :, pl.ds(0, count)]
                return carry
            lax.fori_loop(0, Z * Y, add, 0)
        elif step == 2:
            def add(k, carry):
                value = self.stage[k, carried, cols].astype(F32)
                other_x = self.rx[k, :, cols].astype(F32)
                top = value[0:16] + jnp.where(p.x == 0, other_x, 0.0)
                low = value[16:32] + jnp.where(p.x == 0, 0.0, other_x)
                value = jnp.concatenate([top, low], 0)
                if scale is not None:
                    value = value * scale[0:1, cols]
                self.stage[k, carried, cols] = value.astype(B16)
                return carry
            lax.fori_loop(0, Z * Y, add, 0)
        elif step == 3:
            def add(z, carry):
                k = z * Y + p.y
                self.stage[k, carried, cols] = self.stage[k, carried, cols] + self.ry[z, :, cols]
                return carry
            lax.fori_loop(0, Z, add, 0)
        elif step == 4:
            total = self.stage[p.k, carried, cols].astype(F32)
            for d in range(3):
                total = total + self.rz[d, :, cols].astype(F32)
            self.own[:, cols] = total.astype(B16)
        elif step == 5:
            mine, theirs = self.own[:, cols].astype(F32), self.rf[:, cols].astype(F32)
            left = jnp.where(p.x == 0, mine[0:16], theirs[0:16])
            right = jnp.where(p.x == 0, theirs[16:32], mine[16:32])
            middle = jnp.where(p.x == 0, mine[16:32], mine[0:16]) + jnp.where(p.x == 0, theirs[0:16], theirs[16:32])
            self.fin[half, cols] = jnp.concatenate([left, middle, right], 0).astype(B16)
        if step < 6:
            for copy in self.copies(job, step):
                copy.start()
        if step == 7:
            for earlier in range(6):
                for copy in self.copies(job, earlier):
                    copy.wait_send()


def dot(a, b, ca=1, cb=0):
    return lax.dot_general(a, b, (((ca,), (cb,)), ((), ())), preferred_element_type=F32)


def normalize(value):
    center = value - jnp.mean(value, -1, keepdims=True)
    rate = lax.rsqrt(jnp.mean(center * center, -1, keepdims=True) + EPSILON)
    return center * rate, rate


def head_mask():
    return lax.broadcasted_iota(jnp.int32, (192, D), 0) // 16 == lax.broadcasted_iota(jnp.int32, (192, D), 1) // HEAD


def spread_heads(value):
    return jnp.where(head_mask(), jnp.concatenate([value.astype(F32)] * HEADS, 0), 0.0).astype(B16)


def join_heads(value):
    value = jnp.where(head_mask(), value, 0.0)
    total = value[0:16]
    for head in range(1, HEADS):
        total = total + value[16 * head : 16 * head + 16]
    return total


def row_of(value, index):
    rows = lax.broadcasted_iota(jnp.int32, value.shape, 0)
    return jnp.sum(jnp.where(rows == index, value, 0.0), 0, keepdims=True)


def forward_kernel(
    patches, captions, gain_a, gain_b, gain_c, counts, courier, cheads, aheads, cmerge, amerge, expand, projection,
    full_o, normt_o, mixed_o, shares_o, seen_o, seent_o, hidden_o, n2t_o, d_o, gsum_o, hsum_o, gains_o,
    leaders_o, message_o, mnorm_o, mmix_o, mshare_o, told_o, mout_o, texts_o, xs_o,
    full, xs, lead, caption, leadbuf, norm, normt, mixed, shares, seen, seent, hidden, n2, n2t, dd,
    texts, ssem, rsem, lsem, lead_s, lead_r, text_s, text_r, osem,
):
    p = Pos()
    weights = ((courier, COURIER), (cheads, CHEADS), (aheads, AHEADS), (cmerge, CMERGE), (amerge, AMERGE),
               (expand, EXPAND), (projection, PROJ))
    mine = pl.ds(pl.multiple_of(p.k * 96, 16), 96)
    loads = []
    for index, (ref, start) in enumerate(weights):
        copy = pltpu.make_async_copy(ref, full.at[mine, pl.ds(start, ref.shape[1])], lsem.at[index])
        copy.start()
        loads.append(copy)
    text = captions[...].astype(F32)
    caption[...] = jnp.concatenate([text[:, 128 * r : 128 * r + 128] for r in range(4)] + [jnp.zeros((4, 128), F32)], 0)
    lead[...] = jnp.concatenate([patches[0, 0].astype(F32), jnp.zeros((4, D), F32)], 0)
    square = jnp.concatenate([gain_a[...].astype(F32), gain_b[...].astype(F32), gain_c[...].astype(F32)], 0)
    square = jnp.concatenate([square, jnp.zeros((3, 32), F32)], 1)
    square = jnp.concatenate([square, jnp.zeros((125, 128), F32)], 0)
    full[mine, GAINS : GAINS + 128] = jnp.transpose(square)[0:96].astype(B16)
    leadbuf[p.dp] = lead[...]
    barrier(p.plane() + list(p.team))
    text_hop = Spread(p, caption, texts, text_s, text_r, same=True)
    others = [p.core, p.xp, ((1 - p.x) * 2 + 1 - p.c, p.k)]
    sends = []
    for index, other in enumerate(others):
        copy = pltpu.make_async_remote_copy(
            src_ref=lead, dst_ref=leadbuf.at[p.dp], send_sem=lead_s.at[0, index], recv_sem=lead_r.at[0, index],
            device_id=other, device_id_type=MESH)
        copy.start()
        sends.append(copy)
    for copy in loads:
        copy.wait()
    def block(k, start, count, job):
        first_col, columns = JOBS[job]
        return full.at[pl.ds(pl.multiple_of(k * 96 + start * 16, 16), count * 16), pl.ds(first_col, columns)]

    gather = Gather(p, block, len(JOBS), ssem, rsem)
    lag = (0, 1, 2, 3, 4, 5)
    outs = []

    def out(source, target):
        copy = pltpu.make_async_copy(source, target, osem.at[len(outs)])
        copy.start()
        outs.append(copy)

    ticked, written = [0], [0]

    def upto(job):
        while ticked[0] <= job + lag[4]:
            gather.tick(ticked[0], lag)
            ticked[0] += 1
        while written[0] <= min(job, len(JOBS) - 1):
            cols = pl.ds(*JOBS[written[0]])
            out(full.at[:, cols], full_o.at[:, cols])
            written[0] += 1

    upto(-3)
    for f in range(4):
        xs[f * PAD + 192 : f * PAD + PAD, :] = jnp.zeros((16, D), B16)
        xs[f * PAD : f * PAD + 197, :] = patches[0, :, f, :]
    out(xs, xs_o)
    text_hop.wait()
    text_team = Team(p, texts, texts_o, lead_s.at[1], lead_r.at[1])
    upto(0)
    for index, other in enumerate(others):
        pltpu.make_async_remote_copy(
            src_ref=lead, dst_ref=leadbuf.at[other[0]], send_sem=lead_s.at[0, index], recv_sem=lead_r.at[0, index],
            device_id=other, device_id_type=MESH).wait_recv()
    leaders = jnp.concatenate([leadbuf[index][0:4] for index in range(4)], 0)
    leaders_o[...] = leaders.astype(B16)
    rows = jnp.transpose(full[:, GAINS : GAINS + 128].astype(F32))[0:8]
    gains_o[...] = rows
    courier_gain, attend_gain, expand_gain = rows[0:1], rows[1:2], rows[2:3]
    message = dot(leaders.astype(B16), full[:, COURIER : COURIER + D])
    message_o[...] = message
    xh, _ = normalize(message)
    mnorm = (xh * courier_gain).astype(B16)
    mnorm_o[...] = mnorm

    def norm_frame(f, carry):
        here = pl.ds(pl.multiple_of(f * PAD, 16), PAD)
        xh, _ = normalize(xs[here, :].astype(F32))
        norm[here, :] = (xh * attend_gain).astype(B16)
        return carry

    lax.fori_loop(0, 4, norm_frame, 0)
    upto(3)
    mmix = dot(mnorm, full[:, CHEADS : CHEADS + 3 * D])
    mq, mk, mv = mmix[:, :D].astype(B16), mmix[:, D : 2 * D].astype(B16), mmix[:, 2 * D :].astype(B16)
    mmix_o[...] = mmix.astype(B16)
    scores = dot(spread_heads(mq), mk, 1, 1) * HEAD ** (-0.5)
    frames = lax.broadcasted_iota(jnp.int32, (192, 16), 1)
    scores = jnp.where(frames < counts[0], scores, -1000000000.0)
    raised = jnp.exp(scores - jnp.max(scores, -1, keepdims=True))
    mshare = raised / jnp.sum(raised, -1, keepdims=True)
    mshare_o[...] = mshare
    told = join_heads(dot(mshare.astype(B16), mv)).astype(B16)
    told_o[...] = told

    def heads_tile(base, factor):
        def body(n, carry):
            cols = pl.ds(pl.multiple_of(base + n * 256, 256), 256)
            wcols = pl.ds(pl.multiple_of(AHEADS + base + n * 256, 128), 256)
            mixed[:, cols] = (dot(norm[...], full[:, wcols]) * factor).astype(B16)
            return carry
        lax.fori_loop(0, 3, body, 0)

    upto(4)
    heads_tile(0, HEAD ** (-0.5))
    upto(5)
    heads_tile(D, 1.0)
    upto(6)
    heads_tile(2 * D, 1.0)
    upto(7)
    mout_all = message + dot(told, full[:, CMERGE : CMERGE + D])
    mout = jnp.concatenate([row_of(mout_all, p.dp * 4 + f) for f in range(4)] + [jnp.zeros((4, D), F32)], 0)
    mout_o[...] = mout
    xh, _ = normalize(mout)
    extra = (xh * attend_gain).astype(B16)
    extra_kv = dot(extra, full[:, AHEADS + D : AHEADS + 3 * D])
    extra = extra.astype(F32)
    spot = lax.broadcasted_iota(jnp.int32, (16, 1), 0) == 5
    for f in range(4):
        tail = pl.ds(f * PAD + 192, 16)
        norm[tail, :] = jnp.where(spot, extra[f : f + 1], norm[tail, :].astype(F32)).astype(B16)
        old = mixed[tail, D : 3 * D].astype(F32)
        mixed[tail, D : 3 * D] = jnp.where(spot, extra_kv[f : f + 1], old).astype(B16)
    out(mixed, mixed_o)

    first = lax.broadcasted_iota(jnp.int32, (PAD, 128), 1) < HEAD
    kept = lax.broadcasted_iota(jnp.int32, (PAD, PAD), 0) < 198

    def attend(f, pair):
        here = pl.ds(pl.multiple_of(f * PAD, 16), PAD)
        at = pl.multiple_of(pair * 128, 128)
        q = mixed[here, pl.ds(at, 128)]
        k = mixed[here, pl.ds(pl.multiple_of(D + at, 128), 128)]
        v = mixed[here, pl.ds(pl.multiple_of(2 * D + at, 128), 128)]
        total = None
        for h in range(2):
            mask = first if h == 0 else jnp.logical_not(first)
            kh, vh = jnp.where(mask, k, jnp.zeros_like(k)), jnp.where(mask, v, jnp.zeros_like(v))
            scores = jnp.where(kept, dot(kh, q, 1, 1), -1e30)
            raised = jnp.exp(scores - jnp.max(scores, 0, keepdims=True))
            share = (raised * (1.0 / jnp.sum(raised, 0, keepdims=True))).astype(B16)
            shares[f * HEADS + pair * 2 + h] = share
            part = dot(share, vh, 0, 0)
            total = part if total is None else total + part
        seen[here, pl.ds(at, 128)] = total.astype(B16)

    def attend_frame(f):
        def body(pair, carry):
            attend(f, pair)
            return carry
        lax.fori_loop(0, 6, body, 0, unroll=6)

    def merge_frames():
        def body(n, carry):
            cols = pl.ds(pl.multiple_of(n * 256, 256), 256)
            wcols = pl.ds(pl.multiple_of(AMERGE + n * 256, 128), 256)
            hidden[:, cols] = dot(seen[...], full[:, wcols])
            return carry
        lax.fori_loop(0, 3, body, 0)

    def hidden_frame(f, carry):
        here = pl.ds(pl.multiple_of(f * PAD, 16), PAD)
        value = hidden[here, :] + xs[here, :].astype(F32)
        hidden[here, :] = value
        xh, _ = normalize(value)
        n2[here, :] = (xh * expand_gain).astype(B16)
        return carry

    def row_mask(shape, axis):
        index = lax.broadcasted_iota(jnp.int32, shape, axis)
        good = index < 0
        for f in range(4):
            lost = jnp.where(p.dp * 4 + f < counts[0], 0, ROWS)
            good = jnp.logical_or(good, jnp.logical_and(index >= f * PAD + lost, index < f * PAD + 197 + lost * 0))
        return good

    mask_row = jnp.where(row_mask((16, ROWS), 1), 1.0, 0.0).astype(B16)

    def expand_tile(base, count=3):
        def body(n, carry):
            cols = pl.ds(pl.multiple_of(base + n * 256, 256), 256)
            wcols = pl.ds(pl.multiple_of(EXPAND + base + n * 256, 128), 256)
            grown = dot(n2[...], full[:, wcols])
            s = 0.5 + 0.5 * jnp.tanh(0.851 * grown)
            gated = grown * s
            dd[:, cols] = (s + 1.702 * gated * (1.0 - s)).astype(B16)
            gsum_o[:, cols] = dot(mask_row, gated.astype(B16))[0:8]
            return carry
        lax.fori_loop(0, count, body, 0)

    attend_frame(0)
    upto(8)
    attend_frame(1)
    upto(9)
    attend_frame(2)
    attend_frame(3)
    out(seen, seen_o)
    normt[...] = jnp.transpose(norm[...])
    out(normt, normt_o)
    seent[...] = jnp.transpose(seen[...])
    out(seent, seent_o)
    out(shares, shares_o)
    upto(10)
    merge_frames()
    lax.fori_loop(0, 4, hidden_frame, 0)
    out(hidden, hidden_o)
    mask_col = jnp.where(row_mask((ROWS, D), 0), 1.0, 0.0)
    n2t[...] = jnp.transpose((n2[...].astype(F32) * mask_col).astype(B16))
    out(n2t, n2t_o)
    expand_tile(0)
    upto(11)
    expand_tile(D)
    high = hidden[...].astype(B16)
    low = (hidden[...] - high.astype(F32)).astype(B16)
    hsum_o[...] = (dot(mask_row, high) + dot(mask_row, low))[0:8]
    upto(12)
    expand_tile(2 * D)
    out(dd.at[:, pl.ds(0, 3 * D)], d_o.at[:, pl.ds(0, 3 * D)])
    upto(13)
    expand_tile(3 * D, 2)
    upto(14)
    expand_tile(3 * D + 512, 1)
    out(dd.at[:, pl.ds(3 * D, D)], d_o.at[:, pl.ds(3 * D, D)])
    upto(15)
    for copy in sends:
        copy.wait_send()
    text_team.wait()
    text_team.done()
    text_hop.done()
    for copy in outs:
        copy.wait()


def pack_row(row):
    return jnp.concatenate([row[:, 128 * r : 128 * r + 128] for r in range(6)] + [jnp.zeros((2, 128), F32)], 0)


def unpack_row(value):
    return jnp.concatenate([value[r : r + 1] for r in range(6)], 1)


def twice(value):
    high = value.astype(B16)
    return jnp.concatenate([high, (value - high.astype(F32)).astype(B16)], 0)


RJOBS = ((0, 768), (768, 768), (1536, 768), (2304, 768), (3072, 768), (3840, 768), (4608, 768), (5376, 768))
BUNDLE = 3840
SIXTH = BUNDLE // 6


def rear_kernel(
    xs_h, normt_h, mixed_h, shares, seen_h, seent_h, hidden_h, n2t_h, d_h, full,
    gsum, hsum, shrink, texts, gains, mout, leaders, message, mnorm, mmix, mshare, told, counts, matches,
    patch_h, fin, loss_o, shrink_grad_o, courier_o, cheads_o, cmerge_o, proj_o, gains_grad_o, lead_o,
    stage, rc, rx, ry, rz, own, rf, bundle, wx, wmerge, wheads, mixed, seen, seent, hidden, n2t, dd, sbuf, hg, low, dout,
    projection, vecs, team, gs, gr, ps, pr, rs_, rr, us, ur, gg, first, mog, mog_team, chosen, gain_pack, gain_team, gain_send, gain_all,
    s_r, r_r, s_b, r_b, team_s, team_r, hop_s, hop_r, lsem, psem,
):
    p = Pos()
    pending = ((n2t_h, n2t), (d_h, dd), (full.at[:, pl.ds(PROJ, 512)], projection), (full.at[:, pl.ds(EXPAND, 3072)], wx),
               (hidden_h, hidden), (seent_h, seent), (full.at[:, pl.ds(AMERGE, D)], wmerge), (mixed_h, mixed), (seen_h, seen),
               (full.at[:, pl.ds(AHEADS, 3 * D)], wheads))
    loads = []

    def load(source, target):
        copy = pltpu.make_async_copy(source, target, lsem.at[len(loads)])
        copy.start()
        loads.append(copy)
        return copy

    for source, target in pending:
        load(source, target)
    barrier(p.plane() + list(p.team))
    vecs[:, 0:384] = jnp.concatenate([gsum[0:1, 384 * k : 384 * k + 384] for k in range(8)], 0)
    vecs[:, 384:512] = pack_row(hsum[0:1, :])
    hop = Team(p, vecs, team, team_s.at[0], team_r.at[0])
    reduce = Reduce(p, stage, (rc, rx, ry, rz, own, rf), fin, RJOBS, s_r, r_r)

    def expand_tiles(start):
        stage[:, :, start : start + D] = dot(n2t[...], dd[:, start : start + D]).astype(B16).reshape(8, 96, D)

    text = jnp.concatenate([jnp.concatenate([texts[i, :, r, :] for r in range(4)], 1) for i in range(4)], 0)
    text_unit = (text * lax.rsqrt(jnp.sum(text * text, -1, keepdims=True) + 1e-06)).astype(B16)
    hop.wait()
    total = team[0] + team[1] + team[2] + team[3]
    for k in range(8):
        gs[k] = jnp.broadcast_to(total[k : k + 1, 0:384], (8, 384))
    hop.done()
    hop = Spread(p, gs, gr, hop_s.at[0], hop_r.at[0])
    loads[0].wait()
    loads[1].wait()
    expand_tiles(0)
    reduce.next(0)
    expand_tiles(D)
    reduce.next(1)
    hop.wait()
    gated = jnp.concatenate([gr[v][0:1] for v in range(8)], 0)
    both = dot(twice(gated), shrink[...])
    part = both[0:8] + both[8:16]
    for v in range(8):
        ps[v] = pack_row(part[v : v + 1])
    hop.done()
    hop = Spread(p, ps, pr, hop_s.at[1], hop_r.at[1])
    expand_tiles(2 * D)
    reduce.next(2, 0)
    hop.wait()
    packed = total[:, 384:512]
    for k in range(8):
        packed = packed + pr[k]
    hop.done()
    loads[2].wait()
    denominator = (counts[0] * 197).astype(F32)
    pooled = jnp.broadcast_to(unpack_row(packed / denominator), (8, D))
    embed = dot(pooled.astype(B16), projection[...])
    rate = lax.rsqrt(jnp.sum(embed * embed, -1, keepdims=True) + 1e-06)
    unit = embed * rate
    logits = dot(unit.astype(B16), text_unit, 1, 1) * LOGIT_SCALE
    peak = jnp.max(logits, -1, keepdims=True)
    normalizer = peak + jnp.log(jnp.sum(jnp.exp(logits - peak), -1, keepdims=True))
    matched = lax.broadcasted_iota(jnp.int32, logits.shape, 1) == matches[0]
    loss_o[...] = jnp.broadcast_to(normalizer - jnp.sum(jnp.where(matched, logits, 0.0), -1, keepdims=True), (8, 128))
    slope = (jnp.exp(logits - normalizer) - jnp.where(matched, 1.0, 0.0)).astype(B16)
    unit_grad = dot(slope, text_unit) * LOGIT_SCALE
    embed_grad = (rate * (unit_grad - unit * jnp.sum(unit * unit_grad, -1, keepdims=True))).astype(B16)
    rg = dot(embed_grad, projection[...], 1, 1) / denominator
    rs_[...] = pack_row(rg.astype(B16).astype(F32)[0:1])
    hop = Spread(p, rs_, rr, hop_s.at[2], hop_r.at[2], same=True)

    places = ((0, 0, SIXTH), (1, 4 * D, 128), (1, D, 384), (1, 0, 128))

    def block(k, start, count, job):
        slot, offset, sixth = places[job]
        return bundle.at[slot, k, :, pl.ds(pl.multiple_of(offset + start * sixth, 128), count * sixth)]

    def fill(slot, col, parts):
        for part in parts:
            bundle[slot, p.k, :, col : col + part.shape[1]] = part
            col += part.shape[1]

    gather = Gather(p, block, 4, s_b, r_b)
    top = lax.broadcasted_iota(jnp.int32, (16, 1), 0) == 0
    pooled_rows = jnp.where(top, jnp.concatenate([pooled, pooled], 0), 0.0).astype(B16)
    embed_rows = jnp.where(top, jnp.concatenate([embed_grad.astype(F32)] * 2, 0), 0.0).astype(B16)
    fill(0, 0, (leaders[...], mnorm[...], told[...], pooled_rows, embed_rows, jnp.zeros((16, 256), B16)))
    gather.stage(0, 0)
    expand_tiles(3 * D)
    normt_load = load(normt_h, n2t)
    reduce.next(3, 1)
    hop.wait()
    rows = jnp.concatenate([unpack_row(rr[v]) for v in range(8)], 0).astype(B16)
    grad = dot(rows, shrink[...], 1, 1)
    for v in range(8):
        us[v] = jnp.broadcast_to(grad[v : v + 1], (8, 384))
    hop.done()
    hop = Spread(p, us, ur, hop_s.at[3], hop_r.at[3])
    shrink_grad_o[...] = dot(twice(gated), jnp.concatenate([rows.astype(F32)] * 2, 0).astype(B16), 0, 0)
    reduce.next(2)
    gather.stage(1, 0)
    hop.wait()
    for k in range(8):
        gg[:, 384 * k : 384 * k + 384] = ur[k]
    hop.done()

    def scale_tile(n, carry):
        cols = pl.ds(pl.multiple_of(n * 256, 256), 256)
        dd[:, cols] = (dd[:, cols].astype(F32) * gg[0:1, cols]).astype(B16)
        return carry

    lax.fori_loop(0, 12, scale_tile, 0)
    reduce.next(0, 3, scale=gg)
    loads[3].wait()

    def norm_tile(n):
        hg[:, 256 * n : 256 * n + 256] = dot(dd[...], wx[256 * n : 256 * n + 256, :], 1, 1)

    norm_tile(0)
    reduce.next(1, scale=gg)
    gather.stage(2, 0)
    norm_tile(1)
    reduce.next(2, 0, scale=gg)
    gather.stage(3, 0)
    norm_tile(2)
    weights = [load(full.at[:, pl.ds(CHEADS, 3 * D)], wx.at[:, pl.ds(0, 3 * D)]), load(full.at[:, pl.ds(COURIER, D)], wx.at[:, pl.ds(3 * D, D)])]
    reduce.next(3, scale=gg)
    loads[4].wait()
    attend_gain, expand_gain = gains[1:2, :], gains[2:3, :]

    def hidden_frame(f, total):
        here = pl.ds(pl.multiple_of(f * PAD, 16), PAD)
        limit = jnp.where(p.dp * 4 + f < counts[0], 197, 0)
        good = lax.broadcasted_iota(jnp.int32, (PAD, D), 0) < limit
        xh, rate = normalize(hidden[here, :])
        dy = jnp.where(good, hg[here, :], 0.0)
        e = dy * expand_gain
        grad = rate * (e - jnp.mean(e, -1, keepdims=True) - xh * jnp.mean(e * xh, -1, keepdims=True))
        grad = grad + jnp.where(good, rg[0:1, :], 0.0)
        hg[here, :] = grad
        low[here, :] = grad.astype(B16)
        return total + jnp.sum(dy * xh, 0, keepdims=True)

    expand_gain_grad = lax.fori_loop(0, 4, hidden_frame, jnp.zeros((1, D), F32))
    reduce.next(1, 0)
    gather.stage(4, 0)
    loads[5].wait()
    loads[6].wait()

    def merge_tile(n, carry):
        cols = pl.ds(pl.multiple_of(n * 256, 256), 256)
        stage[:, :, pl.ds(pl.multiple_of(3072 + n * 256, 128), 256)] = dot(seent[...], low[:, cols]).astype(B16).reshape(8, 96, 256)
        dout[:, cols] = dot(low[...], wmerge[cols, :], 1, 1).astype(B16)
        return carry

    lax.fori_loop(0, 3, merge_tile, 0, unroll=3)
    weights.append(load(full.at[:, pl.ds(CMERGE, D)], wmerge))
    reduce.next(4, 2)
    early = bundle[0].reshape(128, BUNDLE)
    pick = jnp.where(
        jnp.logical_and(lax.broadcasted_iota(jnp.int32, (D, 128), 0) == p.k * 96 + lax.broadcasted_iota(jnp.int32, (D, 128), 1),
                        lax.broadcasted_iota(jnp.int32, (D, 128), 1) < 96), 1.0, 0.0).astype(B16)
    for index in range(3):
        chosen[index] = dot(early[:, D * index : D * index + D], pick).astype(B16)
    proj_o[...] = dot(dot(early[:, 3 * D : 4 * D], pick).astype(B16), early[:, 4 * D : 4 * D + 512], 0, 0)[0:96]
    loads[7].wait()
    loads[8].wait()
    normt_load.wait()
    half_lanes = lax.broadcasted_iota(jnp.int32, (PAD, 128), 1) < HEAD

    def fetch(group):
        return pltpu.make_async_copy(shares.at[:, pl.ds(4 * group, 4)], sbuf.at[group % 2], psem.at[group % 2])

    fetch(0).start()

    def attend_group(group):
        if group < 2:
            fetch(group + 1).start()
        fetch(group).wait()
        inputs, outputs = [], []
        for f in range(4):
            for j in range(2):
                here = pl.ds(f * PAD, PAD)
                qs, ks, vs = (pl.ds(b + (2 * group + j) * 128, 128) for b in (0, D, 2 * D))
                inputs.append((here, qs, ks, vs, mixed[here, qs], mixed[here, ks], mixed[here, vs], dout[here, qs], seen[here, qs],
                               [sbuf[group % 2, f, 2 * j + h] for h in range(2)]))
        for here, qs, ks, vs, q, k, v, do, o, share_of in inputs:
            right = jnp.concatenate([do, (-(do.astype(F32) * o.astype(F32))).astype(B16)], 1)
            dq = dk = dv = None
            zero = jnp.zeros_like(q)
            for h in range(2):
                mask = half_lanes if h == 0 else jnp.logical_not(half_lanes)
                share = share_of[h]
                left = jnp.concatenate([jnp.where(mask, v, zero), jnp.where(mask, jnp.ones_like(v), zero)], 1)
                ds = (share.astype(F32) * dot(left, right, 1, 1)).astype(B16)
                pq = dot(ds, jnp.where(mask, k, zero), 0, 0)
                pk = dot(ds, jnp.where(mask, q, zero))
                pv = dot(share, jnp.where(mask, do, zero))
                dq, dk, dv = (pq, pk, pv) if h == 0 else (dq + pq, dk + pk, dv + pv)
            outputs.append((here, qs, ks, vs, (dq * HEAD ** (-0.5)).astype(B16), dk.astype(B16), dv.astype(B16)))
        for here, qs, ks, vs, dq, dk, dv in outputs:
            mixed[here, qs] = dq
            mixed[here, ks] = dk
            mixed[here, vs] = dv

    def heads_tiles(group):
        def body(n, carry):
            cols = pl.ds(pl.multiple_of(n * D + group * 256, 128), 256)
            to = pl.ds(pl.multiple_of(3840 + group * D + n * 256, 128), 256)
            stage[:, :, to] = dot(n2t[...], mixed[:, cols]).astype(B16).reshape(8, 96, 256)
            return carry
        lax.fori_loop(0, 3, body, 0, unroll=3)

    attend_group(0)
    reduce.next(4, 1, 3)
    heads_tiles(0)
    reduce.next(5, 2, 0)
    attend_group(1)
    reduce.next(4, 5, 1, 3)
    heads_tiles(1)
    reduce.next(6, 2, 0)
    attend_group(2)
    tokens = load(xs_h, dout)
    loads[9].wait()
    tails = [mixed[pl.ds(f * PAD + 192, 16), :].astype(F32)[5:6] for f in range(4)]
    tails = jnp.concatenate(tails + [jnp.zeros((12, 3 * D), F32)], 0).astype(B16)
    xh, rate = normalize(mout[...])
    e = dot(tails, wheads[...], 1, 1)[0:8] * attend_gain
    mog[...] = rate * (e - jnp.mean(e, -1, keepdims=True) - xh * jnp.mean(e * xh, -1, keepdims=True))
    hop = Team(p, mog, mog_team, team_s.at[1], team_r.at[1])
    reduce.next(6, 4, 5)
    heads_tiles(2)
    reduce.next(7, 1, 3)
    for copy in weights:
        copy.wait()
    hop.wait()
    out_grad = jnp.concatenate([mog_team[i][0:4] for i in range(4)], 0)
    out_low = out_grad.astype(B16)
    fill(1, 4 * D, (out_low,))
    gather.stage(0, 1)
    courier_gain = gains[0:1, :]
    mq, mk, mv = mmix[:, 0:D], mmix[:, D : 2 * D], mmix[:, 2 * D : 3 * D]
    told_grad = dot(out_low, wmerge[...], 1, 1).astype(B16)
    upstream = spread_heads(told_grad)
    share = mshare[...]
    share_grad = dot(upstream, mv, 1, 1)
    dv = dot(share.astype(B16), upstream, 0, 0)
    inner = jnp.sum(share * share_grad, -1, keepdims=True)
    ds = (share * (share_grad - inner)).astype(B16)
    dq = join_heads(dot(ds, mk)) * HEAD ** (-0.5)
    dk = dot(ds, spread_heads(mq), 0, 0) * HEAD ** (-0.5)
    mixed_grad = jnp.concatenate([dq, dk, dv], 1).astype(B16)
    fill(1, D, (mixed_grad,))
    gather.stage(0, 2)
    reduce.next(7, 6)
    gather.stage(1, 1)
    norm_grad = dot(mixed_grad, wx[:, 0 : 3 * D], 1, 1)
    xh, rate = normalize(message[...])
    e = norm_grad * courier_gain
    grad = rate * (e - jnp.mean(e, -1, keepdims=True) - xh * jnp.mean(e * xh, -1, keepdims=True))
    message_grad = (out_grad + grad).astype(B16)
    fill(1, 0, (message_grad,))
    gather.stage(0, 3)
    gain_own = jnp.sum(norm_grad * xh, 0, keepdims=True)
    reduce.next(4, 2, 5)

    def tokens_tile(n):
        hidden[:, 256 * n : 256 * n + 256] = dot(mixed[...], wheads[256 * n : 256 * n + 256, :], 1, 1)

    gather.stage(1, 2)
    tokens_tile(0)
    gather.stage(2, 1)
    reduce.next(7, 6, 3)
    gather.stage(1, 3)
    tokens_tile(1)
    gather.stage(2, 2)
    gather.stage(3, 1)
    reduce.next(4, 5)
    tokens_tile(2)
    gather.stage(2, 3)
    gather.stage(3, 2)
    reduce.next(7, 6)
    tokens.wait()
    spot = lax.broadcasted_iota(jnp.int32, (PAD, 1), 0) == 197
    place = lax.broadcasted_iota(jnp.int32, (8, D), 0)
    first[...] = jnp.zeros_like(first)

    def token_frame(f, total):
        here = pl.ds(pl.multiple_of(f * PAD, 16), PAD)
        xh, rate = normalize(jnp.where(spot, row_of(mout[...], f), dout[here, :].astype(F32)))
        dy = hidden[here, :]
        e = dy * attend_gain
        grad = rate * (e - jnp.mean(e, -1, keepdims=True) - xh * jnp.mean(e * xh, -1, keepdims=True))
        patch = hg[here, :] + grad
        low[here, :] = patch.astype(B16)
        first[...] = jnp.where(place == f, patch[0:1], first[...])
        return total + jnp.sum(dy * xh, 0, keepdims=True)

    attend_gain_grad = lax.fori_loop(0, 4, token_frame, jnp.zeros((1, D), F32))
    patch_out = load(low, patch_h)
    gain_pack[0:8, :] = pack_row(attend_gain_grad)
    gain_pack[8:16, :] = pack_row(expand_gain_grad)
    gain_hop = Team(p, gain_pack, gain_team, team_s.at[2], team_r.at[2])
    gather.stage(3, 3)
    gather.stage(4, 1)
    reduce.next(4, 5)
    leader_grad = dot(message_grad, wx[:, 3 * D : 4 * D], 1, 1)
    lead_o[...] = jnp.concatenate([row_of(leader_grad, p.dp * 4 + f) for f in range(4)] + [jnp.zeros((4, D), F32)], 0) + first[...]
    gain_hop.wait()
    gain_send[0:16, :] = gain_team[0] + gain_team[1] + gain_team[2] + gain_team[3]
    gain_send[16:24, :] = pack_row(gain_own)
    gain_spread = Spread(p, gain_send, gain_all, hop_s.at[4], hop_r.at[4], same=True)
    reduce.next(7, 6)
    gather.stage(4, 2)

    def late(start, count):
        return bundle[1, :, :, start : start + count].reshape(128, count)

    cmerge_o[...] = dot(chosen[2], late(4 * D, D), 0, 0)[0:96]
    cheads_o[...] = dot(chosen[1], late(D, 3 * D), 0, 0)[0:96]
    reduce.next(6, 5, 4)
    gather.stage(4, 3)
    courier_o[...] = dot(chosen[0], late(0, D), 0, 0)[0:96]
    reduce.next(7)
    gain_spread.wait()
    total_gain = gain_all[0]
    for k in range(1, 8):
        total_gain = total_gain + gain_all[k]
    total_gain = jnp.concatenate([unpack_row(total_gain[8 * i : 8 * i + 8]) for i in range(3)] + [jnp.zeros((5, D), F32)], 0)
    both = dot(pick, twice(total_gain), 0, 1)
    gains_grad_o[...] = both[0:96, 0:8] + both[0:96, 8:16]
    for _ in range(8):
        for job in range(len(RJOBS)):
            if reduce.at[job] < 7:
                reduce.next(job)
    for job in range(len(RJOBS)):
        reduce.next(job)
    for job in range(4):
        gather.stage(5, job)
    gain_hop.done()
    gain_spread.done()
    hop.done()
    patch_out.wait()


def finish_kernel(patch, lead, fin, cgain, courier, cheads, cmerge, proj, shrink, loss,
                  patch_o, gain_a, gain_b, gain_c, heads_o, merge_o, expand_o, courier_o, cheads_o, cmerge_o, proj_o, shrink_o, loss_o):
    for source, target in ((courier, courier_o), (cheads, cheads_o), (cmerge, cmerge_o), (proj, proj_o), (shrink, shrink_o)):
        target[...] = source[...].astype(F32)
    top = lax.broadcasted_iota(jnp.int32, (PAD, 1), 0) == 0
    for f in range(4):
        value = jnp.where(top, lead[f : f + 1, :], patch[f * PAD : f * PAD + PAD, :].astype(F32)).astype(B16)
        patch_o[0, :, f, :] = value[0:197]
    expand_o[...] = fin[:, 0:3072].astype(F32)
    merge_o[...] = fin[:, 3072:3840].astype(F32)
    for group in range(3):
        for n in range(3):
            heads_o[:, n * D + group * 256 : n * D + group * 256 + 256] = fin[
                :, 3840 + group * D + n * 256 : 3840 + group * D + n * 256 + 256].astype(F32)
    own = jnp.concatenate([cgain[...], jnp.zeros((96, 120), F32)], 1)
    own = jnp.transpose(jnp.concatenate([own, jnp.zeros((32, 128), F32)], 0))
    gain_a[...], gain_b[...], gain_c[...] = own[0:1, 0:96], own[1:2, 0:96], own[2:3, 0:96]
    loss_o[...] = loss[0:1, 0:1]


VMEM = 62 * 1024 * 1000


def any_spec():
    return pl.BlockSpec(memory_space=pl.ANY)


def vmem_spec():
    return pl.BlockSpec(memory_space=pltpu.VMEM)


def smem_spec():
    return pl.BlockSpec(memory_space=pltpu.SMEM)


def sds(shape, dtype):
    return jax.ShapeDtypeStruct(shape, dtype)


def dma(*shape):
    return pltpu.SemaphoreType.DMA(shape)


def vm(shape, dtype):
    return pltpu.VMEM(shape, dtype)


def fast(
    patches, counts, captions, matches, courier, courier_gain, courier_heads, courier_merge, attend_gain, attend_heads,
    attend_merge, expand_gain, expand_weight, shrink_weight, projection,
):
    anys, vmem, smem = any_spec(), vmem_spec(), smem_spec()
    (full, normt, mixed, shares, seen, seent, hidden, n2t, dd, gsum, hsum, gains,
     leaders, message, mnorm, mmix, mshare, told, mout, texts, xs) = pl.pallas_call(
        forward_kernel,
        out_shape=(
            sds((D, NCOLS), B16), sds((D, ROWS), B16), sds((ROWS, 3 * D), B16), sds((48, PAD, PAD), B16), sds((ROWS, D), B16),
            sds((D, ROWS), B16), sds((ROWS, D), F32), sds((D, ROWS), B16), sds((ROWS, 4 * D), B16), sds((8, 4 * D), F32),
            sds((8, D), F32), sds((8, D), F32), sds((16, D), B16), sds((16, D), F32), sds((16, D), B16), sds((16, 3 * D), B16),
            sds((192, 16), F32), sds((16, D), B16), sds((8, D), F32), sds((4, 8, 8, 128), F32),
            sds((ROWS, D), B16)),
        in_specs=[vmem] * 5 + [smem] + [anys] * 7,
        out_specs=tuple([anys] * 9 + [vmem] * 11 + [anys]),
        scratch_shapes=[
            vm((D, NCOLS), B16), vm((ROWS, D), B16), vm((8, D), F32), vm((8, 128), F32), vm((4, 8, D), F32), vm((ROWS, D), B16), vm((D, ROWS), B16), vm((ROWS, 3 * D), B16),
            vm((48, PAD, PAD), B16), vm((ROWS, D), B16), vm((D, ROWS), B16), vm((ROWS, D), F32), vm((ROWS, D), B16),
            vm((D, ROWS), B16), vm((ROWS, 4 * D), B16),
            vm((8, 8, 128), F32), dma(len(JOBS), 28), dma(len(JOBS), 28), dma(7), dma(2, 3), dma(2, 3), dma(7), dma(7), dma(32)],
        compiler_params=pltpu.CompilerParams(collective_id=0, has_side_effects=True, vmem_limit_bytes=60 << 20),
        name="forward",
    )(jnp.transpose(patches, (0, 2, 1, 3)), captions, courier_gain[None], attend_gain[None], expand_gain[None], counts, courier, courier_heads, attend_heads, courier_merge, attend_merge, expand_weight, projection)
    (patch, fin, loss, shrink_grad, courier_grad, cheads_grad, cmerge_grad, proj_grad, cgain, leads) = pl.pallas_call(
        rear_kernel,
        out_shape=(
            sds((ROWS, D), B16), sds((96, 6144), B16), sds((8, 128), F32), sds((384, D), F32), sds((96, D), F32),
            sds((96, 3 * D), F32), sds((96, D), F32), sds((96, 512), F32), sds((96, 8), F32), sds((8, D), F32)),
        in_specs=[anys] * 10 + [vmem] * 12 + [smem] * 2,
        out_specs=tuple([anys] + [vmem] * 9),
        scratch_shapes=[
            vm((8, 96, 6144), B16), vm((4, 8, 48, D), B16), vm((8, 16, 6144), B16), vm((4, 32, 6144), B16),
            vm((3, 32, 6144), B16), vm((32, 6144), B16), vm((32, 6144), B16), vm((2, 8, 16, BUNDLE), B16),
            vm((D, 4 * D), B16), vm((D, D), B16), vm((D, 3 * D), B16), vm((ROWS, 3 * D), B16),
            vm((ROWS, D), B16), vm((D, ROWS), B16), vm((ROWS, D), F32), vm((D, ROWS), B16), vm((ROWS, 4 * D), B16),
            vm((2, 4, 4, PAD, PAD), B16), vm((ROWS, D), F32), vm((ROWS, D), B16), vm((ROWS, D), B16),
            vm((D, 512), B16), vm((8, 512), F32), vm((4, 8, 512), F32), vm((8, 8, 384), F32), vm((8, 8, 384), F32),
            vm((8, 8, 128), F32), vm((8, 8, 128), F32), vm((8, 128), F32), vm((8, 8, 128), F32), vm((8, 8, 384), F32),
            vm((8, 8, 384), F32), vm((8, 4 * D), F32), vm((8, D), F32), vm((8, D), F32), vm((4, 8, D), F32),
            vm((3, 128, 128), B16), vm((16, 128), F32), vm((4, 16, 128), F32), vm((24, 128), F32), vm((8, 24, 128), F32),
            dma(len(RJOBS), 11), dma(len(RJOBS), 11), dma(4, 28), dma(4, 28), dma(3, 3), dma(3, 3), dma(5, 7), dma(5, 7),
            dma(16), dma(2)],
        compiler_params=pltpu.CompilerParams(collective_id=1, has_side_effects=True, vmem_limit_bytes=VMEM),
        name="rear",
    )(xs, normt, mixed, shares.reshape(4, HEADS, PAD, PAD), seen, seent, hidden, n2t, dd, full, gsum, hsum, shrink_weight, texts, gains, mout,
      leaders, message, mnorm, mmix, mshare, told, counts, matches)
    patch_grad, gain_a, gain_e, gain_m, heads, merge, expand, courier_out, cheads_out, cmerge_out, proj_out, shrink_out, loss_out = pl.pallas_call(
        finish_kernel,
        out_shape=(
            sds((1, 197, 4, D), B16), sds((1, 96), F32), sds((1, 96), F32), sds((1, 96), F32), sds((96, 3 * D), F32), sds((96, D), F32), sds((96, 4 * D), F32),
            sds((96, D), F32), sds((96, 3 * D), F32), sds((96, D), F32), sds((96, 512), F32), sds((384, D), F32), sds((1, 1), F32)),
        in_specs=[vmem] * 10,
        out_specs=tuple([vmem] * 13),
        compiler_params=pltpu.CompilerParams(vmem_limit_bytes=VMEM),
        name="finish",
    )(patch, leads, fin, cgain, courier_grad, cheads_grad, cmerge_grad, proj_grad, shrink_grad, loss)
    return (
        loss_out[0], jnp.transpose(patch_grad, (0, 2, 1, 3)), courier_out, gain_m[0], cheads_out, cmerge_out, gain_a[0], heads,
        merge, gain_e[0], expand, shrink_out, proj_out,
    )


def joined_2(value, axis, join):
    pieces = jax.tree.map(lambda part: lax.all_gather(part, axis), value)
    head = jax.tree.map(lambda part: part[0], pieces)
    tail = jax.tree.map(lambda part: part[1:], pieces)
    running, _ = lax.scan(lambda running, share: (join(running, share), None), head, tail)
    return running


def layer_norm(value, gain):
    center = value - jnp.mean(value, -1, keepdims=True)
    spread = jnp.mean(center * center, -1, keepdims=True)
    return center * lax.rsqrt(spread + EPSILON) * gain


def norm_back(value, gain, upstream):
    _, pull = jax.vjp(layer_norm, value, gain)
    return pull(upstream)


def quick_gelu(value):
    return value * jax.nn.sigmoid(1.702 * value)


def unit_rows(value):
    return value * lax.rsqrt(jnp.sum(value * value, -1, keepdims=True) + 1e-06)


def split_heads(mixed, query_count):
    batch, length, triple = mixed.shape
    width = triple // 3
    rounded = mixed.astype(jnp.bfloat16)
    queries = rounded[:, :query_count, :width].reshape(batch, query_count, HEADS, HEAD)
    keys = rounded[:, :, width : 2 * width].reshape(batch, length, HEADS, HEAD)
    values = rounded[:, :, 2 * width :].reshape(batch, length, HEADS, HEAD)
    return (queries, keys, values)


def scores_of(queries, keys, key_mask):
    scores = jnp.einsum(
        "bqhd,bkhd->bhqk", queries, keys, preferred_element_type=jnp.float32
    ) * HEAD ** (-0.5)
    if key_mask is not None:
        scores = jnp.where(key_mask[:, None, None, :], scores, -1000000000.0)
    return scores


def attend_forward(queries, keys, values, key_mask):
    scores = scores_of(queries, keys, key_mask)
    peak = jnp.max(scores, -1, keepdims=True)
    raised = jnp.exp(scores - peak)
    total = jnp.sum(raised, -1, keepdims=True)
    shares = (raised / total).astype(jnp.bfloat16)
    joined = jnp.einsum("bhqk,bkhd->bqhd", shares, values, preferred_element_type=jnp.float32)
    batch, count = (joined.shape[0], joined.shape[1])
    return (
        joined.reshape(batch, count, HEADS * HEAD).astype(jnp.bfloat16),
        peak + jnp.log(total),
        shares,
    )


def attend_backward(queries, keys, values, key_mask, normalizer, shares, upstream):
    batch, count, width = upstream.shape
    upstream_low = upstream.astype(jnp.bfloat16).reshape(batch, count, HEADS, HEAD)
    chances = jnp.exp(scores_of(queries, keys, key_mask) - normalizer)
    share_grad = jnp.einsum(
        "bqhd,bkhd->bhqk", upstream_low, values, preferred_element_type=jnp.float32
    )
    value_grad = jnp.einsum(
        "bhqk,bqhd->bkhd", shares, upstream_low, preferred_element_type=jnp.float32
    )
    inner = jnp.sum(chances * share_grad, -1, keepdims=True)
    score_grad = (chances * (share_grad - inner)).astype(jnp.bfloat16)
    query_grad = jnp.einsum(
        "bhqk,bkhd->bqhd", score_grad, keys, preferred_element_type=jnp.float32
    ) * HEAD ** (-0.5)
    key_grad = jnp.einsum(
        "bhqk,bqhd->bkhd", score_grad, queries, preferred_element_type=jnp.float32
    ) * HEAD ** (-0.5)
    length = keys.shape[1]
    return (
        query_grad.reshape(batch, count, width),
        key_grad.reshape(batch, length, width),
        value_grad.reshape(batch, length, width),
    )


def frame_forward(block, message_rows, weights):
    attend_gain, attend_heads, attend_merge, expand_gain, expand_weight, shrink_weight = weights
    frames = block.astype(jnp.float32)
    tokens = jnp.concatenate([frames, message_rows[:, None, :]], 1)
    normed = layer_norm(tokens, attend_gain).astype(jnp.bfloat16)
    mixed = jnp.einsum("btd,de->bte", normed, attend_heads, preferred_element_type=jnp.float32)
    queries, keys, values = split_heads(mixed, block.shape[1])
    seen, normalizer, shares = attend_forward(queries, keys, values, None)
    hidden = frames + jnp.einsum(
        "bpd,de->bpe", seen, attend_merge, preferred_element_type=jnp.float32
    )
    normed_two = layer_norm(hidden, expand_gain).astype(jnp.bfloat16)
    grown = jnp.einsum("bpd,dm->bpm", normed_two, expand_weight, preferred_element_type=jnp.float32)
    gated = quick_gelu(grown).astype(jnp.bfloat16)
    result = hidden + jnp.einsum(
        "bpm,md->bpd", gated, shrink_weight, preferred_element_type=jnp.float32
    )
    kept = (
        tokens,
        normed,
        queries,
        keys,
        values,
        shares,
        normalizer,
        seen,
        hidden,
        normed_two,
        grown,
        gated,
    )
    return (jnp.sum(result, 1), kept)


def frame_backward(kept, upstream, weights):
    attend_gain, attend_heads, attend_merge, expand_gain, expand_weight, shrink_weight = weights
    (
        tokens,
        normed,
        queries,
        keys,
        values,
        shares,
        normalizer,
        seen,
        hidden,
        normed_two,
        grown,
        gated,
    ) = kept
    patch_count = hidden.shape[1]
    upstream_low = upstream.astype(jnp.bfloat16)
    shrink_grad = jnp.einsum("bpm,bd->md", gated, upstream_low, preferred_element_type=jnp.float32)
    gated_grad = jnp.einsum(
        "bd,md->bm", upstream_low, shrink_weight, preferred_element_type=jnp.float32
    )
    _, gelu_pull = jax.vjp(quick_gelu, grown)
    grown_grad = gelu_pull(jnp.broadcast_to(gated_grad[:, None, :], grown.shape))[0].astype(
        jnp.bfloat16
    )
    expand_grad = jnp.einsum(
        "bpd,bpm->dm", normed_two, grown_grad, preferred_element_type=jnp.float32
    )
    normed_two_grad = jnp.einsum(
        "bpm,dm->bpd", grown_grad, expand_weight, preferred_element_type=jnp.float32
    )
    hidden_grad, expand_gain_grad = norm_back(hidden, expand_gain, normed_two_grad)
    hidden_grad = hidden_grad + upstream[:, None, :]
    hidden_low = hidden_grad.astype(jnp.bfloat16)
    merge_grad = jnp.einsum("bpd,bpe->de", seen, hidden_low, preferred_element_type=jnp.float32)
    seen_grad = jnp.einsum(
        "bpe,de->bpd", hidden_low, attend_merge, preferred_element_type=jnp.float32
    )
    query_grad, key_grad, value_grad = attend_backward(
        queries, keys, values, None, normalizer, shares, seen_grad
    )
    length = tokens.shape[1]
    query_grad = jnp.pad(query_grad, ((0, 0), (0, length - patch_count), (0, 0)))
    mixed_grad = jnp.concatenate([query_grad, key_grad, value_grad], 2).astype(jnp.bfloat16)
    heads_grad = jnp.einsum("btd,bte->de", normed, mixed_grad, preferred_element_type=jnp.float32)
    normed_grad = jnp.einsum(
        "bte,de->btd", mixed_grad, attend_heads, preferred_element_type=jnp.float32
    )
    token_grad, attend_gain_grad = norm_back(tokens, attend_gain, normed_grad)
    patch_grad = hidden_grad + token_grad[:, :patch_count]
    block_grads = (
        attend_gain_grad,
        heads_grad,
        merge_grad,
        expand_gain_grad,
        expand_grad,
        shrink_grad,
    )
    return (patch_grad, token_grad[:, patch_count], block_grads)


def shards(
    patches,
    counts,
    captions,
    matches,
    courier,
    courier_gain,
    courier_heads,
    courier_merge,
    attend_gain,
    attend_heads,
    attend_merge,
    expand_gain,
    expand_weight,
    shrink_weight,
    projection,
):
    videos, local_frames, patch_count, width = patches.shape
    frame_total = local_frames * lax.axis_size("dp")
    offset = lax.axis_index("dp") * local_frames
    rows = videos * local_frames
    per_block = rows // MICRO
    courier_full, courier_gain_full, heads_full, merge_full, projection_full = (
        lax.all_gather(courier, "fsdp", axis=0, tiled=True),
        lax.all_gather(courier_gain, "fsdp", axis=0, tiled=True),
        lax.all_gather(courier_heads, "fsdp", axis=0, tiled=True),
        lax.all_gather(courier_merge, "fsdp", axis=0, tiled=True),
        lax.all_gather(projection, "fsdp", axis=0, tiled=True),
    )

    def fetch():
        return (
            lax.all_gather(attend_gain, "fsdp", axis=0, tiled=True),
            lax.all_gather(attend_heads, "fsdp", axis=0, tiled=True),
            lax.all_gather(attend_merge, "fsdp", axis=0, tiled=True),
            lax.all_gather(expand_gain, "fsdp", axis=0, tiled=True),
            lax.all_gather(expand_weight, "fsdp", axis=0, tiled=True),
            lax.all_gather(shrink_weight, "fsdp", axis=0, tiled=True),
        )

    leaders = lax.all_gather(patches[:, :, 0, :], "dp", axis=1, tiled=True)
    present = lax.broadcasted_iota(jnp.int32, (videos, frame_total), 1) < counts[:, None]
    message = jnp.einsum("vfd,de->vfe", leaders, courier_full, preferred_element_type=jnp.float32)
    message_norm = layer_norm(message, courier_gain_full).astype(jnp.bfloat16)
    message_mixed = jnp.einsum(
        "vfd,de->vfe", message_norm, heads_full, preferred_element_type=jnp.float32
    )
    told_queries, told_keys, told_values = split_heads(message_mixed, frame_total)
    told, told_normalizer, told_shares = attend_forward(
        told_queries, told_keys, told_values, present
    )
    message_out = message + jnp.einsum(
        "vfd,de->vfe", told, merge_full, preferred_element_type=jnp.float32
    )
    mine = lax.dynamic_slice_in_dim(message_out, offset, local_frames, 1).reshape(rows, width)
    flat = patches.reshape(rows, patch_count, width)
    frame_weights = fetch()
    kept_blocks = []
    sums = []
    for index in range(MICRO):
        if index > 0:
            frame_weights = fetch()
        start = index * per_block
        frame_sums, kept = frame_forward(
            flat[start : start + per_block], mine[start : start + per_block], frame_weights
        )
        kept_blocks.append(kept)
        sums.append(frame_sums)
    frame_sums = jnp.concatenate(sums, 0).reshape(videos, local_frames, width)
    own_present = lax.dynamic_slice_in_dim(present, offset, local_frames, 1)
    partial_value = jnp.sum(jnp.where(own_present[:, :, None], frame_sums, 0.0), 1)
    pooled_sum = lax.psum(partial_value, "dp")
    denominator = (counts * patch_count).astype(jnp.float32)[:, None]
    pooled = pooled_sum / denominator
    pooled_low = pooled.astype(jnp.bfloat16)
    embed = jnp.dot(pooled_low, projection_full, preferred_element_type=jnp.float32)
    video_unit = unit_rows(embed).astype(jnp.bfloat16)
    segment = lax.axis_index("dp") * (captions.shape[0] * lax.axis_size("fsdp"))

    def scores_for(piece):
        text_unit = unit_rows(piece.astype(jnp.float32)).astype(jnp.bfloat16)
        logits = (
            jnp.einsum("ve,te->vt", video_unit, text_unit, preferred_element_type=jnp.float32)
            * LOGIT_SCALE
        )
        positions = segment + lax.broadcasted_iota(jnp.int32, logits.shape, 1)
        return (text_unit, logits, positions == matches[:, None])

    peak = jnp.full((videos,), -1e30, jnp.float32)
    _, logits, matched = scores_for(lax.all_gather(captions, "fsdp", axis=0, tiled=True))
    fresh = jnp.maximum(peak, jnp.max(logits, 1))
    total = jnp.sum(jnp.exp(logits - fresh[:, None]), 1)
    picked = jnp.sum(jnp.where(matched, logits, 0.0), 1)
    peak, total, picked = (fresh, total, picked)

    def combine(first, second):
        top = jnp.maximum(first[0], second[0])
        joined = first[1] * jnp.exp(first[0] - top) + second[1] * jnp.exp(second[0] - top)
        return (top, joined, first[2] + second[2])

    peak, total, picked = joined_2((peak, total, picked), "dp", combine)
    normalizer = peak + jnp.log(total)
    loss = normalizer - picked
    text_unit, logits, matched = scores_for(lax.all_gather(captions, "fsdp", axis=0, tiled=True))
    slope = (jnp.exp(logits - normalizer[:, None]) - matched.astype(jnp.float32)).astype(
        jnp.bfloat16
    )
    unit_grad = jnp.dot(slope, text_unit, preferred_element_type=jnp.float32) * LOGIT_SCALE
    unit_grad = lax.psum(unit_grad, "dp")
    _, unit_pull = jax.vjp(unit_rows, embed)
    embed_grad = unit_pull(unit_grad)[0].astype(jnp.bfloat16)
    projection_grad = jnp.einsum(
        "vd,ve->de", pooled_low, embed_grad, preferred_element_type=jnp.float32
    )
    pooled_grad = jnp.einsum(
        "ve,de->vd", embed_grad, projection_full, preferred_element_type=jnp.float32
    )
    upstream_all = jnp.where(own_present[:, :, None], (pooled_grad / denominator)[:, None, :], 0.0)
    upstream_all = upstream_all.reshape(rows, width)
    collected = None
    patch_list = []
    message_list = []
    for index in range(MICRO):
        frame_weights = fetch()
        start = index * per_block
        patch_grad, message_token_grad, block_grads = frame_backward(
            kept_blocks[index], upstream_all[start : start + per_block], frame_weights
        )
        patch_list.append(patch_grad)
        message_list.append(message_token_grad)
        block_grads = (
            lax.psum_scatter(
                block_grads[0].astype(jnp.float32), "fsdp", scatter_dimension=0, tiled=True
            ),
            lax.psum_scatter(block_grads[1], "fsdp", scatter_dimension=0, tiled=True),
            lax.psum_scatter(block_grads[2], "fsdp", scatter_dimension=0, tiled=True),
            lax.psum_scatter(
                block_grads[3].astype(jnp.float32), "fsdp", scatter_dimension=0, tiled=True
            ),
            lax.psum_scatter(block_grads[4], "fsdp", scatter_dimension=0, tiled=True),
            lax.psum_scatter(block_grads[5], "fsdp", scatter_dimension=0, tiled=True),
        )
        collected = (
            block_grads if collected is None else jax.tree.map(jnp.add, collected, block_grads)
        )
    collected = (
        lax.psum(collected[0].astype(jnp.bfloat16), "dp").astype(jnp.float32),
        lax.psum(collected[1].astype(jnp.bfloat16), "dp").astype(jnp.float32),
        lax.psum(collected[2].astype(jnp.bfloat16), "dp").astype(jnp.float32),
        lax.psum(collected[3].astype(jnp.bfloat16), "dp").astype(jnp.float32),
        lax.psum(collected[4].astype(jnp.bfloat16), "dp").astype(jnp.float32),
        lax.psum(collected[5].astype(jnp.bfloat16), "dp").astype(jnp.float32),
    )
    message_token_grad = jnp.concatenate(message_list, 0).reshape(videos, local_frames, width)
    out_grad = lax.all_gather(message_token_grad, "dp", axis=1, tiled=True)
    out_low = out_grad.astype(jnp.bfloat16)
    merge_message_grad = jnp.einsum(
        "vfd,vfe->de", told, out_low, preferred_element_type=jnp.float32
    )
    told_grad = jnp.einsum("vfe,de->vfd", out_low, merge_full, preferred_element_type=jnp.float32)
    told_query_grad, told_key_grad, told_value_grad = attend_backward(
        told_queries, told_keys, told_values, present, told_normalizer, told_shares, told_grad
    )
    courier_mixed_grad = jnp.concatenate(
        [told_query_grad, told_key_grad, told_value_grad], 2
    ).astype(jnp.bfloat16)
    heads_message_grad = jnp.einsum(
        "vfd,vfe->de", message_norm, courier_mixed_grad, preferred_element_type=jnp.float32
    )
    message_norm_grad = jnp.einsum(
        "vfe,de->vfd", courier_mixed_grad, heads_full, preferred_element_type=jnp.float32
    )
    message_grad, courier_gain_grad = norm_back(message, courier_gain_full, message_norm_grad)
    message_grad = (message_grad + out_grad).astype(jnp.bfloat16)
    courier_grad = jnp.einsum(
        "vfd,vfe->de", leaders, message_grad, preferred_element_type=jnp.float32
    )
    leader_grad = jnp.einsum(
        "vfe,de->vfd", message_grad, courier_full, preferred_element_type=jnp.float32
    )
    own_leader = lax.dynamic_slice_in_dim(leader_grad, offset, local_frames, 1).reshape(rows, width)
    patch_all = jnp.concatenate(patch_list, 0)
    patch_all = patch_all.at[:, 0, :].add(own_leader)
    patch_out = patch_all.reshape(videos, local_frames, patch_count, width).astype(jnp.bfloat16)
    video_grads = (
        lax.psum_scatter(courier_grad, "fsdp", scatter_dimension=0, tiled=True),
        lax.psum_scatter(
            courier_gain_grad.astype(jnp.float32), "fsdp", scatter_dimension=0, tiled=True
        ),
        lax.psum_scatter(heads_message_grad, "fsdp", scatter_dimension=0, tiled=True),
        lax.psum_scatter(merge_message_grad, "fsdp", scatter_dimension=0, tiled=True),
        lax.psum_scatter(projection_grad, "fsdp", scatter_dimension=0, tiled=True),
    )
    return (
        loss,
        patch_out,
        video_grads[0],
        video_grads[1],
        video_grads[2],
        video_grads[3],
        collected[0],
        collected[1],
        collected[2],
        collected[3],
        collected[4],
        collected[5],
        video_grads[4],
    )


def solution(mesh):
    fitting = mesh.shape['dp'] == 4 and mesh.shape['fsdp'] == Z * Y
    return jax.shard_map(
        fast if fitting else shards,
        mesh=mesh,
        in_specs=(
            P("fsdp", "dp", None, None),
            P("fsdp"),
            P(("dp", "fsdp"), None),
            P("fsdp"),
            P("fsdp", None),
            P("fsdp"),
            P("fsdp", None),
            P("fsdp", None),
            P("fsdp"),
            P("fsdp", None),
            P("fsdp", None),
            P("fsdp"),
            P("fsdp", None),
            P("fsdp", None),
            P("fsdp", None),
        ),
        out_specs=(
            P("fsdp"),
            P("fsdp", "dp", None, None),
            P("fsdp", None),
            P("fsdp"),
            P("fsdp", None),
            P("fsdp", None),
            P("fsdp"),
            P("fsdp", None),
            P("fsdp", None),
            P("fsdp"),
            P("fsdp", None),
            P("fsdp", None),
            P("fsdp", None),
        ),
        check_vma=False,
    )
```

```python
import functools

import jax
import jax.numpy as jnp
from jax import lax
from jax.experimental import pallas as pl
from jax.experimental.pallas import tpu as pltpu
from jax.sharding import PartitionSpec as P

MESH = pl.DeviceIdType.MESH
Z, Y = 4, 2
HEADS = 12
HEAD = 64
EPSILON = 1e-05
LOGIT_SCALE = 64.0
PAD = 208
ROWS = 832
D = 768
F32 = jnp.float32
B16 = jnp.bfloat16

MICRO = 2

COURIER, GAINS, CHEADS, AHEADS, CMERGE, AMERGE, EXPAND, PROJ = 0, 768, 896, 3200, 5504, 6272, 7040, 10112
NCOLS = 10624
JOBS = ((0, 896), (896, 768), (1664, 768), (2432, 768), (3200, 768), (3968, 768), (4736, 768), (5504, 768), (6272, 768),
        (7040, 768), (7808, 768), (8576, 768), (10112, 512), (9344, 512), (9856, 256))


class Pos:
    def __init__(self):
        self.dp = lax.axis_index("dp")
        self.k = lax.axis_index("fsdp")
        self.x, self.c = self.dp // 2, lax.rem(self.dp, 2)
        self.z, self.y = self.k // Y, lax.rem(self.k, Y)
        self.core = (self.x * 2 + 1 - self.c, self.k)
        self.xp = ((1 - self.x) * 2 + self.c, self.k)
        self.cross = ((1 - self.x) * 2 + 1 - self.c, self.k)
        self.yp = (self.dp, self.z * Y + 1 - self.y)
        self.team = (self.core, self.xp, self.cross)

    def ahead(self, d):
        return lax.rem(self.z + d, Z)

    def behind(self, d):
        return lax.rem(self.z - d + Z, Z)

    def column(self):
        return [(self.dp, self.ahead(d) * Y + self.y) for d in (1, 2, 3)]

    def peers(self):
        return [self.core, self.xp, self.yp] + self.column()

    def plane(self):
        return [(self.dp, lax.rem(self.k + d, Z * Y)) for d in range(1, Z * Y)]


def barrier(peers):
    semaphore = pltpu.get_barrier_semaphore()
    for peer in peers:
        pl.semaphore_signal(semaphore, inc=1, device_id=peer, device_id_type=MESH)
    pl.semaphore_wait(semaphore, len(peers))


def remote(source, target, send, receive, device):
    return pltpu.make_async_remote_copy(
        src_ref=source, dst_ref=target, send_sem=send, recv_sem=receive, device_id=device, device_id_type=MESH)


class Gather:
    def __init__(self, p, block, jobs, send, receive):
        self.p, self.block, self.jobs, self.send, self.receive = p, block, jobs, send, receive

    def copy(self, job, index, k, first, count, device):
        ref = self.block(k, first, count, job)
        return remote(ref, ref, self.send.at[job, index], self.receive.at[job, index], device)

    def far(self, d):
        p = self.p
        return p.behind(d + 1) * Y + p.y if d < 3 else p.behind(d - 3) * Y + 1 - p.y

    def stage(self, stage, job):
        if job < 0 or job >= self.jobs:
            return
        p, copy = self.p, self.copy
        own, single = 3 * p.c + p.x, 3 * p.c + 2 * p.x
        other = 3 * p.c + 2 * (1 - p.x)
        if stage == 0:
            for d, device in enumerate(p.column()):
                copy(job, d, p.k, own, 2, device).start()
            copy(job, 3, p.k, own, 2, p.yp).start()
        elif stage == 1:
            for d in range(3):
                k = self.far(d)
                copy(job, d, k, own, 2, p.core).wait_recv()
                copy(job, 4 + d, k, own, 2, p.yp).start()
                copy(job, 7 + d, k, single, 1, p.xp).start()
                copy(job, 14 + d, k, own, 2, p.core).start()
        elif stage == 2:
            for d in range(3, 7):
                k = self.far(d)
                copy(job, d, k, own, 2, p.core).wait_recv()
                copy(job, 7 + d, k, single, 1, p.xp).start()
                copy(job, 14 + d, k, own, 2, p.core).start()
        elif stage == 3:
            for d in range(7):
                k = self.far(d)
                copy(job, 7 + d, k, other, 1, p.core).wait_recv()
                copy(job, 21 + d, k, other, 1, p.core).start()
        elif stage == 4:
            for d in range(7):
                copy(job, 14 + d, self.far(d), 3 * (1 - p.c) + p.x, 2, p.core).wait_recv()
            for d in range(7):
                copy(job, 21 + d, self.far(d), 3 * (1 - p.c) + 2 * (1 - p.x), 1, p.core).wait_recv()
        elif stage == 5:
            for index in range(28):
                copy(job, index, p.k, 0, 2 if index < 7 or 14 <= index < 21 else 1, p.core).wait_send()

    def tick(self, t, lag):
        for stage in (0, 1, 2, 3, 4, 5):
            self.stage(stage, t - lag[stage])


class Spread:
    def __init__(self, p, source, target, send, receive, same=False):
        self.p, self.target = p, target
        count = Z * Y
        self.copies = []
        for d in range(1, count):
            to = lax.rem(p.k + d, count)
            part = source if same else source.at[to]
            self.copies.append(remote(part, target.at[p.k], send.at[d - 1], receive.at[d - 1], (p.dp, to)))
        self.arrivals = []
        for d in range(1, count):
            origin = lax.rem(p.k - d + count, count)
            self.arrivals.append(
                remote(target.at[origin], target.at[origin], send.at[d - 1], receive.at[d - 1], (p.dp, origin)))
        target[p.k] = source[...] if same else source[p.k]
        for copy in self.copies:
            copy.start()

    def wait(self):
        for copy in self.arrivals:
            copy.wait_recv()

    def done(self):
        for copy in self.copies:
            copy.wait_send()


class Team:
    def __init__(self, p, source, target, send, receive):
        self.copies, self.arrivals = [], []
        target[p.dp] = source[...]
        for index, other in enumerate(p.team):
            self.copies.append(remote(source, target.at[p.dp], send.at[index], receive.at[index], other))
            self.arrivals.append(remote(source, target.at[other[0]], send.at[index], receive.at[index], other))
        for copy in self.copies:
            copy.start()

    def wait(self):
        for copy in self.arrivals:
            copy.wait_recv()

    def done(self):
        for copy in self.copies:
            copy.wait_send()


class Reduce:
    def __init__(self, p, stage, buffers, fin, jobs, send, receive):
        self.p, self.stage, self.fin, self.jobs, self.send, self.receive = p, stage, fin, jobs, send, receive
        self.rc, self.rx, self.ry, self.rz, self.own, self.rf = buffers
        self.at = [0] * len(jobs)

    def copies(self, job, step):
        p = self.p
        first, count = self.jobs[job]
        cols = pl.ds(first, count)
        half, other = pl.ds(pl.multiple_of(48 * p.c, 16), 48), pl.ds(pl.multiple_of(48 * (1 - p.c), 16), 48)
        carried = pl.ds(pl.multiple_of((3 * p.c + p.x) * 16, 16), 32)
        away = pl.ds(pl.multiple_of((3 * p.c + 2 * (1 - p.x)) * 16, 16), 16)
        s, r = self.send, self.receive
        if step == 0:
            target = self.rc.at[job % 4, :, :, pl.ds(0, count)]
            return [remote(self.stage.at[:, other, cols], target, s.at[job, 0], r.at[job, 0], p.core)]
        if step == 1:
            return [remote(self.stage.at[:, away, cols], self.rx.at[:, :, cols], s.at[job, 1], r.at[job, 1], p.xp)]
        if step == 2:
            return [remote(self.stage.at[z * Y + 1 - p.y, carried, cols], self.ry.at[z, :, cols], s.at[job, 2 + z],
                           r.at[job, 2 + z], p.yp) for z in range(Z)]
        if step == 3:
            return [remote(self.stage.at[device[1], carried, cols], self.rz.at[d, :, cols], s.at[job, 6 + d],
                           r.at[job, 6 + d], device) for d, device in enumerate(p.column())]
        if step == 4:
            return [remote(self.own.at[:, cols], self.rf.at[:, cols], s.at[job, 9], r.at[job, 9], p.xp)]
        return [remote(self.fin.at[half, cols], self.fin.at[half, cols], s.at[job, 10], r.at[job, 10], p.core)]

    def next(self, *jobs, scale=None):
        for job in jobs:
            self.step(self.at[job], job, scale)
            self.at[job] += 1

    def step(self, step, job, scale):
        p = self.p
        first, count = self.jobs[job]
        cols = pl.ds(first, count)
        half, other = pl.ds(pl.multiple_of(48 * p.c, 16), 48), pl.ds(pl.multiple_of(48 * (1 - p.c), 16), 48)
        carried = pl.ds(pl.multiple_of((3 * p.c + p.x) * 16, 16), 32)
        if step == 6:
            remote(self.fin.at[other, cols], self.fin.at[other, cols], self.send.at[job, 10], self.receive.at[job, 10],
                   p.core).wait_recv()
        elif step > 0 and step < 6:
            for copy in self.copies(job, step - 1):
                copy.wait_recv()
        if step == 1:
            def add(k, carry):
                self.stage[k, half, cols] = self.stage[k, half, cols] + self.rc[job % 4, k, :, pl.ds(0, count)]
                return carry
            lax.fori_loop(0, Z * Y, add, 0, unroll=4)
        elif step == 2:
            def add(k, carry):
                value = self.stage[k, carried, cols].astype(F32)
                other_x = self.rx[k, :, cols].astype(F32)
                top = value[0:16] + jnp.where(p.x == 0, other_x, 0.0)
                low = value[16:32] + jnp.where(p.x == 0, 0.0, other_x)
                value = jnp.concatenate([top, low], 0)
                if scale is not None:
                    value = value * scale[0:1, cols]
                self.stage[k, carried, cols] = value.astype(B16)
                return carry
            lax.fori_loop(0, Z * Y, add, 0, unroll=4)
        elif step == 3:
            def add(z, carry):
                k = z * Y + p.y
                self.stage[k, carried, cols] = self.stage[k, carried, cols] + self.ry[z, :, cols]
                return carry
            lax.fori_loop(0, Z, add, 0, unroll=4)
        elif step == 4:
            total = self.stage[p.k, carried, cols].astype(F32)
            for d in range(3):
                total = total + self.rz[d, :, cols].astype(F32)
            self.own[:, cols] = total.astype(B16)
        elif step == 5:
            mine, theirs = self.own[:, cols].astype(F32), self.rf[:, cols].astype(F32)
            left = jnp.where(p.x == 0, mine[0:16], theirs[0:16])
            right = jnp.where(p.x == 0, theirs[16:32], mine[16:32])
            middle = jnp.where(p.x == 0, mine[16:32], mine[0:16]) + jnp.where(p.x == 0, theirs[0:16], theirs[16:32])
            self.fin[half, cols] = jnp.concatenate([left, middle, right], 0).astype(B16)
        if step < 6:
            for copy in self.copies(job, step):
                copy.start()
        if step == 7:
            for earlier in range(6):
                for copy in self.copies(job, earlier):
                    copy.wait_send()


def dot(a, b, ca=1, cb=0):
    return lax.dot_general(a, b, (((ca,), (cb,)), ((), ())), preferred_element_type=F32)


def normalize(value):
    center = value - jnp.mean(value, -1, keepdims=True)
    rate = lax.rsqrt(jnp.mean(center * center, -1, keepdims=True) + EPSILON)
    return center * rate, rate


def head_mask():
    return lax.broadcasted_iota(jnp.int32, (192, D), 0) // 16 == lax.broadcasted_iota(jnp.int32, (192, D), 1) // HEAD


def spread_heads(value):
    return jnp.where(head_mask(), jnp.concatenate([value.astype(F32)] * HEADS, 0), 0.0).astype(B16)


def join_heads(value):
    value = jnp.where(head_mask(), value, 0.0)
    total = value[0:16]
    for head in range(1, HEADS):
        total = total + value[16 * head : 16 * head + 16]
    return total


def row_of(value, index):
    rows = lax.broadcasted_iota(jnp.int32, value.shape, 0)
    return jnp.sum(jnp.where(rows == index, value, 0.0), 0, keepdims=True)


def forward_kernel(
    patches, captions, gain_a, gain_b, gain_c, counts, courier, cheads, aheads, cmerge, amerge, expand, projection,
    full_o, normt_o, mixed_o, shares_o, seen_o, seent_o, hidden_o, n2t_o, d_o, gsum_o, hsum_o, gains_o,
    leaders_o, message_o, mnorm_o, mmix_o, mshare_o, told_o, mout_o, texts_o, xs_o,
    full, xs, lead, caption, leadbuf, norm, normt, mixed, shares, seen, seent, hidden, n2, n2t, dd,
    texts, ssem, rsem, lsem, lead_s, lead_r, text_s, text_r, osem,
):
    p = Pos()
    weights = ((courier, COURIER), (cheads, CHEADS), (aheads, AHEADS), (cmerge, CMERGE), (amerge, AMERGE),
               (expand, EXPAND), (projection, PROJ))
    mine = pl.ds(pl.multiple_of(p.k * 96, 16), 96)
    loads = []
    for index, (ref, start) in enumerate(weights):
        copy = pltpu.make_async_copy(ref, full.at[mine, pl.ds(start, ref.shape[1])], lsem.at[index])
        copy.start()
        loads.append(copy)
    text = captions[...].astype(F32)
    caption[...] = jnp.concatenate([text[:, 128 * r : 128 * r + 128] for r in range(4)] + [jnp.zeros((4, 128), F32)], 0)
    lead[...] = jnp.concatenate([patches[0, 0].astype(F32), jnp.zeros((4, D), F32)], 0)
    square = jnp.concatenate([gain_a[...].astype(F32), gain_b[...].astype(F32), gain_c[...].astype(F32)], 0)
    square = jnp.concatenate([square, jnp.zeros((3, 32), F32)], 1)
    square = jnp.concatenate([square, jnp.zeros((125, 128), F32)], 0)
    full[mine, GAINS : GAINS + 128] = jnp.transpose(square)[0:96].astype(B16)
    leadbuf[p.dp] = lead[...]
    barrier(p.plane() + list(p.team))
    text_hop = Spread(p, caption, texts, text_s, text_r, same=True)
    others = [p.core, p.xp, ((1 - p.x) * 2 + 1 - p.c, p.k)]
    sends = []
    for index, other in enumerate(others):
        copy = pltpu.make_async_remote_copy(
            src_ref=lead, dst_ref=leadbuf.at[p.dp], send_sem=lead_s.at[0, index], recv_sem=lead_r.at[0, index],
            device_id=other, device_id_type=MESH)
        copy.start()
        sends.append(copy)
    for copy in loads:
        copy.wait()
    def block(k, start, count, job):
        first_col, columns = JOBS[job]
        return full.at[pl.ds(pl.multiple_of(k * 96 + start * 16, 16), count * 16), pl.ds(first_col, columns)]

    gather = Gather(p, block, len(JOBS), ssem, rsem)
    lag = (0, 1, 2, 3, 4, 5)
    outs = []

    def out(source, target):
        copy = pltpu.make_async_copy(source, target, osem.at[len(outs)])
        copy.start()
        outs.append(copy)

    ticked, written = [0], [0]

    def upto(job):
        while ticked[0] <= job + lag[4]:
            gather.tick(ticked[0], lag)
            ticked[0] += 1
        while written[0] <= min(job, len(JOBS) - 1):
            cols = pl.ds(*JOBS[written[0]])
            out(full.at[:, cols], full_o.at[:, cols])
            written[0] += 1

    upto(-3)
    for f in range(4):
        xs[f * PAD + 192 : f * PAD + PAD, :] = jnp.zeros((16, D), B16)
        xs[f * PAD : f * PAD + 197, :] = patches[0, :, f, :]
    out(xs, xs_o)
    text_hop.wait()
    text_team = Team(p, texts, texts_o, lead_s.at[1], lead_r.at[1])
    upto(0)
    for index, other in enumerate(others):
        pltpu.make_async_remote_copy(
            src_ref=lead, dst_ref=leadbuf.at[other[0]], send_sem=lead_s.at[0, index], recv_sem=lead_r.at[0, index],
            device_id=other, device_id_type=MESH).wait_recv()
    leaders = jnp.concatenate([leadbuf[index][0:4] for index in range(4)], 0)
    leaders_o[...] = leaders.astype(B16)
    rows = jnp.transpose(full[:, GAINS : GAINS + 128].astype(F32))[0:8]
    gains_o[...] = rows
    courier_gain, attend_gain, expand_gain = rows[0:1], rows[1:2], rows[2:3]
    message = dot(leaders.astype(B16), full[:, COURIER : COURIER + D])
    message_o[...] = message
    xh, _ = normalize(message)
    mnorm = (xh * courier_gain).astype(B16)
    mnorm_o[...] = mnorm

    def norm_frame(f, carry):
        here = pl.ds(pl.multiple_of(f * PAD, 16), PAD)
        xh, _ = normalize(xs[here, :].astype(F32))
        norm[here, :] = (xh * attend_gain).astype(B16)
        return carry

    lax.fori_loop(0, 4, norm_frame, 0)
    upto(3)
    mmix = dot(mnorm, full[:, CHEADS : CHEADS + 3 * D])
    mq, mk, mv = mmix[:, :D].astype(B16), mmix[:, D : 2 * D].astype(B16), mmix[:, 2 * D :].astype(B16)
    mmix_o[...] = mmix.astype(B16)
    scores = dot(spread_heads(mq), mk, 1, 1) * HEAD ** (-0.5)
    frames = lax.broadcasted_iota(jnp.int32, (192, 16), 1)
    scores = jnp.where(frames < counts[0], scores, -1000000000.0)
    raised = jnp.exp(scores - jnp.max(scores, -1, keepdims=True))
    mshare = raised / jnp.sum(raised, -1, keepdims=True)
    mshare_o[...] = mshare
    told = join_heads(dot(mshare.astype(B16), mv)).astype(B16)
    told_o[...] = told

    def heads_tile(base, factor):
        def body(n, carry):
            cols = pl.ds(pl.multiple_of(base + n * 256, 256), 256)
            wcols = pl.ds(pl.multiple_of(AHEADS + base + n * 256, 128), 256)
            mixed[:, cols] = (dot(norm[...], full[:, wcols]) * factor).astype(B16)
            return carry
        lax.fori_loop(0, 3, body, 0)

    upto(4)
    heads_tile(0, HEAD ** (-0.5))
    upto(5)
    heads_tile(D, 1.0)
    upto(6)
    heads_tile(2 * D, 1.0)
    upto(7)
    mout_all = message + dot(told, full[:, CMERGE : CMERGE + D])
    mout = jnp.concatenate([row_of(mout_all, p.dp * 4 + f) for f in range(4)] + [jnp.zeros((4, D), F32)], 0)
    mout_o[...] = mout
    xh, _ = normalize(mout)
    extra = (xh * attend_gain).astype(B16)
    extra_kv = dot(extra, full[:, AHEADS + D : AHEADS + 3 * D])
    extra = extra.astype(F32)
    spot = lax.broadcasted_iota(jnp.int32, (16, 1), 0) == 5
    for f in range(4):
        tail = pl.ds(f * PAD + 192, 16)
        norm[tail, :] = jnp.where(spot, extra[f : f + 1], norm[tail, :].astype(F32)).astype(B16)
        old = mixed[tail, D : 3 * D].astype(F32)
        mixed[tail, D : 3 * D] = jnp.where(spot, extra_kv[f : f + 1], old).astype(B16)
    out(mixed, mixed_o)

    first = lax.broadcasted_iota(jnp.int32, (PAD, 128), 1) < HEAD
    kept = lax.broadcasted_iota(jnp.int32, (PAD, PAD), 0) < 198

    def attend(f, pair):
        here = pl.ds(pl.multiple_of(f * PAD, 16), PAD)
        at = pl.multiple_of(pair * 128, 128)
        q = mixed[here, pl.ds(at, 128)]
        k = mixed[here, pl.ds(pl.multiple_of(D + at, 128), 128)]
        v = mixed[here, pl.ds(pl.multiple_of(2 * D + at, 128), 128)]
        total = None
        for h in range(2):
            mask = first if h == 0 else jnp.logical_not(first)
            kh, vh = jnp.where(mask, k, jnp.zeros_like(k)), jnp.where(mask, v, jnp.zeros_like(v))
            scores = jnp.where(kept, dot(kh, q, 1, 1), -1e30)
            raised = jnp.exp(scores - jnp.max(scores, 0, keepdims=True))
            share = (raised * (1.0 / jnp.sum(raised, 0, keepdims=True))).astype(B16)
            shares[f * HEADS + pair * 2 + h] = share
            part = dot(share, vh, 0, 0)
            total = part if total is None else total + part
        seen[here, pl.ds(at, 128)] = total.astype(B16)

    def attend_frame(f):
        def body(pair, carry):
            attend(f, pair)
            return carry
        lax.fori_loop(0, 6, body, 0, unroll=6)

    def merge_frames():
        def body(n, carry):
            cols = pl.ds(pl.multiple_of(n * 256, 256), 256)
            wcols = pl.ds(pl.multiple_of(AMERGE + n * 256, 128), 256)
            hidden[:, cols] = dot(seen[...], full[:, wcols])
            return carry
        lax.fori_loop(0, 3, body, 0)

    def hidden_frame(f, carry):
        here = pl.ds(pl.multiple_of(f * PAD, 16), PAD)
        value = hidden[here, :] + xs[here, :].astype(F32)
        hidden[here, :] = value
        xh, _ = normalize(value)
        n2[here, :] = (xh * expand_gain).astype(B16)
        return carry

    def row_mask(shape, axis):
        index = lax.broadcasted_iota(jnp.int32, shape, axis)
        good = index < 0
        for f in range(4):
            lost = jnp.where(p.dp * 4 + f < counts[0], 0, ROWS)
            good = jnp.logical_or(good, jnp.logical_and(index >= f * PAD + lost, index < f * PAD + 197 + lost * 0))
        return good

    mask_row = jnp.where(row_mask((16, ROWS), 1), 1.0, 0.0).astype(B16)

    def expand_tile(base, count=3):
        def body(n, carry):
            cols = pl.ds(pl.multiple_of(base + n * 256, 256), 256)
            wcols = pl.ds(pl.multiple_of(EXPAND + base + n * 256, 128), 256)
            grown = dot(n2[...], full[:, wcols])
            s = 0.5 + 0.5 * jnp.tanh(0.851 * grown)
            gated = grown * s
            dd[:, cols] = (s + 1.702 * gated * (1.0 - s)).astype(B16)
            gsum_o[:, cols] = dot(mask_row, gated.astype(B16))[0:8]
            return carry
        lax.fori_loop(0, count, body, 0)

    attend_frame(0)
    upto(8)
    attend_frame(1)
    upto(9)
    attend_frame(2)
    attend_frame(3)
    out(seen, seen_o)
    normt[...] = jnp.transpose(norm[...])
    out(normt, normt_o)
    seent[...] = jnp.transpose(seen[...])
    out(seent, seent_o)
    out(shares, shares_o)
    upto(10)
    merge_frames()
    lax.fori_loop(0, 4, hidden_frame, 0)
    out(hidden, hidden_o)
    mask_col = jnp.where(row_mask((ROWS, D), 0), 1.0, 0.0)
    n2t[...] = jnp.transpose((n2[...].astype(F32) * mask_col).astype(B16))
    out(n2t, n2t_o)
    expand_tile(0)
    upto(11)
    expand_tile(D)
    high = hidden[...].astype(B16)
    low = (hidden[...] - high.astype(F32)).astype(B16)
    hsum_o[...] = (dot(mask_row, high) + dot(mask_row, low))[0:8]
    upto(12)
    expand_tile(2 * D)
    out(dd.at[:, pl.ds(0, 3 * D)], d_o.at[:, pl.ds(0, 3 * D)])
    upto(13)
    expand_tile(3 * D, 2)
    upto(14)
    expand_tile(3 * D + 512, 1)
    out(dd.at[:, pl.ds(3 * D, D)], d_o.at[:, pl.ds(3 * D, D)])
    upto(15)
    for copy in sends:
        copy.wait_send()
    text_team.wait()
    text_team.done()
    text_hop.done()
    for copy in outs:
        copy.wait()


def pack_row(row):
    return jnp.concatenate([row[:, 128 * r : 128 * r + 128] for r in range(6)] + [jnp.zeros((2, 128), F32)], 0)


def unpack_row(value):
    return jnp.concatenate([value[r : r + 1] for r in range(6)], 1)


def twice(value):
    high = value.astype(B16)
    return jnp.concatenate([high, (value - high.astype(F32)).astype(B16)], 0)


RJOBS = ((0, 768), (768, 768), (1536, 768), (2304, 768), (3072, 768), (3840, 768), (4608, 768), (5376, 768))
BUNDLE = 3840
SIXTH = BUNDLE // 6


def rear_kernel(
    xs_h, normt_h, mixed_h, shares, seen_h, seent_h, hidden_h, n2t_h, d_h, full,
    gsum, hsum, shrink, texts, gains, mout, leaders, message, mnorm, mmix, mshare, told, counts, matches,
    patch_h, fin, loss_o, shrink_grad_o, courier_o, cheads_o, cmerge_o, proj_o, gains_grad_o, lead_o,
    stage, rc, rx, ry, rz, own, rf, bundle, wx, wmerge, wheads, mixed, seen, seent, hidden, n2t, dd, sbuf, hg, low, dout,
    projection, vecs, team, gs, gr, ps, pr, rs_, rr, us, ur, gg, first, mog, mog_team, chosen, gain_pack, gain_team, gain_send, gain_all,
    s_r, r_r, s_b, r_b, team_s, team_r, hop_s, hop_r, lsem, psem,
):
    p = Pos()
    pending = ((n2t_h, n2t), (d_h, dd), (full.at[:, pl.ds(PROJ, 512)], projection), (full.at[:, pl.ds(EXPAND, 3072)], wx),
               (hidden_h, hidden), (seent_h, seent), (full.at[:, pl.ds(AMERGE, D)], wmerge), (mixed_h, mixed), (seen_h, seen),
               (full.at[:, pl.ds(AHEADS, 3 * D)], wheads))
    loads = []

    def load(source, target):
        copy = pltpu.make_async_copy(source, target, lsem.at[len(loads)])
        copy.start()
        loads.append(copy)
        return copy

    for source, target in pending:
        load(source, target)
    barrier(p.plane() + list(p.team))
    vecs[:, 0:384] = jnp.concatenate([gsum[0:1, 384 * k : 384 * k + 384] for k in range(8)], 0)
    vecs[:, 384:512] = pack_row(hsum[0:1, :])
    hop = Team(p, vecs, team, team_s.at[0], team_r.at[0])
    reduce = Reduce(p, stage, (rc, rx, ry, rz, own, rf), fin, RJOBS, s_r, r_r)

    def expand_tiles(start):
        stage[:, :, start : start + D] = dot(n2t[...], dd[:, start : start + D]).astype(B16).reshape(8, 96, D)

    text = jnp.concatenate([jnp.concatenate([texts[i, :, r, :] for r in range(4)], 1) for i in range(4)], 0)
    text_unit = (text * lax.rsqrt(jnp.sum(text * text, -1, keepdims=True) + 1e-06)).astype(B16)
    hop.wait()
    total = team[0] + team[1] + team[2] + team[3]
    for k in range(8):
        gs[k] = jnp.broadcast_to(total[k : k + 1, 0:384], (8, 384))
    hop.done()
    hop = Spread(p, gs, gr, hop_s.at[0], hop_r.at[0])
    loads[0].wait()
    loads[1].wait()
    expand_tiles(0)
    reduce.next(0)
    expand_tiles(D)
    reduce.next(1)
    hop.wait()
    gated = jnp.concatenate([gr[v][0:1] for v in range(8)], 0)
    both = dot(twice(gated), shrink[...])
    part = both[0:8] + both[8:16]
    for v in range(8):
        ps[v] = pack_row(part[v : v + 1])
    hop.done()
    hop = Spread(p, ps, pr, hop_s.at[1], hop_r.at[1])
    expand_tiles(2 * D)
    reduce.next(2, 0)
    hop.wait()
    packed = total[:, 384:512]
    for k in range(8):
        packed = packed + pr[k]
    hop.done()
    loads[2].wait()
    denominator = (counts[0] * 197).astype(F32)
    pooled = jnp.broadcast_to(unpack_row(packed / denominator), (8, D))
    embed = dot(pooled.astype(B16), projection[...])
    rate = lax.rsqrt(jnp.sum(embed * embed, -1, keepdims=True) + 1e-06)
    unit = embed * rate
    logits = dot(unit.astype(B16), text_unit, 1, 1) * LOGIT_SCALE
    peak = jnp.max(logits, -1, keepdims=True)
    normalizer = peak + jnp.log(jnp.sum(jnp.exp(logits - peak), -1, keepdims=True))
    matched = lax.broadcasted_iota(jnp.int32, logits.shape, 1) == matches[0]
    loss_o[...] = jnp.broadcast_to(normalizer - jnp.sum(jnp.where(matched, logits, 0.0), -1, keepdims=True), (8, 128))
    slope = (jnp.exp(logits - normalizer) - jnp.where(matched, 1.0, 0.0)).astype(B16)
    unit_grad = dot(slope, text_unit) * LOGIT_SCALE
    embed_grad = (rate * (unit_grad - unit * jnp.sum(unit * unit_grad, -1, keepdims=True))).astype(B16)
    rg = dot(embed_grad, projection[...], 1, 1) / denominator
    rs_[...] = pack_row(rg.astype(B16).astype(F32)[0:1])
    hop = Spread(p, rs_, rr, hop_s.at[2], hop_r.at[2], same=True)

    places = ((0, 0, SIXTH), (1, 4 * D, 128), (1, D, 384), (1, 0, 128))

    def block(k, start, count, job):
        slot, offset, sixth = places[job]
        return bundle.at[slot, k, :, pl.ds(pl.multiple_of(offset + start * sixth, 128), count * sixth)]

    def fill(slot, col, parts):
        for part in parts:
            bundle[slot, p.k, :, col : col + part.shape[1]] = part
            col += part.shape[1]

    gather = Gather(p, block, 4, s_b, r_b)
    top = lax.broadcasted_iota(jnp.int32, (16, 1), 0) == 0
    pooled_rows = jnp.where(top, jnp.concatenate([pooled, pooled], 0), 0.0).astype(B16)
    embed_rows = jnp.where(top, jnp.concatenate([embed_grad.astype(F32)] * 2, 0), 0.0).astype(B16)
    fill(0, 0, (leaders[...], mnorm[...], told[...], pooled_rows, embed_rows, jnp.zeros((16, 256), B16)))
    gather.stage(0, 0)
    expand_tiles(3 * D)
    normt_load = load(normt_h, n2t)
    reduce.next(3, 1)
    hop.wait()
    rows = jnp.concatenate([unpack_row(rr[v]) for v in range(8)], 0).astype(B16)
    grad = dot(rows, shrink[...], 1, 1)
    for v in range(8):
        us[v] = jnp.broadcast_to(grad[v : v + 1], (8, 384))
    hop.done()
    hop = Spread(p, us, ur, hop_s.at[3], hop_r.at[3])
    shrink_grad_o[...] = dot(twice(gated), jnp.concatenate([rows.astype(F32)] * 2, 0).astype(B16), 0, 0)
    reduce.next(2)
    gather.stage(1, 0)
    hop.wait()
    for k in range(8):
        gg[:, 384 * k : 384 * k + 384] = ur[k]
    hop.done()

    def scale_tile(n, carry):
        cols = pl.ds(pl.multiple_of(n * 256, 256), 256)
        dd[:, cols] = (dd[:, cols].astype(F32) * gg[0:1, cols]).astype(B16)
        return carry

    lax.fori_loop(0, 12, scale_tile, 0, unroll=3)
    reduce.next(0, 3, scale=gg)
    loads[3].wait()

    def norm_tile(n):
        hg[:, 256 * n : 256 * n + 256] = dot(dd[...], wx[256 * n : 256 * n + 256, :], 1, 1)

    norm_tile(0)
    reduce.next(1, scale=gg)
    gather.stage(2, 0)
    norm_tile(1)
    reduce.next(2, 0, scale=gg)
    gather.stage(3, 0)
    norm_tile(2)
    weights = [load(full.at[:, pl.ds(CHEADS, 3 * D)], wx.at[:, pl.ds(0, 3 * D)]), load(full.at[:, pl.ds(COURIER, D)], wx.at[:, pl.ds(3 * D, D)])]
    reduce.next(3, scale=gg)
    loads[4].wait()
    attend_gain, expand_gain = gains[1:2, :], gains[2:3, :]

    def hidden_frame(f, total):
        here = pl.ds(pl.multiple_of(f * PAD, 16), PAD)
        limit = jnp.where(p.dp * 4 + f < counts[0], 197, 0)
        good = lax.broadcasted_iota(jnp.int32, (PAD, D), 0) < limit
        xh, rate = normalize(hidden[here, :])
        dy = jnp.where(good, hg[here, :], 0.0)
        e = dy * expand_gain
        grad = rate * (e - jnp.mean(e, -1, keepdims=True) - xh * jnp.mean(e * xh, -1, keepdims=True))
        grad = grad + jnp.where(good, rg[0:1, :], 0.0)
        hg[here, :] = grad
        low[here, :] = grad.astype(B16)
        return total + jnp.sum(dy * xh, 0, keepdims=True)

    expand_gain_grad = lax.fori_loop(0, 4, hidden_frame, jnp.zeros((1, D), F32))
    reduce.next(1, 0)
    gather.stage(4, 0)
    loads[5].wait()
    loads[6].wait()

    def merge_tile(n, carry):
        cols = pl.ds(pl.multiple_of(n * 256, 256), 256)
        stage[:, :, pl.ds(pl.multiple_of(3072 + n * 256, 128), 256)] = dot(seent[...], low[:, cols]).astype(B16).reshape(8, 96, 256)
        dout[:, cols] = dot(low[...], wmerge[cols, :], 1, 1).astype(B16)
        return carry

    lax.fori_loop(0, 3, merge_tile, 0, unroll=3)
    weights.append(load(full.at[:, pl.ds(CMERGE, D)], wmerge))
    reduce.next(4, 2)
    early = bundle[0].reshape(128, BUNDLE)
    pick = jnp.where(
        jnp.logical_and(lax.broadcasted_iota(jnp.int32, (D, 128), 0) == p.k * 96 + lax.broadcasted_iota(jnp.int32, (D, 128), 1),
                        lax.broadcasted_iota(jnp.int32, (D, 128), 1) < 96), 1.0, 0.0).astype(B16)
    for index in range(3):
        chosen[index] = dot(early[:, D * index : D * index + D], pick).astype(B16)
    proj_o[...] = dot(dot(early[:, 3 * D : 4 * D], pick).astype(B16), early[:, 4 * D : 4 * D + 512], 0, 0)[0:96]
    loads[7].wait()
    loads[8].wait()
    normt_load.wait()
    half_lanes = lax.broadcasted_iota(jnp.int32, (PAD, 128), 1) < HEAD

    def fetch(group):
        return pltpu.make_async_copy(shares.at[:, pl.ds(4 * group, 4)], sbuf.at[group % 2], psem.at[group % 2])

    fetch(0).start()

    def attend_group(group):
        if group < 2:
            fetch(group + 1).start()
        fetch(group).wait()
        inputs, outputs = [], []
        for f in range(4):
            for j in range(2):
                here = pl.ds(f * PAD, PAD)
                qs, ks, vs = (pl.ds(b + (2 * group + j) * 128, 128) for b in (0, D, 2 * D))
                inputs.append((here, qs, ks, vs, mixed[here, qs], mixed[here, ks], mixed[here, vs], dout[here, qs], seen[here, qs],
                               [sbuf[group % 2, f, 2 * j + h] for h in range(2)]))
        for here, qs, ks, vs, q, k, v, do, o, share_of in inputs:
            right = jnp.concatenate([do, (-(do.astype(F32) * o.astype(F32))).astype(B16)], 1)
            dq = dk = dv = None
            zero = jnp.zeros_like(q)
            for h in range(2):
                mask = half_lanes if h == 0 else jnp.logical_not(half_lanes)
                share = share_of[h]
                left = jnp.concatenate([jnp.where(mask, v, zero), jnp.where(mask, jnp.ones_like(v), zero)], 1)
                ds = (share.astype(F32) * dot(left, right, 1, 1)).astype(B16)
                pq = dot(ds, jnp.where(mask, k, zero), 0, 0)
                pk = dot(ds, jnp.where(mask, q, zero))
                pv = dot(share, jnp.where(mask, do, zero))
                dq, dk, dv = (pq, pk, pv) if h == 0 else (dq + pq, dk + pk, dv + pv)
            outputs.append((here, qs, ks, vs, (dq * HEAD ** (-0.5)).astype(B16), dk.astype(B16), dv.astype(B16)))
        for here, qs, ks, vs, dq, dk, dv in outputs:
            mixed[here, qs] = dq
            mixed[here, ks] = dk
            mixed[here, vs] = dv

    def heads_tiles(group):
        def body(n, carry):
            cols = pl.ds(pl.multiple_of(n * D + group * 256, 128), 256)
            to = pl.ds(pl.multiple_of(3840 + group * D + n * 256, 128), 256)
            stage[:, :, to] = dot(n2t[...], mixed[:, cols]).astype(B16).reshape(8, 96, 256)
            return carry
        lax.fori_loop(0, 3, body, 0, unroll=3)

    attend_group(0)
    reduce.next(4, 1, 3)
    heads_tiles(0)
    reduce.next(5, 2, 0)
    attend_group(1)
    reduce.next(4, 5, 1, 3)
    heads_tiles(1)
    reduce.next(6, 2, 0)
    attend_group(2)
    tokens = load(xs_h, dout)
    loads[9].wait()
    tails = [mixed[pl.ds(f * PAD + 192, 16), :].astype(F32)[5:6] for f in range(4)]
    tails = jnp.concatenate(tails + [jnp.zeros((12, 3 * D), F32)], 0).astype(B16)
    xh, rate = normalize(mout[...])
    e = dot(tails, wheads[...], 1, 1)[0:8] * attend_gain
    mog[...] = rate * (e - jnp.mean(e, -1, keepdims=True) - xh * jnp.mean(e * xh, -1, keepdims=True))
    hop = Team(p, mog, mog_team, team_s.at[1], team_r.at[1])
    reduce.next(6, 4, 5)
    heads_tiles(2)
    reduce.next(7, 1, 3)
    for copy in weights:
        copy.wait()
    hop.wait()
    out_grad = jnp.concatenate([mog_team[i][0:4] for i in range(4)], 0)
    out_low = out_grad.astype(B16)
    fill(1, 4 * D, (out_low,))
    gather.stage(0, 1)
    courier_gain = gains[0:1, :]
    mq, mk, mv = mmix[:, 0:D], mmix[:, D : 2 * D], mmix[:, 2 * D : 3 * D]
    told_grad = dot(out_low, wmerge[...], 1, 1).astype(B16)
    upstream = spread_heads(told_grad)
    share = mshare[...]
    share_grad = dot(upstream, mv, 1, 1)
    dv = dot(share.astype(B16), upstream, 0, 0)
    inner = jnp.sum(share * share_grad, -1, keepdims=True)
    ds = (share * (share_grad - inner)).astype(B16)
    dq = join_heads(dot(ds, mk)) * HEAD ** (-0.5)
    dk = dot(ds, spread_heads(mq), 0, 0) * HEAD ** (-0.5)
    mixed_grad = jnp.concatenate([dq, dk, dv], 1).astype(B16)
    fill(1, D, (mixed_grad,))
    gather.stage(0, 2)
    reduce.next(7, 6)
    gather.stage(1, 1)
    norm_grad = dot(mixed_grad, wx[:, 0 : 3 * D], 1, 1)
    xh, rate = normalize(message[...])
    e = norm_grad * courier_gain
    grad = rate * (e - jnp.mean(e, -1, keepdims=True) - xh * jnp.mean(e * xh, -1, keepdims=True))
    message_grad = (out_grad + grad).astype(B16)
    fill(1, 0, (message_grad,))
    gather.stage(0, 3)
    gain_own = jnp.sum(norm_grad * xh, 0, keepdims=True)
    reduce.next(4, 2, 5)

    def tokens_tile(n):
        hidden[:, 256 * n : 256 * n + 256] = dot(mixed[...], wheads[256 * n : 256 * n + 256, :], 1, 1)

    gather.stage(1, 2)
    tokens_tile(0)
    gather.stage(2, 1)
    reduce.next(7, 6, 3)
    gather.stage(1, 3)
    tokens_tile(1)
    gather.stage(2, 2)
    gather.stage(3, 1)
    reduce.next(4, 5)
    tokens_tile(2)
    gather.stage(2, 3)
    gather.stage(3, 2)
    reduce.next(7, 6)
    tokens.wait()
    spot = lax.broadcasted_iota(jnp.int32, (PAD, 1), 0) == 197
    place = lax.broadcasted_iota(jnp.int32, (8, D), 0)
    first[...] = jnp.zeros_like(first)

    def token_frame(f, total):
        here = pl.ds(pl.multiple_of(f * PAD, 16), PAD)
        xh, rate = normalize(jnp.where(spot, row_of(mout[...], f), dout[here, :].astype(F32)))
        dy = hidden[here, :]
        e = dy * attend_gain
        grad = rate * (e - jnp.mean(e, -1, keepdims=True) - xh * jnp.mean(e * xh, -1, keepdims=True))
        patch = hg[here, :] + grad
        low[here, :] = patch.astype(B16)
        first[...] = jnp.where(place == f, patch[0:1], first[...])
        return total + jnp.sum(dy * xh, 0, keepdims=True)

    attend_gain_grad = lax.fori_loop(0, 4, token_frame, jnp.zeros((1, D), F32))
    patch_out = load(low, patch_h)
    gain_pack[0:8, :] = pack_row(attend_gain_grad)
    gain_pack[8:16, :] = pack_row(expand_gain_grad)
    gain_hop = Team(p, gain_pack, gain_team, team_s.at[2], team_r.at[2])
    gather.stage(3, 3)
    gather.stage(4, 1)
    reduce.next(4, 5)
    leader_grad = dot(message_grad, wx[:, 3 * D : 4 * D], 1, 1)
    lead_o[...] = jnp.concatenate([row_of(leader_grad, p.dp * 4 + f) for f in range(4)] + [jnp.zeros((4, D), F32)], 0) + first[...]
    gain_hop.wait()
    gain_send[0:16, :] = gain_team[0] + gain_team[1] + gain_team[2] + gain_team[3]
    gain_send[16:24, :] = pack_row(gain_own)
    gain_spread = Spread(p, gain_send, gain_all, hop_s.at[4], hop_r.at[4], same=True)
    reduce.next(7, 6)
    gather.stage(4, 2)

    def late(start, count):
        return bundle[1, :, :, start : start + count].reshape(128, count)

    cmerge_o[...] = dot(chosen[2], late(4 * D, D), 0, 0)[0:96]
    cheads_o[...] = dot(chosen[1], late(D, 3 * D), 0, 0)[0:96]
    reduce.next(6, 5, 4)
    gather.stage(4, 3)
    courier_o[...] = dot(chosen[0], late(0, D), 0, 0)[0:96]
    reduce.next(7)
    gain_spread.wait()
    total_gain = gain_all[0]
    for k in range(1, 8):
        total_gain = total_gain + gain_all[k]
    total_gain = jnp.concatenate([unpack_row(total_gain[8 * i : 8 * i + 8]) for i in range(3)] + [jnp.zeros((5, D), F32)], 0)
    both = dot(pick, twice(total_gain), 0, 1)
    gains_grad_o[...] = both[0:96, 0:8] + both[0:96, 8:16]
    for _ in range(8):
        for job in range(len(RJOBS)):
            if reduce.at[job] < 7:
                reduce.next(job)
    for job in range(len(RJOBS)):
        reduce.next(job)
    for job in range(4):
        gather.stage(5, job)
    gain_hop.done()
    gain_spread.done()
    hop.done()
    patch_out.wait()


def finish_kernel(patch, lead, fin, cgain, courier, cheads, cmerge, proj, shrink, loss,
                  patch_o, gain_a, gain_b, gain_c, heads_o, merge_o, expand_o, courier_o, cheads_o, cmerge_o, proj_o, shrink_o, loss_o):
    for source, target in ((courier, courier_o), (cheads, cheads_o), (cmerge, cmerge_o), (proj, proj_o), (shrink, shrink_o)):
        target[...] = source[...].astype(F32)
    top = lax.broadcasted_iota(jnp.int32, (PAD, 1), 0) == 0
    for f in range(4):
        value = jnp.where(top, lead[f : f + 1, :], patch[f * PAD : f * PAD + PAD, :].astype(F32)).astype(B16)
        patch_o[0, :, f, :] = value[0:197]
    expand_o[...] = fin[:, 0:3072].astype(F32)
    merge_o[...] = fin[:, 3072:3840].astype(F32)
    for group in range(3):
        for n in range(3):
            heads_o[:, n * D + group * 256 : n * D + group * 256 + 256] = fin[
                :, 3840 + group * D + n * 256 : 3840 + group * D + n * 256 + 256].astype(F32)
    own = jnp.concatenate([cgain[...], jnp.zeros((96, 120), F32)], 1)
    own = jnp.transpose(jnp.concatenate([own, jnp.zeros((32, 128), F32)], 0))
    gain_a[...], gain_b[...], gain_c[...] = own[0:1, 0:96], own[1:2, 0:96], own[2:3, 0:96]
    loss_o[...] = loss[0:1, 0:1]


VMEM = 62 * 1024 * 1000


def any_spec():
    return pl.BlockSpec(memory_space=pl.ANY)


def vmem_spec():
    return pl.BlockSpec(memory_space=pltpu.VMEM)


def smem_spec():
    return pl.BlockSpec(memory_space=pltpu.SMEM)


def sds(shape, dtype):
    return jax.ShapeDtypeStruct(shape, dtype)


def dma(*shape):
    return pltpu.SemaphoreType.DMA(shape)


def vm(shape, dtype):
    return pltpu.VMEM(shape, dtype)


def fast(
    patches, counts, captions, matches, courier, courier_gain, courier_heads, courier_merge, attend_gain, attend_heads,
    attend_merge, expand_gain, expand_weight, shrink_weight, projection,
):
    anys, vmem, smem = any_spec(), vmem_spec(), smem_spec()
    (full, normt, mixed, shares, seen, seent, hidden, n2t, dd, gsum, hsum, gains,
     leaders, message, mnorm, mmix, mshare, told, mout, texts, xs) = pl.pallas_call(
        forward_kernel,
        out_shape=(
            sds((D, NCOLS), B16), sds((D, ROWS), B16), sds((ROWS, 3 * D), B16), sds((48, PAD, PAD), B16), sds((ROWS, D), B16),
            sds((D, ROWS), B16), sds((ROWS, D), F32), sds((D, ROWS), B16), sds((ROWS, 4 * D), B16), sds((8, 4 * D), F32),
            sds((8, D), F32), sds((8, D), F32), sds((16, D), B16), sds((16, D), F32), sds((16, D), B16), sds((16, 3 * D), B16),
            sds((192, 16), F32), sds((16, D), B16), sds((8, D), F32), sds((4, 8, 8, 128), F32),
            sds((ROWS, D), B16)),
        in_specs=[vmem] * 5 + [smem] + [anys] * 7,
        out_specs=tuple([anys] * 9 + [vmem] * 11 + [anys]),
        scratch_shapes=[
            vm((D, NCOLS), B16), vm((ROWS, D), B16), vm((8, D), F32), vm((8, 128), F32), vm((4, 8, D), F32), vm((ROWS, D), B16), vm((D, ROWS), B16), vm((ROWS, 3 * D), B16),
            vm((48, PAD, PAD), B16), vm((ROWS, D), B16), vm((D, ROWS), B16), vm((ROWS, D), F32), vm((ROWS, D), B16),
            vm((D, ROWS), B16), vm((ROWS, 4 * D), B16),
            vm((8, 8, 128), F32), dma(len(JOBS), 28), dma(len(JOBS), 28), dma(7), dma(2, 3), dma(2, 3), dma(7), dma(7), dma(32)],
        compiler_params=pltpu.CompilerParams(collective_id=0, has_side_effects=True, vmem_limit_bytes=60 << 20),
        name="forward",
    )(jnp.transpose(patches, (0, 2, 1, 3)), captions, courier_gain[None], attend_gain[None], expand_gain[None], counts, courier, courier_heads, attend_heads, courier_merge, attend_merge, expand_weight, projection)
    (patch, fin, loss, shrink_grad, courier_grad, cheads_grad, cmerge_grad, proj_grad, cgain, leads) = pl.pallas_call(
        rear_kernel,
        out_shape=(
            sds((ROWS, D), B16), sds((96, 6144), B16), sds((8, 128), F32), sds((384, D), F32), sds((96, D), F32),
            sds((96, 3 * D), F32), sds((96, D), F32), sds((96, 512), F32), sds((96, 8), F32), sds((8, D), F32)),
        in_specs=[anys] * 10 + [vmem] * 12 + [smem] * 2,
        out_specs=tuple([anys] + [vmem] * 9),
        scratch_shapes=[
            vm((8, 96, 6144), B16), vm((4, 8, 48, D), B16), vm((8, 16, 6144), B16), vm((4, 32, 6144), B16),
            vm((3, 32, 6144), B16), vm((32, 6144), B16), vm((32, 6144), B16), vm((2, 8, 16, BUNDLE), B16),
            vm((D, 4 * D), B16), vm((D, D), B16), vm((D, 3 * D), B16), vm((ROWS, 3 * D), B16),
            vm((ROWS, D), B16), vm((D, ROWS), B16), vm((ROWS, D), F32), vm((D, ROWS), B16), vm((ROWS, 4 * D), B16),
            vm((2, 4, 4, PAD, PAD), B16), vm((ROWS, D), F32), vm((ROWS, D), B16), vm((ROWS, D), B16),
            vm((D, 512), B16), vm((8, 512), F32), vm((4, 8, 512), F32), vm((8, 8, 384), F32), vm((8, 8, 384), F32),
            vm((8, 8, 128), F32), vm((8, 8, 128), F32), vm((8, 128), F32), vm((8, 8, 128), F32), vm((8, 8, 384), F32),
            vm((8, 8, 384), F32), vm((8, 4 * D), F32), vm((8, D), F32), vm((8, D), F32), vm((4, 8, D), F32),
            vm((3, 128, 128), B16), vm((16, 128), F32), vm((4, 16, 128), F32), vm((24, 128), F32), vm((8, 24, 128), F32),
            dma(len(RJOBS), 11), dma(len(RJOBS), 11), dma(4, 28), dma(4, 28), dma(3, 3), dma(3, 3), dma(5, 7), dma(5, 7),
            dma(16), dma(2)],
        compiler_params=pltpu.CompilerParams(collective_id=1, has_side_effects=True, vmem_limit_bytes=VMEM),
        name="rear",
    )(xs, normt, mixed, shares.reshape(4, HEADS, PAD, PAD), seen, seent, hidden, n2t, dd, full, gsum, hsum, shrink_weight, texts, gains, mout,
      leaders, message, mnorm, mmix, mshare, told, counts, matches)
    patch_grad, gain_a, gain_e, gain_m, heads, merge, expand, courier_out, cheads_out, cmerge_out, proj_out, shrink_out, loss_out = pl.pallas_call(
        finish_kernel,
        out_shape=(
            sds((1, 197, 4, D), B16), sds((1, 96), F32), sds((1, 96), F32), sds((1, 96), F32), sds((96, 3 * D), F32), sds((96, D), F32), sds((96, 4 * D), F32),
            sds((96, D), F32), sds((96, 3 * D), F32), sds((96, D), F32), sds((96, 512), F32), sds((384, D), F32), sds((1, 1), F32)),
        in_specs=[vmem] * 10,
        out_specs=tuple([vmem] * 13),
        compiler_params=pltpu.CompilerParams(vmem_limit_bytes=VMEM),
        name="finish",
    )(patch, leads, fin, cgain, courier_grad, cheads_grad, cmerge_grad, proj_grad, shrink_grad, loss)
    return (
        loss_out[0], jnp.transpose(patch_grad, (0, 2, 1, 3)), courier_out, gain_m[0], cheads_out, cmerge_out, gain_a[0], heads,
        merge, gain_e[0], expand, shrink_out, proj_out,
    )


def joined_2(value, axis, join):
    pieces = jax.tree.map(lambda part: lax.all_gather(part, axis), value)
    head = jax.tree.map(lambda part: part[0], pieces)
    tail = jax.tree.map(lambda part: part[1:], pieces)
    running, _ = lax.scan(lambda running, share: (join(running, share), None), head, tail)
    return running


def layer_norm(value, gain):
    center = value - jnp.mean(value, -1, keepdims=True)
    spread = jnp.mean(center * center, -1, keepdims=True)
    return center * lax.rsqrt(spread + EPSILON) * gain


def norm_back(value, gain, upstream):
    _, pull = jax.vjp(layer_norm, value, gain)
    return pull(upstream)


def quick_gelu(value):
    return value * jax.nn.sigmoid(1.702 * value)


def unit_rows(value):
    return value * lax.rsqrt(jnp.sum(value * value, -1, keepdims=True) + 1e-06)


def split_heads(mixed, query_count):
    batch, length, triple = mixed.shape
    width = triple // 3
    rounded = mixed.astype(jnp.bfloat16)
    queries = rounded[:, :query_count, :width].reshape(batch, query_count, HEADS, HEAD)
    keys = rounded[:, :, width : 2 * width].reshape(batch, length, HEADS, HEAD)
    values = rounded[:, :, 2 * width :].reshape(batch, length, HEADS, HEAD)
    return (queries, keys, values)


def scores_of(queries, keys, key_mask):
    scores = jnp.einsum(
        "bqhd,bkhd->bhqk", queries, keys, preferred_element_type=jnp.float32
    ) * HEAD ** (-0.5)
    if key_mask is not None:
        scores = jnp.where(key_mask[:, None, None, :], scores, -1000000000.0)
    return scores


def attend_forward(queries, keys, values, key_mask):
    scores = scores_of(queries, keys, key_mask)
    peak = jnp.max(scores, -1, keepdims=True)
    raised = jnp.exp(scores - peak)
    total = jnp.sum(raised, -1, keepdims=True)
    shares = (raised / total).astype(jnp.bfloat16)
    joined = jnp.einsum("bhqk,bkhd->bqhd", shares, values, preferred_element_type=jnp.float32)
    batch, count = (joined.shape[0], joined.shape[1])
    return (
        joined.reshape(batch, count, HEADS * HEAD).astype(jnp.bfloat16),
        peak + jnp.log(total),
        shares,
    )


def attend_backward(queries, keys, values, key_mask, normalizer, shares, upstream):
    batch, count, width = upstream.shape
    upstream_low = upstream.astype(jnp.bfloat16).reshape(batch, count, HEADS, HEAD)
    chances = jnp.exp(scores_of(queries, keys, key_mask) - normalizer)
    share_grad = jnp.einsum(
        "bqhd,bkhd->bhqk", upstream_low, values, preferred_element_type=jnp.float32
    )
    value_grad = jnp.einsum(
        "bhqk,bqhd->bkhd", shares, upstream_low, preferred_element_type=jnp.float32
    )
    inner = jnp.sum(chances * share_grad, -1, keepdims=True)
    score_grad = (chances * (share_grad - inner)).astype(jnp.bfloat16)
    query_grad = jnp.einsum(
        "bhqk,bkhd->bqhd", score_grad, keys, preferred_element_type=jnp.float32
    ) * HEAD ** (-0.5)
    key_grad = jnp.einsum(
        "bhqk,bqhd->bkhd", score_grad, queries, preferred_element_type=jnp.float32
    ) * HEAD ** (-0.5)
    length = keys.shape[1]
    return (
        query_grad.reshape(batch, count, width),
        key_grad.reshape(batch, length, width),
        value_grad.reshape(batch, length, width),
    )


def frame_forward(block, message_rows, weights):
    attend_gain, attend_heads, attend_merge, expand_gain, expand_weight, shrink_weight = weights
    frames = block.astype(jnp.float32)
    tokens = jnp.concatenate([frames, message_rows[:, None, :]], 1)
    normed = layer_norm(tokens, attend_gain).astype(jnp.bfloat16)
    mixed = jnp.einsum("btd,de->bte", normed, attend_heads, preferred_element_type=jnp.float32)
    queries, keys, values = split_heads(mixed, block.shape[1])
    seen, normalizer, shares = attend_forward(queries, keys, values, None)
    hidden = frames + jnp.einsum(
        "bpd,de->bpe", seen, attend_merge, preferred_element_type=jnp.float32
    )
    normed_two = layer_norm(hidden, expand_gain).astype(jnp.bfloat16)
    grown = jnp.einsum("bpd,dm->bpm", normed_two, expand_weight, preferred_element_type=jnp.float32)
    gated = quick_gelu(grown).astype(jnp.bfloat16)
    result = hidden + jnp.einsum(
        "bpm,md->bpd", gated, shrink_weight, preferred_element_type=jnp.float32
    )
    kept = (
        tokens,
        normed,
        queries,
        keys,
        values,
        shares,
        normalizer,
        seen,
        hidden,
        normed_two,
        grown,
        gated,
    )
    return (jnp.sum(result, 1), kept)


def frame_backward(kept, upstream, weights):
    attend_gain, attend_heads, attend_merge, expand_gain, expand_weight, shrink_weight = weights
    (
        tokens,
        normed,
        queries,
        keys,
        values,
        shares,
        normalizer,
        seen,
        hidden,
        normed_two,
        grown,
        gated,
    ) = kept
    patch_count = hidden.shape[1]
    upstream_low = upstream.astype(jnp.bfloat16)
    shrink_grad = jnp.einsum("bpm,bd->md", gated, upstream_low, preferred_element_type=jnp.float32)
    gated_grad = jnp.einsum(
        "bd,md->bm", upstream_low, shrink_weight, preferred_element_type=jnp.float32
    )
    _, gelu_pull = jax.vjp(quick_gelu, grown)
    grown_grad = gelu_pull(jnp.broadcast_to(gated_grad[:, None, :], grown.shape))[0].astype(
        jnp.bfloat16
    )
    expand_grad = jnp.einsum(
        "bpd,bpm->dm", normed_two, grown_grad, preferred_element_type=jnp.float32
    )
    normed_two_grad = jnp.einsum(
        "bpm,dm->bpd", grown_grad, expand_weight, preferred_element_type=jnp.float32
    )
    hidden_grad, expand_gain_grad = norm_back(hidden, expand_gain, normed_two_grad)
    hidden_grad = hidden_grad + upstream[:, None, :]
    hidden_low = hidden_grad.astype(jnp.bfloat16)
    merge_grad = jnp.einsum("bpd,bpe->de", seen, hidden_low, preferred_element_type=jnp.float32)
    seen_grad = jnp.einsum(
        "bpe,de->bpd", hidden_low, attend_merge, preferred_element_type=jnp.float32
    )
    query_grad, key_grad, value_grad = attend_backward(
        queries, keys, values, None, normalizer, shares, seen_grad
    )
    length = tokens.shape[1]
    query_grad = jnp.pad(query_grad, ((0, 0), (0, length - patch_count), (0, 0)))
    mixed_grad = jnp.concatenate([query_grad, key_grad, value_grad], 2).astype(jnp.bfloat16)
    heads_grad = jnp.einsum("btd,bte->de", normed, mixed_grad, preferred_element_type=jnp.float32)
    normed_grad = jnp.einsum(
        "bte,de->btd", mixed_grad, attend_heads, preferred_element_type=jnp.float32
    )
    token_grad, attend_gain_grad = norm_back(tokens, attend_gain, normed_grad)
    patch_grad = hidden_grad + token_grad[:, :patch_count]
    block_grads = (
        attend_gain_grad,
        heads_grad,
        merge_grad,
        expand_gain_grad,
        expand_grad,
        shrink_grad,
    )
    return (patch_grad, token_grad[:, patch_count], block_grads)


def shards(
    patches,
    counts,
    captions,
    matches,
    courier,
    courier_gain,
    courier_heads,
    courier_merge,
    attend_gain,
    attend_heads,
    attend_merge,
    expand_gain,
    expand_weight,
    shrink_weight,
    projection,
):
    videos, local_frames, patch_count, width = patches.shape
    frame_total = local_frames * lax.axis_size("dp")
    offset = lax.axis_index("dp") * local_frames
    rows = videos * local_frames
    per_block = rows // MICRO
    courier_full, courier_gain_full, heads_full, merge_full, projection_full = (
        lax.all_gather(courier, "fsdp", axis=0, tiled=True),
        lax.all_gather(courier_gain, "fsdp", axis=0, tiled=True),
        lax.all_gather(courier_heads, "fsdp", axis=0, tiled=True),
        lax.all_gather(courier_merge, "fsdp", axis=0, tiled=True),
        lax.all_gather(projection, "fsdp", axis=0, tiled=True),
    )

    def fetch():
        return (
            lax.all_gather(attend_gain, "fsdp", axis=0, tiled=True),
            lax.all_gather(attend_heads, "fsdp", axis=0, tiled=True),
            lax.all_gather(attend_merge, "fsdp", axis=0, tiled=True),
            lax.all_gather(expand_gain, "fsdp", axis=0, tiled=True),
            lax.all_gather(expand_weight, "fsdp", axis=0, tiled=True),
            lax.all_gather(shrink_weight, "fsdp", axis=0, tiled=True),
        )

    leaders = lax.all_gather(patches[:, :, 0, :], "dp", axis=1, tiled=True)
    present = lax.broadcasted_iota(jnp.int32, (videos, frame_total), 1) < counts[:, None]
    message = jnp.einsum("vfd,de->vfe", leaders, courier_full, preferred_element_type=jnp.float32)
    message_norm = layer_norm(message, courier_gain_full).astype(jnp.bfloat16)
    message_mixed = jnp.einsum(
        "vfd,de->vfe", message_norm, heads_full, preferred_element_type=jnp.float32
    )
    told_queries, told_keys, told_values = split_heads(message_mixed, frame_total)
    told, told_normalizer, told_shares = attend_forward(
        told_queries, told_keys, told_values, present
    )
    message_out = message + jnp.einsum(
        "vfd,de->vfe", told, merge_full, preferred_element_type=jnp.float32
    )
    mine = lax.dynamic_slice_in_dim(message_out, offset, local_frames, 1).reshape(rows, width)
    flat = patches.reshape(rows, patch_count, width)
    frame_weights = fetch()
    kept_blocks = []
    sums = []
    for index in range(MICRO):
        if index > 0:
            frame_weights = fetch()
        start = index * per_block
        frame_sums, kept = frame_forward(
            flat[start : start + per_block], mine[start : start + per_block], frame_weights
        )
        kept_blocks.append(kept)
        sums.append(frame_sums)
    frame_sums = jnp.concatenate(sums, 0).reshape(videos, local_frames, width)
    own_present = lax.dynamic_slice_in_dim(present, offset, local_frames, 1)
    partial_value = jnp.sum(jnp.where(own_present[:, :, None], frame_sums, 0.0), 1)
    pooled_sum = lax.psum(partial_value, "dp")
    denominator = (counts * patch_count).astype(jnp.float32)[:, None]
    pooled = pooled_sum / denominator
    pooled_low = pooled.astype(jnp.bfloat16)
    embed = jnp.dot(pooled_low, projection_full, preferred_element_type=jnp.float32)
    video_unit = unit_rows(embed).astype(jnp.bfloat16)
    segment = lax.axis_index("dp") * (captions.shape[0] * lax.axis_size("fsdp"))

    def scores_for(piece):
        text_unit = unit_rows(piece.astype(jnp.float32)).astype(jnp.bfloat16)
        logits = (
            jnp.einsum("ve,te->vt", video_unit, text_unit, preferred_element_type=jnp.float32)
            * LOGIT_SCALE
        )
        positions = segment + lax.broadcasted_iota(jnp.int32, logits.shape, 1)
        return (text_unit, logits, positions == matches[:, None])

    peak = jnp.full((videos,), -1e30, jnp.float32)
    _, logits, matched = scores_for(lax.all_gather(captions, "fsdp", axis=0, tiled=True))
    fresh = jnp.maximum(peak, jnp.max(logits, 1))
    total = jnp.sum(jnp.exp(logits - fresh[:, None]), 1)
    picked = jnp.sum(jnp.where(matched, logits, 0.0), 1)
    peak, total, picked = (fresh, total, picked)

    def combine(first, second):
        top = jnp.maximum(first[0], second[0])
        joined = first[1] * jnp.exp(first[0] - top) + second[1] * jnp.exp(second[0] - top)
        return (top, joined, first[2] + second[2])

    peak, total, picked = joined_2((peak, total, picked), "dp", combine)
    normalizer = peak + jnp.log(total)
    loss = normalizer - picked
    text_unit, logits, matched = scores_for(lax.all_gather(captions, "fsdp", axis=0, tiled=True))
    slope = (jnp.exp(logits - normalizer[:, None]) - matched.astype(jnp.float32)).astype(
        jnp.bfloat16
    )
    unit_grad = jnp.dot(slope, text_unit, preferred_element_type=jnp.float32) * LOGIT_SCALE
    unit_grad = lax.psum(unit_grad, "dp")
    _, unit_pull = jax.vjp(unit_rows, embed)
    embed_grad = unit_pull(unit_grad)[0].astype(jnp.bfloat16)
    projection_grad = jnp.einsum(
        "vd,ve->de", pooled_low, embed_grad, preferred_element_type=jnp.float32
    )
    pooled_grad = jnp.einsum(
        "ve,de->vd", embed_grad, projection_full, preferred_element_type=jnp.float32
    )
    upstream_all = jnp.where(own_present[:, :, None], (pooled_grad / denominator)[:, None, :], 0.0)
    upstream_all = upstream_all.reshape(rows, width)
    collected = None
    patch_list = []
    message_list = []
    for index in range(MICRO):
        frame_weights = fetch()
        start = index * per_block
        patch_grad, message_token_grad, block_grads = frame_backward(
            kept_blocks[index], upstream_all[start : start + per_block], frame_weights
        )
        patch_list.append(patch_grad)
        message_list.append(message_token_grad)
        block_grads = (
            lax.psum_scatter(
                block_grads[0].astype(jnp.float32), "fsdp", scatter_dimension=0, tiled=True
            ),
            lax.psum_scatter(block_grads[1], "fsdp", scatter_dimension=0, tiled=True),
            lax.psum_scatter(block_grads[2], "fsdp", scatter_dimension=0, tiled=True),
            lax.psum_scatter(
                block_grads[3].astype(jnp.float32), "fsdp", scatter_dimension=0, tiled=True
            ),
            lax.psum_scatter(block_grads[4], "fsdp", scatter_dimension=0, tiled=True),
            lax.psum_scatter(block_grads[5], "fsdp", scatter_dimension=0, tiled=True),
        )
        collected = (
            block_grads if collected is None else jax.tree.map(jnp.add, collected, block_grads)
        )
    collected = (
        lax.psum(collected[0].astype(jnp.bfloat16), "dp").astype(jnp.float32),
        lax.psum(collected[1].astype(jnp.bfloat16), "dp").astype(jnp.float32),
        lax.psum(collected[2].astype(jnp.bfloat16), "dp").astype(jnp.float32),
        lax.psum(collected[3].astype(jnp.bfloat16), "dp").astype(jnp.float32),
        lax.psum(collected[4].astype(jnp.bfloat16), "dp").astype(jnp.float32),
        lax.psum(collected[5].astype(jnp.bfloat16), "dp").astype(jnp.float32),
    )
    message_token_grad = jnp.concatenate(message_list, 0).reshape(videos, local_frames, width)
    out_grad = lax.all_gather(message_token_grad, "dp", axis=1, tiled=True)
    out_low = out_grad.astype(jnp.bfloat16)
    merge_message_grad = jnp.einsum(
        "vfd,vfe->de", told, out_low, preferred_element_type=jnp.float32
    )
    told_grad = jnp.einsum("vfe,de->vfd", out_low, merge_full, preferred_element_type=jnp.float32)
    told_query_grad, told_key_grad, told_value_grad = attend_backward(
        told_queries, told_keys, told_values, present, told_normalizer, told_shares, told_grad
    )
    courier_mixed_grad = jnp.concatenate(
        [told_query_grad, told_key_grad, told_value_grad], 2
    ).astype(jnp.bfloat16)
    heads_message_grad = jnp.einsum(
        "vfd,vfe->de", message_norm, courier_mixed_grad, preferred_element_type=jnp.float32
    )
    message_norm_grad = jnp.einsum(
        "vfe,de->vfd", courier_mixed_grad, heads_full, preferred_element_type=jnp.float32
    )
    message_grad, courier_gain_grad = norm_back(message, courier_gain_full, message_norm_grad)
    message_grad = (message_grad + out_grad).astype(jnp.bfloat16)
    courier_grad = jnp.einsum(
        "vfd,vfe->de", leaders, message_grad, preferred_element_type=jnp.float32
    )
    leader_grad = jnp.einsum(
        "vfe,de->vfd", message_grad, courier_full, preferred_element_type=jnp.float32
    )
    own_leader = lax.dynamic_slice_in_dim(leader_grad, offset, local_frames, 1).reshape(rows, width)
    patch_all = jnp.concatenate(patch_list, 0)
    patch_all = patch_all.at[:, 0, :].add(own_leader)
    patch_out = patch_all.reshape(videos, local_frames, patch_count, width).astype(jnp.bfloat16)
    video_grads = (
        lax.psum_scatter(courier_grad, "fsdp", scatter_dimension=0, tiled=True),
        lax.psum_scatter(
            courier_gain_grad.astype(jnp.float32), "fsdp", scatter_dimension=0, tiled=True
        ),
        lax.psum_scatter(heads_message_grad, "fsdp", scatter_dimension=0, tiled=True),
        lax.psum_scatter(merge_message_grad, "fsdp", scatter_dimension=0, tiled=True),
        lax.psum_scatter(projection_grad, "fsdp", scatter_dimension=0, tiled=True),
    )
    return (
        loss,
        patch_out,
        video_grads[0],
        video_grads[1],
        video_grads[2],
        video_grads[3],
        collected[0],
        collected[1],
        collected[2],
        collected[3],
        collected[4],
        collected[5],
        video_grads[4],
    )


def solution(mesh):
    fitting = mesh.shape['dp'] == 4 and mesh.shape['fsdp'] == Z * Y
    return jax.shard_map(
        fast if fitting else shards,
        mesh=mesh,
        in_specs=(
            P("fsdp", "dp", None, None),
            P("fsdp"),
            P(("dp", "fsdp"), None),
            P("fsdp"),
            P("fsdp", None),
            P("fsdp"),
            P("fsdp", None),
            P("fsdp", None),
            P("fsdp"),
            P("fsdp", None),
            P("fsdp", None),
            P("fsdp"),
            P("fsdp", None),
            P("fsdp", None),
            P("fsdp", None),
        ),
        out_specs=(
            P("fsdp"),
            P("fsdp", "dp", None, None),
            P("fsdp", None),
            P("fsdp"),
            P("fsdp", None),
            P("fsdp", None),
            P("fsdp"),
            P("fsdp", None),
            P("fsdp", None),
            P("fsdp"),
            P("fsdp", None),
            P("fsdp", None),
            P("fsdp", None),
        ),
        check_vma=False,
    )
```
